32 devices in a mesh: groups: 2 (over y), seq: 4 (over z), tp: 4 (over x, core).
Axes of the slice: x: 2, y: 2, z: 4, core: 2. Of those that a mesh axis runs over, the one named last changes fastest.
Arguments:
- lengths: int32 [8], P('groups'), parts along dimension 0, may hold values from 1 to 4096, 8192 in all
- owner_map: int32 [1024], P(('groups', 'seq')), parts along dimension 0, may hold values from 0 to 3, as said below
- row_request: int32 [128], P('groups'), parts along dimension 0, may hold values from 0 to 3
- deltas: bfloat16 [16384, 2, 512], P(('groups', 'seq'), None, 'tp'), parts along dimension 0, may hold values from -6 to 6
- anchors: float32 [1024, 2, 512], P(('groups', 'seq'), None, 'tp'), parts along dimension 0, may hold values from -6 to 6
- scales: float32 [4, 512], P('groups', 'tp'), parts along dimension 0, may hold values from 0.1 to 0.8
- queries: bfloat16 [128, 2, 4096], P('groups', None, 'tp'), parts along dimension 0, may hold values from -200 to 200
- new_kv: bfloat16 [128, 2, 2, 512], P(('groups', 'seq'), None, None, 'tp'), parts along dimension 0, may hold values from -8 to 8
Outputs:
- pages: bfloat16 [1024, 16, 2, 512], P(('groups', 'seq'), None, None, 'tp'), parts along dimension 0
- attended: bfloat16 [128, 2, 4096], P(('groups', 'seq'), None, 'tp'), parts along dimension 0
The draws below stay inside these ranges and needn't reach their ends.
There are 2 independent parts, one for each index of `groups`. The reference program is written for one: setup_inputs(seed, part) draws one part's arguments, and reference() takes and returns one part's arrays. A program takes and returns all parts, laid end to end along the dimension named above; each array names one. Nothing has to cross between parts.
Inputs may be any that keep to these rules, and one draw needn't show every extreme that they name: `owner_map`: the 128 blocks of each prefill owner name every decode owner exactly 32 times.
All inputs are finite; a program needn't handle non-finite values.
Results may differ from the reference program's by a relative error of at most 0.0055.
Values may be sent and summed in bfloat16 or wider, within the bound.
No kernel may reach another device: no remote copies, remote signals or barrier semaphores. Data moves between devices by JAX's collectives and lax.ppermute only.
A program may use at most 128 MiB of HBM per device.

```python
import math
import jax
import jax.numpy as jnp
import numpy as np
from jax import lax

HD = 128
KVH = 4
GQ = 8
BLK = 16
BLK_DEV = 128
REQS = 4
ROWS = 64
CAP = 32
BLOCKS = 512
TOKENS = 8192
QH = 32
N_SEQ = 4


def draw_owner_map(key, part):
    key = jax.random.fold_in(key, 5)
    sender_keys = jax.random.split(key, N_SEQ)
    shuffled = jax.vmap(lambda one_key: jax.random.permutation(one_key, BLK_DEV))(sender_keys)
    return (shuffled // CAP).reshape(-1).astype(jnp.int32)


def draw_queries(key, part):
    key = jax.random.fold_in(key, 7)
    drawn = jax.random.normal(key, (ROWS, 2, QH * HD), jnp.float32)
    return jnp.clip(drawn, -200.0, 200.0).astype(jnp.bfloat16)


def draw_new_kv(key, part):
    key = jax.random.fold_in(key, 3)
    drawn = jax.random.normal(key, (ROWS, 2, 2, KVH * HD), jnp.float32)
    return jnp.clip(drawn, -8.0, 8.0).astype(jnp.bfloat16)


def plant(array, stream_key, least, top_value):
    extent = array.shape
    spot = [jax.random.randint(jax.random.fold_in(stream_key, axis), (), 0, extent[axis]) for axis in range(len(extent))]
    array = array.at[tuple(spot)].set(least)
    longest = extent.index(max(extent))
    spot[longest] = (spot[longest] + 1) % extent[longest]
    return array.at[tuple(spot)].set(top_value)


def levels(own_key, dims, cuts, low, top_value):
    def one(position, blocks):
        steps = jax.random.uniform(jax.random.fold_in(jax.random.fold_in(own_key, 6), position), (blocks,), jnp.float32, low / len(cuts), top_value / len(cuts))
        return jnp.repeat(jnp.exp(steps), dims[position] // blocks).reshape((-1,) + (1,) * (len(dims) - position - 1))

    level = one(*cuts[0])
    for cut in cuts[1:]:
        level = level * one(*cut)
    return level


def split_up(number_of, total, most, lean):
    loads = [(1 << 20) // math.isqrt(standing ** lean) + 1 for standing in range(2, number_of + 1)]
    rest, given = total - most - (number_of - 1), [1] * (number_of - 1)
    while rest > 0:
        candidates = [i for i in range(number_of - 1) if given[i] < most]
        mass, remaining = sum([loads[i] for i in candidates]), rest
        for i in candidates:
            addition = min(most - given[i], max(1, remaining * loads[i] // mass), rest)
            given[i] = given[i] + addition
            rest = rest - addition
    return np.array([most] + given)


def ragged(stream_key, amount, total, reach, skew):
    if amount == 2:
        one = jax.random.randint(stream_key, (), max(1, total - reach), min(reach, total - 1) + 1)
        return jnp.stack([one, total - one])
    sizes = jnp.asarray(split_up(amount, total, reach, skew), jnp.int32)
    pairs = (amount - 1) // 2
    donor, receiver = sizes[1:1 + 2 * pairs:2], sizes[2:2 + 2 * pairs:2]
    margin = jnp.minimum(donor - 1, reach - receiver)
    passed = jax.random.randint(jax.random.fold_in(stream_key, 1), (pairs,), 0, 1 << 20) % (margin + 1)
    sizes = sizes.at[1:1 + 2 * pairs:2].set(donor - passed).at[2:2 + 2 * pairs:2].set(receiver + passed)
    return sizes[jax.random.permutation(jax.random.fold_in(stream_key, 2), amount)]


def normal_values(rng, shape, scale, most, shards=(), kind=jnp.bfloat16):
    array = scale * jax.random.normal(rng, shape, jnp.float32)
    if shards:
        array = array * levels(rng, shape, shards, -0.22, 0.18)
    return jnp.clip(array, -most, most).astype(kind)


def setup_inputs(seed: int = 0, part: int = 0) -> dict:
    streams_of = jax.random.split(jax.random.key(seed), 9)
    part_splits = jax.random.split(jax.random.fold_in(streams_of[8], part), 9)
    return {
        "lengths": ragged(part_splits[0], REQS, TOKENS, TOKENS // 2, 2).astype(jnp.int32),
        "owner_map": draw_owner_map(jax.random.fold_in(jax.random.fold_in(streams_of[8], part), 71), part),
        "row_request": plant(jax.random.randint(part_splits[2], (ROWS,), 0, REQS), jax.random.fold_in(part_splits[2], 1), 0, REQS - 1).astype(jnp.int32),
        "deltas": normal_values(part_splits[3], (TOKENS, 2, KVH * HD), 1.0, 6.0, ((0, 4), (2, 4))),
        "anchors": normal_values(part_splits[4], (BLOCKS, 2, KVH * HD), 1.0, 6.0, ((0, 4), (2, 4)), jnp.float32),
        "scales": jnp.clip(jnp.exp(math.log(0.8) - 2.0794415 * jax.random.uniform(part_splits[5], (2, KVH * HD), jnp.float32) ** levels(part_splits[5], (2, KVH * HD), ((1, 4),), -0.2, 0.2)), 0.1, 0.8),
        "queries": draw_queries(jax.random.fold_in(jax.random.fold_in(streams_of[8], part), 71), part),
        "new_kv": draw_new_kv(jax.random.fold_in(jax.random.fold_in(streams_of[8], part), 71), part),
    }


def reference(lengths, owner_map, row_request, deltas, anchors, scales, queries, new_kv):
    width = KVH * HD
    decoded = (anchors[:, None] + scales * deltas.reshape(BLOCKS, BLK, 2, width).astype(jnp.float32)).astype(jnp.bfloat16)
    owner_table = owner_map.reshape(N_SEQ, BLK_DEV)
    matches = (owner_table[:, :, None] == jnp.arange(N_SEQ, dtype=jnp.int32)[None, None, :]).astype(jnp.int32)
    ranking = jnp.sum((jnp.cumsum(matches, axis=1) - 1) * matches, axis=2)
    senders = jnp.arange(N_SEQ, dtype=jnp.int32)[:, None]
    page_index = (owner_table * BLK_DEV + senders * CAP + ranking).reshape(-1).astype(jnp.int32)
    pages = jnp.zeros_like(decoded).at[page_index].set(decoded)
    request_ends = jnp.cumsum(lengths)
    positions = jnp.arange(TOKENS, dtype=jnp.int32)
    token_req = jnp.sum((positions[:, None] >= request_ends[None, :]).astype(jnp.int32), axis=1)
    cache_rows = decoded.reshape(TOKENS, 2, KVH, HD).astype(jnp.float32)
    key_rows = cache_rows[:, 0]
    value_rows = cache_rows[:, 1]
    factor = HD ** -0.5
    query_all = queries.reshape(ROWS // 4, 4, 2, KVH, GQ, HD)
    own_all = new_kv.reshape(ROWS // 4, 4, 2, 2, KVH, HD)
    req_all = row_request.reshape(ROWS // 4, 4)
    causal = (jnp.arange(2)[None, :] <= jnp.arange(2)[:, None])[None, :, None, None, :]

    def one_block(items):
        query_blk, own_blk, req_blk = items
        query_f = query_blk.astype(jnp.float32)
        own_f = own_blk.astype(jnp.float32)
        scored = jnp.einsum('rsagd,kad->rsagk', query_f, key_rows) * factor
        mask = (req_blk[:, None] == token_req[None, :])[:, None, None, None, :]
        own_scored = jnp.einsum('rsagd,rtad->rsagt', query_f, own_f[:, :, 0]) * factor
        top_cache = jnp.max(jnp.where(mask, scored, -jnp.inf), axis=-1)
        top_own = jnp.max(jnp.where(causal, own_scored, -jnp.inf), axis=-1)
        top_all = jnp.maximum(top_cache, top_own)
        weights = jnp.where(mask, jnp.exp(scored - top_all[..., None]), 0.0)
        own_weights = jnp.where(causal, jnp.exp(own_scored - top_all[..., None]), 0.0)
        total = jnp.sum(weights, axis=-1) + jnp.sum(own_weights, axis=-1)
        low = weights.astype(jnp.bfloat16).astype(jnp.float32)
        own_low = own_weights.astype(jnp.bfloat16).astype(jnp.float32)
        summed = jnp.einsum('rsagk,kad->rsagd', low, value_rows)
        summed = summed + jnp.einsum('rsagt,rtad->rsagd', own_low, own_f[:, :, 1])
        return (summed / total[..., None]).astype(jnp.bfloat16)

    attended = lax.map(one_block, (query_all, own_all, req_all))
    return pages, attended.reshape(ROWS, 2, QH * HD)
```

```python
import functools

import jax
import jax.numpy as jnp
from jax import lax
from jax.experimental import pallas as pl
from jax.experimental.pallas import tpu as pltpu
from jax.sharding import PartitionSpec as P

HD = 128
GQ = 8
STEPS = 2
STAT_ROWS = 16
FAR = -1e30
RATE = HD ** (-0.5) * 1.4426950408889634

VMEM = pl.BlockSpec(memory_space=pltpu.VMEM)
SMEM = pl.BlockSpec(memory_space=pltpu.SMEM)


def place_kernel(capacity, owner_ref, deltas_ref, anchors_ref, scales_ref, out_ref, count_ref):
    blocks = owner_ref.shape[0]
    rows = deltas_ref.shape[0] // blocks
    for owner in range(count_ref.shape[0]):
        count_ref[owner] = owner * capacity
    odd = lax.broadcasted_iota(jnp.int32, (8, HD), 0) % 2 == 1
    scale = jnp.where(odd, scales_ref[1:2, :], scales_ref[0:1, :])[None]

    def one_block(block, carry):
        owner = owner_ref[block]
        slot = count_ref[owner]
        count_ref[owner] = slot + 1
        anchor = jnp.where(
            odd, anchors_ref[pl.ds(2 * block + 1, 1), :], anchors_ref[pl.ds(2 * block, 1), :]
        )[None]
        delta = deltas_ref[pl.ds(block * rows, rows), :].astype(jnp.float32)
        decoded = anchor + scale * delta.reshape(rows // 8, 8, HD)
        out_ref[pl.ds(pl.multiple_of(slot * rows, rows), rows), :] = decoded.reshape(rows, HD).astype(
            jnp.bfloat16
        )
        return carry

    lax.fori_loop(0, blocks, one_block, 0, unroll=4)


def pieces(values):
    high = values.astype(jnp.bfloat16)
    rest = values - high.astype(jnp.float32)
    middle = rest.astype(jnp.bfloat16)
    low = (rest - middle.astype(jnp.float32)).astype(jnp.bfloat16)
    return [high, middle, low]


def attend_kernel(
    position_ref,
    lengths_ref,
    request_ref,
    deltas_ref,
    anchors_ref,
    scales_ref,
    queries_ref,
    mine_ref,
    new_ref,
    out_ref,
    own_ref,
    wide_ref,
    keys_ref,
    values_ref,
    asked_ref,
):
    blocks = anchors_ref.shape[0] // 2
    rows = deltas_ref.shape[0] // blocks
    tokens = rows // 2
    requests = lengths_ref.shape[0]
    asked = queries_ref.shape[0]
    per_row = asked // request_ref.shape[0]
    receivers, _, width = out_ref.shape

    wide_ref[...] = deltas_ref[...].astype(jnp.float32)
    scale_key = scales_ref[0:1, :]
    scale_value = scales_ref[1:2, :]

    def one_block(block, carry):
        here = pl.ds(pl.multiple_of(block * tokens, tokens), tokens)
        key = wide_ref[pl.ds(block * rows, tokens, stride=2), :]
        value = wide_ref[pl.ds(block * rows + 1, tokens, stride=2), :]
        keys_ref[here, 0:HD] = (anchors_ref[pl.ds(2 * block, 1), :] + scale_key * key).astype(jnp.bfloat16)
        values_ref[here, :] = (anchors_ref[pl.ds(2 * block + 1, 1), :] + scale_value * value).astype(
            jnp.bfloat16
        )
        return carry

    lax.fori_loop(0, blocks, one_block, 0, unroll=4)

    lane = lax.broadcasted_iota(jnp.int32, (1, HD), 1)
    first = jnp.zeros((1, HD), jnp.int32)
    last = jnp.zeros((1, HD), jnp.int32)
    end = 0 - position_ref[0]
    for request in range(requests):
        start = end
        end = end + lengths_ref[request]
        first = jnp.where(lane == request, start, first)
        last = jnp.where(lane == request, end, last)
    place = lax.broadcasted_iota(jnp.int32, (blocks * tokens, HD), 0)
    keys_ref[:, HD:] = jnp.where((place >= first) & (place < last), 1.0, 0.0).astype(jnp.bfloat16)

    asked_ref[:, 0:HD] = queries_ref[...]
    wide_lane = lax.broadcasted_iota(jnp.int32, (per_row, HD), 1)

    def one_row(row, carry):
        asked_ref[pl.ds(pl.multiple_of(row * per_row, per_row), per_row), HD:] = jnp.where(
            (wide_lane == request_ref[row]) | (wide_lane >= requests), 0.0, FAR
        ).astype(jnp.bfloat16)
        return carry

    lax.fori_loop(0, request_ref.shape[0], one_row, 0, unroll=4)

    tile = min(256, asked)
    parts = max(1, tile // width)

    def one_tile(index, carry):
        here = asked_ref[pl.ds(pl.multiple_of(index * tile, tile), tile), :]
        scores = lax.dot_general(
            keys_ref[...], here, (((1,), (1,)), ((), ())), preferred_element_type=jnp.float32
        )
        top = jnp.max(scores, axis=0, keepdims=True)
        weights = jnp.exp2((scores - top) * RATE)
        total = jnp.sum(weights, axis=0, keepdims=True)
        summed = lax.dot_general(
            values_ref[...],
            weights.astype(jnp.bfloat16),
            (((0,), (0,)), ((), ())),
            preferred_element_type=jnp.float32,
        )
        stats = pieces(top) + pieces(total)
        stats = jnp.concatenate(
            stats + [jnp.zeros((STAT_ROWS - len(stats), tile), jnp.bfloat16)], axis=0
        )
        both = jnp.concatenate([summed.astype(jnp.bfloat16), stats], axis=0)
        for part in range(parts):
            out_ref[index * parts + part] = both[:, part * width : (part + 1) * width]
        return carry

    lax.fori_loop(0, asked // tile, one_tile, 0)

    fresh = new_ref.shape[0] // 4
    new = new_ref[...].astype(jnp.float32).reshape(fresh, 4, HD)
    mine = mine_ref[...]
    of_row = lax.broadcasted_iota(jnp.int32, (fresh, width), 1) // (GQ * STEPS)
    same = of_row == lax.broadcasted_iota(jnp.int32, (fresh, width), 0)
    step = lax.broadcasted_iota(jnp.int32, (1, width), 1) % STEPS
    own_scores = []
    for which in range(STEPS):
        scored = lax.dot_general(
            new[:, 2 * which, :].astype(jnp.bfloat16),
            mine,
            (((1,), (1,)), ((), ())),
            preferred_element_type=jnp.float32,
        )
        picked = jnp.sum(jnp.where(same, scored, 0.0), axis=0, keepdims=True)
        own_scores.append(jnp.where(step >= which, picked, FAR))
    own_top = jnp.maximum(own_scores[0], own_scores[1])
    own_total = jnp.zeros((1, width), jnp.float32)
    own_summed = jnp.zeros((HD, width), jnp.float32)
    for which in range(STEPS):
        weight = jnp.exp2((own_scores[which] - own_top) * RATE)
        own_total = own_total + weight
        spread = jnp.where(same, weight, 0.0).astype(jnp.bfloat16)
        own_summed = own_summed + lax.dot_general(
            new[:, 2 * which + 1, :].astype(jnp.bfloat16),
            spread,
            (((0,), (0,)), ((), ())),
            preferred_element_type=jnp.float32,
        )
    own_ref[0:HD, :] = own_summed
    own_ref[HD:, :] = jnp.concatenate(
        [own_top, own_total, jnp.zeros((6, width), jnp.float32)], axis=0
    )


def join_kernel(partial_ref, own_ref, out_ref):
    senders = partial_ref.shape[0]
    tops = [own_ref[HD : HD + 1, :]]
    totals = [own_ref[HD + 1 : HD + 2, :]]
    for sender in range(senders):
        stats = partial_ref[sender, HD:, :].astype(jnp.float32)
        tops.append(stats[0:1] + stats[1:2] + stats[2:3])
        totals.append(stats[3:4] + stats[4:5] + stats[5:6])
    top = functools.reduce(jnp.maximum, tops)
    scale = jnp.exp2((tops[0] - top) * RATE)
    total = totals[0] * scale
    summed = own_ref[0:HD, :] * scale
    for sender in range(senders):
        scale = jnp.exp2((tops[sender + 1] - top) * RATE)
        total = total + totals[sender + 1] * scale
        summed = summed + partial_ref[sender, 0:HD, :].astype(jnp.float32) * scale
    out_ref[...] = (summed / total).T.astype(jnp.bfloat16)


def per_device(lengths, owner_map, row_request, deltas, anchors, scales, queries, new_kv):
    blocks = anchors.shape[0]
    tokens = deltas.shape[0]
    senders = lax.axis_size("seq")
    me = lax.axis_index("seq")
    rows, steps, _ = queries.shape
    rows_dev = new_kv.shape[0]
    width = rows_dev * GQ * steps
    limit = pltpu.CompilerParams(vmem_limit_bytes=48 * 1024 * 1024)

    flat_deltas = deltas.reshape(tokens * 2, HD)
    flat_anchors = anchors.reshape(blocks * 2, HD)
    flat_queries = queries.reshape(rows, steps, GQ, HD).transpose(0, 2, 1, 3).reshape(-1, HD)
    flat_new = new_kv.reshape(rows_dev * 4, HD)

    outgoing = pl.pallas_call(
        functools.partial(place_kernel, blocks // senders),
        out_shape=jax.ShapeDtypeStruct(flat_deltas.shape, jnp.bfloat16),
        in_specs=[SMEM, VMEM, VMEM, VMEM],
        out_specs=VMEM,
        scratch_shapes=[pltpu.SMEM((senders,), jnp.int32)],
        compiler_params=limit,
        name="place",
    )(owner_map, flat_deltas, flat_anchors, scales)
    pages = lax.all_to_all(
        outgoing.reshape(blocks, tokens // blocks, 2, HD), "seq", split_axis=0, concat_axis=0, tiled=True
    )

    mine = lax.dynamic_slice_in_dim(flat_queries, me * width, width, 0)
    partial, own = pl.pallas_call(
        attend_kernel,
        out_shape=(
            jax.ShapeDtypeStruct((senders, HD + STAT_ROWS, width), jnp.bfloat16),
            jax.ShapeDtypeStruct((HD + 8, width), jnp.float32),
        ),
        in_specs=[SMEM, SMEM, SMEM] + [VMEM] * 6,
        out_specs=(VMEM, VMEM),
        scratch_shapes=[
            pltpu.VMEM((tokens * 2, HD), jnp.float32),
            pltpu.VMEM((tokens, 2 * HD), jnp.bfloat16),
            pltpu.VMEM((tokens, HD), jnp.bfloat16),
            pltpu.VMEM((rows * GQ * steps, 2 * HD), jnp.bfloat16),
        ],
        compiler_params=limit,
        name="attend",
    )(
        (me * tokens).astype(jnp.int32).reshape(1),
        lengths,
        row_request,
        flat_deltas,
        flat_anchors,
        scales,
        flat_queries,
        mine,
        flat_new,
    )
    received = lax.all_to_all(partial, "seq", split_axis=0, concat_axis=0, tiled=True)
    attended = pl.pallas_call(
        join_kernel,
        out_shape=jax.ShapeDtypeStruct((width, HD), jnp.bfloat16),
        in_specs=[VMEM, VMEM],
        out_specs=VMEM,
        compiler_params=limit,
        name="join",
    )(received, own)
    attended = (
        attended.reshape(rows_dev, GQ, steps, HD).transpose(0, 2, 1, 3).reshape(rows_dev, steps, GQ * HD)
    )
    return pages, attended


def solution(mesh):
    placed = (
        P("groups"),
        P(("groups", "seq")),
        P("groups"),
        P(("groups", "seq"), None, "tp"),
        P(("groups", "seq"), None, "tp"),
        P("groups", "tp"),
        P("groups", None, "tp"),
        P(("groups", "seq"), None, None, "tp"),
    )
    return jax.shard_map(
        per_device,
        mesh=mesh,
        in_specs=placed,
        out_specs=(P(("groups", "seq"), None, None, "tp"), P(("groups", "seq"), None, "tp")),
        check_vma=False,
    )
```

```python
import functools

import jax
import jax.numpy as jnp
from jax import lax
from jax.experimental import pallas as pl
from jax.experimental.pallas import tpu as pltpu
from jax.sharding import PartitionSpec as P

HD = 128
GQ = 8
STEPS = 2
STAT_ROWS = 16
FAR = -1e30
RATE = HD ** (-0.5) * 1.4426950408889634

VMEM = pl.BlockSpec(memory_space=pltpu.VMEM)
SMEM = pl.BlockSpec(memory_space=pltpu.SMEM)


def place_kernel(capacity, owner_ref, deltas_ref, anchors_ref, scales_ref, out_ref, count_ref):
    blocks = owner_ref.shape[0]
    rows = deltas_ref.shape[0] // blocks
    for owner in range(count_ref.shape[0]):
        count_ref[owner] = owner * capacity
    odd = lax.broadcasted_iota(jnp.int32, (8, HD), 0) % 2 == 1
    scale = jnp.where(odd, scales_ref[1:2, :], scales_ref[0:1, :])[None]

    def one_block(block, carry):
        owner = owner_ref[block]
        slot = count_ref[owner]
        count_ref[owner] = slot + 1
        anchor = jnp.where(
            odd, anchors_ref[pl.ds(2 * block + 1, 1), :], anchors_ref[pl.ds(2 * block, 1), :]
        )[None]
        delta = deltas_ref[pl.ds(block * rows, rows), :].astype(jnp.float32)
        decoded = anchor + scale * delta.reshape(rows // 8, 8, HD)
        out_ref[pl.ds(pl.multiple_of(slot * rows, rows), rows), :] = decoded.reshape(rows, HD).astype(
            jnp.bfloat16
        )
        return carry

    lax.fori_loop(0, blocks, one_block, 0, unroll=4)


def pieces(values):
    high = values.astype(jnp.bfloat16)
    rest = values - high.astype(jnp.float32)
    middle = rest.astype(jnp.bfloat16)
    low = (rest - middle.astype(jnp.float32)).astype(jnp.bfloat16)
    return [high, middle, low]


def attend_kernel(
    me_ref,
    lengths_ref,
    request_ref,
    deltas_ref,
    anchors_ref,
    scales_ref,
    queries_ref,
    new_ref,
    out_ref,
    own_ref,
    wide_ref,
    keys_ref,
    values_ref,
    asked_ref,
):
    blocks = anchors_ref.shape[0] // 2
    rows = deltas_ref.shape[0] // blocks
    tokens = rows // 2
    requests = lengths_ref.shape[0]
    asked = queries_ref.shape[0]
    per_row = asked // request_ref.shape[0]
    receivers, _, width = out_ref.shape

    wide_ref[...] = deltas_ref[...].astype(jnp.float32)
    scale_key = scales_ref[0:1, :]
    scale_value = scales_ref[1:2, :]

    def one_block(block, carry):
        here = pl.ds(pl.multiple_of(block * tokens, tokens), tokens)
        key = wide_ref[pl.ds(block * rows, tokens, stride=2), :]
        value = wide_ref[pl.ds(block * rows + 1, tokens, stride=2), :]
        keys_ref[here, 0:HD] = (anchors_ref[pl.ds(2 * block, 1), :] + scale_key * key).astype(jnp.bfloat16)
        values_ref[here, :] = (anchors_ref[pl.ds(2 * block + 1, 1), :] + scale_value * value).astype(
            jnp.bfloat16
        )
        return carry

    lax.fori_loop(0, blocks, one_block, 0, unroll=4)

    lane = lax.broadcasted_iota(jnp.int32, (1, HD), 1)
    first = jnp.zeros((1, HD), jnp.int32)
    last = jnp.zeros((1, HD), jnp.int32)
    end = 0 - me_ref[0] * (blocks * tokens)
    for request in range(requests):
        start = end
        end = end + lengths_ref[request]
        first = jnp.where(lane == request, start, first)
        last = jnp.where(lane == request, end, last)
    place = lax.broadcasted_iota(jnp.int32, (blocks * tokens, HD), 0)
    keys_ref[:, HD:] = jnp.where((place >= first) & (place < last), 1.0, 0.0).astype(jnp.bfloat16)

    asked_ref[:, 0:HD] = queries_ref[...]
    wide_lane = lax.broadcasted_iota(jnp.int32, (per_row, HD), 1)

    def one_row(row, carry):
        asked_ref[pl.ds(pl.multiple_of(row * per_row, per_row), per_row), HD:] = jnp.where(
            (wide_lane == request_ref[row]) | (wide_lane >= requests), 0.0, FAR
        ).astype(jnp.bfloat16)
        return carry

    lax.fori_loop(0, request_ref.shape[0], one_row, 0, unroll=4)

    tile = min(256, asked)
    parts = max(1, tile // width)

    def one_tile(index, carry):
        here = asked_ref[pl.ds(pl.multiple_of(index * tile, tile), tile), :]
        scores = lax.dot_general(
            keys_ref[...], here, (((1,), (1,)), ((), ())), preferred_element_type=jnp.float32
        )
        top = jnp.max(scores, axis=0, keepdims=True)
        weights = jnp.exp2((scores - top) * RATE)
        total = jnp.sum(weights, axis=0, keepdims=True)
        summed = lax.dot_general(
            values_ref[...],
            weights.astype(jnp.bfloat16),
            (((0,), (0,)), ((), ())),
            preferred_element_type=jnp.float32,
        )
        stats = pieces(top) + pieces(total)
        stats = jnp.concatenate(
            stats + [jnp.zeros((STAT_ROWS - len(stats), tile), jnp.bfloat16)], axis=0
        )
        both = jnp.concatenate([summed.astype(jnp.bfloat16), stats], axis=0)
        for part in range(parts):
            out_ref[index * parts + part] = both[:, part * width : (part + 1) * width]
        return carry

    lax.fori_loop(0, asked // tile, one_tile, 0)

    fresh = new_ref.shape[0] // 4
    new = new_ref[...].astype(jnp.float32).reshape(fresh, 4, HD)
    mine = queries_ref[pl.ds(pl.multiple_of(me_ref[0] * width, width), width), :]
    of_row = lax.broadcasted_iota(jnp.int32, (fresh, width), 1) // (GQ * STEPS)
    same = of_row == lax.broadcasted_iota(jnp.int32, (fresh, width), 0)
    step = lax.broadcasted_iota(jnp.int32, (1, width), 1) % STEPS
    own_scores = []
    for which in range(STEPS):
        scored = lax.dot_general(
            new[:, 2 * which, :].astype(jnp.bfloat16),
            mine,
            (((1,), (1,)), ((), ())),
            preferred_element_type=jnp.float32,
        )
        picked = jnp.sum(jnp.where(same, scored, 0.0), axis=0, keepdims=True)
        own_scores.append(jnp.where(step >= which, picked, FAR))
    own_top = jnp.maximum(own_scores[0], own_scores[1])
    own_total = jnp.zeros((1, width), jnp.float32)
    own_summed = jnp.zeros((HD, width), jnp.float32)
    for which in range(STEPS):
        weight = jnp.exp2((own_scores[which] - own_top) * RATE)
        own_total = own_total + weight
        spread = jnp.where(same, weight, 0.0).astype(jnp.bfloat16)
        own_summed = own_summed + lax.dot_general(
            new[:, 2 * which + 1, :].astype(jnp.bfloat16),
            spread,
            (((0,), (0,)), ((), ())),
            preferred_element_type=jnp.float32,
        )
    own_ref[0:HD, :] = own_summed
    own_ref[HD:, :] = jnp.concatenate(
        [own_top, own_total, jnp.zeros((6, width), jnp.float32)], axis=0
    )


def join_kernel(partial_ref, own_ref, out_ref):
    senders = partial_ref.shape[0]
    tops = [own_ref[HD : HD + 1, :]]
    totals = [own_ref[HD + 1 : HD + 2, :]]
    for sender in range(senders):
        stats = partial_ref[sender, HD:, :].astype(jnp.float32)
        tops.append(stats[0:1] + stats[1:2] + stats[2:3])
        totals.append(stats[3:4] + stats[4:5] + stats[5:6])
    top = functools.reduce(jnp.maximum, tops)
    scale = jnp.exp2((tops[0] - top) * RATE)
    total = totals[0] * scale
    summed = own_ref[0:HD, :] * scale
    for sender in range(senders):
        scale = jnp.exp2((tops[sender + 1] - top) * RATE)
        total = total + totals[sender + 1] * scale
        summed = summed + partial_ref[sender, 0:HD, :].astype(jnp.float32) * scale
    out_ref[...] = (summed / total).T.astype(jnp.bfloat16)


def per_device(lengths, owner_map, row_request, deltas, anchors, scales, queries, new_kv):
    blocks = anchors.shape[0]
    tokens = deltas.shape[0]
    senders = lax.axis_size("seq")
    me = lax.axis_index("seq")
    rows, steps, _ = queries.shape
    rows_dev = new_kv.shape[0]
    width = rows_dev * GQ * steps
    limit = pltpu.CompilerParams(vmem_limit_bytes=48 * 1024 * 1024)

    flat_deltas = deltas.reshape(tokens * 2, HD)
    flat_anchors = anchors.reshape(blocks * 2, HD)
    flat_queries = queries.reshape(rows, steps, GQ, HD).transpose(0, 2, 1, 3).reshape(-1, HD)
    flat_new = new_kv.reshape(rows_dev * 4, HD)

    outgoing = pl.pallas_call(
        functools.partial(place_kernel, blocks // senders),
        out_shape=jax.ShapeDtypeStruct(flat_deltas.shape, jnp.bfloat16),
        in_specs=[SMEM, VMEM, VMEM, VMEM],
        out_specs=VMEM,
        scratch_shapes=[pltpu.SMEM((senders,), jnp.int32)],
        compiler_params=limit,
        name="place",
    )(owner_map, flat_deltas, flat_anchors, scales)
    outgoing, late_deltas = lax.optimization_barrier((outgoing, flat_deltas))
    pages = lax.all_to_all(
        outgoing.reshape(blocks, tokens // blocks, 2, HD), "seq", split_axis=0, concat_axis=0, tiled=True
    )
    partial, own = pl.pallas_call(
        attend_kernel,
        out_shape=(
            jax.ShapeDtypeStruct((senders, HD + STAT_ROWS, width), jnp.bfloat16),
            jax.ShapeDtypeStruct((HD + 8, width), jnp.float32),
        ),
        in_specs=[SMEM, SMEM, SMEM] + [VMEM] * 5,
        out_specs=(VMEM, VMEM),
        scratch_shapes=[
            pltpu.VMEM((tokens * 2, HD), jnp.float32),
            pltpu.VMEM((tokens, 2 * HD), jnp.bfloat16),
            pltpu.VMEM((tokens, HD), jnp.bfloat16),
            pltpu.VMEM((rows * GQ * steps, 2 * HD), jnp.bfloat16),
        ],
        compiler_params=limit,
        name="attend",
    )(
        me.astype(jnp.int32).reshape(1),
        lengths,
        row_request,
        late_deltas,
        flat_anchors,
        scales,
        flat_queries,
        flat_new,
    )
    received = lax.all_to_all(partial, "seq", split_axis=0, concat_axis=0, tiled=True)
    attended = pl.pallas_call(
        join_kernel,
        out_shape=jax.ShapeDtypeStruct((width, HD), jnp.bfloat16),
        in_specs=[VMEM, VMEM],
        out_specs=VMEM,
        compiler_params=limit,
        name="join",
    )(received, own)
    attended = (
        attended.reshape(rows_dev, GQ, steps, HD).transpose(0, 2, 1, 3).reshape(rows_dev, steps, GQ * HD)
    )
    return pages, attended


def solution(mesh):
    placed = (
        P("groups"),
        P(("groups", "seq")),
        P("groups"),
        P(("groups", "seq"), None, "tp"),
        P(("groups", "seq"), None, "tp"),
        P("groups", "tp"),
        P("groups", None, "tp"),
        P(("groups", "seq"), None, None, "tp"),
    )
    return jax.shard_map(
        per_device,
        mesh=mesh,
        in_specs=placed,
        out_specs=(P(("groups", "seq"), None, None, "tp"), P(("groups", "seq"), None, "tp")),
        check_vma=False,
    )
```

```python
import functools

import jax
import jax.numpy as jnp
from jax import lax
from jax.experimental import pallas as pl
from jax.experimental.pallas import tpu as pltpu
from jax.sharding import PartitionSpec as P

HD = 128
GQ = 8
STEPS = 2
STAT_ROWS = 16
FAR = -1e30
RATE = HD ** (-0.5) * 1.4426950408889634

VMEM = pl.BlockSpec(memory_space=pltpu.VMEM)
ANY = pl.BlockSpec(memory_space=pl.ANY)
SMEM = pl.BlockSpec(memory_space=pltpu.SMEM)


def partner(me, k, count):
    if count & (count - 1) == 0:
        return me ^ k
    return lax.rem(me + k, count)


def source_of(me, k, count):
    if count & (count - 1) == 0:
        return me ^ k
    return lax.rem(me + count - k, count)


def exchange(sent, count):
    got = []
    for k, message in enumerate(sent, start=1):
        power = count & (count - 1) == 0
        pairs = [(i, i ^ k if power else (i + k) % count) for i in range(count)]
        got.append(lax.ppermute(message, "seq", pairs))
    return got


def place_kernel(owner_any, deltas_any, anchors_any, scales_any, *refs):
    receivers = lax.axis_size("seq")
    me = lax.axis_index("seq")
    sent, pages = refs[: receivers - 1], refs[receivers - 1]
    owner_ref, source_ref, count_ref, deltas_ref, anchors_ref, scales_ref, placed_ref, sems = refs[receivers:]
    blocks = owner_ref.shape[0]
    rows = deltas_ref.shape[0] // blocks
    capacity = blocks // receivers
    loads = [
        pltpu.make_async_copy(source, target, sems.at[index])
        for index, (source, target) in enumerate(
            [
                (owner_any, owner_ref),
                (scales_any, scales_ref),
                (anchors_any, anchors_ref),
                (deltas_any, deltas_ref),
            ]
        )
    ]
    for load in loads:
        load.start()
    for owner in range(receivers):
        count_ref[owner] = owner * capacity
    loads[0].wait()

    def find(block, carry):
        owner = owner_ref[block]
        slot = count_ref[owner]
        count_ref[owner] = slot + 1
        source_ref[slot] = block
        return carry

    lax.fori_loop(0, blocks, find, 0, unroll=8)
    for load in loads[1:]:
        load.wait()
    odd = lax.broadcasted_iota(jnp.int32, (8, HD), 0) % 2 == 1
    scale = jnp.where(odd, scales_ref[1:2, :], scales_ref[0:1, :])[None]
    stores = []
    for k in reversed(range(receivers)):
        first = partner(me, k, receivers) * capacity

        def one_slot(slot, carry, k=k, first=first):
            block = source_ref[first + slot]
            anchor = jnp.where(
                odd, anchors_ref[pl.ds(2 * block + 1, 1), :], anchors_ref[pl.ds(2 * block, 1), :]
            )[None]
            here = pl.ds(pl.multiple_of(block * rows, rows), rows)
            delta = deltas_ref[here, :].astype(jnp.float32)
            decoded = anchor + scale * delta.reshape(rows // 8, 8, HD)
            placed_ref[k, pl.ds(pl.multiple_of(slot * rows, rows), rows), :] = decoded.reshape(
                rows, HD
            ).astype(jnp.bfloat16)
            return carry

        lax.fori_loop(0, capacity, one_slot, 0, unroll=min(8, capacity))
        own = pages.at[pl.ds(pl.multiple_of(me * capacity * rows, capacity * rows), capacity * rows), :]
        store = pltpu.make_async_copy(placed_ref.at[k], sent[k - 1] if k else own, sems.at[4 + k])
        store.start()
        stores.append(store)
    for store in stores:
        store.wait()


def settle_kernel(*refs):
    receivers = lax.axis_size("seq")
    me = lax.axis_index("seq")
    got, pages, sems = refs[1:receivers], refs[receivers], refs[receivers + 1]
    size = got[0].shape[0]
    copies = []
    for k in range(1, receivers):
        first = pl.multiple_of(source_of(me, k, receivers) * size, size)
        copy = pltpu.make_async_copy(got[k - 1], pages.at[pl.ds(first, size), :], sems.at[k - 1])
        copy.start()
        copies.append(copy)
    for copy in copies:
        copy.wait()


def pieces(values):
    high = values.astype(jnp.bfloat16)
    rest = values - high.astype(jnp.float32)
    middle = rest.astype(jnp.bfloat16)
    low = (rest - middle.astype(jnp.float32)).astype(jnp.bfloat16)
    return [high, middle, low]


def attend_kernel(
    lengths_ref,
    request_ref,
    deltas_ref,
    anchors_ref,
    scales_ref,
    queries_ref,
    new_ref,
    *refs,
):
    receivers = lax.axis_size("seq")
    me = lax.axis_index("seq")
    outs = refs[:receivers]
    own_ref, wide_ref, keys_ref, values_ref, asked_ref, out_ref, sems = refs[receivers:]
    blocks = anchors_ref.shape[0] // 2
    rows = deltas_ref.shape[0] // blocks
    tokens = rows // 2
    requests = lengths_ref.shape[0]
    asked = queries_ref.shape[0]
    per_row = asked // request_ref.shape[0]
    width = out_ref.shape[2]

    wide_ref[...] = deltas_ref[...].astype(jnp.float32)
    scale_key = scales_ref[0:1, :]
    scale_value = scales_ref[1:2, :]

    def one_block(block, carry):
        here = pl.ds(pl.multiple_of(block * tokens, tokens), tokens)
        key = wide_ref[pl.ds(block * rows, tokens, stride=2), :]
        value = wide_ref[pl.ds(block * rows + 1, tokens, stride=2), :]
        keys_ref[here, 0:HD] = (anchors_ref[pl.ds(2 * block, 1), :] + scale_key * key).astype(jnp.bfloat16)
        values_ref[here, :] = (anchors_ref[pl.ds(2 * block + 1, 1), :] + scale_value * value).astype(
            jnp.bfloat16
        )
        return carry

    lax.fori_loop(0, blocks, one_block, 0, unroll=4)

    lane = lax.broadcasted_iota(jnp.int32, (1, HD), 1)
    first = jnp.zeros((1, HD), jnp.int32)
    last = jnp.zeros((1, HD), jnp.int32)
    end = 0 - me * (blocks * tokens)
    for request in range(requests):
        start = end
        end = end + lengths_ref[request]
        first = jnp.where(lane == request, start, first)
        last = jnp.where(lane == request, end, last)
    place = lax.broadcasted_iota(jnp.int32, (blocks * tokens, HD), 0)
    keys_ref[:, HD:] = jnp.where((place >= first) & (place < last), 1.0, 0.0).astype(jnp.bfloat16)

    asked_ref[:, 0:HD] = queries_ref[...]
    wide_lane = lax.broadcasted_iota(jnp.int32, (per_row, HD), 1)

    def one_row(row, carry):
        asked_ref[pl.ds(pl.multiple_of(row * per_row, per_row), per_row), HD:] = jnp.where(
            (wide_lane == request_ref[row]) | (wide_lane >= requests), 0.0, FAR
        ).astype(jnp.bfloat16)
        return carry

    lax.fori_loop(0, request_ref.shape[0], one_row, 0, unroll=4)

    tile = min(256, asked)
    parts = max(1, tile // width)

    def one_tile(index, carry):
        here = asked_ref[pl.ds(pl.multiple_of(index * tile, tile), tile), :]
        scores = lax.dot_general(
            keys_ref[...], here, (((1,), (1,)), ((), ())), preferred_element_type=jnp.float32
        )
        top = jnp.max(scores, axis=0, keepdims=True)
        weights = jnp.exp2((scores - top) * RATE)
        total = jnp.sum(weights, axis=0, keepdims=True)
        summed = lax.dot_general(
            values_ref[...],
            weights.astype(jnp.bfloat16),
            (((0,), (0,)), ((), ())),
            preferred_element_type=jnp.float32,
        )
        stats = pieces(top) + pieces(total)
        stats = jnp.concatenate(
            stats + [jnp.zeros((STAT_ROWS - len(stats), tile), jnp.bfloat16)], axis=0
        )
        both = jnp.concatenate([summed.astype(jnp.bfloat16), stats], axis=0)
        for part in range(parts):
            out_ref[index * parts + part] = both[:, part * width : (part + 1) * width]
        return carry

    lax.fori_loop(0, asked // tile, one_tile, 0)

    stores = []
    for k in range(receivers):
        copy = pltpu.make_async_copy(out_ref.at[partner(me, k, receivers)], outs[k], sems.at[k])
        copy.start()
        stores.append(copy)

    fresh = new_ref.shape[0] // 4
    new = new_ref[...].astype(jnp.float32).reshape(fresh, 4, HD)
    mine = queries_ref[pl.ds(pl.multiple_of(me * width, width), width), :]
    of_row = lax.broadcasted_iota(jnp.int32, (fresh, width), 1) // (GQ * STEPS)
    same = of_row == lax.broadcasted_iota(jnp.int32, (fresh, width), 0)
    step = lax.broadcasted_iota(jnp.int32, (1, width), 1) % STEPS
    own_scores = []
    for which in range(STEPS):
        scored = lax.dot_general(
            new[:, 2 * which, :].astype(jnp.bfloat16),
            mine,
            (((1,), (1,)), ((), ())),
            preferred_element_type=jnp.float32,
        )
        picked = jnp.sum(jnp.where(same, scored, 0.0), axis=0, keepdims=True)
        own_scores.append(jnp.where(step >= which, picked, FAR))
    own_top = jnp.maximum(own_scores[0], own_scores[1])
    own_total = jnp.zeros((1, width), jnp.float32)
    own_summed = jnp.zeros((HD, width), jnp.float32)
    for which in range(STEPS):
        weight = jnp.exp2((own_scores[which] - own_top) * RATE)
        own_total = own_total + weight
        spread = jnp.where(same, weight, 0.0).astype(jnp.bfloat16)
        own_summed = own_summed + lax.dot_general(
            new[:, 2 * which + 1, :].astype(jnp.bfloat16),
            spread,
            (((0,), (0,)), ((), ())),
            preferred_element_type=jnp.float32,
        )
    own_ref[0:HD, :] = own_summed
    own_ref[HD:, :] = jnp.concatenate(
        [own_top, own_total, jnp.zeros((6, width), jnp.float32)], axis=0
    )
    for copy in stores:
        copy.wait()


def join_kernel(own_ref, *refs):
    partials, out_ref = refs[:-1], refs[-1]
    tops = [own_ref[HD : HD + 1, :]]
    totals = [own_ref[HD + 1 : HD + 2, :]]
    for partial_ref in partials:
        stats = partial_ref[HD:, :].astype(jnp.float32)
        tops.append(stats[0:1] + stats[1:2] + stats[2:3])
        totals.append(stats[3:4] + stats[4:5] + stats[5:6])
    top = functools.reduce(jnp.maximum, tops)
    scale = jnp.exp2((tops[0] - top) * RATE)
    total = totals[0] * scale
    summed = own_ref[0:HD, :] * scale
    for index, partial_ref in enumerate(partials, start=1):
        scale = jnp.exp2((tops[index] - top) * RATE)
        total = total + totals[index] * scale
        summed = summed + partial_ref[0:HD, :].astype(jnp.float32) * scale
    out_ref[...] = (summed / total).T.astype(jnp.bfloat16)


def per_device(lengths, owner_map, row_request, deltas, anchors, scales, queries, new_kv):
    blocks = anchors.shape[0]
    tokens = deltas.shape[0]
    senders = lax.axis_size("seq")
    me = lax.axis_index("seq")
    rows, steps, _ = queries.shape
    rows_dev = new_kv.shape[0]
    width = rows_dev * GQ * steps
    limit = pltpu.CompilerParams(vmem_limit_bytes=60 * 1024 * 1024)
    small = pltpu.CompilerParams(vmem_limit_bytes=8 * 1024 * 1024)

    flat_deltas = deltas.reshape(tokens * 2, HD)
    flat_anchors = anchors.reshape(blocks * 2, HD)
    flat_queries = queries.reshape(rows, steps, GQ, HD).transpose(0, 2, 1, 3).reshape(-1, HD)
    flat_new = new_kv.reshape(rows_dev * 4, HD)

    hand = jax.ShapeDtypeStruct((tokens * 2 // senders, HD), jnp.bfloat16)
    *sent, pages = pl.pallas_call(
        place_kernel,
        out_shape=[hand] * (senders - 1) + [jax.ShapeDtypeStruct((tokens * 2, HD), jnp.bfloat16)],
        in_specs=[ANY] * 4,
        out_specs=[ANY] * senders,
        scratch_shapes=[
            pltpu.SMEM((blocks,), jnp.int32),
            pltpu.SMEM((blocks,), jnp.int32),
            pltpu.SMEM((senders,), jnp.int32),
            pltpu.VMEM((tokens * 2, HD), jnp.bfloat16),
            pltpu.VMEM((blocks * 2, HD), jnp.float32),
            pltpu.VMEM((2, HD), jnp.float32),
            pltpu.VMEM((senders, tokens * 2 // senders, HD), jnp.bfloat16),
            pltpu.SemaphoreType.DMA((4 + senders,)),
        ],
        compiler_params=limit,
        name="place",
    )(owner_map, flat_deltas, flat_anchors, scales)
    sent, late_deltas = lax.optimization_barrier((sent, flat_deltas))
    got = exchange(sent, senders)

    *partials, own = pl.pallas_call(
        attend_kernel,
        out_shape=[jax.ShapeDtypeStruct((HD + STAT_ROWS, width), jnp.bfloat16)] * senders
        + [jax.ShapeDtypeStruct((HD + 8, width), jnp.float32)],
        in_specs=[SMEM, SMEM] + [VMEM] * 5,
        out_specs=[ANY] * senders + [VMEM],
        scratch_shapes=[
            pltpu.VMEM((tokens * 2, HD), jnp.float32),
            pltpu.VMEM((tokens, 2 * HD), jnp.bfloat16),
            pltpu.VMEM((tokens, HD), jnp.bfloat16),
            pltpu.VMEM((rows * GQ * steps, 2 * HD), jnp.bfloat16),
            pltpu.VMEM((senders, HD + STAT_ROWS, width), jnp.bfloat16),
            pltpu.SemaphoreType.DMA((senders,)),
        ],
        compiler_params=limit,
        cost_estimate=pl.CostEstimate(
            flops=6 * rows * GQ * steps * tokens * HD,
            bytes_accessed=tokens * 4 * HD + rows * GQ * steps * 4 * HD,
            transcendentals=rows * GQ * steps * tokens,
        ),
        name="attend",
    )(lengths, row_request, late_deltas, flat_anchors, scales, flat_queries, flat_new)
    joined = [partials[0]] + exchange(partials[1:], senders)
    attended = pl.pallas_call(
        join_kernel,
        out_shape=jax.ShapeDtypeStruct((width, HD), jnp.bfloat16),
        in_specs=[VMEM] * (senders + 1),
        out_specs=VMEM,
        compiler_params=small,
        name="join",
    )(own, *joined)
    pages = pl.pallas_call(
        settle_kernel,
        out_shape=jax.ShapeDtypeStruct((tokens * 2, HD), jnp.bfloat16),
        in_specs=[ANY] * senders,
        out_specs=ANY,
        scratch_shapes=[pltpu.SemaphoreType.DMA((senders - 1,))],
        input_output_aliases={0: 0},
        compiler_params=small,
        name="settle",
    )(pages, *got)
    pages = pages.reshape(blocks, tokens // blocks, 2, HD)
    attended = (
        attended.reshape(rows_dev, GQ, steps, HD).transpose(0, 2, 1, 3).reshape(rows_dev, steps, GQ * HD)
    )
    return pages, attended


def solution(mesh):
    placed = (
        P("groups"),
        P(("groups", "seq")),
        P("groups"),
        P(("groups", "seq"), None, "tp"),
        P(("groups", "seq"), None, "tp"),
        P("groups", "tp"),
        P("groups", None, "tp"),
        P(("groups", "seq"), None, None, "tp"),
    )
    return jax.shard_map(
        per_device,
        mesh=mesh,
        in_specs=placed,
        out_specs=(P(("groups", "seq"), None, None, "tp"), P(("groups", "seq"), None, "tp")),
        check_vma=False,
    )
```

```python
import functools

import jax
import jax.numpy as jnp
from jax import lax
from jax.experimental import pallas as pl
from jax.experimental.pallas import tpu as pltpu
from jax.sharding import PartitionSpec as P

HD = 128
GQ = 8
STEPS = 2
STAT_ROWS = 16
KEEP_ROWS = 8
FAR = -1e30
RATE = HD ** (-0.5) * 1.4426950408889634

VMEM = pl.BlockSpec(memory_space=pltpu.VMEM)
ANY = pl.BlockSpec(memory_space=pl.ANY)
SMEM = pl.BlockSpec(memory_space=pltpu.SMEM)


def exchange(message, k):
    count = lax.axis_size("seq")
    return lax.ppermute(message, "seq", [(i, i ^ k) for i in range(count)])


def place_kernel(partners, owner_any, deltas_any, anchors_any, scales_any, *refs):
    receivers = lax.axis_size("seq")
    me = lax.axis_index("seq")
    outs = refs[: len(partners)]
    owner_ref, source_ref, count_ref, deltas_ref, anchors_ref, scales_ref, placed_ref, sems = refs[
        len(partners) :
    ]
    blocks = owner_ref.shape[0]
    rows = deltas_ref.shape[0] // blocks
    capacity = blocks // receivers
    loads = [
        pltpu.make_async_copy(source, target, sems.at[index])
        for index, (source, target) in enumerate(
            [
                (owner_any, owner_ref),
                (scales_any, scales_ref),
                (anchors_any, anchors_ref),
                (deltas_any, deltas_ref),
            ]
        )
    ]
    for load in loads:
        load.start()
    if len(partners) > 1:
        for owner in range(receivers):
            count_ref[owner] = owner * capacity
    loads[0].wait()

    def find(block, carry):
        owner = owner_ref[block]
        slot = count_ref[owner]
        count_ref[owner] = slot + 1
        source_ref[slot] = block
        return carry

    def find_one(block, slot):
        source_ref[slot] = block
        return slot + (owner_ref[block] == (me ^ partners[0])).astype(jnp.int32)

    if len(partners) > 1:
        lax.fori_loop(0, blocks, find, 0, unroll=8)
    else:
        lax.fori_loop(0, blocks, find_one, 0, unroll=8)
    for load in loads[1:]:
        load.wait()
    odd = lax.broadcasted_iota(jnp.int32, (8, HD), 0) % 2 == 1
    scale = jnp.where(odd, scales_ref[1:2, :], scales_ref[0:1, :])[None]
    stores = []
    for index, k in enumerate(partners):
        first = (me ^ k) * capacity if len(partners) > 1 else 0

        def one_slot(slot, carry, index=index, first=first):
            block = source_ref[first + slot]
            anchor = jnp.where(
                odd, anchors_ref[pl.ds(2 * block + 1, 1), :], anchors_ref[pl.ds(2 * block, 1), :]
            )[None]
            here = pl.ds(pl.multiple_of(block * rows, rows), rows)
            delta = deltas_ref[here, :].astype(jnp.float32)
            decoded = anchor + scale * delta.reshape(rows // 8, 8, HD)
            placed_ref[index, pl.ds(pl.multiple_of(slot * rows, rows), rows), :] = decoded.reshape(
                rows, HD
            ).astype(jnp.bfloat16)
            return carry

        lax.fori_loop(0, capacity, one_slot, 0, unroll=min(8, capacity))
        size = capacity * rows
        target = outs[index] if k else outs[index].at[pl.ds(pl.multiple_of(me * size, size), size), :]
        store = pltpu.make_async_copy(placed_ref.at[index], target, sems.at[4 + index])
        store.start()
        stores.append(store)
    for store in stores:
        store.wait()


def settle_kernel(*refs):
    receivers = lax.axis_size("seq")
    me = lax.axis_index("seq")
    got, pages, sems = refs[1:receivers], refs[receivers], refs[receivers + 1]
    size = got[0].shape[0]
    copies = []
    for k in range(1, receivers):
        first = pl.multiple_of((me ^ k) * size, size)
        copy = pltpu.make_async_copy(got[k - 1], pages.at[pl.ds(first, size), :], sems.at[k - 1])
        copy.start()
        copies.append(copy)
    for copy in copies:
        copy.wait()


def pieces(values):
    high = values.astype(jnp.bfloat16)
    rest = values - high.astype(jnp.float32)
    middle = rest.astype(jnp.bfloat16)
    low = (rest - middle.astype(jnp.float32)).astype(jnp.bfloat16)
    return [high, middle, low]


def packed(partial):
    summed, top, total = partial
    stats = pieces(top) + pieces(total)
    rest = jnp.zeros((STAT_ROWS - len(stats), top.shape[1]), jnp.bfloat16)
    return jnp.concatenate([summed.astype(jnp.bfloat16)] + stats + [rest], axis=0)


def unpacked(block):
    stats = block[HD:, :].astype(jnp.float32)
    top = stats[0:1] + stats[1:2] + stats[2:3]
    total = stats[3:4] + stats[4:5] + stats[5:6]
    return block[0:HD, :].astype(jnp.float32), top, total


def held(partial):
    summed, top, total = partial
    rest = jnp.zeros((KEEP_ROWS - 2, top.shape[1]), jnp.float32)
    return jnp.concatenate([summed, top, total, rest], axis=0)


def taken(block):
    return block[0:HD, :], block[HD : HD + 1, :], block[HD + 1 : HD + 2, :]


def joined(one, other):
    top = jnp.maximum(one[1], other[1])
    scale_one = jnp.exp2((one[1] - top) * RATE)
    scale_other = jnp.exp2((other[1] - top) * RATE)
    return (
        one[0] * scale_one + other[0] * scale_other,
        top,
        one[2] * scale_one + other[2] * scale_other,
    )


def attend_kernel(
    lengths_ref,
    request_ref,
    deltas_ref,
    anchors_ref,
    scales_ref,
    queries_ref,
    new_ref,
    *refs,
):
    me = lax.axis_index("seq")
    send_ref, keep_ref, wide_ref, keys_ref, values_ref, asked_ref = refs
    blocks = anchors_ref.shape[0] // 2
    rows = deltas_ref.shape[0] // blocks
    tokens = rows // 2
    requests = lengths_ref.shape[0]
    asked = queries_ref.shape[0]
    per_row = asked // request_ref.shape[0]
    width = keep_ref.shape[2]

    wide_ref[...] = deltas_ref[...].astype(jnp.float32)
    scale_key = scales_ref[0:1, :]
    scale_value = scales_ref[1:2, :]

    def one_block(block, carry):
        here = pl.ds(pl.multiple_of(block * tokens, tokens), tokens)
        key = wide_ref[pl.ds(block * rows, tokens, stride=2), :]
        value = wide_ref[pl.ds(block * rows + 1, tokens, stride=2), :]
        keys_ref[here, 0:HD] = (anchors_ref[pl.ds(2 * block, 1), :] + scale_key * key).astype(jnp.bfloat16)
        values_ref[here, :] = (anchors_ref[pl.ds(2 * block + 1, 1), :] + scale_value * value).astype(
            jnp.bfloat16
        )
        return carry

    lax.fori_loop(0, blocks, one_block, 0, unroll=4)

    lane = lax.broadcasted_iota(jnp.int32, (1, HD), 1)
    first = jnp.zeros((1, HD), jnp.int32)
    last = jnp.zeros((1, HD), jnp.int32)
    end = 0 - me * (blocks * tokens)
    for request in range(requests):
        start = end
        end = end + lengths_ref[request]
        first = jnp.where(lane == request, start, first)
        last = jnp.where(lane == request, end, last)
    place = lax.broadcasted_iota(jnp.int32, (blocks * tokens, HD), 0)
    keys_ref[:, HD:] = jnp.where((place >= first) & (place < last), 1.0, 0.0).astype(jnp.bfloat16)

    asked_ref[:, 0:HD] = queries_ref[...]
    wide_lane = lax.broadcasted_iota(jnp.int32, (per_row, HD), 1)

    def one_row(row, carry):
        asked_ref[pl.ds(pl.multiple_of(row * per_row, per_row), per_row), HD:] = jnp.where(
            (wide_lane == request_ref[row]) | (wide_lane >= requests), 0.0, FAR
        ).astype(jnp.bfloat16)
        return carry

    lax.fori_loop(0, request_ref.shape[0], one_row, 0, unroll=4)

    tile = min(256, asked)
    parts = max(1, tile // width)

    def one_tile(index, carry):
        here = asked_ref[pl.ds(pl.multiple_of(index * tile, tile), tile), :]
        scores = lax.dot_general(
            keys_ref[...], here, (((1,), (1,)), ((), ())), preferred_element_type=jnp.float32
        )
        top = jnp.max(scores, axis=0, keepdims=True)
        weights = jnp.exp2((scores - top) * RATE)
        total = jnp.sum(weights, axis=0, keepdims=True)
        summed = lax.dot_general(
            values_ref[...],
            weights.astype(jnp.bfloat16),
            (((0,), (0,)), ((), ())),
            preferred_element_type=jnp.float32,
        )
        for part in range(parts):
            lanes = slice(part * width, (part + 1) * width)
            partial = summed[:, lanes], top[:, lanes], total[:, lanes]
            apart = (index * parts + part) ^ me

            @pl.when(apart % 2 == 1)
            def _(partial=partial, apart=apart):
                send_ref[apart // 2] = packed(partial)

            @pl.when(apart % 2 == 0)
            def _(partial=partial, apart=apart):
                keep_ref[apart // 2] = held(partial)

        return carry

    lax.fori_loop(0, asked // tile, one_tile, 0)

    fresh = new_ref.shape[0] // 4
    new = new_ref[...].astype(jnp.float32).reshape(fresh, 4, HD)
    mine = queries_ref[pl.ds(pl.multiple_of(me * width, width), width), :]
    of_row = lax.broadcasted_iota(jnp.int32, (fresh, width), 1) // (GQ * STEPS)
    same = of_row == lax.broadcasted_iota(jnp.int32, (fresh, width), 0)
    step = lax.broadcasted_iota(jnp.int32, (1, width), 1) % STEPS
    own_scores = []
    for which in range(STEPS):
        scored = lax.dot_general(
            new[:, 2 * which, :].astype(jnp.bfloat16),
            mine,
            (((1,), (1,)), ((), ())),
            preferred_element_type=jnp.float32,
        )
        picked = jnp.sum(jnp.where(same, scored, 0.0), axis=0, keepdims=True)
        own_scores.append(jnp.where(step >= which, picked, FAR))
    own_top = jnp.maximum(own_scores[0], own_scores[1])
    own_total = jnp.zeros((1, width), jnp.float32)
    own_summed = jnp.zeros((HD, width), jnp.float32)
    for which in range(STEPS):
        weight = jnp.exp2((own_scores[which] - own_top) * RATE)
        own_total = own_total + weight
        spread = jnp.where(same, weight, 0.0).astype(jnp.bfloat16)
        own_summed = own_summed + lax.dot_general(
            new[:, 2 * which + 1, :].astype(jnp.bfloat16),
            spread,
            (((0,), (0,)), ((), ())),
            preferred_element_type=jnp.float32,
        )
    keep_ref[0] = held(joined(taken(keep_ref[0]), (own_summed, own_top, own_total)))


def join_kernel(keep_ref, got_ref, send_ref, next_ref):
    for index in range(keep_ref.shape[0]):
        partial = joined(taken(keep_ref[index]), unpacked(got_ref[index]))
        if index % 2 == 1:
            send_ref[index // 2] = packed(partial)
        else:
            next_ref[index // 2] = held(partial)


def finish_kernel(keep_ref, got_ref, out_ref):
    summed, _, total = joined(taken(keep_ref[0]), unpacked(got_ref[0]))
    out_ref[...] = (summed / total).T.astype(jnp.bfloat16)


def per_device(lengths, owner_map, row_request, deltas, anchors, scales, queries, new_kv):
    blocks = anchors.shape[0]
    tokens = deltas.shape[0]
    senders = lax.axis_size("seq")
    me = lax.axis_index("seq")
    rows, steps, _ = queries.shape
    rows_dev = new_kv.shape[0]
    width = rows_dev * GQ * steps
    limit = pltpu.CompilerParams(vmem_limit_bytes=60 * 1024 * 1024)
    small = pltpu.CompilerParams(vmem_limit_bytes=8 * 1024 * 1024)

    flat_deltas = deltas.reshape(tokens * 2, HD)
    flat_anchors = anchors.reshape(blocks * 2, HD)
    flat_queries = queries.reshape(rows, steps, GQ, HD).transpose(0, 2, 1, 3).reshape(-1, HD)
    flat_new = new_kv.reshape(rows_dev * 4, HD)

    hand = jax.ShapeDtypeStruct((tokens * 2 // senders, HD), jnp.bfloat16)
    whole = jax.ShapeDtypeStruct((tokens * 2, HD), jnp.bfloat16)

    def place(partners, deltas):
        return pl.pallas_call(
            functools.partial(place_kernel, partners),
            out_shape=[hand if k else whole for k in partners],
            in_specs=[ANY] * 4,
            out_specs=[ANY] * len(partners),
            scratch_shapes=[
                pltpu.SMEM((blocks,), jnp.int32),
                pltpu.SMEM((blocks,), jnp.int32),
                pltpu.SMEM((senders,), jnp.int32),
                pltpu.VMEM((tokens * 2, HD), jnp.bfloat16),
                pltpu.VMEM((blocks * 2, HD), jnp.float32),
                pltpu.VMEM((2, HD), jnp.float32),
                pltpu.VMEM((len(partners),) + hand.shape, jnp.bfloat16),
                pltpu.SemaphoreType.DMA((4 + len(partners),)),
            ],
            compiler_params=limit,
            name="place",
        )(owner_map, deltas, flat_anchors, scales)

    (farthest,) = place([senders - 1], flat_deltas)
    farthest, late_deltas = lax.optimization_barrier((farthest, flat_deltas))
    got = [exchange(farthest, senders - 1)]
    *sent, pages = place(list(reversed(range(senders - 1))), late_deltas)
    sent, late_deltas = lax.optimization_barrier((sent, late_deltas))
    for k, message in zip(reversed(range(1, senders - 1)), sent):
        got.append(exchange(message, k))
    got.reverse()

    def parted(count):
        return [
            jax.ShapeDtypeStruct((count // 2, HD + STAT_ROWS, width), jnp.bfloat16),
            jax.ShapeDtypeStruct((count // 2, HD + KEEP_ROWS, width), jnp.float32),
        ]

    send, keep = pl.pallas_call(
        attend_kernel,
        out_shape=parted(senders),
        in_specs=[SMEM, SMEM] + [VMEM] * 5,
        out_specs=[VMEM] * 2,
        scratch_shapes=[
            pltpu.VMEM((tokens * 2, HD), jnp.float32),
            pltpu.VMEM((tokens, 2 * HD), jnp.bfloat16),
            pltpu.VMEM((tokens, HD), jnp.bfloat16),
            pltpu.VMEM((rows * GQ * steps, 2 * HD), jnp.bfloat16),
        ],
        compiler_params=pltpu.CompilerParams(vmem_limit_bytes=32 * 1024 * 1024),
        cost_estimate=pl.CostEstimate(
            flops=6 * rows * GQ * steps * tokens * HD,
            bytes_accessed=tokens * 4 * HD + rows * GQ * steps * 4 * HD,
            transcendentals=rows * GQ * steps * tokens,
        ),
        name="attend",
    )(lengths, row_request, late_deltas, flat_anchors, scales, flat_queries, flat_new)

    k, count = 1, senders // 2
    while count > 1:
        send, keep = pl.pallas_call(
            join_kernel,
            out_shape=parted(count),
            in_specs=[VMEM] * 2,
            out_specs=[VMEM] * 2,
            compiler_params=small,
            name="join",
        )(keep, exchange(send, k))
        k, count = 2 * k, count // 2
    attended = pl.pallas_call(
        finish_kernel,
        out_shape=jax.ShapeDtypeStruct((width, HD), jnp.bfloat16),
        in_specs=[VMEM] * 2,
        out_specs=VMEM,
        compiler_params=small,
        name="finish",
    )(keep, exchange(send, k))
    pages = pl.pallas_call(
        settle_kernel,
        out_shape=whole,
        in_specs=[ANY] * senders,
        out_specs=ANY,
        scratch_shapes=[pltpu.SemaphoreType.DMA((senders - 1,))],
        input_output_aliases={0: 0},
        compiler_params=small,
        name="settle",
    )(pages, *got)
    pages = pages.reshape(blocks, tokens // blocks, 2, HD)
    attended = (
        attended.reshape(rows_dev, GQ, steps, HD).transpose(0, 2, 1, 3).reshape(rows_dev, steps, GQ * HD)
    )
    return pages, attended


def solution(mesh):
    placed = (
        P("groups"),
        P(("groups", "seq")),
        P("groups"),
        P(("groups", "seq"), None, "tp"),
        P(("groups", "seq"), None, "tp"),
        P("groups", "tp"),
        P("groups", None, "tp"),
        P(("groups", "seq"), None, None, "tp"),
    )
    return jax.shard_map(
        per_device,
        mesh=mesh,
        in_specs=placed,
        out_specs=(P(("groups", "seq"), None, None, "tp"), P(("groups", "seq"), None, "tp")),
        check_vma=False,
    )
```

```python
import functools

import jax
import jax.numpy as jnp
from jax import lax
from jax.experimental import pallas as pl
from jax.experimental.pallas import tpu as pltpu
from jax.sharding import PartitionSpec as P

HD = 128
GQ = 8
STEPS = 2
STAT_ROWS = 16
KEEP_ROWS = 8
FAR = -1e30
RATE = HD ** (-0.5) * 1.4426950408889634

VMEM = pl.BlockSpec(memory_space=pltpu.VMEM)
HBM = pl.BlockSpec(memory_space=pltpu.HBM)
ANY = pl.BlockSpec(memory_space=pl.ANY)
SMEM = pl.BlockSpec(memory_space=pltpu.SMEM)


def exchange(message, k):
    count = lax.axis_size("seq")
    return lax.ppermute(message, "seq", [(i, i ^ k) for i in range(count)])


def place_kernel(owner_any, deltas_any, anchors_any, scales_any, *refs):
    receivers = lax.axis_size("seq")
    me = lax.axis_index("seq")
    outs = refs[:receivers]
    owner_ref, source_ref, count_ref, deltas_ref, anchors_ref, scales_ref, sems = refs[receivers:]
    blocks = owner_ref.shape[0]
    rows = deltas_ref.shape[0] // blocks
    capacity = blocks // receivers
    loads = [
        pltpu.make_async_copy(source, target, sems.at[index])
        for index, (source, target) in enumerate(
            [
                (owner_any, owner_ref),
                (scales_any, scales_ref),
                (anchors_any, anchors_ref),
                (deltas_any, deltas_ref),
            ]
        )
    ]
    for load in loads:
        load.start()
    bits = capacity.bit_length()
    narrow = receivers * bits < 32
    if not narrow:
        for owner in range(receivers):
            count_ref[owner] = owner * capacity
    loads[0].wait()

    def find(block, counts):
        owner = owner_ref[block]
        if narrow:
            shift = owner * bits
            slot = owner * capacity + ((counts >> shift) & ((1 << bits) - 1))
            counts = counts + (jnp.int32(1) << shift)
        else:
            slot = count_ref[owner]
            count_ref[owner] = slot + 1
        source_ref[slot] = block
        return counts

    lax.fori_loop(0, blocks, find, jnp.int32(0), unroll=8)
    for load in loads[1:]:
        load.wait()
    odd = lax.broadcasted_iota(jnp.int32, (8, HD), 0) % 2 == 1
    scale = jnp.where(odd, scales_ref[1:2, :], scales_ref[0:1, :])[None]
    for k, out_ref in zip(reversed(range(receivers)), outs):
        first = (me ^ k) * capacity

        def one_slot(slot, carry, first=first, out_ref=out_ref):
            block = source_ref[first + slot]
            anchor = jnp.where(
                odd, anchors_ref[pl.ds(2 * block + 1, 1), :], anchors_ref[pl.ds(2 * block, 1), :]
            )[None]
            here = pl.ds(pl.multiple_of(block * rows, rows), rows)
            delta = deltas_ref[here, :].astype(jnp.float32)
            decoded = anchor + scale * delta.reshape(rows // 8, 8, HD)
            out_ref[pl.ds(pl.multiple_of(slot * rows, rows), rows), :] = decoded.reshape(rows, HD).astype(
                jnp.bfloat16
            )
            return carry

        lax.fori_loop(0, capacity, one_slot, 0, unroll=min(8, capacity))


def settle_kernel(*refs):
    receivers = lax.axis_size("seq")
    me = lax.axis_index("seq")
    got, pages, sems = refs[1:receivers], refs[receivers], refs[receivers + 1]
    size = got[0].shape[0]
    copies = []
    for k in range(1, receivers):
        first = pl.multiple_of((me ^ k) * size, size)
        copy = pltpu.make_async_copy(got[-k], pages.at[pl.ds(first, size), :], sems.at[k - 1])
        copy.start()
        copies.append(copy)
    for copy in copies:
        copy.wait()


def pieces(values):
    high = values.astype(jnp.bfloat16)
    rest = values - high.astype(jnp.float32)
    middle = rest.astype(jnp.bfloat16)
    low = (rest - middle.astype(jnp.float32)).astype(jnp.bfloat16)
    return [high, middle, low]


def packed(partial):
    summed, top, total = partial
    stats = pieces(top) + pieces(total)
    rest = jnp.zeros((STAT_ROWS - len(stats), top.shape[1]), jnp.bfloat16)
    return jnp.concatenate([summed.astype(jnp.bfloat16)] + stats + [rest], axis=0)


def unpacked(block):
    stats = block[HD:, :].astype(jnp.float32)
    top = stats[0:1] + stats[1:2] + stats[2:3]
    total = stats[3:4] + stats[4:5] + stats[5:6]
    return block[0:HD, :].astype(jnp.float32), top, total


def held(partial):
    summed, top, total = partial
    rest = jnp.zeros((KEEP_ROWS - 2, top.shape[1]), jnp.float32)
    return jnp.concatenate([summed, top, total, rest], axis=0)


def taken(block):
    return block[0:HD, :], block[HD : HD + 1, :], block[HD + 1 : HD + 2, :]


def joined(one, other):
    top = jnp.maximum(one[1], other[1])
    scale_one = jnp.exp2((one[1] - top) * RATE)
    scale_other = jnp.exp2((other[1] - top) * RATE)
    return (
        one[0] * scale_one + other[0] * scale_other,
        top,
        one[2] * scale_one + other[2] * scale_other,
    )


def attend_kernel(
    lengths_ref,
    request_ref,
    deltas_ref,
    anchors_ref,
    scales_ref,
    queries_ref,
    new_ref,
    mine_any,
    *refs,
):
    me = lax.axis_index("seq")
    send_ref, keep_ref, pages_any, wide_ref, keys_ref, values_ref, asked_ref, sem = refs
    size = mine_any.shape[0]
    own_pages = pltpu.make_async_copy(
        mine_any, pages_any.at[pl.ds(pl.multiple_of(me * size, size), size), :], sem
    )
    own_pages.start()
    blocks = anchors_ref.shape[0] // 2
    rows = deltas_ref.shape[0] // blocks
    tokens = rows // 2
    requests = lengths_ref.shape[0]
    asked = queries_ref.shape[0]
    per_row = asked // request_ref.shape[0]
    width = keep_ref.shape[2]

    wide_ref[...] = deltas_ref[...].astype(jnp.float32)
    scale_key = scales_ref[0:1, :]
    scale_value = scales_ref[1:2, :]

    def one_block(block, carry):
        here = pl.ds(pl.multiple_of(block * tokens, tokens), tokens)
        key = wide_ref[pl.ds(block * rows, tokens, stride=2), :]
        value = wide_ref[pl.ds(block * rows + 1, tokens, stride=2), :]
        keys_ref[here, 0:HD] = (anchors_ref[pl.ds(2 * block, 1), :] + scale_key * key).astype(jnp.bfloat16)
        values_ref[here, :] = (anchors_ref[pl.ds(2 * block + 1, 1), :] + scale_value * value).astype(
            jnp.bfloat16
        )
        return carry

    lax.fori_loop(0, blocks, one_block, 0, unroll=4)

    lane = lax.broadcasted_iota(jnp.int32, (1, HD), 1)
    first = jnp.zeros((1, HD), jnp.int32)
    last = jnp.zeros((1, HD), jnp.int32)
    end = 0 - me * (blocks * tokens)
    for request in range(requests):
        start = end
        end = end + lengths_ref[request]
        first = jnp.where(lane == request, start, first)
        last = jnp.where(lane == request, end, last)
    place = lax.broadcasted_iota(jnp.int32, (blocks * tokens, HD), 0)
    keys_ref[:, HD:] = jnp.where((place >= first) & (place < last), 1.0, 0.0).astype(jnp.bfloat16)

    asked_ref[:, 0:HD] = queries_ref[...]
    wide_lane = lax.broadcasted_iota(jnp.int32, (per_row, HD), 1)

    def one_row(row, carry):
        asked_ref[pl.ds(pl.multiple_of(row * per_row, per_row), per_row), HD:] = jnp.where(
            (wide_lane == request_ref[row]) | (wide_lane >= requests), 0.0, FAR
        ).astype(jnp.bfloat16)
        return carry

    lax.fori_loop(0, request_ref.shape[0], one_row, 0, unroll=4)

    tile = min(256, asked)
    parts = max(1, tile // width)

    def one_tile(index, carry):
        here = asked_ref[pl.ds(pl.multiple_of(index * tile, tile), tile), :]
        scores = lax.dot_general(
            keys_ref[...], here, (((1,), (1,)), ((), ())), preferred_element_type=jnp.float32
        )
        top = jnp.max(scores, axis=0, keepdims=True)
        weights = jnp.exp2((scores - top) * RATE)
        total = jnp.sum(weights, axis=0, keepdims=True)
        summed = lax.dot_general(
            values_ref[...],
            weights.astype(jnp.bfloat16),
            (((0,), (0,)), ((), ())),
            preferred_element_type=jnp.float32,
        )
        for part in range(parts):
            lanes = slice(part * width, (part + 1) * width)
            partial = summed[:, lanes], top[:, lanes], total[:, lanes]
            apart = (index * parts + part) ^ me

            @pl.when(apart % 2 == 1)
            def _(partial=partial, apart=apart):
                send_ref[apart // 2] = packed(partial)

            @pl.when(apart % 2 == 0)
            def _(partial=partial, apart=apart):
                keep_ref[apart // 2] = held(partial)

        return carry

    lax.fori_loop(0, asked // tile, one_tile, 0)

    fresh = new_ref.shape[0] // 4
    new = new_ref[...].astype(jnp.float32).reshape(fresh, 4, HD)
    mine = queries_ref[pl.ds(pl.multiple_of(me * width, width), width), :]
    of_row = lax.broadcasted_iota(jnp.int32, (fresh, width), 1) // (GQ * STEPS)
    same = of_row == lax.broadcasted_iota(jnp.int32, (fresh, width), 0)
    step = lax.broadcasted_iota(jnp.int32, (1, width), 1) % STEPS
    own_scores = []
    for which in range(STEPS):
        scored = lax.dot_general(
            new[:, 2 * which, :].astype(jnp.bfloat16),
            mine,
            (((1,), (1,)), ((), ())),
            preferred_element_type=jnp.float32,
        )
        picked = jnp.sum(jnp.where(same, scored, 0.0), axis=0, keepdims=True)
        own_scores.append(jnp.where(step >= which, picked, FAR))
    own_top = jnp.maximum(own_scores[0], own_scores[1])
    own_total = jnp.zeros((1, width), jnp.float32)
    own_summed = jnp.zeros((HD, width), jnp.float32)
    for which in range(STEPS):
        weight = jnp.exp2((own_scores[which] - own_top) * RATE)
        own_total = own_total + weight
        spread = jnp.where(same, weight, 0.0).astype(jnp.bfloat16)
        own_summed = own_summed + lax.dot_general(
            new[:, 2 * which + 1, :].astype(jnp.bfloat16),
            spread,
            (((0,), (0,)), ((), ())),
            preferred_element_type=jnp.float32,
        )
    keep_ref[0] = held(joined(taken(keep_ref[0]), (own_summed, own_top, own_total)))
    own_pages.wait()


def join_kernel(keep_ref, got_ref, send_ref, next_ref):
    for index in range(keep_ref.shape[0]):
        partial = joined(taken(keep_ref[index]), unpacked(got_ref[index]))
        if index % 2 == 1:
            send_ref[index // 2] = packed(partial)
        else:
            next_ref[index // 2] = held(partial)


def finish_kernel(keep_ref, got_ref, out_ref):
    summed, _, total = joined(taken(keep_ref[0]), unpacked(got_ref[0]))
    out_ref[...] = (summed / total).T.astype(jnp.bfloat16)


def per_device(lengths, owner_map, row_request, deltas, anchors, scales, queries, new_kv):
    blocks = anchors.shape[0]
    tokens = deltas.shape[0]
    senders = lax.axis_size("seq")
    me = lax.axis_index("seq")
    rows, steps, _ = queries.shape
    rows_dev = new_kv.shape[0]
    width = rows_dev * GQ * steps
    small = pltpu.CompilerParams(vmem_limit_bytes=8 * 1024 * 1024)

    flat_deltas = deltas.reshape(tokens * 2, HD)
    flat_anchors = anchors.reshape(blocks * 2, HD)
    flat_queries = queries.reshape(rows, steps, GQ, HD).transpose(0, 2, 1, 3).reshape(-1, HD)
    flat_new = new_kv.reshape(rows_dev * 4, HD)

    hand = jax.ShapeDtypeStruct((tokens * 2 // senders, HD), jnp.bfloat16)
    whole = jax.ShapeDtypeStruct((tokens * 2, HD), jnp.bfloat16)

    *sent, mine = pl.pallas_call(
        place_kernel,
        out_shape=[hand] * senders,
        in_specs=[HBM] * 4,
        out_specs=[VMEM] * senders,
        scratch_shapes=[
            pltpu.SMEM((blocks,), jnp.int32),
            pltpu.SMEM((blocks,), jnp.int32),
            pltpu.SMEM((senders,), jnp.int32),
            pltpu.VMEM((tokens * 2, HD), jnp.bfloat16),
            pltpu.VMEM((blocks * 2, HD), jnp.float32),
            pltpu.VMEM((2, HD), jnp.float32),
            pltpu.SemaphoreType.DMA((4,)),
        ],
        compiler_params=small,
        name="place",
    )(*[pltpu.with_memory_space_constraint(x, pltpu.HBM) for x in (owner_map, flat_deltas, flat_anchors, scales)])
    sent = [mine] + sent[::-1]

    got = [None] * senders
    sent, mine, late_deltas = lax.optimization_barrier((sent, mine, flat_deltas))
    for k in reversed(range(1, senders)):
        got[k] = exchange(sent[k], k)

    def parted(count):
        return [
            jax.ShapeDtypeStruct((count // 2, HD + STAT_ROWS, width), jnp.bfloat16),
            jax.ShapeDtypeStruct((count // 2, HD + KEEP_ROWS, width), jnp.float32),
        ]

    send, keep, pages = pl.pallas_call(
        attend_kernel,
        out_shape=parted(senders) + [whole],
        in_specs=[SMEM, SMEM] + [VMEM] * 5 + [ANY],
        out_specs=[VMEM] * 2 + [HBM],
        scratch_shapes=[
            pltpu.VMEM((tokens * 2, HD), jnp.float32),
            pltpu.VMEM((tokens, 2 * HD), jnp.bfloat16),
            pltpu.VMEM((tokens, HD), jnp.bfloat16),
            pltpu.VMEM((rows * GQ * steps, 2 * HD), jnp.bfloat16),
            pltpu.SemaphoreType.DMA,
        ],
        compiler_params=pltpu.CompilerParams(vmem_limit_bytes=32 * 1024 * 1024),
        cost_estimate=pl.CostEstimate(
            flops=6 * rows * GQ * steps * tokens * HD,
            bytes_accessed=tokens * 4 * HD + rows * GQ * steps * 4 * HD,
            transcendentals=rows * GQ * steps * tokens,
        ),
        name="attend",
    )(lengths, row_request, late_deltas, flat_anchors, scales, flat_queries, flat_new, mine)

    k, count = 1, senders // 2
    passed = exchange(send, k)
    while count > 1:
        send, keep = pl.pallas_call(
            join_kernel,
            out_shape=parted(count),
            in_specs=[VMEM] * 2,
            out_specs=[VMEM] * 2,
            compiler_params=small,
            name="join",
        )(keep, passed)
        k, count = 2 * k, count // 2
        passed = exchange(send, k)
    attended = pl.pallas_call(
        finish_kernel,
        out_shape=jax.ShapeDtypeStruct((width, HD), jnp.bfloat16),
        in_specs=[VMEM] * 2,
        out_specs=VMEM,
        compiler_params=small,
        name="finish",
    )(keep, passed)
    pages = pl.pallas_call(
        settle_kernel,
        out_shape=whole,
        in_specs=[HBM] + [ANY] * (senders - 1),
        out_specs=HBM,
        scratch_shapes=[pltpu.SemaphoreType.DMA((senders - 1,))],
        input_output_aliases={0: 0},
        compiler_params=small,
        name="settle",
    )(pages, *reversed(got[1:]))
    pages = pages.reshape(blocks, tokens // blocks, 2, HD)
    attended = (
        attended.reshape(rows_dev, GQ, steps, HD).transpose(0, 2, 1, 3).reshape(rows_dev, steps, GQ * HD)
    )
    return pages, attended


def solution(mesh):
    placed = (
        P("groups"),
        P(("groups", "seq")),
        P("groups"),
        P(("groups", "seq"), None, "tp"),
        P(("groups", "seq"), None, "tp"),
        P("groups", "tp"),
        P("groups", None, "tp"),
        P(("groups", "seq"), None, None, "tp"),
    )
    return jax.shard_map(
        per_device,
        mesh=mesh,
        in_specs=placed,
        out_specs=(P(("groups", "seq"), None, None, "tp"), P(("groups", "seq"), None, "tp")),
        check_vma=False,
    )
```

```python
import functools

import jax
import jax.numpy as jnp
from jax import lax
from jax.experimental import pallas as pl
from jax.experimental.pallas import tpu as pltpu
from jax.sharding import PartitionSpec as P

HD = 128
GQ = 8
STEPS = 2
STAT_ROWS = 16
KEEP_ROWS = 8
HEIGHTS = (80, 64)
PIECES = len(HEIGHTS)
FAR = -1e30
RATE = HD ** (-0.5) * 1.4426950408889634

VMEM = pl.BlockSpec(memory_space=pltpu.VMEM)
HBM = pl.BlockSpec(memory_space=pltpu.HBM)
ANY = pl.BlockSpec(memory_space=pl.ANY)
SMEM = pl.BlockSpec(memory_space=pltpu.SMEM)


def exchange(message, k):
    count = lax.axis_size("seq")
    return lax.ppermute(message, "seq", [(i, i ^ k) for i in range(count)])


def place_kernel(owner_any, deltas_any, anchors_any, scales_any, *refs):
    receivers = lax.axis_size("seq")
    me = lax.axis_index("seq")
    outs = refs[:receivers]
    owner_ref, source_ref, count_ref, deltas_ref, anchors_ref, scales_ref, sems = refs[receivers:]
    blocks = owner_ref.shape[0]
    rows = deltas_ref.shape[0] // blocks
    capacity = blocks // receivers
    loads = [
        pltpu.make_async_copy(source, target, sems.at[index])
        for index, (source, target) in enumerate(
            [
                (owner_any, owner_ref),
                (scales_any, scales_ref),
                (anchors_any, anchors_ref),
                (deltas_any, deltas_ref),
            ]
        )
    ]
    for load in loads:
        load.start()
    bits = capacity.bit_length()
    narrow = receivers * bits < 32
    if not narrow:
        for owner in range(receivers):
            count_ref[owner] = owner * capacity
    loads[0].wait()

    def find(block, counts):
        owner = owner_ref[block]
        if narrow:
            shift = owner * bits
            slot = owner * capacity + ((counts >> shift) & ((1 << bits) - 1))
            counts = counts + (jnp.int32(1) << shift)
        else:
            slot = count_ref[owner]
            count_ref[owner] = slot + 1
        source_ref[slot] = block
        return counts

    lax.fori_loop(0, blocks, find, jnp.int32(0), unroll=8)
    for load in loads[1:]:
        load.wait()
    odd = lax.broadcasted_iota(jnp.int32, (8, HD), 0) % 2 == 1
    scale = jnp.where(odd, scales_ref[1:2, :], scales_ref[0:1, :])[None]
    for k, out_ref in zip(reversed(range(receivers)), outs):
        first = (me ^ k) * capacity

        def one_slot(slot, carry, first=first, out_ref=out_ref):
            block = source_ref[first + slot]
            anchor = jnp.where(
                odd, anchors_ref[pl.ds(2 * block + 1, 1), :], anchors_ref[pl.ds(2 * block, 1), :]
            )[None]
            here = pl.ds(pl.multiple_of(block * rows, rows), rows)
            delta = deltas_ref[here, :].astype(jnp.float32)
            decoded = anchor + scale * delta.reshape(rows // 8, 8, HD)
            out_ref[pl.ds(pl.multiple_of(slot * rows, rows), rows), :] = decoded.reshape(rows, HD).astype(
                jnp.bfloat16
            )
            return carry

        lax.fori_loop(0, capacity, one_slot, 0, unroll=min(8, capacity))


def settle_kernel(*refs):
    receivers = lax.axis_size("seq")
    me = lax.axis_index("seq")
    got, pages, sems = refs[1:receivers], refs[receivers], refs[receivers + 1]
    size = got[0].shape[0]
    copies = []
    for k in range(1, receivers):
        first = pl.multiple_of((me ^ k) * size, size)
        copy = pltpu.make_async_copy(got[-k], pages.at[pl.ds(first, size), :], sems.at[k - 1])
        copy.start()
        copies.append(copy)
    for copy in copies:
        copy.wait()


def pieces(values):
    high = values.astype(jnp.bfloat16)
    rest = values - high.astype(jnp.float32)
    middle = rest.astype(jnp.bfloat16)
    low = (rest - middle.astype(jnp.float32)).astype(jnp.bfloat16)
    return [high, middle, low]


def pack(refs, index, partial):
    summed, top, total = partial
    stats = pieces(top) + pieces(total)
    rest = jnp.zeros((STAT_ROWS - len(stats), top.shape[1]), jnp.bfloat16)
    block = jnp.concatenate([summed.astype(jnp.bfloat16)] + stats + [rest], axis=0)
    first = 0
    for height, ref in zip(HEIGHTS, refs):
        ref[index] = block[first : first + height]
        first += height


def unpacked(refs, index):
    block = jnp.concatenate([ref[index] for ref in refs], axis=0)
    stats = block[HD:, :].astype(jnp.float32)
    top = stats[0:1] + stats[1:2] + stats[2:3]
    total = stats[3:4] + stats[4:5] + stats[5:6]
    return block[0:HD, :].astype(jnp.float32), top, total


def held(partial):
    summed, top, total = partial
    rest = jnp.zeros((KEEP_ROWS - 2, top.shape[1]), jnp.float32)
    return jnp.concatenate([summed, top, total, rest], axis=0)


def taken(block):
    return block[0:HD, :], block[HD : HD + 1, :], block[HD + 1 : HD + 2, :]


def joined(one, other):
    top = jnp.maximum(one[1], other[1])
    scale_one = jnp.exp2((one[1] - top) * RATE)
    scale_other = jnp.exp2((other[1] - top) * RATE)
    return (
        one[0] * scale_one + other[0] * scale_other,
        top,
        one[2] * scale_one + other[2] * scale_other,
    )


def attend_kernel(*refs):
    me = lax.axis_index("seq")
    sources, mine_any, refs = refs[:7], refs[7], refs[8:]
    send, refs = refs[:PIECES], refs[PIECES:]
    keep_ref, pages_any, *targets, wide_ref, keys_ref, values_ref, asked_ref, sems = refs
    loads = [
        pltpu.make_async_copy(source, target, sems.at[index])
        for index, (source, target) in enumerate(zip(sources, targets))
    ]
    for load in loads:
        load.start()
    size = mine_any.shape[0]
    own_pages = pltpu.make_async_copy(
        mine_any, pages_any.at[pl.ds(pl.multiple_of(me * size, size), size), :], sems.at[len(loads)]
    )
    own_pages.start()
    deltas_ref, anchors_ref, scales_ref, lengths_ref, request_ref, queries_ref, new_ref = targets
    blocks = anchors_ref.shape[0] // 2
    rows = deltas_ref.shape[0] // blocks
    tokens = rows // 2
    requests = lengths_ref.shape[0]
    asked = queries_ref.shape[0]
    per_row = asked // request_ref.shape[0]
    width = keep_ref.shape[2]

    for load in loads:
        load.wait()
    wide_ref[...] = deltas_ref[...].astype(jnp.float32)
    scale_key = scales_ref[0:1, :]
    scale_value = scales_ref[1:2, :]

    def one_block(block, carry):
        here = pl.ds(pl.multiple_of(block * tokens, tokens), tokens)
        key = wide_ref[pl.ds(block * rows, tokens, stride=2), :]
        value = wide_ref[pl.ds(block * rows + 1, tokens, stride=2), :]
        keys_ref[here, 0:HD] = (anchors_ref[pl.ds(2 * block, 1), :] + scale_key * key).astype(jnp.bfloat16)
        values_ref[here, :] = (anchors_ref[pl.ds(2 * block + 1, 1), :] + scale_value * value).astype(
            jnp.bfloat16
        )
        return carry

    lax.fori_loop(0, blocks, one_block, 0, unroll=4)

    lane = lax.broadcasted_iota(jnp.int32, (1, HD), 1)
    first = jnp.zeros((1, HD), jnp.int32)
    last = jnp.zeros((1, HD), jnp.int32)
    end = 0 - me * (blocks * tokens)
    for request in range(requests):
        start = end
        end = end + lengths_ref[request]
        first = jnp.where(lane == request, start, first)
        last = jnp.where(lane == request, end, last)
    place = lax.broadcasted_iota(jnp.int32, (blocks * tokens, HD), 0)
    keys_ref[:, HD:] = jnp.where((place >= first) & (place < last), 1.0, 0.0).astype(jnp.bfloat16)

    asked_ref[:, 0:HD] = queries_ref[...]
    wide_lane = lax.broadcasted_iota(jnp.int32, (per_row, HD), 1)

    def one_row(row, carry):
        asked_ref[pl.ds(pl.multiple_of(row * per_row, per_row), per_row), HD:] = jnp.where(
            (wide_lane == request_ref[row]) | (wide_lane >= requests), 0.0, FAR
        ).astype(jnp.bfloat16)
        return carry

    lax.fori_loop(0, request_ref.shape[0], one_row, 0, unroll=4)

    tile = min(256, asked)
    parts = max(1, tile // width)

    def one_tile(index, carry):
        here = asked_ref[pl.ds(pl.multiple_of(index * tile, tile), tile), :]
        scores = lax.dot_general(
            keys_ref[...], here, (((1,), (1,)), ((), ())), preferred_element_type=jnp.float32
        )
        top = jnp.max(scores, axis=0, keepdims=True)
        weights = jnp.exp2((scores - top) * RATE)
        total = jnp.sum(weights, axis=0, keepdims=True)
        summed = lax.dot_general(
            values_ref[...],
            weights.astype(jnp.bfloat16),
            (((0,), (0,)), ((), ())),
            preferred_element_type=jnp.float32,
        )
        for part in range(parts):
            lanes = slice(part * width, (part + 1) * width)
            partial = summed[:, lanes], top[:, lanes], total[:, lanes]
            apart = (index * parts + part) ^ me

            @pl.when(apart % 2 == 1)
            def _(partial=partial, apart=apart):
                pack(send, apart // 2, partial)

            @pl.when(apart % 2 == 0)
            def _(partial=partial, apart=apart):
                keep_ref[apart // 2] = held(partial)

        return carry

    lax.fori_loop(0, asked // tile, one_tile, 0)

    fresh = new_ref.shape[0] // 4
    new = new_ref[...].astype(jnp.float32).reshape(fresh, 4, HD)
    mine = queries_ref[pl.ds(pl.multiple_of(me * width, width), width), :]
    of_row = lax.broadcasted_iota(jnp.int32, (fresh, width), 1) // (GQ * STEPS)
    same = of_row == lax.broadcasted_iota(jnp.int32, (fresh, width), 0)
    step = lax.broadcasted_iota(jnp.int32, (1, width), 1) % STEPS
    own_scores = []
    for which in range(STEPS):
        scored = lax.dot_general(
            new[:, 2 * which, :].astype(jnp.bfloat16),
            mine,
            (((1,), (1,)), ((), ())),
            preferred_element_type=jnp.float32,
        )
        picked = jnp.sum(jnp.where(same, scored, 0.0), axis=0, keepdims=True)
        own_scores.append(jnp.where(step >= which, picked, FAR))
    own_top = jnp.maximum(own_scores[0], own_scores[1])
    own_total = jnp.zeros((1, width), jnp.float32)
    own_summed = jnp.zeros((HD, width), jnp.float32)
    for which in range(STEPS):
        weight = jnp.exp2((own_scores[which] - own_top) * RATE)
        own_total = own_total + weight
        spread = jnp.where(same, weight, 0.0).astype(jnp.bfloat16)
        own_summed = own_summed + lax.dot_general(
            new[:, 2 * which + 1, :].astype(jnp.bfloat16),
            spread,
            (((0,), (0,)), ((), ())),
            preferred_element_type=jnp.float32,
        )
    keep_ref[0] = held(joined(taken(keep_ref[0]), (own_summed, own_top, own_total)))
    own_pages.wait()


def join_kernel(keep_ref, *refs):
    got, send, next_ref = refs[:PIECES], refs[PIECES : 2 * PIECES], refs[2 * PIECES]
    for index in range(keep_ref.shape[0]):
        partial = joined(taken(keep_ref[index]), unpacked(got, index))
        if index % 2 == 1:
            pack(send, index // 2, partial)
        else:
            next_ref[index // 2] = held(partial)


def finish_kernel(keep_ref, *refs):
    summed, _, total = joined(taken(keep_ref[0]), unpacked(refs[:PIECES], 0))
    refs[PIECES][...] = (summed / total).T.astype(jnp.bfloat16)


def in_hbm(arrays):
    return [pltpu.with_memory_space_constraint(array, pltpu.HBM) for array in arrays]


def per_device(lengths, owner_map, row_request, deltas, anchors, scales, queries, new_kv):
    blocks = anchors.shape[0]
    tokens = deltas.shape[0]
    senders = lax.axis_size("seq")
    me = lax.axis_index("seq")
    rows, steps, _ = queries.shape
    rows_dev = new_kv.shape[0]
    width = rows_dev * GQ * steps
    small = pltpu.CompilerParams(vmem_limit_bytes=8 * 1024 * 1024)

    flat_deltas = deltas.reshape(tokens * 2, HD)
    flat_anchors = anchors.reshape(blocks * 2, HD)
    flat_queries = queries.reshape(rows, steps, GQ, HD).transpose(0, 2, 1, 3).reshape(-1, HD)
    flat_new = new_kv.reshape(rows_dev * 4, HD)

    hand = jax.ShapeDtypeStruct((tokens * 2 // senders, HD), jnp.bfloat16)
    whole = jax.ShapeDtypeStruct((tokens * 2, HD), jnp.bfloat16)

    *sent, mine = pl.pallas_call(
        place_kernel,
        out_shape=[hand] * senders,
        in_specs=[HBM] * 4,
        out_specs=[VMEM] * senders,
        scratch_shapes=[
            pltpu.SMEM((blocks,), jnp.int32),
            pltpu.SMEM((blocks,), jnp.int32),
            pltpu.SMEM((senders,), jnp.int32),
            pltpu.VMEM((tokens * 2, HD), jnp.bfloat16),
            pltpu.VMEM((blocks * 2, HD), jnp.float32),
            pltpu.VMEM((2, HD), jnp.float32),
            pltpu.SemaphoreType.DMA((4,)),
        ],
        compiler_params=small,
        name="place",
    )(*in_hbm([owner_map, flat_deltas, flat_anchors, scales]))
    sent = [mine] + sent[::-1]

    got = [None] * senders
    sent, mine, late_deltas = lax.optimization_barrier((sent, mine, flat_deltas))
    for k in reversed(range(1, senders)):
        got[k] = exchange(sent[k], k)

    def parted(count):
        return [jax.ShapeDtypeStruct((count // 2, height, width), jnp.bfloat16) for height in HEIGHTS] + [
            jax.ShapeDtypeStruct((count // 2, HD + KEEP_ROWS, width), jnp.float32)
        ]

    needed = (late_deltas, flat_anchors, scales, lengths, row_request, flat_queries, flat_new)
    *send, keep, pages = pl.pallas_call(
        attend_kernel,
        out_shape=parted(senders) + [whole],
        in_specs=[HBM] * len(needed) + [ANY],
        out_specs=[VMEM] * (PIECES + 1) + [HBM],
        scratch_shapes=[
            (pltpu.SMEM if array.dtype == jnp.int32 else pltpu.VMEM)(array.shape, array.dtype)
            for array in needed
        ]
        + [
            pltpu.VMEM((tokens * 2, HD), jnp.float32),
            pltpu.VMEM((tokens, 2 * HD), jnp.bfloat16),
            pltpu.VMEM((tokens, HD), jnp.bfloat16),
            pltpu.VMEM((rows * GQ * steps, 2 * HD), jnp.bfloat16),
            pltpu.SemaphoreType.DMA((len(needed) + 1,)),
        ],
        compiler_params=pltpu.CompilerParams(vmem_limit_bytes=32 * 1024 * 1024),
        cost_estimate=pl.CostEstimate(
            flops=6 * rows * GQ * steps * tokens * HD,
            bytes_accessed=tokens * 4 * HD + rows * GQ * steps * 4 * HD,
            transcendentals=rows * GQ * steps * tokens,
        ),
        name="attend",
    )(*in_hbm(needed), mine)

    k, count = 1, senders // 2
    while count > 1:
        *send, keep = pl.pallas_call(
            join_kernel,
            out_shape=parted(count),
            in_specs=[VMEM] * (PIECES + 1),
            out_specs=[VMEM] * (PIECES + 1),
            compiler_params=small,
            name="join",
        )(keep, *[exchange(piece, k) for piece in send])
        k, count = 2 * k, count // 2
    attended = pl.pallas_call(
        finish_kernel,
        out_shape=jax.ShapeDtypeStruct((width, HD), jnp.bfloat16),
        in_specs=[VMEM] * (PIECES + 1),
        out_specs=VMEM,
        compiler_params=small,
        name="finish",
    )(keep, *[exchange(piece, k) for piece in send])
    pages = pl.pallas_call(
        settle_kernel,
        out_shape=whole,
        in_specs=[HBM] + [ANY] * (senders - 1),
        out_specs=HBM,
        scratch_shapes=[pltpu.SemaphoreType.DMA((senders - 1,))],
        input_output_aliases={0: 0},
        compiler_params=small,
        name="settle",
    )(pages, *reversed(got[1:]))
    pages = pages.reshape(blocks, tokens // blocks, 2, HD)
    attended = (
        attended.reshape(rows_dev, GQ, steps, HD).transpose(0, 2, 1, 3).reshape(rows_dev, steps, GQ * HD)
    )
    return pages, attended


def solution(mesh):
    placed = (
        P("groups"),
        P(("groups", "seq")),
        P("groups"),
        P(("groups", "seq"), None, "tp"),
        P(("groups", "seq"), None, "tp"),
        P("groups", "tp"),
        P("groups", None, "tp"),
        P(("groups", "seq"), None, None, "tp"),
    )
    return jax.shard_map(
        per_device,
        mesh=mesh,
        in_specs=placed,
        out_specs=(P(("groups", "seq"), None, None, "tp"), P(("groups", "seq"), None, "tp")),
        check_vma=False,
    )
```

```python
import functools

import jax
import jax.numpy as jnp
from jax import lax
from jax.experimental import pallas as pl
from jax.experimental.pallas import tpu as pltpu
from jax.sharding import PartitionSpec as P

HD = 128
GQ = 8
STEPS = 2
STAT_ROWS = 16
KEEP_ROWS = 8
FAR = -1e30
RATE = HD ** (-0.5) * 1.4426950408889634

VMEM = pl.BlockSpec(memory_space=pltpu.VMEM)
HBM = pl.BlockSpec(memory_space=pltpu.HBM)
ANY = pl.BlockSpec(memory_space=pl.ANY)
SMEM = pl.BlockSpec(memory_space=pltpu.SMEM)


def exchange(message, k):
    count = lax.axis_size("seq")
    return lax.ppermute(message, "seq", [(i, i ^ k) for i in range(count)])


def messages(count, capacity):
    far = [(k, 0, capacity) for k in reversed(range(count // 2, count))]
    half = capacity // 2
    near = [(k, first, half) for k in reversed(range(1, count // 2)) for first in (0, half)]
    return far + near + [(0, 0, capacity)]


def place_kernel(owner_any, deltas_any, anchors_any, scales_any, *refs):
    receivers = lax.axis_size("seq")
    me = lax.axis_index("seq")
    outs = refs[:-7]
    owner_ref, source_ref, count_ref, deltas_ref, anchors_ref, scales_ref, sems = refs[-7:]
    blocks = owner_ref.shape[0]
    rows = deltas_ref.shape[0] // blocks
    capacity = blocks // receivers
    loads = [
        pltpu.make_async_copy(source, target, sems.at[index])
        for index, (source, target) in enumerate(
            [
                (owner_any, owner_ref),
                (scales_any, scales_ref),
                (anchors_any, anchors_ref),
                (deltas_any, deltas_ref),
            ]
        )
    ]
    for load in loads:
        load.start()
    bits = capacity.bit_length()
    narrow = receivers * bits < 32
    if not narrow:
        for owner in range(receivers):
            count_ref[owner] = owner * capacity
    loads[0].wait()

    def find(block, counts):
        owner = owner_ref[block]
        if narrow:
            shift = owner * bits
            slot = owner * capacity + ((counts >> shift) & ((1 << bits) - 1))
            counts = counts + (jnp.int32(1) << shift)
        else:
            slot = count_ref[owner]
            count_ref[owner] = slot + 1
        source_ref[slot] = block
        return counts

    lax.fori_loop(0, blocks, find, jnp.int32(0), unroll=8)
    for load in loads[1:]:
        load.wait()
    odd = lax.broadcasted_iota(jnp.int32, (8, HD), 0) % 2 == 1
    scale = jnp.where(odd, scales_ref[1:2, :], scales_ref[0:1, :])[None]
    for (k, start, count), out_ref in zip(messages(receivers, capacity), outs):
        first = (me ^ k) * capacity + start

        def one_slot(slot, carry, first=first, out_ref=out_ref):
            block = source_ref[first + slot]
            anchor = jnp.where(
                odd, anchors_ref[pl.ds(2 * block + 1, 1), :], anchors_ref[pl.ds(2 * block, 1), :]
            )[None]
            here = pl.ds(pl.multiple_of(block * rows, rows), rows)
            delta = deltas_ref[here, :].astype(jnp.float32)
            decoded = anchor + scale * delta.reshape(rows // 8, 8, HD)
            out_ref[pl.ds(pl.multiple_of(slot * rows, rows), rows), :] = decoded.reshape(rows, HD).astype(
                jnp.bfloat16
            )
            return carry

        lax.fori_loop(0, count, one_slot, 0, unroll=min(8, count))


def settle_kernel(*refs):
    receivers = lax.axis_size("seq")
    me = lax.axis_index("seq")
    got, pages, sems = refs[1:-2], refs[-2], refs[-1]
    capacity = pages.shape[0] // receivers
    copies = []
    for index, (k, start, count) in enumerate(messages(receivers, capacity)[:-1]):
        first = pl.multiple_of((me ^ k) * capacity + start, count)
        copy = pltpu.make_async_copy(got[index], pages.at[pl.ds(first, count), :], sems.at[index])
        copy.start()
        copies.append(copy)
    for copy in copies:
        copy.wait()


def pieces(values):
    high = values.astype(jnp.bfloat16)
    rest = values - high.astype(jnp.float32)
    middle = rest.astype(jnp.bfloat16)
    low = (rest - middle.astype(jnp.float32)).astype(jnp.bfloat16)
    return [high, middle, low]


def pack(refs, index, partial):
    summed, top, total = partial
    stats = pieces(top) + pieces(total)
    rest = jnp.zeros((STAT_ROWS - len(stats), top.shape[1]), jnp.bfloat16)
    block = jnp.concatenate([summed.astype(jnp.bfloat16)] + stats + [rest], axis=0)
    first = 0
    for ref in refs:
        ref[index] = block[first : first + ref.shape[1]]
        first += ref.shape[1]


def unpacked(refs, index):
    block = jnp.concatenate([ref[index] for ref in refs], axis=0)
    stats = block[HD:, :].astype(jnp.float32)
    top = stats[0:1] + stats[1:2] + stats[2:3]
    total = stats[3:4] + stats[4:5] + stats[5:6]
    return block[0:HD, :].astype(jnp.float32), top, total


def held(partial):
    summed, top, total = partial
    rest = jnp.zeros((KEEP_ROWS - 2, top.shape[1]), jnp.float32)
    return jnp.concatenate([summed, top, total, rest], axis=0)


def taken(block):
    return block[0:HD, :], block[HD : HD + 1, :], block[HD + 1 : HD + 2, :]


def joined(one, other):
    top = jnp.maximum(one[1], other[1])
    scale_one = jnp.exp2((one[1] - top) * RATE)
    scale_other = jnp.exp2((other[1] - top) * RATE)
    return (
        one[0] * scale_one + other[0] * scale_other,
        top,
        one[2] * scale_one + other[2] * scale_other,
    )


def attend_kernel(*refs):
    me = lax.axis_index("seq")
    sources, mine_any, *send, keep_ref, pages_any = refs[:7], refs[7], *refs[8:-12]
    *targets, wide_ref, keys_ref, values_ref, asked_ref, sems = refs[-12:]
    loads = [
        pltpu.make_async_copy(source, target, sems.at[index])
        for index, (source, target) in enumerate(zip(sources, targets))
    ]
    for load in loads:
        load.start()
    size = mine_any.shape[0]
    own_pages = pltpu.make_async_copy(
        mine_any, pages_any.at[pl.ds(pl.multiple_of(me * size, size), size), :], sems.at[len(loads)]
    )
    own_pages.start()
    deltas_ref, anchors_ref, scales_ref, lengths_ref, request_ref, queries_ref, new_ref = targets
    blocks = anchors_ref.shape[0] // 2
    rows = deltas_ref.shape[0] // blocks
    tokens = rows // 2
    requests = lengths_ref.shape[0]
    asked = queries_ref.shape[0]
    per_row = asked // request_ref.shape[0]
    width = keep_ref.shape[2]

    for load in loads:
        load.wait()
    wide_ref[...] = deltas_ref[...].astype(jnp.float32)
    scale_key = scales_ref[0:1, :]
    scale_value = scales_ref[1:2, :]

    def one_block(block, carry):
        here = pl.ds(pl.multiple_of(block * tokens, tokens), tokens)
        key = wide_ref[pl.ds(block * rows, tokens, stride=2), :]
        value = wide_ref[pl.ds(block * rows + 1, tokens, stride=2), :]
        keys_ref[here, 0:HD] = (anchors_ref[pl.ds(2 * block, 1), :] + scale_key * key).astype(jnp.bfloat16)
        values_ref[here, :] = (anchors_ref[pl.ds(2 * block + 1, 1), :] + scale_value * value).astype(
            jnp.bfloat16
        )
        return carry

    lax.fori_loop(0, blocks, one_block, 0, unroll=4)

    lane = lax.broadcasted_iota(jnp.int32, (1, HD), 1)
    first = jnp.zeros((1, HD), jnp.int32)
    last = jnp.zeros((1, HD), jnp.int32)
    end = 0 - me * (blocks * tokens)
    for request in range(requests):
        start = end
        end = end + lengths_ref[request]
        first = jnp.where(lane == request, start, first)
        last = jnp.where(lane == request, end, last)
    place = lax.broadcasted_iota(jnp.int32, (blocks * tokens, HD), 0)
    keys_ref[:, HD:] = jnp.where((place >= first) & (place < last), 1.0, 0.0).astype(jnp.bfloat16)

    asked_ref[:, 0:HD] = queries_ref[...]
    wide_lane = lax.broadcasted_iota(jnp.int32, (per_row, HD), 1)

    def one_row(row, carry):
        asked_ref[pl.ds(pl.multiple_of(row * per_row, per_row), per_row), HD:] = jnp.where(
            (wide_lane == request_ref[row]) | (wide_lane >= requests), 0.0, FAR
        ).astype(jnp.bfloat16)
        return carry

    lax.fori_loop(0, request_ref.shape[0], one_row, 0, unroll=4)

    tile = min(256, asked)
    parts = max(1, tile // width)

    def one_tile(index, carry):
        here = asked_ref[pl.ds(pl.multiple_of(index * tile, tile), tile), :]
        scores = lax.dot_general(
            keys_ref[...], here, (((1,), (1,)), ((), ())), preferred_element_type=jnp.float32
        )
        top = jnp.max(scores, axis=0, keepdims=True)
        weights = jnp.exp2((scores - top) * RATE)
        total = jnp.sum(weights, axis=0, keepdims=True)
        summed = lax.dot_general(
            values_ref[...],
            weights.astype(jnp.bfloat16),
            (((0,), (0,)), ((), ())),
            preferred_element_type=jnp.float32,
        )
        for part in range(parts):
            lanes = slice(part * width, (part + 1) * width)
            partial = summed[:, lanes], top[:, lanes], total[:, lanes]
            apart = (index * parts + part) ^ me

            @pl.when(apart % 2 == 1)
            def _(partial=partial, apart=apart):
                pack(send, apart // 2, partial)

            @pl.when(apart % 2 == 0)
            def _(partial=partial, apart=apart):
                keep_ref[apart // 2] = held(partial)

        return carry

    lax.fori_loop(0, asked // tile, one_tile, 0)

    fresh = new_ref.shape[0] // 4
    new = new_ref[...].astype(jnp.float32).reshape(fresh, 4, HD)
    mine = queries_ref[pl.ds(pl.multiple_of(me * width, width), width), :]
    of_row = lax.broadcasted_iota(jnp.int32, (fresh, width), 1) // (GQ * STEPS)
    same = of_row == lax.broadcasted_iota(jnp.int32, (fresh, width), 0)
    step = lax.broadcasted_iota(jnp.int32, (1, width), 1) % STEPS
    own_scores = []
    for which in range(STEPS):
        scored = lax.dot_general(
            new[:, 2 * which, :].astype(jnp.bfloat16),
            mine,
            (((1,), (1,)), ((), ())),
            preferred_element_type=jnp.float32,
        )
        picked = jnp.sum(jnp.where(same, scored, 0.0), axis=0, keepdims=True)
        own_scores.append(jnp.where(step >= which, picked, FAR))
    own_top = jnp.maximum(own_scores[0], own_scores[1])
    own_total = jnp.zeros((1, width), jnp.float32)
    own_summed = jnp.zeros((HD, width), jnp.float32)
    for which in range(STEPS):
        weight = jnp.exp2((own_scores[which] - own_top) * RATE)
        own_total = own_total + weight
        spread = jnp.where(same, weight, 0.0).astype(jnp.bfloat16)
        own_summed = own_summed + lax.dot_general(
            new[:, 2 * which + 1, :].astype(jnp.bfloat16),
            spread,
            (((0,), (0,)), ((), ())),
            preferred_element_type=jnp.float32,
        )
    keep_ref[0] = held(joined(taken(keep_ref[0]), (own_summed, own_top, own_total)))
    own_pages.wait()


def join_kernel(came, keep_ref, *refs):
    got, send, next_ref = refs[:came], refs[came:-1], refs[-1]
    for index in range(keep_ref.shape[0]):
        partial = joined(taken(keep_ref[index]), unpacked(got, index))
        if index % 2 == 1:
            pack(send, index // 2, partial)
        else:
            next_ref[index // 2] = held(partial)


def finish_kernel(keep_ref, *refs):
    summed, _, total = joined(taken(keep_ref[0]), unpacked(refs[:-1], 0))
    refs[-1][...] = (summed / total).T.astype(jnp.bfloat16)


def in_hbm(arrays):
    return [pltpu.with_memory_space_constraint(array, pltpu.HBM) for array in arrays]


def per_device(lengths, owner_map, row_request, deltas, anchors, scales, queries, new_kv):
    blocks = anchors.shape[0]
    tokens = deltas.shape[0]
    senders = lax.axis_size("seq")
    me = lax.axis_index("seq")
    rows, steps, _ = queries.shape
    rows_dev = new_kv.shape[0]
    width = rows_dev * GQ * steps
    small = pltpu.CompilerParams(vmem_limit_bytes=8 * 1024 * 1024)

    flat_deltas = deltas.reshape(tokens * 2, HD)
    flat_anchors = anchors.reshape(blocks * 2, HD)
    flat_queries = queries.reshape(rows, steps, GQ, HD).transpose(0, 2, 1, 3).reshape(-1, HD)
    flat_new = new_kv.reshape(rows_dev * 4, HD)

    whole = jax.ShapeDtypeStruct((tokens * 2, HD), jnp.bfloat16)
    plan = messages(senders, blocks // senders)
    block_rows = tokens * 2 // blocks
    *sent, mine = pl.pallas_call(
        place_kernel,
        out_shape=[jax.ShapeDtypeStruct((slots * block_rows, HD), jnp.bfloat16) for _, _, slots in plan],
        in_specs=[HBM] * 4,
        out_specs=[VMEM] * len(plan),
        scratch_shapes=[
            pltpu.SMEM((blocks,), jnp.int32),
            pltpu.SMEM((blocks,), jnp.int32),
            pltpu.SMEM((senders,), jnp.int32),
            pltpu.VMEM((tokens * 2, HD), jnp.bfloat16),
            pltpu.VMEM((blocks * 2, HD), jnp.float32),
            pltpu.VMEM((2, HD), jnp.float32),
            pltpu.SemaphoreType.DMA((4,)),
        ],
        compiler_params=small,
        name="place",
    )(*in_hbm([owner_map, flat_deltas, flat_anchors, scales]))

    sent, mine, late_deltas = lax.optimization_barrier((sent, mine, flat_deltas))
    distant = senders // 2
    got = [exchange(message, k) for message, (k, _, _) in zip(sent[:distant], plan)]

    def parted(count):
        heights = (HD // 2 + STAT_ROWS, HD // 2) if count > 2 else (HD + STAT_ROWS,)
        return [jax.ShapeDtypeStruct((count // 2, height, width), jnp.bfloat16) for height in heights] + [
            jax.ShapeDtypeStruct((count // 2, HD + KEEP_ROWS, width), jnp.float32)
        ]

    needed = (late_deltas, flat_anchors, scales, lengths, row_request, flat_queries, flat_new)
    *send, keep, pages = pl.pallas_call(
        attend_kernel,
        out_shape=parted(senders) + [whole],
        in_specs=[HBM] * len(needed) + [ANY],
        out_specs=[VMEM] * len(parted(senders)) + [HBM],
        scratch_shapes=[
            (pltpu.SMEM if array.dtype == jnp.int32 else pltpu.VMEM)(array.shape, array.dtype)
            for array in needed
        ]
        + [
            pltpu.VMEM((tokens * 2, HD), jnp.float32),
            pltpu.VMEM((tokens, 2 * HD), jnp.bfloat16),
            pltpu.VMEM((tokens, HD), jnp.bfloat16),
            pltpu.VMEM((rows * GQ * steps, 2 * HD), jnp.bfloat16),
            pltpu.SemaphoreType.DMA((len(needed) + 1,)),
        ],
        compiler_params=pltpu.CompilerParams(vmem_limit_bytes=32 * 1024 * 1024),
        cost_estimate=pl.CostEstimate(
            flops=6 * rows * GQ * steps * tokens * HD,
            bytes_accessed=tokens * 4 * HD + rows * GQ * steps * 4 * HD,
            transcendentals=rows * GQ * steps * tokens,
        ),
        name="attend",
    )(*in_hbm(needed), mine)

    k, count = 1, senders // 2
    passed = [exchange(piece, k) for piece in send]
    rest, passed = lax.optimization_barrier((sent[distant:], passed))
    got += [exchange(message, k) for message, (k, _, _) in zip(rest, plan[distant:])]
    while count > 1:
        *send, keep = pl.pallas_call(
            functools.partial(join_kernel, len(passed)),
            out_shape=parted(count),
            in_specs=[VMEM] * (len(passed) + 1),
            out_specs=[VMEM] * len(parted(count)),
            compiler_params=small,
            name="join",
        )(keep, *passed)
        k, count = 2 * k, count // 2
        passed = [exchange(piece, k) for piece in send]
    attended = pl.pallas_call(
        finish_kernel,
        out_shape=jax.ShapeDtypeStruct((width, HD), jnp.bfloat16),
        in_specs=[VMEM] * (len(passed) + 1),
        out_specs=VMEM,
        compiler_params=small,
        name="finish",
    )(keep, *passed)
    pages = pl.pallas_call(
        settle_kernel,
        out_shape=whole,
        in_specs=[HBM] + [ANY] * len(got),
        out_specs=HBM,
        scratch_shapes=[pltpu.SemaphoreType.DMA((len(got),))],
        input_output_aliases={0: 0},
        compiler_params=small,
        name="settle",
    )(pages, *got)
    pages = pages.reshape(blocks, tokens // blocks, 2, HD)
    attended = (
        attended.reshape(rows_dev, GQ, steps, HD).transpose(0, 2, 1, 3).reshape(rows_dev, steps, GQ * HD)
    )
    return pages, attended


def solution(mesh):
    placed = (
        P("groups"),
        P(("groups", "seq")),
        P("groups"),
        P(("groups", "seq"), None, "tp"),
        P(("groups", "seq"), None, "tp"),
        P("groups", "tp"),
        P("groups", None, "tp"),
        P(("groups", "seq"), None, None, "tp"),
    )
    return jax.shard_map(
        per_device,
        mesh=mesh,
        in_specs=placed,
        out_specs=(P(("groups", "seq"), None, None, "tp"), P(("groups", "seq"), None, "tp")),
        check_vma=False,
    )
```

```python
import functools

import jax
import jax.numpy as jnp
from jax import lax
from jax.experimental import pallas as pl
from jax.experimental.pallas import tpu as pltpu
from jax.sharding import PartitionSpec as P

HD = 128
GQ = 8
STEPS = 2
STAT_ROWS = 16
KEEP_ROWS = 8
FAR = -1e30
RATE = HD ** (-0.5) * 1.4426950408889634

VMEM = pl.BlockSpec(memory_space=pltpu.VMEM)
HBM = pl.BlockSpec(memory_space=pltpu.HBM)
ANY = pl.BlockSpec(memory_space=pl.ANY)
SMEM = pl.BlockSpec(memory_space=pltpu.SMEM)


def exchange(message, k):
    count = lax.axis_size("seq")
    return lax.ppermute(message, "seq", [(i, i ^ k) for i in range(count)])


def messages(count, capacity):
    far = [(k, 0, capacity) for k in reversed(range(count // 2, count))]
    half = capacity // 2
    near = [(k, first, half) for k in reversed(range(1, count // 2)) for first in (0, half)]
    return far + near + [(0, 0, capacity)]


def place_kernel(owner_any, deltas_any, anchors_any, scales_any, *refs):
    receivers = lax.axis_size("seq")
    me = lax.axis_index("seq")
    outs = refs[:-7]
    owner_ref, source_ref, count_ref, deltas_ref, anchors_ref, scales_ref, sems = refs[-7:]
    blocks = owner_ref.shape[0]
    rows = deltas_ref.shape[0] // blocks
    capacity = blocks // receivers
    loads = [
        pltpu.make_async_copy(source, target, sems.at[index])
        for index, (source, target) in enumerate(
            [
                (owner_any, owner_ref),
                (scales_any, scales_ref),
                (anchors_any, anchors_ref),
                (deltas_any, deltas_ref),
            ]
        )
    ]
    for load in loads:
        load.start()
    bits = capacity.bit_length()
    narrow = receivers * bits < 32
    if not narrow:
        for owner in range(receivers):
            count_ref[owner] = owner * capacity
    loads[0].wait()

    def find(block, counts):
        owner = owner_ref[block]
        if narrow:
            shift = owner * bits
            slot = owner * capacity + ((counts >> shift) & ((1 << bits) - 1))
            counts = counts + (jnp.int32(1) << shift)
        else:
            slot = count_ref[owner]
            count_ref[owner] = slot + 1
        source_ref[slot] = block
        return counts

    lax.fori_loop(0, blocks, find, jnp.int32(0), unroll=8)
    for load in loads[1:]:
        load.wait()
    odd = lax.broadcasted_iota(jnp.int32, (8, HD), 0) % 2 == 1
    scale = jnp.where(odd, scales_ref[1:2, :], scales_ref[0:1, :])[None]
    for (k, start, count), out_ref in zip(messages(receivers, capacity), outs):
        first = (me ^ k) * capacity + start

        def one_slot(slot, carry, first=first, out_ref=out_ref):
            block = source_ref[first + slot]
            anchor = jnp.where(
                odd, anchors_ref[pl.ds(2 * block + 1, 1), :], anchors_ref[pl.ds(2 * block, 1), :]
            )[None]
            here = pl.ds(pl.multiple_of(block * rows, rows), rows)
            delta = deltas_ref[here, :].astype(jnp.float32)
            decoded = anchor + scale * delta.reshape(rows // 8, 8, HD)
            out_ref[pl.ds(pl.multiple_of(slot * rows, rows), rows), :] = decoded.reshape(rows, HD).astype(
                jnp.bfloat16
            )
            return carry

        lax.fori_loop(0, count, one_slot, 0, unroll=min(8, count))


def settle_kernel(*refs):
    receivers = lax.axis_size("seq")
    me = lax.axis_index("seq")
    got, pages, sems = refs[1:-2], refs[-2], refs[-1]
    capacity = pages.shape[0] // receivers
    copies = []
    for index, (k, start, count) in enumerate(messages(receivers, capacity)[:-1]):
        first = pl.multiple_of((me ^ k) * capacity + start, count)
        copy = pltpu.make_async_copy(got[index], pages.at[pl.ds(first, count), :], sems.at[index])
        copy.start()
        copies.append(copy)
    for copy in copies:
        copy.wait()


def pieces(values):
    high = values.astype(jnp.bfloat16)
    rest = values - high.astype(jnp.float32)
    middle = rest.astype(jnp.bfloat16)
    low = (rest - middle.astype(jnp.float32)).astype(jnp.bfloat16)
    return [high, middle, low]


def pack(refs, index, partial):
    summed, top, total = partial
    stats = pieces(top) + pieces(total)
    rest = jnp.zeros((STAT_ROWS - len(stats), top.shape[1]), jnp.bfloat16)
    block = jnp.concatenate([summed.astype(jnp.bfloat16)] + stats + [rest], axis=0)
    first = 0
    for ref in refs:
        ref[index] = block[first : first + ref.shape[1]]
        first += ref.shape[1]


def unpacked(refs, index):
    block = jnp.concatenate([ref[index] for ref in refs], axis=0)
    stats = block[HD:, :].astype(jnp.float32)
    top = stats[0:1] + stats[1:2] + stats[2:3]
    total = stats[3:4] + stats[4:5] + stats[5:6]
    return block[0:HD, :].astype(jnp.float32), top, total


def held(partial):
    summed, top, total = partial
    rest = jnp.zeros((KEEP_ROWS - 2, top.shape[1]), jnp.float32)
    return jnp.concatenate([summed, top, total, rest], axis=0)


def taken(block):
    return block[0:HD, :], block[HD : HD + 1, :], block[HD + 1 : HD + 2, :]


def joined(one, other):
    top = jnp.maximum(one[1], other[1])
    scale_one = jnp.exp2((one[1] - top) * RATE)
    scale_other = jnp.exp2((other[1] - top) * RATE)
    return (
        one[0] * scale_one + other[0] * scale_other,
        top,
        one[2] * scale_one + other[2] * scale_other,
    )


def attend_kernel(*refs):
    me = lax.axis_index("seq")
    sources, mine_any, *send, keep_ref, pages_any = refs[:7], refs[7], *refs[8:-12]
    *targets, wide_ref, keys_ref, values_ref, asked_ref, sems = refs[-12:]
    loads = [
        pltpu.make_async_copy(source, target, sems.at[index])
        for index, (source, target) in enumerate(zip(sources, targets))
    ]
    for load in loads:
        load.start()
    size = mine_any.shape[0]
    own_pages = pltpu.make_async_copy(
        mine_any, pages_any.at[pl.ds(pl.multiple_of(me * size, size), size), :], sems.at[len(loads)]
    )
    own_pages.start()
    deltas_ref, anchors_ref, scales_ref, lengths_ref, request_ref, queries_ref, new_ref = targets
    blocks = anchors_ref.shape[0] // 2
    rows = deltas_ref.shape[0] // blocks
    tokens = rows // 2
    requests = lengths_ref.shape[0]
    asked = queries_ref.shape[0]
    per_row = asked // request_ref.shape[0]
    width = keep_ref.shape[2]

    for load in loads:
        load.wait()
    wide_ref[...] = deltas_ref[...].astype(jnp.float32)
    scale_key = scales_ref[0:1, :]
    scale_value = scales_ref[1:2, :]

    def one_block(block, carry):
        here = pl.ds(pl.multiple_of(block * tokens, tokens), tokens)
        key = wide_ref[pl.ds(block * rows, tokens, stride=2), :]
        value = wide_ref[pl.ds(block * rows + 1, tokens, stride=2), :]
        keys_ref[here, 0:HD] = (anchors_ref[pl.ds(2 * block, 1), :] + scale_key * key).astype(jnp.bfloat16)
        values_ref[here, :] = (anchors_ref[pl.ds(2 * block + 1, 1), :] + scale_value * value).astype(
            jnp.bfloat16
        )
        return carry

    lax.fori_loop(0, blocks, one_block, 0, unroll=4)

    lane = lax.broadcasted_iota(jnp.int32, (1, HD), 1)
    first = jnp.zeros((1, HD), jnp.int32)
    last = jnp.zeros((1, HD), jnp.int32)
    end = 0 - me * (blocks * tokens)
    for request in range(requests):
        start = end
        end = end + lengths_ref[request]
        first = jnp.where(lane == request, start, first)
        last = jnp.where(lane == request, end, last)
    place = lax.broadcasted_iota(jnp.int32, (blocks * tokens, HD), 0)
    keys_ref[:, HD:] = jnp.where((place >= first) & (place < last), 1.0, 0.0).astype(jnp.bfloat16)

    asked_ref[:, 0:HD] = queries_ref[...]
    wide_lane = lax.broadcasted_iota(jnp.int32, (per_row, HD), 1)

    def one_row(row, carry):
        asked_ref[pl.ds(pl.multiple_of(row * per_row, per_row), per_row), HD:] = jnp.where(
            (wide_lane == request_ref[row]) | (wide_lane >= requests), 0.0, FAR
        ).astype(jnp.bfloat16)
        return carry

    lax.fori_loop(0, request_ref.shape[0], one_row, 0, unroll=4)

    tile = min(256, asked)
    parts = max(1, tile // width)

    def one_tile(index, carry):
        here = asked_ref[pl.ds(pl.multiple_of(index * tile, tile), tile), :]
        scores = lax.dot_general(
            keys_ref[...], here, (((1,), (1,)), ((), ())), preferred_element_type=jnp.float32
        )
        top = jnp.max(scores, axis=0, keepdims=True)
        weights = jnp.exp2((scores - top) * RATE)
        total = jnp.sum(weights, axis=0, keepdims=True)
        summed = lax.dot_general(
            values_ref[...],
            weights.astype(jnp.bfloat16),
            (((0,), (0,)), ((), ())),
            preferred_element_type=jnp.float32,
        )
        for part in range(parts):
            lanes = slice(part * width, (part + 1) * width)
            partial = summed[:, lanes], top[:, lanes], total[:, lanes]
            apart = (index * parts + part) ^ me

            @pl.when(apart % 2 == 1)
            def _(partial=partial, apart=apart):
                pack(send, apart // 2, partial)

            @pl.when(apart % 2 == 0)
            def _(partial=partial, apart=apart):
                keep_ref[apart // 2] = held(partial)

        return carry

    lax.fori_loop(0, asked // tile, one_tile, 0)

    fresh = new_ref.shape[0] // 4
    new = new_ref[...].astype(jnp.float32).reshape(fresh, 4, HD)
    mine = queries_ref[pl.ds(pl.multiple_of(me * width, width), width), :]
    of_row = lax.broadcasted_iota(jnp.int32, (fresh, width), 1) // (GQ * STEPS)
    same = of_row == lax.broadcasted_iota(jnp.int32, (fresh, width), 0)
    step = lax.broadcasted_iota(jnp.int32, (1, width), 1) % STEPS
    own_scores = []
    for which in range(STEPS):
        scored = lax.dot_general(
            new[:, 2 * which, :].astype(jnp.bfloat16),
            mine,
            (((1,), (1,)), ((), ())),
            preferred_element_type=jnp.float32,
        )
        picked = jnp.sum(jnp.where(same, scored, 0.0), axis=0, keepdims=True)
        own_scores.append(jnp.where(step >= which, picked, FAR))
    own_top = jnp.maximum(own_scores[0], own_scores[1])
    own_total = jnp.zeros((1, width), jnp.float32)
    own_summed = jnp.zeros((HD, width), jnp.float32)
    for which in range(STEPS):
        weight = jnp.exp2((own_scores[which] - own_top) * RATE)
        own_total = own_total + weight
        spread = jnp.where(same, weight, 0.0).astype(jnp.bfloat16)
        own_summed = own_summed + lax.dot_general(
            new[:, 2 * which + 1, :].astype(jnp.bfloat16),
            spread,
            (((0,), (0,)), ((), ())),
            preferred_element_type=jnp.float32,
        )
    keep_ref[0] = held(joined(taken(keep_ref[0]), (own_summed, own_top, own_total)))
    own_pages.wait()


def join_kernel(came, keep_ref, *refs):
    got, send, next_ref = refs[:came], refs[came:-1], refs[-1]
    for index in range(keep_ref.shape[0]):
        partial = joined(taken(keep_ref[index]), unpacked(got, index))
        if index % 2 == 1:
            pack(send, index // 2, partial)
        else:
            next_ref[index // 2] = held(partial)


def finish_kernel(keep_ref, *refs):
    summed, _, total = joined(taken(keep_ref[0]), unpacked(refs[:-1], 0))
    refs[-1][...] = (summed / total).T.astype(jnp.bfloat16)


def in_hbm(arrays):
    return [pltpu.with_memory_space_constraint(array, pltpu.HBM) for array in arrays]


def per_device(lengths, owner_map, row_request, deltas, anchors, scales, queries, new_kv):
    blocks = anchors.shape[0]
    tokens = deltas.shape[0]
    senders = lax.axis_size("seq")
    me = lax.axis_index("seq")
    rows, steps, _ = queries.shape
    rows_dev = new_kv.shape[0]
    width = rows_dev * GQ * steps
    small = pltpu.CompilerParams(vmem_limit_bytes=8 * 1024 * 1024)

    flat_deltas = deltas.reshape(tokens * 2, HD)
    flat_anchors = anchors.reshape(blocks * 2, HD)
    flat_queries = queries.reshape(rows, steps, GQ, HD).transpose(0, 2, 1, 3).reshape(-1, HD)
    flat_new = new_kv.reshape(rows_dev * 4, HD)

    whole = jax.ShapeDtypeStruct((tokens * 2, HD), jnp.bfloat16)
    plan = messages(senders, blocks // senders)
    block_rows = tokens * 2 // blocks
    *sent, mine = pl.pallas_call(
        place_kernel,
        out_shape=[jax.ShapeDtypeStruct((slots * block_rows, HD), jnp.bfloat16) for _, _, slots in plan],
        in_specs=[HBM] * 4,
        out_specs=[VMEM] * len(plan),
        scratch_shapes=[
            pltpu.SMEM((blocks,), jnp.int32),
            pltpu.SMEM((blocks,), jnp.int32),
            pltpu.SMEM((senders,), jnp.int32),
            pltpu.VMEM((tokens * 2, HD), jnp.bfloat16),
            pltpu.VMEM((blocks * 2, HD), jnp.float32),
            pltpu.VMEM((2, HD), jnp.float32),
            pltpu.SemaphoreType.DMA((4,)),
        ],
        compiler_params=small,
        name="place",
    )(*in_hbm([owner_map, flat_deltas, flat_anchors, scales]))

    sent, mine, late_deltas = lax.optimization_barrier((sent, mine, flat_deltas))
    distant = senders // 2
    got = [exchange(message, k) for message, (k, _, _) in zip(sent[:distant], plan)]

    def parted(count):
        heights = (HD // 2 + STAT_ROWS, HD // 2) if count > 2 else (HD + STAT_ROWS,)
        return [jax.ShapeDtypeStruct((count // 2, height, width), jnp.bfloat16) for height in heights] + [
            jax.ShapeDtypeStruct((count // 2, HD + KEEP_ROWS, width), jnp.float32)
        ]

    needed = (late_deltas, flat_anchors, scales, lengths, row_request, flat_queries, flat_new)
    *send, keep, pages = pl.pallas_call(
        attend_kernel,
        out_shape=parted(senders) + [whole],
        in_specs=[HBM] * len(needed) + [ANY],
        out_specs=[VMEM] * len(parted(senders)) + [HBM],
        scratch_shapes=[
            (pltpu.SMEM if array.dtype == jnp.int32 else pltpu.VMEM)(array.shape, array.dtype)
            for array in needed
        ]
        + [
            pltpu.VMEM((tokens * 2, HD), jnp.float32),
            pltpu.VMEM((tokens, 2 * HD), jnp.bfloat16),
            pltpu.VMEM((tokens, HD), jnp.bfloat16),
            pltpu.VMEM((rows * GQ * steps, 2 * HD), jnp.bfloat16),
            pltpu.SemaphoreType.DMA((len(needed) + 1,)),
        ],
        compiler_params=pltpu.CompilerParams(vmem_limit_bytes=32 * 1024 * 1024),
        cost_estimate=pl.CostEstimate(
            flops=6 * rows * GQ * steps * tokens * HD,
            bytes_accessed=tokens * 4 * HD + rows * GQ * steps * 4 * HD,
            transcendentals=rows * GQ * steps * tokens,
        ),
        name="attend",
    )(*in_hbm(needed), mine)

    k, count = 1, senders // 2
    rest, send = lax.optimization_barrier((sent[distant:], send))
    passed = [exchange(piece, k) for piece in send]
    got += [exchange(message, k) for message, (k, _, _) in zip(rest, plan[distant:])]
    while count > 1:
        *send, keep = pl.pallas_call(
            functools.partial(join_kernel, len(passed)),
            out_shape=parted(count),
            in_specs=[VMEM] * (len(passed) + 1),
            out_specs=[VMEM] * len(parted(count)),
            compiler_params=small,
            name="join",
        )(keep, *passed)
        k, count = 2 * k, count // 2
        passed = [exchange(piece, k) for piece in send]
    attended = pl.pallas_call(
        finish_kernel,
        out_shape=jax.ShapeDtypeStruct((width, HD), jnp.bfloat16),
        in_specs=[VMEM] * (len(passed) + 1),
        out_specs=VMEM,
        compiler_params=small,
        name="finish",
    )(keep, *passed)
    pages = pl.pallas_call(
        settle_kernel,
        out_shape=whole,
        in_specs=[HBM] + [ANY] * len(got),
        out_specs=HBM,
        scratch_shapes=[pltpu.SemaphoreType.DMA((len(got),))],
        input_output_aliases={0: 0},
        compiler_params=small,
        name="settle",
    )(pages, *got)
    pages = pages.reshape(blocks, tokens // blocks, 2, HD)
    attended = (
        attended.reshape(rows_dev, GQ, steps, HD).transpose(0, 2, 1, 3).reshape(rows_dev, steps, GQ * HD)
    )
    return pages, attended


def solution(mesh):
    placed = (
        P("groups"),
        P(("groups", "seq")),
        P("groups"),
        P(("groups", "seq"), None, "tp"),
        P(("groups", "seq"), None, "tp"),
        P("groups", "tp"),
        P("groups", None, "tp"),
        P(("groups", "seq"), None, None, "tp"),
    )
    return jax.shard_map(
        per_device,
        mesh=mesh,
        in_specs=placed,
        out_specs=(P(("groups", "seq"), None, None, "tp"), P(("groups", "seq"), None, "tp")),
        check_vma=False,
    )
```

```python
import functools

import jax
import jax.numpy as jnp
from jax import lax
from jax.experimental import pallas as pl
from jax.experimental.pallas import tpu as pltpu
from jax.sharding import PartitionSpec as P

HD = 128
GQ = 8
STEPS = 2
STAT_ROWS = 16
KEEP_ROWS = 8
FAR = -1e30
RATE = HD ** (-0.5) * 1.4426950408889634

VMEM = pl.BlockSpec(memory_space=pltpu.VMEM)
HBM = pl.BlockSpec(memory_space=pltpu.HBM)
ANY = pl.BlockSpec(memory_space=pl.ANY)
SMEM = pl.BlockSpec(memory_space=pltpu.SMEM)


def exchange(message, k):
    count = lax.axis_size("seq")
    return lax.ppermute(message, "seq", [(i, i ^ k) for i in range(count)])


def messages(count, capacity):
    far = [(k, 0, capacity) for k in reversed(range(count // 2, count))]
    half = capacity // 2
    near = [(k, first, half) for k in reversed(range(1, count // 2)) for first in (0, half)]
    return far + near + [(0, 0, capacity)]


def place_kernel(plan, owner_any, deltas_any, anchors_any, scales_any, *refs):
    receivers = lax.axis_size("seq")
    me = lax.axis_index("seq")
    outs = refs[:-7]
    owner_ref, source_ref, count_ref, deltas_ref, anchors_ref, scales_ref, sems = refs[-7:]
    blocks = owner_ref.shape[0]
    rows = deltas_ref.shape[0] // blocks
    capacity = blocks // receivers
    loads = [
        pltpu.make_async_copy(source, target, sems.at[index])
        for index, (source, target) in enumerate(
            [
                (owner_any, owner_ref),
                (scales_any, scales_ref),
                (anchors_any, anchors_ref),
                (deltas_any, deltas_ref),
            ]
        )
    ]
    for load in loads:
        load.start()
    bits = capacity.bit_length()
    single = len(plan) == 1
    narrow = receivers * bits < 32
    if not narrow and not single:
        for owner in range(receivers):
            count_ref[owner] = owner * capacity
    loads[0].wait()

    def find(block, counts):
        owner = owner_ref[block]
        if narrow:
            shift = owner * bits
            slot = owner * capacity + ((counts >> shift) & ((1 << bits) - 1))
            counts = counts + (jnp.int32(1) << shift)
        else:
            slot = count_ref[owner]
            count_ref[owner] = slot + 1
        source_ref[slot] = block
        return counts

    def find_one(block, slot):
        source_ref[slot] = block
        return slot + (owner_ref[block] == (me ^ plan[0][0])).astype(jnp.int32)

    lax.fori_loop(0, blocks, find_one if single else find, jnp.int32(0), unroll=8)
    for load in loads[1:]:
        load.wait()
    odd = lax.broadcasted_iota(jnp.int32, (8, HD), 0) % 2 == 1
    scale = jnp.where(odd, scales_ref[1:2, :], scales_ref[0:1, :])[None]
    for (k, start, count), out_ref in zip(plan, outs):
        first = start if single else (me ^ k) * capacity + start

        def one_slot(slot, carry, first=first, out_ref=out_ref):
            block = source_ref[first + slot]
            anchor = jnp.where(
                odd, anchors_ref[pl.ds(2 * block + 1, 1), :], anchors_ref[pl.ds(2 * block, 1), :]
            )[None]
            here = pl.ds(pl.multiple_of(block * rows, rows), rows)
            delta = deltas_ref[here, :].astype(jnp.float32)
            decoded = anchor + scale * delta.reshape(rows // 8, 8, HD)
            out_ref[pl.ds(pl.multiple_of(slot * rows, rows), rows), :] = decoded.reshape(rows, HD).astype(
                jnp.bfloat16
            )
            return carry

        lax.fori_loop(0, count, one_slot, 0, unroll=min(8, count))


def pieces(values):
    high = values.astype(jnp.bfloat16)
    rest = values - high.astype(jnp.float32)
    middle = rest.astype(jnp.bfloat16)
    low = (rest - middle.astype(jnp.float32)).astype(jnp.bfloat16)
    return [high, middle, low]


def packed(partial):
    summed, top, total = partial
    stats = pieces(top) + pieces(total)
    rest = jnp.zeros((STAT_ROWS - len(stats), top.shape[1]), jnp.bfloat16)
    return jnp.concatenate([summed.astype(jnp.bfloat16)] + stats + [rest], axis=0)


def unpacked(block):
    stats = block[HD:, :].astype(jnp.float32)
    top = stats[0:1] + stats[1:2] + stats[2:3]
    total = stats[3:4] + stats[4:5] + stats[5:6]
    return block[0:HD, :].astype(jnp.float32), top, total


def held(partial):
    summed, top, total = partial
    rest = jnp.zeros((KEEP_ROWS - 2, top.shape[1]), jnp.float32)
    return jnp.concatenate([summed, top, total, rest], axis=0)


def taken(block):
    return block[0:HD, :], block[HD : HD + 1, :], block[HD + 1 : HD + 2, :]


def joined(one, other):
    top = jnp.maximum(one[1], other[1])
    scale_one = jnp.exp2((one[1] - top) * RATE)
    scale_other = jnp.exp2((other[1] - top) * RATE)
    return (
        one[0] * scale_one + other[0] * scale_other,
        top,
        one[2] * scale_one + other[2] * scale_other,
    )


def attend_kernel(*refs):
    me = lax.axis_index("seq")
    sources, mine_any, send_ref, keep_ref, pages_any = refs[:7], *refs[7:-12]
    *targets, wide_ref, keys_ref, values_ref, asked_ref, sems = refs[-12:]
    loads = [
        pltpu.make_async_copy(source, target, sems.at[index])
        for index, (source, target) in enumerate(zip(sources, targets))
    ]
    for load in loads:
        load.start()
    size = mine_any.shape[0]
    own_pages = pltpu.make_async_copy(
        mine_any, pages_any.at[pl.ds(pl.multiple_of(me * size, size), size), :], sems.at[len(loads)]
    )
    own_pages.start()
    deltas_ref, anchors_ref, scales_ref, lengths_ref, request_ref, queries_ref, new_ref = targets
    blocks = anchors_ref.shape[0] // 2
    rows = deltas_ref.shape[0] // blocks
    tokens = rows // 2
    requests = lengths_ref.shape[0]
    asked = queries_ref.shape[0]
    per_row = asked // request_ref.shape[0]
    width = keep_ref.shape[2]

    for load in loads:
        load.wait()
    wide_ref[...] = deltas_ref[...].astype(jnp.float32)
    scale_key = scales_ref[0:1, :]
    scale_value = scales_ref[1:2, :]

    def one_block(block, carry):
        here = pl.ds(pl.multiple_of(block * tokens, tokens), tokens)
        key = wide_ref[pl.ds(block * rows, tokens, stride=2), :]
        value = wide_ref[pl.ds(block * rows + 1, tokens, stride=2), :]
        keys_ref[here, 0:HD] = (anchors_ref[pl.ds(2 * block, 1), :] + scale_key * key).astype(jnp.bfloat16)
        values_ref[here, :] = (anchors_ref[pl.ds(2 * block + 1, 1), :] + scale_value * value).astype(
            jnp.bfloat16
        )
        return carry

    lax.fori_loop(0, blocks, one_block, 0, unroll=4)

    lane = lax.broadcasted_iota(jnp.int32, (1, HD), 1)
    first = jnp.zeros((1, HD), jnp.int32)
    last = jnp.zeros((1, HD), jnp.int32)
    end = 0 - me * (blocks * tokens)
    for request in range(requests):
        start = end
        end = end + lengths_ref[request]
        first = jnp.where(lane == request, start, first)
        last = jnp.where(lane == request, end, last)
    place = lax.broadcasted_iota(jnp.int32, (blocks * tokens, HD), 0)
    keys_ref[:, HD:] = jnp.where((place >= first) & (place < last), 1.0, 0.0).astype(jnp.bfloat16)

    asked_ref[:, 0:HD] = queries_ref[...]
    wide_lane = lax.broadcasted_iota(jnp.int32, (per_row, HD), 1)

    def one_row(row, carry):
        asked_ref[pl.ds(pl.multiple_of(row * per_row, per_row), per_row), HD:] = jnp.where(
            (wide_lane == request_ref[row]) | (wide_lane >= requests), 0.0, FAR
        ).astype(jnp.bfloat16)
        return carry

    lax.fori_loop(0, request_ref.shape[0], one_row, 0, unroll=4)

    tile = min(256, asked)
    parts = max(1, tile // width)

    def one_tile(index, carry):
        here = asked_ref[pl.ds(pl.multiple_of(index * tile, tile), tile), :]
        scores = lax.dot_general(
            keys_ref[...], here, (((1,), (1,)), ((), ())), preferred_element_type=jnp.float32
        )
        top = jnp.max(scores, axis=0, keepdims=True)
        weights = jnp.exp2((scores - top) * RATE)
        total = jnp.sum(weights, axis=0, keepdims=True)
        summed = lax.dot_general(
            values_ref[...],
            weights.astype(jnp.bfloat16),
            (((0,), (0,)), ((), ())),
            preferred_element_type=jnp.float32,
        )
        for part in range(parts):
            lanes = slice(part * width, (part + 1) * width)
            partial = summed[:, lanes], top[:, lanes], total[:, lanes]
            apart = (index * parts + part) ^ me

            @pl.when(apart % 2 == 1)
            def _(partial=partial, apart=apart):
                send_ref[apart // 2] = packed(partial)

            @pl.when(apart % 2 == 0)
            def _(partial=partial, apart=apart):
                keep_ref[apart // 2] = held(partial)

        return carry

    lax.fori_loop(0, asked // tile, one_tile, 0)

    fresh = new_ref.shape[0] // 4
    new = new_ref[...].astype(jnp.float32).reshape(fresh, 4, HD)
    mine = queries_ref[pl.ds(pl.multiple_of(me * width, width), width), :]
    of_row = lax.broadcasted_iota(jnp.int32, (fresh, width), 1) // (GQ * STEPS)
    same = of_row == lax.broadcasted_iota(jnp.int32, (fresh, width), 0)
    step = lax.broadcasted_iota(jnp.int32, (1, width), 1) % STEPS
    own_scores = []
    for which in range(STEPS):
        scored = lax.dot_general(
            new[:, 2 * which, :].astype(jnp.bfloat16),
            mine,
            (((1,), (1,)), ((), ())),
            preferred_element_type=jnp.float32,
        )
        picked = jnp.sum(jnp.where(same, scored, 0.0), axis=0, keepdims=True)
        own_scores.append(jnp.where(step >= which, picked, FAR))
    own_top = jnp.maximum(own_scores[0], own_scores[1])
    own_total = jnp.zeros((1, width), jnp.float32)
    own_summed = jnp.zeros((HD, width), jnp.float32)
    for which in range(STEPS):
        weight = jnp.exp2((own_scores[which] - own_top) * RATE)
        own_total = own_total + weight
        spread = jnp.where(same, weight, 0.0).astype(jnp.bfloat16)
        own_summed = own_summed + lax.dot_general(
            new[:, 2 * which + 1, :].astype(jnp.bfloat16),
            spread,
            (((0,), (0,)), ((), ())),
            preferred_element_type=jnp.float32,
        )
    keep_ref[0] = held(joined(taken(keep_ref[0]), (own_summed, own_top, own_total)))
    own_pages.wait()


def join_kernel(keep_ref, got_ref, send_ref, next_ref):
    for index in range(keep_ref.shape[0]):
        partial = joined(taken(keep_ref[index]), unpacked(got_ref[index]))
        if index % 2 == 1:
            send_ref[index // 2] = packed(partial)
        else:
            next_ref[index // 2] = held(partial)


def finish_kernel(keep_ref, got_ref, _, *refs):
    *handed, out_ref, pages, sems = refs
    receivers = lax.axis_size("seq")
    me = lax.axis_index("seq")
    size = pages.shape[0] // receivers
    copies = []
    for index, (k, start, count) in enumerate(messages(receivers, size)[:-1]):
        first = pl.multiple_of((me ^ k) * size + start, count)
        copy = pltpu.make_async_copy(handed[index], pages.at[pl.ds(first, count), :], sems.at[index])
        copy.start()
        copies.append(copy)
    summed, _, total = joined(taken(keep_ref[0]), unpacked(got_ref[0]))
    out_ref[...] = (summed / total).T.astype(jnp.bfloat16)
    for copy in copies:
        copy.wait()


def in_hbm(arrays):
    return [pltpu.with_memory_space_constraint(array, pltpu.HBM) for array in arrays]


def per_device(lengths, owner_map, row_request, deltas, anchors, scales, queries, new_kv):
    blocks = anchors.shape[0]
    tokens = deltas.shape[0]
    senders = lax.axis_size("seq")
    me = lax.axis_index("seq")
    rows, steps, _ = queries.shape
    rows_dev = new_kv.shape[0]
    width = rows_dev * GQ * steps
    small = pltpu.CompilerParams(vmem_limit_bytes=8 * 1024 * 1024)

    flat_deltas = deltas.reshape(tokens * 2, HD)
    flat_anchors = anchors.reshape(blocks * 2, HD)
    flat_queries = queries.reshape(rows, steps, GQ, HD).transpose(0, 2, 1, 3).reshape(-1, HD)
    flat_new = new_kv.reshape(rows_dev * 4, HD)

    whole = jax.ShapeDtypeStruct((tokens * 2, HD), jnp.bfloat16)
    plan = messages(senders, blocks // senders)
    block_rows = tokens * 2 // blocks

    def place(plan, deltas):
        return pl.pallas_call(
            functools.partial(place_kernel, plan),
            out_shape=[jax.ShapeDtypeStruct((slots * block_rows, HD), jnp.bfloat16) for _, _, slots in plan],
            in_specs=[HBM] * 4,
            out_specs=[VMEM] * len(plan),
            scratch_shapes=[
                pltpu.SMEM((blocks,), jnp.int32),
                pltpu.SMEM((blocks,), jnp.int32),
                pltpu.SMEM((senders,), jnp.int32),
                pltpu.VMEM((tokens * 2, HD), jnp.bfloat16),
                pltpu.VMEM((blocks * 2, HD), jnp.float32),
                pltpu.VMEM((2, HD), jnp.float32),
                pltpu.SemaphoreType.DMA((4,)),
            ],
            compiler_params=small,
            name="place",
        )(*in_hbm([owner_map, deltas, flat_anchors, scales]))

    (farthest,) = place(plan[:1], flat_deltas)
    farthest, late_deltas = lax.optimization_barrier((farthest, flat_deltas))
    *sent, mine = place(plan[1:], late_deltas)
    sent, mine, late_deltas = lax.optimization_barrier((sent, mine, late_deltas))
    sent = [farthest] + sent
    distant = senders // 2
    got = [exchange(message, k) for message, (k, _, _) in zip(sent[:distant], plan)]

    def parted(count):
        return [
            jax.ShapeDtypeStruct((count // 2, HD + STAT_ROWS, width), jnp.bfloat16),
            jax.ShapeDtypeStruct((count // 2, HD + KEEP_ROWS, width), jnp.float32),
        ]

    needed = (late_deltas, flat_anchors, scales, lengths, row_request, flat_queries, flat_new)
    send, keep, pages = pl.pallas_call(
        attend_kernel,
        out_shape=parted(senders) + [whole],
        in_specs=[HBM] * len(needed) + [ANY],
        out_specs=[VMEM] * 2 + [HBM],
        scratch_shapes=[
            (pltpu.SMEM if array.dtype == jnp.int32 else pltpu.VMEM)(array.shape, array.dtype)
            for array in needed
        ]
        + [
            pltpu.VMEM((tokens * 2, HD), jnp.float32),
            pltpu.VMEM((tokens, 2 * HD), jnp.bfloat16),
            pltpu.VMEM((tokens, HD), jnp.bfloat16),
            pltpu.VMEM((rows * GQ * steps, 2 * HD), jnp.bfloat16),
            pltpu.SemaphoreType.DMA((len(needed) + 1,)),
        ],
        compiler_params=pltpu.CompilerParams(vmem_limit_bytes=32 * 1024 * 1024),
        cost_estimate=pl.CostEstimate(
            flops=6 * rows * GQ * steps * tokens * HD,
            bytes_accessed=tokens * 4 * HD + rows * GQ * steps * 4 * HD,
            transcendentals=rows * GQ * steps * tokens,
        ),
        name="attend",
    )(*in_hbm(needed), mine)

    k, count = 1, senders // 2
    rest, send = lax.optimization_barrier((sent[distant:], send))
    passed = exchange(send, k)
    got += [exchange(message, k) for message, (k, _, _) in zip(rest, plan[distant:])]
    while count > 1:
        send, keep = pl.pallas_call(
            join_kernel,
            out_shape=parted(count),
            in_specs=[VMEM] * 2,
            out_specs=[VMEM] * 2,
            compiler_params=small,
            name="join",
        )(keep, passed)
        k, count = 2 * k, count // 2
        passed = exchange(send, k)
    attended, pages = pl.pallas_call(
        finish_kernel,
        out_shape=[jax.ShapeDtypeStruct((width, HD), jnp.bfloat16), whole],
        in_specs=[VMEM] * 2 + [HBM] + [ANY] * len(got),
        out_specs=[VMEM, HBM],
        scratch_shapes=[pltpu.SemaphoreType.DMA((len(got),))],
        input_output_aliases={2: 1},
        compiler_params=small,
        name="finish",
    )(keep, passed, pages, *got)
    pages = pages.reshape(blocks, tokens // blocks, 2, HD)
    attended = (
        attended.reshape(rows_dev, GQ, steps, HD).transpose(0, 2, 1, 3).reshape(rows_dev, steps, GQ * HD)
    )
    return pages, attended


def solution(mesh):
    placed = (
        P("groups"),
        P(("groups", "seq")),
        P("groups"),
        P(("groups", "seq"), None, "tp"),
        P(("groups", "seq"), None, "tp"),
        P("groups", "tp"),
        P("groups", None, "tp"),
        P(("groups", "seq"), None, None, "tp"),
    )
    return jax.shard_map(
        per_device,
        mesh=mesh,
        in_specs=placed,
        out_specs=(P(("groups", "seq"), None, None, "tp"), P(("groups", "seq"), None, "tp")),
        check_vma=False,
    )
```

```python
import functools

import jax
import jax.numpy as jnp
from jax import lax
from jax.experimental import pallas as pl
from jax.experimental.pallas import tpu as pltpu
from jax.sharding import PartitionSpec as P

HD = 128
GQ = 8
STEPS = 2
STAT_ROWS = 16
KEEP_ROWS = 8
FAR = -1e30
RATE = HD ** (-0.5) * 1.4426950408889634

VMEM = pl.BlockSpec(memory_space=pltpu.VMEM)
HBM = pl.BlockSpec(memory_space=pltpu.HBM)
ANY = pl.BlockSpec(memory_space=pl.ANY)
SMEM = pl.BlockSpec(memory_space=pltpu.SMEM)


def exchange(message, k):
    count = lax.axis_size("seq")
    return lax.ppermute(message, "seq", [(i, i ^ k) for i in range(count)])


def messages(count, capacity):
    early = [(k, 0, capacity) for k in [count - 1] + list(range(1, count // 2))]
    half = capacity // 2
    late = [(k, first, half) for k in range(count // 2, count - 1) for first in (0, half)]
    return early + late + [(0, 0, capacity)]


def place_kernel(plan, owner_any, deltas_any, anchors_any, scales_any, *refs):
    receivers = lax.axis_size("seq")
    me = lax.axis_index("seq")
    outs = refs[:-7]
    owner_ref, source_ref, count_ref, deltas_ref, anchors_ref, scales_ref, sems = refs[-7:]
    blocks = owner_ref.shape[0]
    rows = deltas_ref.shape[0] // blocks
    capacity = blocks // receivers
    loads = [
        pltpu.make_async_copy(source, target, sems.at[index])
        for index, (source, target) in enumerate(
            [
                (owner_any, owner_ref),
                (scales_any, scales_ref),
                (anchors_any, anchors_ref),
                (deltas_any, deltas_ref),
            ]
        )
    ]
    for load in loads:
        load.start()
    bits = capacity.bit_length()
    single = len(plan) == 1
    narrow = receivers * bits < 32
    if not narrow and not single:
        for owner in range(receivers):
            count_ref[owner] = owner * capacity
    loads[0].wait()

    def find(block, counts):
        owner = owner_ref[block]
        if narrow:
            shift = owner * bits
            slot = owner * capacity + ((counts >> shift) & ((1 << bits) - 1))
            counts = counts + (jnp.int32(1) << shift)
        else:
            slot = count_ref[owner]
            count_ref[owner] = slot + 1
        source_ref[slot] = block
        return counts

    def find_one(block, slot):
        source_ref[slot] = block
        return slot + (owner_ref[block] == (me ^ plan[0][0])).astype(jnp.int32)

    lax.fori_loop(0, blocks, find_one if single else find, jnp.int32(0), unroll=8)
    for load in loads[1:]:
        load.wait()
    odd = lax.broadcasted_iota(jnp.int32, (8, HD), 0) % 2 == 1
    scale = jnp.where(odd, scales_ref[1:2, :], scales_ref[0:1, :])[None]
    for (k, start, count), out_ref in zip(plan, outs):
        first = start if single else (me ^ k) * capacity + start

        def one_slot(slot, carry, first=first, out_ref=out_ref):
            block = source_ref[first + slot]
            anchor = jnp.where(
                odd, anchors_ref[pl.ds(2 * block + 1, 1), :], anchors_ref[pl.ds(2 * block, 1), :]
            )[None]
            here = pl.ds(pl.multiple_of(block * rows, rows), rows)
            delta = deltas_ref[here, :].astype(jnp.float32)
            decoded = anchor + scale * delta.reshape(rows // 8, 8, HD)
            out_ref[pl.ds(pl.multiple_of(slot * rows, rows), rows), :] = decoded.reshape(rows, HD).astype(
                jnp.bfloat16
            )
            return carry

        lax.fori_loop(0, count, one_slot, 0, unroll=min(8, count))


def pieces(values):
    high = values.astype(jnp.bfloat16)
    rest = values - high.astype(jnp.float32)
    middle = rest.astype(jnp.bfloat16)
    low = (rest - middle.astype(jnp.float32)).astype(jnp.bfloat16)
    return [high, middle, low]


def packed(partial):
    summed, top, total = partial
    stats = pieces(top) + pieces(total)
    rest = jnp.zeros((STAT_ROWS - len(stats), top.shape[1]), jnp.bfloat16)
    return jnp.concatenate([summed.astype(jnp.bfloat16)] + stats + [rest], axis=0)


def unpacked(block):
    stats = block[HD:, :].astype(jnp.float32)
    top = stats[0:1] + stats[1:2] + stats[2:3]
    total = stats[3:4] + stats[4:5] + stats[5:6]
    return block[0:HD, :].astype(jnp.float32), top, total


def held(partial):
    summed, top, total = partial
    rest = jnp.zeros((KEEP_ROWS - 2, top.shape[1]), jnp.float32)
    return jnp.concatenate([summed, top, total, rest], axis=0)


def taken(block):
    return block[0:HD, :], block[HD : HD + 1, :], block[HD + 1 : HD + 2, :]


def joined(one, other):
    top = jnp.maximum(one[1], other[1])
    scale_one = jnp.exp2((one[1] - top) * RATE)
    scale_other = jnp.exp2((other[1] - top) * RATE)
    return (
        one[0] * scale_one + other[0] * scale_other,
        top,
        one[2] * scale_one + other[2] * scale_other,
    )


def attend_kernel(*refs):
    me = lax.axis_index("seq")
    sources, mine_any, send_ref, keep_ref, pages_any = refs[:7], *refs[7:-12]
    *targets, wide_ref, keys_ref, values_ref, asked_ref, sems = refs[-12:]
    loads = [
        pltpu.make_async_copy(source, target, sems.at[index])
        for index, (source, target) in enumerate(zip(sources, targets))
    ]
    for load in loads:
        load.start()
    size = mine_any.shape[0]
    own_pages = pltpu.make_async_copy(
        mine_any, pages_any.at[pl.ds(pl.multiple_of(me * size, size), size), :], sems.at[len(loads)]
    )
    own_pages.start()
    deltas_ref, anchors_ref, scales_ref, lengths_ref, request_ref, queries_ref, new_ref = targets
    blocks = anchors_ref.shape[0] // 2
    rows = deltas_ref.shape[0] // blocks
    tokens = rows // 2
    requests = lengths_ref.shape[0]
    asked = queries_ref.shape[0]
    per_row = asked // request_ref.shape[0]
    width = keep_ref.shape[2]

    for load in loads:
        load.wait()
    wide_ref[...] = deltas_ref[...].astype(jnp.float32)
    scale_key = scales_ref[0:1, :]
    scale_value = scales_ref[1:2, :]

    def one_block(block, carry):
        here = pl.ds(pl.multiple_of(block * tokens, tokens), tokens)
        key = wide_ref[pl.ds(block * rows, tokens, stride=2), :]
        value = wide_ref[pl.ds(block * rows + 1, tokens, stride=2), :]
        keys_ref[here, 0:HD] = (anchors_ref[pl.ds(2 * block, 1), :] + scale_key * key).astype(jnp.bfloat16)
        values_ref[here, :] = (anchors_ref[pl.ds(2 * block + 1, 1), :] + scale_value * value).astype(
            jnp.bfloat16
        )
        return carry

    lax.fori_loop(0, blocks, one_block, 0, unroll=4)

    lane = lax.broadcasted_iota(jnp.int32, (1, HD), 1)
    first = jnp.zeros((1, HD), jnp.int32)
    last = jnp.zeros((1, HD), jnp.int32)
    end = 0 - me * (blocks * tokens)
    for request in range(requests):
        start = end
        end = end + lengths_ref[request]
        first = jnp.where(lane == request, start, first)
        last = jnp.where(lane == request, end, last)
    place = lax.broadcasted_iota(jnp.int32, (blocks * tokens, HD), 0)
    keys_ref[:, HD:] = jnp.where((place >= first) & (place < last), 1.0, 0.0).astype(jnp.bfloat16)

    asked_ref[:, 0:HD] = queries_ref[...]
    wide_lane = lax.broadcasted_iota(jnp.int32, (per_row, HD), 1)

    def one_row(row, carry):
        asked_ref[pl.ds(pl.multiple_of(row * per_row, per_row), per_row), HD:] = jnp.where(
            (wide_lane == request_ref[row]) | (wide_lane >= requests), 0.0, FAR
        ).astype(jnp.bfloat16)
        return carry

    lax.fori_loop(0, request_ref.shape[0], one_row, 0, unroll=4)

    tile = min(256, asked)
    parts = max(1, tile // width)

    def one_tile(index, carry):
        here = asked_ref[pl.ds(pl.multiple_of(index * tile, tile), tile), :]
        scores = lax.dot_general(
            keys_ref[...], here, (((1,), (1,)), ((), ())), preferred_element_type=jnp.float32
        )
        top = jnp.max(scores, axis=0, keepdims=True)
        weights = jnp.exp2((scores - top) * RATE)
        total = jnp.sum(weights, axis=0, keepdims=True)
        summed = lax.dot_general(
            values_ref[...],
            weights.astype(jnp.bfloat16),
            (((0,), (0,)), ((), ())),
            preferred_element_type=jnp.float32,
        )
        for part in range(parts):
            lanes = slice(part * width, (part + 1) * width)
            partial = summed[:, lanes], top[:, lanes], total[:, lanes]
            apart = (index * parts + part) ^ me

            @pl.when(apart % 2 == 1)
            def _(partial=partial, apart=apart):
                send_ref[apart // 2] = packed(partial)

            @pl.when(apart % 2 == 0)
            def _(partial=partial, apart=apart):
                keep_ref[apart // 2] = held(partial)

        return carry

    lax.fori_loop(0, asked // tile, one_tile, 0)

    fresh = new_ref.shape[0] // 4
    new = new_ref[...].astype(jnp.float32).reshape(fresh, 4, HD)
    mine = queries_ref[pl.ds(pl.multiple_of(me * width, width), width), :]
    of_row = lax.broadcasted_iota(jnp.int32, (fresh, width), 1) // (GQ * STEPS)
    same = of_row == lax.broadcasted_iota(jnp.int32, (fresh, width), 0)
    step = lax.broadcasted_iota(jnp.int32, (1, width), 1) % STEPS
    own_scores = []
    for which in range(STEPS):
        scored = lax.dot_general(
            new[:, 2 * which, :].astype(jnp.bfloat16),
            mine,
            (((1,), (1,)), ((), ())),
            preferred_element_type=jnp.float32,
        )
        picked = jnp.sum(jnp.where(same, scored, 0.0), axis=0, keepdims=True)
        own_scores.append(jnp.where(step >= which, picked, FAR))
    own_top = jnp.maximum(own_scores[0], own_scores[1])
    own_total = jnp.zeros((1, width), jnp.float32)
    own_summed = jnp.zeros((HD, width), jnp.float32)
    for which in range(STEPS):
        weight = jnp.exp2((own_scores[which] - own_top) * RATE)
        own_total = own_total + weight
        spread = jnp.where(same, weight, 0.0).astype(jnp.bfloat16)
        own_summed = own_summed + lax.dot_general(
            new[:, 2 * which + 1, :].astype(jnp.bfloat16),
            spread,
            (((0,), (0,)), ((), ())),
            preferred_element_type=jnp.float32,
        )
    keep_ref[0] = held(joined(taken(keep_ref[0]), (own_summed, own_top, own_total)))
    own_pages.wait()


def join_kernel(keep_ref, got_ref, send_ref, next_ref):
    for index in range(keep_ref.shape[0]):
        partial = joined(taken(keep_ref[index]), unpacked(got_ref[index]))
        if index % 2 == 1:
            send_ref[index // 2] = packed(partial)
        else:
            next_ref[index // 2] = held(partial)


def finish_kernel(keep_ref, got_ref, _, *refs):
    *handed, out_any, pages, out_ref, sems = refs
    receivers = lax.axis_size("seq")
    me = lax.axis_index("seq")
    size = pages.shape[0] // receivers
    copies = []
    for index, (k, start, count) in enumerate(messages(receivers, size)[:-1]):
        first = pl.multiple_of((me ^ k) * size + start, count)
        copy = pltpu.make_async_copy(handed[index], pages.at[pl.ds(first, count), :], sems.at[index])
        copy.start()
        copies.append(copy)
    summed, _, total = joined(taken(keep_ref[0]), unpacked(got_ref[0]))
    out_ref[...] = (summed / total).T.astype(jnp.bfloat16)
    copies.append(pltpu.make_async_copy(out_ref, out_any, sems.at[len(copies)]))
    copies[-1].start()
    for copy in copies:
        copy.wait()


def in_hbm(arrays):
    return [pltpu.with_memory_space_constraint(array, pltpu.HBM) for array in arrays]


def per_device(lengths, owner_map, row_request, deltas, anchors, scales, queries, new_kv):
    blocks = anchors.shape[0]
    tokens = deltas.shape[0]
    senders = lax.axis_size("seq")
    me = lax.axis_index("seq")
    rows, steps, _ = queries.shape
    rows_dev = new_kv.shape[0]
    width = rows_dev * GQ * steps
    small = pltpu.CompilerParams(vmem_limit_bytes=8 * 1024 * 1024)

    flat_deltas = deltas.reshape(tokens * 2, HD)
    flat_anchors = anchors.reshape(blocks * 2, HD)
    flat_queries = queries.reshape(rows, steps, GQ, HD).transpose(0, 2, 1, 3).reshape(-1, HD)
    flat_new = new_kv.reshape(rows_dev * 4, HD)

    whole = jax.ShapeDtypeStruct((tokens * 2, HD), jnp.bfloat16)
    plan = messages(senders, blocks // senders)
    block_rows = tokens * 2 // blocks

    def place(plan, deltas):
        return pl.pallas_call(
            functools.partial(place_kernel, plan),
            out_shape=[jax.ShapeDtypeStruct((slots * block_rows, HD), jnp.bfloat16) for _, _, slots in plan],
            in_specs=[HBM] * 4,
            out_specs=[VMEM] * len(plan),
            scratch_shapes=[
                pltpu.SMEM((blocks,), jnp.int32),
                pltpu.SMEM((blocks,), jnp.int32),
                pltpu.SMEM((senders,), jnp.int32),
                pltpu.VMEM((tokens * 2, HD), jnp.bfloat16),
                pltpu.VMEM((blocks * 2, HD), jnp.float32),
                pltpu.VMEM((2, HD), jnp.float32),
                pltpu.SemaphoreType.DMA((4,)),
            ],
            compiler_params=small,
            name="place",
        )(*in_hbm([owner_map, deltas, flat_anchors, scales]))

    (farthest,) = place(plan[:1], flat_deltas)
    farthest, late_deltas = lax.optimization_barrier((farthest, flat_deltas))
    *sent, mine = place(plan[1:], late_deltas)
    sent, mine, late_deltas = lax.optimization_barrier((sent, mine, late_deltas))
    sent = [farthest] + sent
    distant = senders // 2
    got = [exchange(message, k) for message, (k, _, _) in zip(sent[:distant], plan)]

    def parted(count):
        return [
            jax.ShapeDtypeStruct((count // 2, HD + STAT_ROWS, width), jnp.bfloat16),
            jax.ShapeDtypeStruct((count // 2, HD + KEEP_ROWS, width), jnp.float32),
        ]

    needed = (late_deltas, flat_anchors, scales, lengths, row_request, flat_queries, flat_new)
    send, keep, pages = pl.pallas_call(
        attend_kernel,
        out_shape=parted(senders) + [whole],
        in_specs=[HBM] * len(needed) + [ANY],
        out_specs=[VMEM] * 2 + [HBM],
        scratch_shapes=[
            (pltpu.SMEM if array.dtype == jnp.int32 else pltpu.VMEM)(array.shape, array.dtype)
            for array in needed
        ]
        + [
            pltpu.VMEM((tokens * 2, HD), jnp.float32),
            pltpu.VMEM((tokens, 2 * HD), jnp.bfloat16),
            pltpu.VMEM((tokens, HD), jnp.bfloat16),
            pltpu.VMEM((rows * GQ * steps, 2 * HD), jnp.bfloat16),
            pltpu.SemaphoreType.DMA((len(needed) + 1,)),
        ],
        compiler_params=pltpu.CompilerParams(vmem_limit_bytes=32 * 1024 * 1024),
        cost_estimate=pl.CostEstimate(
            flops=6 * rows * GQ * steps * tokens * HD,
            bytes_accessed=tokens * 4 * HD + rows * GQ * steps * 4 * HD,
            transcendentals=rows * GQ * steps * tokens,
        ),
        name="attend",
    )(*in_hbm(needed), mine)

    k, count = 1, senders // 2
    rest, send = lax.optimization_barrier((sent[distant:], send))
    passed = exchange(send, k)
    got += [exchange(message, k) for message, (k, _, _) in zip(rest, plan[distant:])]
    while count > 1:
        send, keep = pl.pallas_call(
            join_kernel,
            out_shape=parted(count),
            in_specs=[VMEM] * 2,
            out_specs=[VMEM] * 2,
            compiler_params=small,
            name="join",
        )(keep, passed)
        k, count = 2 * k, count // 2
        passed = exchange(send, k)
    attended, pages = pl.pallas_call(
        finish_kernel,
        out_shape=[jax.ShapeDtypeStruct((width, HD), jnp.bfloat16), whole],
        in_specs=[VMEM] * 2 + [HBM] + [ANY] * len(got),
        out_specs=[HBM, HBM],
        scratch_shapes=[
            pltpu.VMEM((width, HD), jnp.bfloat16),
            pltpu.SemaphoreType.DMA((len(got) + 1,)),
        ],
        input_output_aliases={2: 1},
        compiler_params=small,
        name="finish",
    )(keep, passed, pages, *got)
    pages = pages.reshape(blocks, tokens // blocks, 2, HD)
    attended = (
        attended.reshape(rows_dev, GQ, steps, HD).transpose(0, 2, 1, 3).reshape(rows_dev, steps, GQ * HD)
    )
    return pages, attended


def solution(mesh):
    placed = (
        P("groups"),
        P(("groups", "seq")),
        P("groups"),
        P(("groups", "seq"), None, "tp"),
        P(("groups", "seq"), None, "tp"),
        P("groups", "tp"),
        P("groups", None, "tp"),
        P(("groups", "seq"), None, None, "tp"),
    )
    return jax.shard_map(
        per_device,
        mesh=mesh,
        in_specs=placed,
        out_specs=(P(("groups", "seq"), None, None, "tp"), P(("groups", "seq"), None, "tp")),
        check_vma=False,
    )
```

```python
import functools

import jax
import jax.numpy as jnp
from jax import lax
from jax.experimental import pallas as pl
from jax.experimental.pallas import tpu as pltpu
from jax.sharding import PartitionSpec as P

HD = 128
GQ = 8
STEPS = 2
STAT_ROWS = 16
KEEP_ROWS = 8
FAR = -1e30
RATE = HD ** (-0.5) * 1.4426950408889634

VMEM = pl.BlockSpec(memory_space=pltpu.VMEM)
HBM = pl.BlockSpec(memory_space=pltpu.HBM)
ANY = pl.BlockSpec(memory_space=pl.ANY)
SMEM = pl.BlockSpec(memory_space=pltpu.SMEM)


def exchange(message, k):
    count = lax.axis_size("seq")
    return lax.ppermute(message, "seq", [(i, i ^ k) for i in range(count)])


def messages(count, capacity):
    early = [(k, 0, capacity) for k in [count - 1] + list(range(1, count // 2))]
    half = capacity // 2
    late = [(k, first, half) for k in range(count // 2, count - 1) for first in (0, half)]
    return early, late + [(0, 0, capacity)]


def place_kernel(plan, owner_any, deltas_any, anchors_any, scales_any, *refs):
    receivers = lax.axis_size("seq")
    me = lax.axis_index("seq")
    outs = refs[:-7]
    owner_ref, source_ref, count_ref, deltas_ref, anchors_ref, scales_ref, sems = refs[-7:]
    blocks = owner_ref.shape[0]
    rows = deltas_ref.shape[0] // blocks
    capacity = blocks // receivers
    loads = [
        pltpu.make_async_copy(source, target, sems.at[index])
        for index, (source, target) in enumerate(
            [
                (owner_any, owner_ref),
                (scales_any, scales_ref),
                (anchors_any, anchors_ref),
                (deltas_any, deltas_ref),
            ]
        )
    ]
    for load in loads:
        load.start()
    bits = capacity.bit_length()
    narrow = receivers * bits < 32
    if not narrow:
        for owner in range(receivers):
            count_ref[owner] = owner * capacity
    loads[0].wait()

    def find(block, counts):
        owner = owner_ref[block]
        if narrow:
            shift = owner * bits
            slot = owner * capacity + ((counts >> shift) & ((1 << bits) - 1))
            counts = counts + (jnp.int32(1) << shift)
        else:
            slot = count_ref[owner]
            count_ref[owner] = slot + 1
        source_ref[slot] = block
        return counts

    lax.fori_loop(0, blocks, find, jnp.int32(0), unroll=16)
    for load in loads[1:]:
        load.wait()
    odd = lax.broadcasted_iota(jnp.int32, (8, HD), 0) % 2 == 1
    scale = jnp.where(odd, scales_ref[1:2, :], scales_ref[0:1, :])[None]
    for (k, start, count), out_ref in zip(plan, outs):
        first = (me ^ k) * capacity + start

        def one_slot(slot, carry, first=first, out_ref=out_ref):
            block = source_ref[first + slot]
            anchor = jnp.where(
                odd, anchors_ref[pl.ds(2 * block + 1, 1), :], anchors_ref[pl.ds(2 * block, 1), :]
            )[None]
            here = pl.ds(pl.multiple_of(block * rows, rows), rows)
            delta = deltas_ref[here, :].astype(jnp.float32)
            decoded = anchor + scale * delta.reshape(rows // 8, 8, HD)
            out_ref[pl.ds(pl.multiple_of(slot * rows, rows), rows), :] = decoded.reshape(rows, HD).astype(
                jnp.bfloat16
            )
            return carry

        lax.fori_loop(0, count, one_slot, 0, unroll=min(8, count))


def pieces(values):
    high = values.astype(jnp.bfloat16)
    rest = values - high.astype(jnp.float32)
    middle = rest.astype(jnp.bfloat16)
    low = (rest - middle.astype(jnp.float32)).astype(jnp.bfloat16)
    return [high, middle, low]


def packed(partial):
    summed, top, total = partial
    stats = pieces(top) + pieces(total)
    rest = jnp.zeros((STAT_ROWS - len(stats), top.shape[1]), jnp.bfloat16)
    return jnp.concatenate([summed.astype(jnp.bfloat16)] + stats + [rest], axis=0)


def unpacked(block):
    stats = block[HD:, :].astype(jnp.float32)
    top = stats[0:1] + stats[1:2] + stats[2:3]
    total = stats[3:4] + stats[4:5] + stats[5:6]
    return block[0:HD, :].astype(jnp.float32), top, total


def held(partial):
    summed, top, total = partial
    rest = jnp.zeros((KEEP_ROWS - 2, top.shape[1]), jnp.float32)
    return jnp.concatenate([summed, top, total, rest], axis=0)


def taken(block):
    return block[0:HD, :], block[HD : HD + 1, :], block[HD + 1 : HD + 2, :]


def joined(one, other):
    top = jnp.maximum(one[1], other[1])
    scale_one = jnp.exp2((one[1] - top) * RATE)
    scale_other = jnp.exp2((other[1] - top) * RATE)
    return (
        one[0] * scale_one + other[0] * scale_other,
        top,
        one[2] * scale_one + other[2] * scale_other,
    )


def attend_kernel(*refs):
    receivers = lax.axis_size("seq")
    me = lax.axis_index("seq")
    sources, send_ref, keep_ref, *targets = refs[:7], *refs[7:-7]
    wide_ref, keys_ref, values_ref, turned_ref, asked_ref, own_ref, sems = refs[-7:]
    loads = [
        pltpu.make_async_copy(source, target, sems.at[index])
        for index, (source, target) in enumerate(zip(sources, targets))
    ]
    for load in loads:
        load.start()
    deltas_ref, anchors_ref, scales_ref, lengths_ref, request_ref, queries_ref, new_ref = targets
    blocks = anchors_ref.shape[0] // 2
    rows = deltas_ref.shape[0] // blocks
    tokens = rows // 2
    requests = lengths_ref.shape[0]
    asked = queries_ref.shape[0]
    per_row = asked // request_ref.shape[0]
    width = keep_ref.shape[2]
    for load in loads[2:]:
        load.wait()

    lane = lax.broadcasted_iota(jnp.int32, (1, HD), 1)
    first = jnp.zeros((1, HD), jnp.int32)
    last = jnp.zeros((1, HD), jnp.int32)
    end = 0 - me * (blocks * tokens)
    for request in range(requests):
        start = end
        end = end + lengths_ref[request]
        first = jnp.where(lane == request, start, first)
        last = jnp.where(lane == request, end, last)
    place = lax.broadcasted_iota(jnp.int32, (blocks * tokens, HD), 0)
    keys_ref[:, HD:] = jnp.where((place >= first) & (place < last), 1.0, 0.0).astype(jnp.bfloat16)

    asked_ref[:, 0:HD] = queries_ref[...]
    wide_lane = lax.broadcasted_iota(jnp.int32, (per_row, HD), 1)

    def one_row(row, carry):
        asked_ref[pl.ds(pl.multiple_of(row * per_row, per_row), per_row), HD:] = jnp.where(
            (wide_lane == request_ref[row]) | (wide_lane >= requests), 0.0, FAR
        ).astype(jnp.bfloat16)
        return carry

    lax.fori_loop(0, request_ref.shape[0], one_row, 0, unroll=16)

    fresh = new_ref.shape[0] // 4
    new = new_ref[...].astype(jnp.float32).reshape(fresh, 4, HD)
    mine = queries_ref[pl.ds(pl.multiple_of(me * width, width), width), :]
    of_row = lax.broadcasted_iota(jnp.int32, (fresh, width), 1) // (GQ * STEPS)
    same = of_row == lax.broadcasted_iota(jnp.int32, (fresh, width), 0)
    step = lax.broadcasted_iota(jnp.int32, (1, width), 1) % STEPS
    own_scores = []
    for which in range(STEPS):
        scored = lax.dot_general(
            new[:, 2 * which, :].astype(jnp.bfloat16),
            mine,
            (((1,), (1,)), ((), ())),
            preferred_element_type=jnp.float32,
        )
        picked = jnp.sum(jnp.where(same, scored, 0.0), axis=0, keepdims=True)
        own_scores.append(jnp.where(step >= which, picked, FAR))
    own_top = jnp.maximum(own_scores[0], own_scores[1])
    own_total = jnp.zeros((1, width), jnp.float32)
    own_summed = jnp.zeros((HD, width), jnp.float32)
    for which in range(STEPS):
        weight = jnp.exp2((own_scores[which] - own_top) * RATE)
        own_total = own_total + weight
        spread = jnp.where(same, weight, 0.0).astype(jnp.bfloat16)
        own_summed = own_summed + lax.dot_general(
            new[:, 2 * which + 1, :].astype(jnp.bfloat16),
            spread,
            (((0,), (0,)), ((), ())),
            preferred_element_type=jnp.float32,
        )
    own_ref[...] = held((own_summed, own_top, own_total))

    for load in loads[:2]:
        load.wait()
    wide_ref[...] = deltas_ref[...].astype(jnp.float32)
    scale_key = scales_ref[0:1, :]
    scale_value = scales_ref[1:2, :]

    def one_block(block, carry):
        here = pl.ds(pl.multiple_of(block * tokens, tokens), tokens)
        key = wide_ref[pl.ds(block * rows, tokens, stride=2), :]
        value = wide_ref[pl.ds(block * rows + 1, tokens, stride=2), :]
        keys_ref[here, 0:HD] = (anchors_ref[pl.ds(2 * block, 1), :] + scale_key * key).astype(jnp.bfloat16)
        values_ref[here, :] = (anchors_ref[pl.ds(2 * block + 1, 1), :] + scale_value * value).astype(
            jnp.bfloat16
        )
        return carry

    lax.fori_loop(0, blocks, one_block, 0, unroll=16)
    turned_ref[...] = values_ref[...].T

    def partial_of(here):
        scores = lax.dot_general(
            keys_ref[...], here, (((1,), (1,)), ((), ())), preferred_element_type=jnp.float32
        )
        top = jnp.max(scores, axis=0, keepdims=True)
        weights = jnp.exp2((scores - top) * RATE)
        total = jnp.sum(weights, axis=0, keepdims=True)
        summed = jnp.dot(turned_ref[...], weights.astype(jnp.bfloat16), preferred_element_type=jnp.float32)
        return summed, top, total

    if width % HD == 0:
        for apart in range(receivers):
            there = pl.ds(pl.multiple_of((me ^ apart) * width, width), width)
            partial = partial_of(asked_ref[there, :])
            if apart % 2 == 1:
                send_ref[apart // 2] = packed(partial)
            elif apart:
                keep_ref[apart // 2] = held(partial)
            else:
                keep_ref[0] = held(joined(partial, taken(own_ref[...])))
    else:
        tile = min(2 * HD, asked)
        parts = tile // width

        def one_tile(index, carry):
            here = asked_ref[pl.ds(pl.multiple_of(index * tile, tile), tile), :]
            summed, top, total = partial_of(here)
            for part in range(parts):
                lanes = slice(part * width, (part + 1) * width)
                partial = summed[:, lanes], top[:, lanes], total[:, lanes]
                apart = (index * parts + part) ^ me

                @pl.when(apart % 2 == 1)
                def _(partial=partial, apart=apart):
                    send_ref[apart // 2] = packed(partial)

                @pl.when(apart % 2 == 0)
                def _(partial=partial, apart=apart):
                    keep_ref[apart // 2] = held(partial)

            return carry

        lax.fori_loop(0, asked // tile, one_tile, 0)
        keep_ref[0] = held(joined(taken(keep_ref[0]), taken(own_ref[...])))


def join_kernel(keep_ref, got_ref, send_ref, next_ref):
    for index in range(keep_ref.shape[0]):
        partial = joined(taken(keep_ref[index]), unpacked(got_ref[index]))
        if index % 2 == 1:
            send_ref[index // 2] = packed(partial)
        else:
            next_ref[index // 2] = held(partial)


def finish_kernel(keep_ref, got_ref, *refs):
    *handed, out_any, pages, out_ref, sems = refs
    receivers = lax.axis_size("seq")
    me = lax.axis_index("seq")
    size = pages.shape[0] // receivers
    copies = []
    for index, (k, start, count) in enumerate(sum(messages(receivers, size), [])):
        first = pl.multiple_of((me ^ k) * size + start, count)
        copy = pltpu.make_async_copy(handed[index], pages.at[pl.ds(first, count), :], sems.at[index])
        copy.start()
        copies.append(copy)
    summed, _, total = joined(taken(keep_ref[0]), unpacked(got_ref[0]))
    out_ref[...] = (summed / total).T.astype(jnp.bfloat16)
    copies.append(pltpu.make_async_copy(out_ref, out_any, sems.at[len(copies)]))
    copies[-1].start()
    for copy in copies:
        copy.wait()


def in_hbm(arrays):
    return [pltpu.with_memory_space_constraint(array, pltpu.HBM) for array in arrays]


def per_device(lengths, owner_map, row_request, deltas, anchors, scales, queries, new_kv):
    blocks = anchors.shape[0]
    tokens = deltas.shape[0]
    senders = lax.axis_size("seq")
    me = lax.axis_index("seq")
    rows, steps, _ = queries.shape
    rows_dev = new_kv.shape[0]
    width = rows_dev * GQ * steps
    small = pltpu.CompilerParams(vmem_limit_bytes=8 * 1024 * 1024)

    flat_deltas = deltas.reshape(tokens * 2, HD)
    flat_anchors = anchors.reshape(blocks * 2, HD)
    flat_queries = queries.reshape(rows, steps, GQ, HD).transpose(0, 2, 1, 3).reshape(-1, HD)
    flat_new = new_kv.reshape(rows_dev * 4, HD)

    whole = jax.ShapeDtypeStruct((tokens * 2, HD), jnp.bfloat16)
    early, late = messages(senders, blocks // senders)
    block_rows = tokens * 2 // blocks

    def place(plan, deltas):
        return pl.pallas_call(
            functools.partial(place_kernel, plan),
            out_shape=[jax.ShapeDtypeStruct((slots * block_rows, HD), jnp.bfloat16) for _, _, slots in plan],
            in_specs=[HBM] * 4,
            out_specs=[VMEM] * len(plan),
            scratch_shapes=[
                pltpu.SMEM((blocks,), jnp.int32),
                pltpu.SMEM((blocks,), jnp.int32),
                pltpu.SMEM((senders,), jnp.int32),
                pltpu.VMEM((tokens * 2, HD), jnp.bfloat16),
                pltpu.VMEM((blocks * 2, HD), jnp.float32),
                pltpu.VMEM((2, HD), jnp.float32),
                pltpu.SemaphoreType.DMA((4,)),
            ],
            compiler_params=small,
            name="place",
        )(*in_hbm([owner_map, deltas, flat_anchors, scales]))

    sent = place(early, flat_deltas)
    sent, late_deltas = lax.optimization_barrier((sent, flat_deltas))
    got = [exchange(message, k) for message, (k, _, _) in zip(sent, early)]

    def parted(count):
        return [
            jax.ShapeDtypeStruct((count // 2, HD + STAT_ROWS, width), jnp.bfloat16),
            jax.ShapeDtypeStruct((count // 2, HD + KEEP_ROWS, width), jnp.float32),
        ]

    needed = (late_deltas, flat_anchors, scales, lengths, row_request, flat_queries, flat_new)
    send, keep = pl.pallas_call(
        attend_kernel,
        out_shape=parted(senders),
        in_specs=[HBM] * len(needed),
        out_specs=[VMEM] * 2,
        scratch_shapes=[
            (pltpu.SMEM if array.dtype == jnp.int32 else pltpu.VMEM)(array.shape, array.dtype)
            for array in needed
        ]
        + [
            pltpu.VMEM((tokens * 2, HD), jnp.float32),
            pltpu.VMEM((tokens, 2 * HD), jnp.bfloat16),
            pltpu.VMEM((tokens, HD), jnp.bfloat16),
            pltpu.VMEM((HD, tokens), jnp.bfloat16),
            pltpu.VMEM((rows * GQ * steps, 2 * HD), jnp.bfloat16),
            pltpu.VMEM((HD + KEEP_ROWS, width), jnp.float32),
            pltpu.SemaphoreType.DMA((len(needed),)),
        ],
        compiler_params=pltpu.CompilerParams(vmem_limit_bytes=32 * 1024 * 1024),
        cost_estimate=pl.CostEstimate(
            flops=6 * rows * GQ * steps * tokens * HD,
            bytes_accessed=tokens * 4 * HD + rows * GQ * steps * 4 * HD,
            transcendentals=rows * GQ * steps * tokens,
        ),
        name="attend",
    )(*in_hbm(needed))

    k, count = 1, senders // 2
    send, late_deltas = lax.optimization_barrier((send, late_deltas))
    passed = exchange(send, k)
    *sent, mine = place(late, late_deltas)
    got += [exchange(message, k) for message, (k, _, _) in zip(sent, late)] + [mine]
    while count > 1:
        send, keep = pl.pallas_call(
            join_kernel,
            out_shape=parted(count),
            in_specs=[VMEM] * 2,
            out_specs=[VMEM] * 2,
            compiler_params=small,
            name="join",
        )(keep, passed)
        k, count = 2 * k, count // 2
        passed = exchange(send, k)
    attended, pages = pl.pallas_call(
        finish_kernel,
        out_shape=[jax.ShapeDtypeStruct((width, HD), jnp.bfloat16), whole],
        in_specs=[VMEM] * 2 + [ANY] * len(got),
        out_specs=[HBM, HBM],
        scratch_shapes=[
            pltpu.VMEM((width, HD), jnp.bfloat16),
            pltpu.SemaphoreType.DMA((len(got) + 1,)),
        ],
        compiler_params=small,
        name="finish",
    )(keep, passed, *got)
    pages = pages.reshape(blocks, tokens // blocks, 2, HD)
    attended = (
        attended.reshape(rows_dev, GQ, steps, HD).transpose(0, 2, 1, 3).reshape(rows_dev, steps, GQ * HD)
    )
    return pages, attended


def solution(mesh):
    placed = (
        P("groups"),
        P(("groups", "seq")),
        P("groups"),
        P(("groups", "seq"), None, "tp"),
        P(("groups", "seq"), None, "tp"),
        P("groups", "tp"),
        P("groups", None, "tp"),
        P(("groups", "seq"), None, None, "tp"),
    )
    return jax.shard_map(
        per_device,
        mesh=mesh,
        in_specs=placed,
        out_specs=(P(("groups", "seq"), None, None, "tp"), P(("groups", "seq"), None, "tp")),
        check_vma=False,
    )
```

```python
import functools

import jax
import jax.numpy as jnp
from jax import lax
from jax.experimental import pallas as pl
from jax.experimental.pallas import tpu as pltpu
from jax.sharding import PartitionSpec as P

HD = 128
GQ = 8
STEPS = 2
STAT_ROWS = 16
KEEP_ROWS = 8
FAR = -1e30
RATE = HD ** (-0.5) * 1.4426950408889634

VMEM = pl.BlockSpec(memory_space=pltpu.VMEM)
HBM = pl.BlockSpec(memory_space=pltpu.HBM)
ANY = pl.BlockSpec(memory_space=pl.ANY)
SMEM = pl.BlockSpec(memory_space=pltpu.SMEM)


def exchange(message, k):
    count = lax.axis_size("seq")
    return lax.ppermute(message, "seq", [(i, i ^ k) for i in range(count)])


def messages(count, capacity):
    half = capacity // 2
    ahead = [(count - 1, 0, capacity)]
    beyond = [(k, first, half) for k in range(count // 2, count - 1) for first in (0, half)]
    near = [(k, first, half) for k in range(1, count // 2) for first in (0, half)]
    return ahead, beyond, near, [(0, 0, capacity)]


def place_kernel(plan, owner_any, deltas_any, anchors_any, scales_any, *refs):
    receivers = lax.axis_size("seq")
    me = lax.axis_index("seq")
    outs = refs[:-7]
    owner_ref, source_ref, count_ref, deltas_ref, anchors_ref, scales_ref, sems = refs[-7:]
    blocks = owner_ref.shape[0]
    rows = deltas_ref.shape[0] // blocks
    capacity = blocks // receivers
    loads = [
        pltpu.make_async_copy(source, target, sems.at[index])
        for index, (source, target) in enumerate(
            [
                (owner_any, owner_ref),
                (scales_any, scales_ref),
                (anchors_any, anchors_ref),
                (deltas_any, deltas_ref),
            ]
        )
    ]
    for load in loads:
        load.start()
    bits = capacity.bit_length()
    narrow = receivers * bits < 32
    if not narrow:
        for owner in range(receivers):
            count_ref[owner] = owner * capacity
    loads[0].wait()

    def find(block, counts):
        owner = owner_ref[block]
        if narrow:
            shift = owner * bits
            slot = owner * capacity + ((counts >> shift) & ((1 << bits) - 1))
            counts = counts + (jnp.int32(1) << shift)
        else:
            slot = count_ref[owner]
            count_ref[owner] = slot + 1
        source_ref[slot] = block
        return counts

    lax.fori_loop(0, blocks, find, jnp.int32(0), unroll=16)
    for load in loads[1:]:
        load.wait()
    odd = lax.broadcasted_iota(jnp.int32, (8, HD), 0) % 2 == 1
    scale = jnp.where(odd, scales_ref[1:2, :], scales_ref[0:1, :])[None]
    for (k, start, count), out_ref in zip(plan, outs):
        first = (me ^ k) * capacity + start

        def one_slot(slot, carry, first=first, out_ref=out_ref):
            block = source_ref[first + slot]
            anchor = jnp.where(
                odd, anchors_ref[pl.ds(2 * block + 1, 1), :], anchors_ref[pl.ds(2 * block, 1), :]
            )[None]
            here = pl.ds(pl.multiple_of(block * rows, rows), rows)
            delta = deltas_ref[here, :].astype(jnp.float32)
            decoded = anchor + scale * delta.reshape(rows // 8, 8, HD)
            out_ref[pl.ds(pl.multiple_of(slot * rows, rows), rows), :] = decoded.reshape(rows, HD).astype(
                jnp.bfloat16
            )
            return carry

        lax.fori_loop(0, count, one_slot, 0, unroll=min(8, count))


def pieces(values):
    high = values.astype(jnp.bfloat16)
    rest = values - high.astype(jnp.float32)
    middle = rest.astype(jnp.bfloat16)
    low = (rest - middle.astype(jnp.float32)).astype(jnp.bfloat16)
    return [high, middle, low]


def packed(partial):
    summed, top, total = partial
    stats = pieces(top) + pieces(total)
    rest = jnp.zeros((STAT_ROWS - len(stats), top.shape[1]), jnp.bfloat16)
    return jnp.concatenate([summed.astype(jnp.bfloat16)] + stats + [rest], axis=0)


def unpacked(block):
    stats = block[HD:, :].astype(jnp.float32)
    top = stats[0:1] + stats[1:2] + stats[2:3]
    total = stats[3:4] + stats[4:5] + stats[5:6]
    return block[0:HD, :].astype(jnp.float32), top, total


def held(partial):
    summed, top, total = partial
    rest = jnp.zeros((KEEP_ROWS - 2, top.shape[1]), jnp.float32)
    return jnp.concatenate([summed, top, total, rest], axis=0)


def taken(block):
    return block[0:HD, :], block[HD : HD + 1, :], block[HD + 1 : HD + 2, :]


def joined(one, other):
    top = jnp.maximum(one[1], other[1])
    scale_one = jnp.exp2((one[1] - top) * RATE)
    scale_other = jnp.exp2((other[1] - top) * RATE)
    return (
        one[0] * scale_one + other[0] * scale_other,
        top,
        one[2] * scale_one + other[2] * scale_other,
    )


def attend(parity, width, keys_ref, turned_ref, asked_ref, store):
    me = lax.axis_index("seq")
    asked = asked_ref.shape[0]

    def partial_of(here):
        scores = lax.dot_general(
            keys_ref[...], here, (((1,), (1,)), ((), ())), preferred_element_type=jnp.float32
        )
        top = jnp.max(scores, axis=0, keepdims=True)
        weights = jnp.exp2((scores - top) * RATE)
        total = jnp.sum(weights, axis=0, keepdims=True)
        summed = jnp.dot(turned_ref[...], weights.astype(jnp.bfloat16), preferred_element_type=jnp.float32)
        return summed, top, total

    if width % HD == 0:
        for index in range(asked // width // 2):
            there = (me ^ (2 * index + parity)) * width
            store(index, partial_of(asked_ref[pl.ds(pl.multiple_of(there, width), width), :]))
        return
    tile = min(2 * HD, asked)
    parts = tile // width

    def one_tile(tile_index, carry):
        here = asked_ref[pl.ds(pl.multiple_of(tile_index * tile, tile), tile), :]
        summed, top, total = partial_of(here)
        for part in range(parts):
            lanes = slice(part * width, (part + 1) * width)
            apart = (tile_index * parts + part) ^ me

            @pl.when(apart % 2 == parity)
            def _(lanes=lanes, apart=apart):
                store(apart // 2, (summed[:, lanes], top[:, lanes], total[:, lanes]))

        return carry

    lax.fori_loop(0, asked // tile, one_tile, 0)


def first_kernel(*refs):
    me = lax.axis_index("seq")
    sources, send_ref, keys_ref, turned_ref, asked_ref, own_ref, *targets = refs[:7], *refs[7:-3]
    wide_ref, values_ref, sems = refs[-3:]
    loads = [
        pltpu.make_async_copy(source, target, sems.at[index])
        for index, (source, target) in enumerate(zip(sources, targets))
    ]
    for load in loads:
        load.start()
    deltas_ref, anchors_ref, scales_ref, lengths_ref, request_ref, queries_ref, new_ref = targets
    blocks = anchors_ref.shape[0] // 2
    rows = deltas_ref.shape[0] // blocks
    tokens = rows // 2
    requests = lengths_ref.shape[0]
    asked = queries_ref.shape[0]
    per_row = asked // request_ref.shape[0]
    width = send_ref.shape[2]
    for load in loads[2:]:
        load.wait()

    lane = lax.broadcasted_iota(jnp.int32, (1, HD), 1)
    first = jnp.zeros((1, HD), jnp.int32)
    last = jnp.zeros((1, HD), jnp.int32)
    end = 0 - me * (blocks * tokens)
    for request in range(requests):
        start = end
        end = end + lengths_ref[request]
        first = jnp.where(lane == request, start, first)
        last = jnp.where(lane == request, end, last)
    place = lax.broadcasted_iota(jnp.int32, (blocks * tokens, HD), 0)
    keys_ref[:, HD:] = jnp.where((place >= first) & (place < last), 1.0, 0.0).astype(jnp.bfloat16)

    asked_ref[:, 0:HD] = queries_ref[...]
    wide_lane = lax.broadcasted_iota(jnp.int32, (per_row, HD), 1)

    def one_row(row, carry):
        asked_ref[pl.ds(pl.multiple_of(row * per_row, per_row), per_row), HD:] = jnp.where(
            (wide_lane == request_ref[row]) | (wide_lane >= requests), 0.0, FAR
        ).astype(jnp.bfloat16)
        return carry

    lax.fori_loop(0, request_ref.shape[0], one_row, 0, unroll=16)

    fresh = new_ref.shape[0] // 4
    new = new_ref[...].astype(jnp.float32).reshape(fresh, 4, HD)
    mine = queries_ref[pl.ds(pl.multiple_of(me * width, width), width), :]
    of_row = lax.broadcasted_iota(jnp.int32, (fresh, width), 1) // (GQ * STEPS)
    same = of_row == lax.broadcasted_iota(jnp.int32, (fresh, width), 0)
    step = lax.broadcasted_iota(jnp.int32, (1, width), 1) % STEPS
    own_scores = []
    for which in range(STEPS):
        scored = lax.dot_general(
            new[:, 2 * which, :].astype(jnp.bfloat16),
            mine,
            (((1,), (1,)), ((), ())),
            preferred_element_type=jnp.float32,
        )
        picked = jnp.sum(jnp.where(same, scored, 0.0), axis=0, keepdims=True)
        own_scores.append(jnp.where(step >= which, picked, FAR))
    own_top = jnp.maximum(own_scores[0], own_scores[1])
    own_total = jnp.zeros((1, width), jnp.float32)
    own_summed = jnp.zeros((HD, width), jnp.float32)
    for which in range(STEPS):
        weight = jnp.exp2((own_scores[which] - own_top) * RATE)
        own_total = own_total + weight
        spread = jnp.where(same, weight, 0.0).astype(jnp.bfloat16)
        own_summed = own_summed + lax.dot_general(
            new[:, 2 * which + 1, :].astype(jnp.bfloat16),
            spread,
            (((0,), (0,)), ((), ())),
            preferred_element_type=jnp.float32,
        )
    own_ref[...] = held((own_summed, own_top, own_total))

    for load in loads[:2]:
        load.wait()
    wide_ref[...] = deltas_ref[...].astype(jnp.float32)
    scale_key = scales_ref[0:1, :]
    scale_value = scales_ref[1:2, :]

    def one_block(block, carry):
        here = pl.ds(pl.multiple_of(block * tokens, tokens), tokens)
        key = wide_ref[pl.ds(block * rows, tokens, stride=2), :]
        value = wide_ref[pl.ds(block * rows + 1, tokens, stride=2), :]
        keys_ref[here, 0:HD] = (anchors_ref[pl.ds(2 * block, 1), :] + scale_key * key).astype(jnp.bfloat16)
        values_ref[here, :] = (anchors_ref[pl.ds(2 * block + 1, 1), :] + scale_value * value).astype(
            jnp.bfloat16
        )
        return carry

    lax.fori_loop(0, blocks, one_block, 0, unroll=16)
    turned_ref[...] = values_ref[...].T

    def store(index, partial):
        send_ref[index] = packed(partial)

    attend(1, width, keys_ref, turned_ref, asked_ref, store)


def second_kernel(keys_ref, turned_ref, asked_ref, own_ref, keep_ref):
    def store(index, partial):
        keep_ref[index] = held(partial)

    attend(0, keep_ref.shape[2], keys_ref, turned_ref, asked_ref, store)
    keep_ref[0] = held(joined(taken(keep_ref[0]), taken(own_ref[...])))


def join_kernel(keep_ref, got_ref, send_ref, next_ref):
    for index in range(keep_ref.shape[0]):
        partial = joined(taken(keep_ref[index]), unpacked(got_ref[index]))
        if index % 2 == 1:
            send_ref[index // 2] = packed(partial)
        else:
            next_ref[index // 2] = held(partial)


def settle(plan, handed, pages, sems):
    receivers = lax.axis_size("seq")
    me = lax.axis_index("seq")
    rows = pages.shape[0] // receivers
    copies = []
    for index, (k, start, slots) in enumerate(plan):
        size = handed[index].shape[0]
        first = pl.multiple_of((me ^ k) * rows + start * (size // slots), size)
        copies.append(pltpu.make_async_copy(handed[index], pages.at[pl.ds(first, size), :], sems.at[index]))
        copies[-1].start()
    return copies


def settle_kernel(plan, *refs):
    *handed, pages, sems = refs
    for copy in settle(plan, handed, pages, sems):
        copy.wait()


def finish_kernel(plan, keep_ref, got_ref, _, *refs):
    *handed, out_any, pages, out_ref, sems = refs
    copies = settle(plan, handed, pages, sems)
    summed, _, total = joined(taken(keep_ref[0]), unpacked(got_ref[0]))
    out_ref[...] = (summed / total).T.astype(jnp.bfloat16)
    copies.append(pltpu.make_async_copy(out_ref, out_any, sems.at[len(copies)]))
    copies[-1].start()
    for copy in copies:
        copy.wait()


def in_hbm(arrays):
    return [pltpu.with_memory_space_constraint(array, pltpu.HBM) for array in arrays]


def per_device(lengths, owner_map, row_request, deltas, anchors, scales, queries, new_kv):
    blocks = anchors.shape[0]
    tokens = deltas.shape[0]
    senders = lax.axis_size("seq")
    me = lax.axis_index("seq")
    rows, steps, _ = queries.shape
    rows_dev = new_kv.shape[0]
    width = rows_dev * GQ * steps
    small = pltpu.CompilerParams(vmem_limit_bytes=8 * 1024 * 1024)

    flat_deltas = deltas.reshape(tokens * 2, HD)
    flat_anchors = anchors.reshape(blocks * 2, HD)
    flat_queries = queries.reshape(rows, steps, GQ, HD).transpose(0, 2, 1, 3).reshape(-1, HD)
    flat_new = new_kv.reshape(rows_dev * 4, HD)

    whole = jax.ShapeDtypeStruct((tokens * 2, HD), jnp.bfloat16)
    ahead, beyond, near, own = messages(senders, blocks // senders)
    block_rows = tokens * 2 // blocks

    def place(plan, deltas):
        return pl.pallas_call(
            functools.partial(place_kernel, plan),
            out_shape=[jax.ShapeDtypeStruct((slots * block_rows, HD), jnp.bfloat16) for _, _, slots in plan],
            in_specs=[HBM] * 4,
            out_specs=[VMEM] * len(plan),
            scratch_shapes=[
                pltpu.SMEM((blocks,), jnp.int32),
                pltpu.SMEM((blocks,), jnp.int32),
                pltpu.SMEM((senders,), jnp.int32),
                pltpu.VMEM((tokens * 2, HD), jnp.bfloat16),
                pltpu.VMEM((blocks * 2, HD), jnp.float32),
                pltpu.VMEM((2, HD), jnp.float32),
                pltpu.SemaphoreType.DMA((4,)),
            ],
            compiler_params=small,
            name="place",
        )(*in_hbm([owner_map, deltas, flat_anchors, scales]))

    def hand(sent, plan):
        return [exchange(message, k) for message, (k, _, _) in zip(sent, plan)]

    sent = place(ahead, flat_deltas)
    sent, late_deltas = lax.optimization_barrier((sent, flat_deltas))
    got_ahead = hand(sent, ahead)

    def leaving(count):
        return jax.ShapeDtypeStruct((count // 2, HD + STAT_ROWS, width), jnp.bfloat16)

    def staying(count):
        return jax.ShapeDtypeStruct((count // 2, HD + KEEP_ROWS, width), jnp.float32)

    needed = (late_deltas, flat_anchors, scales, lengths, row_request, flat_queries, flat_new)
    roomy = pltpu.CompilerParams(vmem_limit_bytes=32 * 1024 * 1024)
    send, *common = pl.pallas_call(
        first_kernel,
        out_shape=[
            leaving(senders),
            jax.ShapeDtypeStruct((tokens, 2 * HD), jnp.bfloat16),
            jax.ShapeDtypeStruct((HD, tokens), jnp.bfloat16),
            jax.ShapeDtypeStruct((rows * GQ * steps, 2 * HD), jnp.bfloat16),
            jax.ShapeDtypeStruct((HD + KEEP_ROWS, width), jnp.float32),
        ],
        in_specs=[HBM] * len(needed),
        out_specs=[VMEM] * 5,
        scratch_shapes=[
            (pltpu.SMEM if array.dtype == jnp.int32 else pltpu.VMEM)(array.shape, array.dtype)
            for array in needed
        ]
        + [
            pltpu.VMEM((tokens * 2, HD), jnp.float32),
            pltpu.VMEM((tokens, HD), jnp.bfloat16),
            pltpu.SemaphoreType.DMA((len(needed),)),
        ],
        compiler_params=roomy,
        name="attend_leaving",
    )(*in_hbm(needed))

    k, count = 1, senders // 2
    send, late_deltas = lax.optimization_barrier((send, late_deltas))
    passed = exchange(send, k)
    *sent, mine = place(beyond + near + own, late_deltas)
    got = hand(sent[: len(beyond)], beyond)
    sent = sent[len(beyond) :]
    keep = pl.pallas_call(
        second_kernel,
        out_shape=staying(senders),
        in_specs=[VMEM] * 4,
        out_specs=VMEM,
        compiler_params=roomy,
        name="attend_staying",
    )(*common)
    while count > 1:
        send, keep = pl.pallas_call(
            join_kernel,
            out_shape=[leaving(count), staying(count)],
            in_specs=[VMEM] * 2,
            out_specs=[VMEM] * 2,
            compiler_params=small,
            name="join",
        )(keep, passed)
        if k == 1:
            sent, send = lax.optimization_barrier((sent, send))
            got += hand(sent, near)
        k, count = 2 * k, count // 2
        if count == 1:
            settled = ahead + own
            pages = pl.pallas_call(
                functools.partial(settle_kernel, settled),
                out_shape=whole,
                in_specs=[ANY] * len(settled),
                out_specs=HBM,
                scratch_shapes=[pltpu.SemaphoreType.DMA((len(settled),))],
                compiler_params=small,
                name="settle",
            )(*got_ahead, mine)
            send, pages = lax.optimization_barrier((send, pages))
        passed = exchange(send, k)
    attended, pages = pl.pallas_call(
        functools.partial(finish_kernel, beyond + near),
        out_shape=[jax.ShapeDtypeStruct((width, HD), jnp.bfloat16), whole],
        in_specs=[VMEM] * 2 + [HBM] + [ANY] * len(got),
        out_specs=[HBM, HBM],
        scratch_shapes=[
            pltpu.VMEM((width, HD), jnp.bfloat16),
            pltpu.SemaphoreType.DMA((len(got) + 1,)),
        ],
        input_output_aliases={2: 1},
        compiler_params=small,
        name="finish",
    )(keep, passed, pages, *got)
    pages = pages.reshape(blocks, tokens // blocks, 2, HD)
    attended = (
        attended.reshape(rows_dev, GQ, steps, HD).transpose(0, 2, 1, 3).reshape(rows_dev, steps, GQ * HD)
    )
    return pages, attended


def solution(mesh):
    placed = (
        P("groups"),
        P(("groups", "seq")),
        P("groups"),
        P(("groups", "seq"), None, "tp"),
        P(("groups", "seq"), None, "tp"),
        P("groups", "tp"),
        P("groups", None, "tp"),
        P(("groups", "seq"), None, None, "tp"),
    )
    return jax.shard_map(
        per_device,
        mesh=mesh,
        in_specs=placed,
        out_specs=(P(("groups", "seq"), None, None, "tp"), P(("groups", "seq"), None, "tp")),
        check_vma=False,
    )
```

```python
import functools

import jax
import jax.numpy as jnp
from jax import lax
from jax.experimental import pallas as pl
from jax.experimental.pallas import tpu as pltpu
from jax.sharding import PartitionSpec as P

HD = 128
GQ = 8
STEPS = 2
STAT_ROWS = 16
KEEP_ROWS = 8
FAR = -1e30
RATE = HD ** (-0.5) * 1.4426950408889634

VMEM = pl.BlockSpec(memory_space=pltpu.VMEM)
HBM = pl.BlockSpec(memory_space=pltpu.HBM)
ANY = pl.BlockSpec(memory_space=pl.ANY)
SMEM = pl.BlockSpec(memory_space=pltpu.SMEM)


def inner(device, count):
    return (device ^ (device // (count // 2))) & 1


def partner(device, k, count):
    far = count // 2
    if k == far:
        return device ^ (1 + inner(device, count) * (far - 1))
    if k == 1:
        return device ^ (far - inner(device, count) * (far - 1))
    return device ^ k


def source(device, k, count):
    far = count // 2
    if k == far:
        return device ^ (far - inner(device, count) * (far - 1))
    if k == 1:
        return device ^ (1 + inner(device, count) * (far - 1))
    return device ^ k


def exchange(message, k):
    count = lax.axis_size("seq")
    return lax.ppermute(message, "seq", [(i, i ^ k) for i in range(count)])


def hand(message, k):
    count = lax.axis_size("seq")
    return lax.ppermute(message, "seq", [(i, partner(i, k, count)) for i in range(count)])


def messages(count, capacity):
    half = capacity // 2
    ahead = [(k, 0, capacity) for k in reversed(range(count // 2, count))]
    behind = [(k, first, half) for k in reversed(range(1, count // 2)) for first in (0, half)]
    return ahead, behind, [(0, 0, capacity)]


def place_kernel(plan, owner_any, deltas_any, anchors_any, scales_any, *refs):
    receivers = lax.axis_size("seq")
    me = lax.axis_index("seq")
    outs = refs[:-7]
    owner_ref, source_ref, count_ref, deltas_ref, anchors_ref, scales_ref, sems = refs[-7:]
    blocks = owner_ref.shape[0]
    rows = deltas_ref.shape[0] // blocks
    capacity = blocks // receivers
    loads = [
        pltpu.make_async_copy(source, target, sems.at[index])
        for index, (source, target) in enumerate(
            [
                (owner_any, owner_ref),
                (scales_any, scales_ref),
                (anchors_any, anchors_ref),
                (deltas_any, deltas_ref),
            ]
        )
    ]
    for load in loads:
        load.start()
    bits = capacity.bit_length()
    narrow = receivers * bits < 32
    if not narrow:
        for owner in range(receivers):
            count_ref[owner] = owner * capacity
    loads[0].wait()

    def find(block, counts):
        owner = owner_ref[block]
        if narrow:
            shift = owner * bits
            slot = owner * capacity + ((counts >> shift) & ((1 << bits) - 1))
            counts = counts + (jnp.int32(1) << shift)
        else:
            slot = count_ref[owner]
            count_ref[owner] = slot + 1
        source_ref[slot] = block
        return counts

    lax.fori_loop(0, blocks, find, jnp.int32(0), unroll=16)
    for load in loads[1:]:
        load.wait()
    odd = lax.broadcasted_iota(jnp.int32, (8, HD), 0) % 2 == 1
    scale = jnp.where(odd, scales_ref[1:2, :], scales_ref[0:1, :])[None]
    for (k, start, count), out_ref in zip(plan, outs):
        first = partner(me, k, receivers) * capacity + start

        def one_slot(slot, carry, first=first, out_ref=out_ref):
            block = source_ref[first + slot]
            anchor = jnp.where(
                odd, anchors_ref[pl.ds(2 * block + 1, 1), :], anchors_ref[pl.ds(2 * block, 1), :]
            )[None]
            here = pl.ds(pl.multiple_of(block * rows, rows), rows)
            delta = deltas_ref[here, :].astype(jnp.float32)
            decoded = anchor + scale * delta.reshape(rows // 8, 8, HD)
            out_ref[pl.ds(pl.multiple_of(slot * rows, rows), rows), :] = decoded.reshape(rows, HD).astype(
                jnp.bfloat16
            )
            return carry

        lax.fori_loop(0, count, one_slot, 0, unroll=min(8, count))


def pieces(values):
    high = values.astype(jnp.bfloat16)
    rest = values - high.astype(jnp.float32)
    middle = rest.astype(jnp.bfloat16)
    low = (rest - middle.astype(jnp.float32)).astype(jnp.bfloat16)
    return [high, middle, low]


def packed(partial):
    summed, top, total = partial
    stats = pieces(top) + pieces(total)
    rest = jnp.zeros((STAT_ROWS - len(stats), top.shape[1]), jnp.bfloat16)
    return jnp.concatenate([summed.astype(jnp.bfloat16)] + stats + [rest], axis=0)


def unpacked(block):
    stats = block[HD:, :].astype(jnp.float32)
    top = stats[0:1] + stats[1:2] + stats[2:3]
    total = stats[3:4] + stats[4:5] + stats[5:6]
    return block[0:HD, :].astype(jnp.float32), top, total


def held(partial):
    summed, top, total = partial
    rest = jnp.zeros((KEEP_ROWS - 2, top.shape[1]), jnp.float32)
    return jnp.concatenate([summed, top, total, rest], axis=0)


def taken(block):
    return block[0:HD, :], block[HD : HD + 1, :], block[HD + 1 : HD + 2, :]


def joined(one, other):
    top = jnp.maximum(one[1], other[1])
    scale_one = jnp.exp2((one[1] - top) * RATE)
    scale_other = jnp.exp2((other[1] - top) * RATE)
    return (
        one[0] * scale_one + other[0] * scale_other,
        top,
        one[2] * scale_one + other[2] * scale_other,
    )


def attend(parity, width, keys_ref, turned_ref, asked_ref, store):
    me = lax.axis_index("seq")
    asked = asked_ref.shape[0]

    def partial_of(here):
        scores = lax.dot_general(
            keys_ref[...], here, (((1,), (1,)), ((), ())), preferred_element_type=jnp.float32
        )
        top = jnp.max(scores, axis=0, keepdims=True)
        weights = jnp.exp2((scores - top) * RATE)
        total = jnp.sum(weights, axis=0, keepdims=True)
        summed = jnp.dot(turned_ref[...], weights.astype(jnp.bfloat16), preferred_element_type=jnp.float32)
        return summed, top, total

    if width % HD == 0:
        for index in range(asked // width // 2):
            there = (me ^ (2 * index + parity)) * width
            store(index, partial_of(asked_ref[pl.ds(pl.multiple_of(there, width), width), :]))
        return
    tile = min(2 * HD, asked)
    parts = tile // width

    def one_tile(tile_index, carry):
        here = asked_ref[pl.ds(pl.multiple_of(tile_index * tile, tile), tile), :]
        summed, top, total = partial_of(here)
        for part in range(parts):
            lanes = slice(part * width, (part + 1) * width)
            apart = (tile_index * parts + part) ^ me

            @pl.when(apart % 2 == parity)
            def _(lanes=lanes, apart=apart):
                store(apart // 2, (summed[:, lanes], top[:, lanes], total[:, lanes]))

        return carry

    lax.fori_loop(0, asked // tile, one_tile, 0)


def first_kernel(*refs):
    me = lax.axis_index("seq")
    sources, send_ref, keys_ref, turned_ref, asked_ref, own_ref, *targets = refs[:7], *refs[7:-3]
    wide_ref, values_ref, sems = refs[-3:]
    loads = [
        pltpu.make_async_copy(source, target, sems.at[index])
        for index, (source, target) in enumerate(zip(sources, targets))
    ]
    for load in loads:
        load.start()
    deltas_ref, anchors_ref, scales_ref, lengths_ref, request_ref, queries_ref, new_ref = targets
    blocks = anchors_ref.shape[0] // 2
    rows = deltas_ref.shape[0] // blocks
    tokens = rows // 2
    requests = lengths_ref.shape[0]
    asked = queries_ref.shape[0]
    per_row = asked // request_ref.shape[0]
    width = send_ref.shape[2]
    for load in loads[2:]:
        load.wait()

    lane = lax.broadcasted_iota(jnp.int32, (1, HD), 1)
    first = jnp.zeros((1, HD), jnp.int32)
    last = jnp.zeros((1, HD), jnp.int32)
    end = 0 - me * (blocks * tokens)
    for request in range(requests):
        start = end
        end = end + lengths_ref[request]
        first = jnp.where(lane == request, start, first)
        last = jnp.where(lane == request, end, last)
    place = lax.broadcasted_iota(jnp.int32, (blocks * tokens, HD), 0)
    keys_ref[:, HD:] = jnp.where((place >= first) & (place < last), 1.0, 0.0).astype(jnp.bfloat16)

    asked_ref[:, 0:HD] = queries_ref[...]
    wide_lane = lax.broadcasted_iota(jnp.int32, (per_row, HD), 1)

    def one_row(row, carry):
        asked_ref[pl.ds(pl.multiple_of(row * per_row, per_row), per_row), HD:] = jnp.where(
            (wide_lane == request_ref[row]) | (wide_lane >= requests), 0.0, FAR
        ).astype(jnp.bfloat16)
        return carry

    lax.fori_loop(0, request_ref.shape[0], one_row, 0, unroll=16)

    fresh = new_ref.shape[0] // 4
    new = new_ref[...].astype(jnp.float32).reshape(fresh, 4, HD)
    mine = queries_ref[pl.ds(pl.multiple_of(me * width, width), width), :]
    of_row = lax.broadcasted_iota(jnp.int32, (fresh, width), 1) // (GQ * STEPS)
    same = of_row == lax.broadcasted_iota(jnp.int32, (fresh, width), 0)
    step = lax.broadcasted_iota(jnp.int32, (1, width), 1) % STEPS
    own_scores = []
    for which in range(STEPS):
        scored = lax.dot_general(
            new[:, 2 * which, :].astype(jnp.bfloat16),
            mine,
            (((1,), (1,)), ((), ())),
            preferred_element_type=jnp.float32,
        )
        picked = jnp.sum(jnp.where(same, scored, 0.0), axis=0, keepdims=True)
        own_scores.append(jnp.where(step >= which, picked, FAR))
    own_top = jnp.maximum(own_scores[0], own_scores[1])
    own_total = jnp.zeros((1, width), jnp.float32)
    own_summed = jnp.zeros((HD, width), jnp.float32)
    for which in range(STEPS):
        weight = jnp.exp2((own_scores[which] - own_top) * RATE)
        own_total = own_total + weight
        spread = jnp.where(same, weight, 0.0).astype(jnp.bfloat16)
        own_summed = own_summed + lax.dot_general(
            new[:, 2 * which + 1, :].astype(jnp.bfloat16),
            spread,
            (((0,), (0,)), ((), ())),
            preferred_element_type=jnp.float32,
        )
    own_ref[...] = held((own_summed, own_top, own_total))

    for load in loads[:2]:
        load.wait()
    wide_ref[...] = deltas_ref[...].astype(jnp.float32)
    scale_key = scales_ref[0:1, :]
    scale_value = scales_ref[1:2, :]

    def one_block(block, carry):
        here = pl.ds(pl.multiple_of(block * tokens, tokens), tokens)
        key = wide_ref[pl.ds(block * rows, tokens, stride=2), :]
        value = wide_ref[pl.ds(block * rows + 1, tokens, stride=2), :]
        keys_ref[here, 0:HD] = (anchors_ref[pl.ds(2 * block, 1), :] + scale_key * key).astype(jnp.bfloat16)
        values_ref[here, :] = (anchors_ref[pl.ds(2 * block + 1, 1), :] + scale_value * value).astype(
            jnp.bfloat16
        )
        return carry

    lax.fori_loop(0, blocks, one_block, 0, unroll=16)
    turned_ref[...] = values_ref[...].T

    def store(index, partial):
        send_ref[index] = packed(partial)

    attend(1, width, keys_ref, turned_ref, asked_ref, store)


def second_kernel(keys_ref, turned_ref, asked_ref, own_ref, keep_ref):
    def store(index, partial):
        keep_ref[index] = held(partial)

    attend(0, keep_ref.shape[2], keys_ref, turned_ref, asked_ref, store)
    keep_ref[0] = held(joined(taken(keep_ref[0]), taken(own_ref[...])))


def join_kernel(keep_ref, got_ref, send_ref, next_ref):
    for index in range(keep_ref.shape[0]):
        partial = joined(taken(keep_ref[index]), unpacked(got_ref[index]))
        if index % 2 == 1:
            send_ref[index // 2] = packed(partial)
        else:
            next_ref[index // 2] = held(partial)


def finish_kernel(plan, keep_ref, got_ref, *refs):
    *handed, out_any, pages, out_ref, sems = refs
    receivers = lax.axis_size("seq")
    me = lax.axis_index("seq")
    rows = pages.shape[0] // receivers
    copies = []
    for index, (k, start, slots) in enumerate(plan):
        size = handed[index].shape[0]
        sender = source(me, k, receivers) if k else me
        first = pl.multiple_of(sender * rows + start * (size // slots), size)
        copies.append(pltpu.make_async_copy(handed[index], pages.at[pl.ds(first, size), :], sems.at[index]))
        copies[-1].start()
    summed, _, total = joined(taken(keep_ref[0]), unpacked(got_ref[0]))
    out_ref[...] = (summed / total).T.astype(jnp.bfloat16)
    copies.append(pltpu.make_async_copy(out_ref, out_any, sems.at[len(copies)]))
    copies[-1].start()
    for copy in copies:
        copy.wait()


def in_hbm(arrays):
    return [pltpu.with_memory_space_constraint(array, pltpu.HBM) for array in arrays]


def per_device(lengths, owner_map, row_request, deltas, anchors, scales, queries, new_kv):
    blocks = anchors.shape[0]
    tokens = deltas.shape[0]
    senders = lax.axis_size("seq")
    me = lax.axis_index("seq")
    rows, steps, _ = queries.shape
    rows_dev = new_kv.shape[0]
    width = rows_dev * GQ * steps
    small = pltpu.CompilerParams(vmem_limit_bytes=8 * 1024 * 1024)

    flat_deltas = deltas.reshape(tokens * 2, HD)
    flat_anchors = anchors.reshape(blocks * 2, HD)
    flat_queries = queries.reshape(rows, steps, GQ, HD).transpose(0, 2, 1, 3).reshape(-1, HD)
    flat_new = new_kv.reshape(rows_dev * 4, HD)

    whole = jax.ShapeDtypeStruct((tokens * 2, HD), jnp.bfloat16)
    ahead, behind, own = messages(senders, blocks // senders)
    block_rows = tokens * 2 // blocks

    def place(plan, deltas):
        return pl.pallas_call(
            functools.partial(place_kernel, plan),
            out_shape=[jax.ShapeDtypeStruct((slots * block_rows, HD), jnp.bfloat16) for _, _, slots in plan],
            in_specs=[HBM] * 4,
            out_specs=[VMEM] * len(plan),
            scratch_shapes=[
                pltpu.SMEM((blocks,), jnp.int32),
                pltpu.SMEM((blocks,), jnp.int32),
                pltpu.SMEM((senders,), jnp.int32),
                pltpu.VMEM((tokens * 2, HD), jnp.bfloat16),
                pltpu.VMEM((blocks * 2, HD), jnp.float32),
                pltpu.VMEM((2, HD), jnp.float32),
                pltpu.SemaphoreType.DMA((4,)),
            ],
            compiler_params=small,
            name="place",
        )(*in_hbm([owner_map, deltas, flat_anchors, scales]))

    (farthest,) = place(ahead[:1], flat_deltas)
    farthest, late_deltas = lax.optimization_barrier((farthest, flat_deltas))
    sent = place(ahead[1:] + behind + own, late_deltas)
    sent, late_deltas = lax.optimization_barrier((sent, late_deltas))
    sent = [farthest, *sent]
    got = [hand(message, k) for message, (k, _, _) in zip(sent, ahead)]

    def leaving(count):
        return jax.ShapeDtypeStruct((count // 2, HD + STAT_ROWS, width), jnp.bfloat16)

    def staying(count):
        return jax.ShapeDtypeStruct((count // 2, HD + KEEP_ROWS, width), jnp.float32)

    needed = (late_deltas, flat_anchors, scales, lengths, row_request, flat_queries, flat_new)
    roomy = pltpu.CompilerParams(vmem_limit_bytes=32 * 1024 * 1024)
    send, *common = pl.pallas_call(
        first_kernel,
        out_shape=[
            leaving(senders),
            jax.ShapeDtypeStruct((tokens, 2 * HD), jnp.bfloat16),
            jax.ShapeDtypeStruct((HD, tokens), jnp.bfloat16),
            jax.ShapeDtypeStruct((rows * GQ * steps, 2 * HD), jnp.bfloat16),
            jax.ShapeDtypeStruct((HD + KEEP_ROWS, width), jnp.float32),
        ],
        in_specs=[HBM] * len(needed),
        out_specs=[VMEM] * 5,
        scratch_shapes=[
            (pltpu.SMEM if array.dtype == jnp.int32 else pltpu.VMEM)(array.shape, array.dtype)
            for array in needed
        ]
        + [
            pltpu.VMEM((tokens * 2, HD), jnp.float32),
            pltpu.VMEM((tokens, HD), jnp.bfloat16),
            pltpu.SemaphoreType.DMA((len(needed),)),
        ],
        compiler_params=roomy,
        name="attend_leaving",
    )(*in_hbm(needed))

    k, count = 1, senders // 2
    rest, send = lax.optimization_barrier((sent[len(ahead) : -1], send))
    passed = exchange(send, k)
    got += [hand(message, k) for message, (k, _, _) in zip(rest, behind)] + sent[-1:]
    keep = pl.pallas_call(
        second_kernel,
        out_shape=staying(senders),
        in_specs=[VMEM] * 4,
        out_specs=VMEM,
        compiler_params=roomy,
        name="attend_staying",
    )(*common)
    while count > 1:
        send, keep = pl.pallas_call(
            join_kernel,
            out_shape=[leaving(count), staying(count)],
            in_specs=[VMEM] * 2,
            out_specs=[VMEM] * 2,
            compiler_params=small,
            name="join",
        )(keep, passed)
        k, count = 2 * k, count // 2
        passed = exchange(send, k)
    attended, pages = pl.pallas_call(
        functools.partial(finish_kernel, ahead + behind + own),
        out_shape=[jax.ShapeDtypeStruct((width, HD), jnp.bfloat16), whole],
        in_specs=[VMEM] * 2 + [ANY] * len(got),
        out_specs=[HBM, HBM],
        scratch_shapes=[
            pltpu.VMEM((width, HD), jnp.bfloat16),
            pltpu.SemaphoreType.DMA((len(got) + 1,)),
        ],
        compiler_params=small,
        name="finish",
    )(keep, passed, *got)
    pages = pages.reshape(blocks, tokens // blocks, 2, HD)
    attended = (
        attended.reshape(rows_dev, GQ, steps, HD).transpose(0, 2, 1, 3).reshape(rows_dev, steps, GQ * HD)
    )
    return pages, attended


def solution(mesh):
    placed = (
        P("groups"),
        P(("groups", "seq")),
        P("groups"),
        P(("groups", "seq"), None, "tp"),
        P(("groups", "seq"), None, "tp"),
        P("groups", "tp"),
        P("groups", None, "tp"),
        P(("groups", "seq"), None, None, "tp"),
    )
    return jax.shard_map(
        per_device,
        mesh=mesh,
        in_specs=placed,
        out_specs=(P(("groups", "seq"), None, None, "tp"), P(("groups", "seq"), None, "tp")),
        check_vma=False,
    )
```

```python
import functools

import jax
import jax.numpy as jnp
from jax import lax
from jax.experimental import pallas as pl
from jax.experimental.pallas import tpu as pltpu
from jax.sharding import PartitionSpec as P

HD = 128
GQ = 8
STEPS = 2
STAT_ROWS = 16
KEEP_ROWS = 8
FAR = -1e30
RATE = HD ** (-0.5) * 1.4426950408889634

VMEM = pl.BlockSpec(memory_space=pltpu.VMEM)
HBM = pl.BlockSpec(memory_space=pltpu.HBM)
ANY = pl.BlockSpec(memory_space=pl.ANY)
SMEM = pl.BlockSpec(memory_space=pltpu.SMEM)


def inner(device, count):
    return (device ^ (device // (count // 2))) & 1


def partner(device, k, count):
    far = count // 2
    if k == far:
        return device ^ (1 + inner(device, count) * (far - 1))
    if k == 1:
        return device ^ (far - inner(device, count) * (far - 1))
    return device ^ k


def source(device, k, count):
    far = count // 2
    if k == far:
        return device ^ (far - inner(device, count) * (far - 1))
    if k == 1:
        return device ^ (1 + inner(device, count) * (far - 1))
    return device ^ k


def exchange(message, k):
    count = lax.axis_size("seq")
    return lax.ppermute(message, "seq", [(i, i ^ k) for i in range(count)])


def hand(message, k):
    count = lax.axis_size("seq")
    return lax.ppermute(message, "seq", [(i, partner(i, k, count)) for i in range(count)])


def messages(count, capacity):
    half = capacity // 2
    ahead = [(k, 0, capacity) for k in reversed(range(count // 2, count))]
    behind = [(k, first, half) for k in reversed(range(1, count // 2)) for first in (0, half)]
    return ahead, behind, [(0, 0, capacity)]


def place_kernel(plan, owner_any, deltas_any, anchors_any, scales_any, *refs):
    receivers = lax.axis_size("seq")
    me = lax.axis_index("seq")
    outs = refs[:-7]
    owner_ref, source_ref, count_ref, deltas_ref, anchors_ref, scales_ref, sems = refs[-7:]
    blocks = owner_ref.shape[0]
    rows = deltas_ref.shape[0] // blocks
    capacity = blocks // receivers
    loads = [
        pltpu.make_async_copy(source, target, sems.at[index])
        for index, (source, target) in enumerate(
            [
                (owner_any, owner_ref),
                (scales_any, scales_ref),
                (anchors_any, anchors_ref),
                (deltas_any, deltas_ref),
            ]
        )
    ]
    for load in loads:
        load.start()
    bits = capacity.bit_length()
    narrow = receivers * bits < 32
    if not narrow:
        for owner in range(receivers):
            count_ref[owner] = owner * capacity
    loads[0].wait()

    def find(block, counts):
        owner = owner_ref[block]
        if narrow:
            shift = owner * bits
            slot = owner * capacity + ((counts >> shift) & ((1 << bits) - 1))
            counts = counts + (jnp.int32(1) << shift)
        else:
            slot = count_ref[owner]
            count_ref[owner] = slot + 1
        source_ref[slot] = block
        return counts

    lax.fori_loop(0, blocks, find, jnp.int32(0), unroll=16)
    for load in loads[1:]:
        load.wait()
    odd = lax.broadcasted_iota(jnp.int32, (8, HD), 0) % 2 == 1
    scale = jnp.where(odd, scales_ref[1:2, :], scales_ref[0:1, :])[None]
    for (k, start, count), out_ref in zip(plan, outs):
        first = partner(me, k, receivers) * capacity + start

        def one_slot(slot, carry, first=first, out_ref=out_ref):
            block = source_ref[first + slot]
            anchor = jnp.where(
                odd, anchors_ref[pl.ds(2 * block + 1, 1), :], anchors_ref[pl.ds(2 * block, 1), :]
            )[None]
            here = pl.ds(pl.multiple_of(block * rows, rows), rows)
            delta = deltas_ref[here, :].astype(jnp.float32)
            decoded = anchor + scale * delta.reshape(rows // 8, 8, HD)
            out_ref[pl.ds(pl.multiple_of(slot * rows, rows), rows), :] = decoded.reshape(rows, HD).astype(
                jnp.bfloat16
            )
            return carry

        lax.fori_loop(0, count, one_slot, 0, unroll=min(8, count))


def pieces(values):
    high = values.astype(jnp.bfloat16)
    rest = values - high.astype(jnp.float32)
    middle = rest.astype(jnp.bfloat16)
    low = (rest - middle.astype(jnp.float32)).astype(jnp.bfloat16)
    return [high, middle, low]


def packed(partial):
    summed, top, total = partial
    stats = pieces(top) + pieces(total)
    rest = jnp.zeros((STAT_ROWS - len(stats), top.shape[1]), jnp.bfloat16)
    return jnp.concatenate([summed.astype(jnp.bfloat16)] + stats + [rest], axis=0)


def unpacked(block):
    stats = block[HD:, :].astype(jnp.float32)
    top = stats[0:1] + stats[1:2] + stats[2:3]
    total = stats[3:4] + stats[4:5] + stats[5:6]
    return block[0:HD, :].astype(jnp.float32), top, total


def held(partial):
    summed, top, total = partial
    rest = jnp.zeros((KEEP_ROWS - 2, top.shape[1]), jnp.float32)
    return jnp.concatenate([summed, top, total, rest], axis=0)


def taken(block):
    return block[0:HD, :], block[HD : HD + 1, :], block[HD + 1 : HD + 2, :]


def joined(one, other):
    top = jnp.maximum(one[1], other[1])
    scale_one = jnp.exp2((one[1] - top) * RATE)
    scale_other = jnp.exp2((other[1] - top) * RATE)
    return (
        one[0] * scale_one + other[0] * scale_other,
        top,
        one[2] * scale_one + other[2] * scale_other,
    )


def attend(parity, width, keys_ref, turned_ref, asked_ref, store):
    me = lax.axis_index("seq")
    asked = asked_ref.shape[0]

    def partial_of(here):
        scores = lax.dot_general(
            keys_ref[...], here, (((1,), (1,)), ((), ())), preferred_element_type=jnp.float32
        )
        top = jnp.max(scores, axis=0, keepdims=True)
        weights = jnp.exp2((scores - top) * RATE)
        total = jnp.sum(weights, axis=0, keepdims=True)
        summed = jnp.dot(turned_ref[...], weights.astype(jnp.bfloat16), preferred_element_type=jnp.float32)
        return summed, top, total

    if width % HD == 0:
        for index in range(asked // width // 2):
            there = (me ^ (2 * index + parity)) * width
            store(index, partial_of(asked_ref[pl.ds(pl.multiple_of(there, width), width), :]))
        return
    tile = min(2 * HD, asked)
    parts = tile // width

    def one_tile(tile_index, carry):
        here = asked_ref[pl.ds(pl.multiple_of(tile_index * tile, tile), tile), :]
        summed, top, total = partial_of(here)
        for part in range(parts):
            lanes = slice(part * width, (part + 1) * width)
            apart = (tile_index * parts + part) ^ me

            @pl.when(apart % 2 == parity)
            def _(lanes=lanes, apart=apart):
                store(apart // 2, (summed[:, lanes], top[:, lanes], total[:, lanes]))

        return carry

    lax.fori_loop(0, asked // tile, one_tile, 0)


def first_kernel(*refs):
    me = lax.axis_index("seq")
    sources, send_ref, keys_ref, turned_ref, asked_ref, own_ref, *targets = refs[:7], *refs[7:-3]
    wide_ref, values_ref, sems = refs[-3:]
    loads = [
        pltpu.make_async_copy(source, target, sems.at[index])
        for index, (source, target) in enumerate(zip(sources, targets))
    ]
    for load in loads:
        load.start()
    deltas_ref, anchors_ref, scales_ref, lengths_ref, request_ref, queries_ref, new_ref = targets
    blocks = anchors_ref.shape[0] // 2
    rows = deltas_ref.shape[0] // blocks
    tokens = rows // 2
    requests = lengths_ref.shape[0]
    asked = queries_ref.shape[0]
    per_row = asked // request_ref.shape[0]
    width = send_ref.shape[2]
    for load in loads[2:]:
        load.wait()

    lane = lax.broadcasted_iota(jnp.int32, (1, HD), 1)
    first = jnp.zeros((1, HD), jnp.int32)
    last = jnp.zeros((1, HD), jnp.int32)
    end = 0 - me * (blocks * tokens)
    for request in range(requests):
        start = end
        end = end + lengths_ref[request]
        first = jnp.where(lane == request, start, first)
        last = jnp.where(lane == request, end, last)
    place = lax.broadcasted_iota(jnp.int32, (blocks * tokens, HD), 0)
    keys_ref[:, HD:] = jnp.where((place >= first) & (place < last), 1.0, 0.0).astype(jnp.bfloat16)

    asked_ref[:, 0:HD] = queries_ref[...]
    wide_lane = lax.broadcasted_iota(jnp.int32, (per_row, HD), 1)

    def one_row(row, carry):
        asked_ref[pl.ds(pl.multiple_of(row * per_row, per_row), per_row), HD:] = jnp.where(
            (wide_lane == request_ref[row]) | (wide_lane >= requests), 0.0, FAR
        ).astype(jnp.bfloat16)
        return carry

    lax.fori_loop(0, request_ref.shape[0], one_row, 0, unroll=16)

    fresh = new_ref.shape[0] // 4
    new = new_ref[...].astype(jnp.float32).reshape(fresh, 4, HD)
    mine = queries_ref[pl.ds(pl.multiple_of(me * width, width), width), :]
    of_row = lax.broadcasted_iota(jnp.int32, (fresh, width), 1) // (GQ * STEPS)
    same = of_row == lax.broadcasted_iota(jnp.int32, (fresh, width), 0)
    step = lax.broadcasted_iota(jnp.int32, (1, width), 1) % STEPS
    own_scores = []
    for which in range(STEPS):
        scored = lax.dot_general(
            new[:, 2 * which, :].astype(jnp.bfloat16),
            mine,
            (((1,), (1,)), ((), ())),
            preferred_element_type=jnp.float32,
        )
        picked = jnp.sum(jnp.where(same, scored, 0.0), axis=0, keepdims=True)
        own_scores.append(jnp.where(step >= which, picked, FAR))
    own_top = jnp.maximum(own_scores[0], own_scores[1])
    own_total = jnp.zeros((1, width), jnp.float32)
    own_summed = jnp.zeros((HD, width), jnp.float32)
    for which in range(STEPS):
        weight = jnp.exp2((own_scores[which] - own_top) * RATE)
        own_total = own_total + weight
        spread = jnp.where(same, weight, 0.0).astype(jnp.bfloat16)
        own_summed = own_summed + lax.dot_general(
            new[:, 2 * which + 1, :].astype(jnp.bfloat16),
            spread,
            (((0,), (0,)), ((), ())),
            preferred_element_type=jnp.float32,
        )
    own_ref[...] = held((own_summed, own_top, own_total))

    for load in loads[:2]:
        load.wait()
    wide_ref[...] = deltas_ref[...].astype(jnp.float32)
    scale_key = scales_ref[0:1, :]
    scale_value = scales_ref[1:2, :]

    def one_block(block, carry):
        here = pl.ds(pl.multiple_of(block * tokens, tokens), tokens)
        key = wide_ref[pl.ds(block * rows, tokens, stride=2), :]
        value = wide_ref[pl.ds(block * rows + 1, tokens, stride=2), :]
        keys_ref[here, 0:HD] = (anchors_ref[pl.ds(2 * block, 1), :] + scale_key * key).astype(jnp.bfloat16)
        values_ref[here, :] = (anchors_ref[pl.ds(2 * block + 1, 1), :] + scale_value * value).astype(
            jnp.bfloat16
        )
        return carry

    lax.fori_loop(0, blocks, one_block, 0, unroll=16)
    turned_ref[...] = values_ref[...].T

    def store(index, partial):
        send_ref[index] = packed(partial)

    attend(1, width, keys_ref, turned_ref, asked_ref, store)


def second_kernel(keys_ref, turned_ref, asked_ref, own_ref, keep_ref):
    def store(index, partial):
        keep_ref[index] = held(partial)

    attend(0, keep_ref.shape[2], keys_ref, turned_ref, asked_ref, store)
    keep_ref[0] = held(joined(taken(keep_ref[0]), taken(own_ref[...])))


def join_kernel(keep_ref, got_ref, send_ref, next_ref):
    for index in range(keep_ref.shape[0]):
        partial = joined(taken(keep_ref[index]), unpacked(got_ref[index]))
        if index % 2 == 1:
            send_ref[index // 2] = packed(partial)
        else:
            next_ref[index // 2] = held(partial)


def settle(plan, handed, pages, sems):
    receivers = lax.axis_size("seq")
    me = lax.axis_index("seq")
    rows = pages.shape[0] // receivers
    copies = []
    for index, (k, start, slots) in enumerate(plan):
        size = handed[index].shape[0]
        sender = source(me, k, receivers) if k else me
        first = pl.multiple_of(sender * rows + start * (size // slots), size)
        copies.append(pltpu.make_async_copy(handed[index], pages.at[pl.ds(first, size), :], sems.at[index]))
        copies[-1].start()
    return copies


def settle_kernel(plan, *refs):
    *handed, pages, sems = refs
    for copy in settle(plan, handed, pages, sems):
        copy.wait()


def finish_kernel(plan, keep_ref, got_ref, _, *refs):
    *handed, out_any, pages, out_ref, sems = refs
    copies = settle(plan, handed, pages, sems)
    summed, _, total = joined(taken(keep_ref[0]), unpacked(got_ref[0]))
    out_ref[...] = (summed / total).T.astype(jnp.bfloat16)
    copies.append(pltpu.make_async_copy(out_ref, out_any, sems.at[len(copies)]))
    copies[-1].start()
    for copy in copies:
        copy.wait()


def in_hbm(arrays):
    return [pltpu.with_memory_space_constraint(array, pltpu.HBM) for array in arrays]


def per_device(lengths, owner_map, row_request, deltas, anchors, scales, queries, new_kv):
    blocks = anchors.shape[0]
    tokens = deltas.shape[0]
    senders = lax.axis_size("seq")
    me = lax.axis_index("seq")
    rows, steps, _ = queries.shape
    rows_dev = new_kv.shape[0]
    width = rows_dev * GQ * steps
    small = pltpu.CompilerParams(vmem_limit_bytes=8 * 1024 * 1024)

    flat_deltas = deltas.reshape(tokens * 2, HD)
    flat_anchors = anchors.reshape(blocks * 2, HD)
    flat_queries = queries.reshape(rows, steps, GQ, HD).transpose(0, 2, 1, 3).reshape(-1, HD)
    flat_new = new_kv.reshape(rows_dev * 4, HD)

    whole = jax.ShapeDtypeStruct((tokens * 2, HD), jnp.bfloat16)
    ahead, behind, own = messages(senders, blocks // senders)
    block_rows = tokens * 2 // blocks

    def place(plan, deltas):
        return pl.pallas_call(
            functools.partial(place_kernel, plan),
            out_shape=[jax.ShapeDtypeStruct((slots * block_rows, HD), jnp.bfloat16) for _, _, slots in plan],
            in_specs=[HBM] * 4,
            out_specs=[VMEM] * len(plan),
            scratch_shapes=[
                pltpu.SMEM((blocks,), jnp.int32),
                pltpu.SMEM((blocks,), jnp.int32),
                pltpu.SMEM((senders,), jnp.int32),
                pltpu.VMEM((tokens * 2, HD), jnp.bfloat16),
                pltpu.VMEM((blocks * 2, HD), jnp.float32),
                pltpu.VMEM((2, HD), jnp.float32),
                pltpu.SemaphoreType.DMA((4,)),
            ],
            compiler_params=small,
            name="place",
        )(*in_hbm([owner_map, deltas, flat_anchors, scales]))

    sent = place(ahead, flat_deltas)
    sent, late_deltas = lax.optimization_barrier((sent, flat_deltas))
    got_ahead = [hand(message, k) for message, (k, _, _) in zip(sent, ahead)]

    def leaving(count):
        return jax.ShapeDtypeStruct((count // 2, HD + STAT_ROWS, width), jnp.bfloat16)

    def staying(count):
        return jax.ShapeDtypeStruct((count // 2, HD + KEEP_ROWS, width), jnp.float32)

    needed = (late_deltas, flat_anchors, scales, lengths, row_request, flat_queries, flat_new)
    roomy = pltpu.CompilerParams(vmem_limit_bytes=32 * 1024 * 1024)
    send, *common = pl.pallas_call(
        first_kernel,
        out_shape=[
            leaving(senders),
            jax.ShapeDtypeStruct((tokens, 2 * HD), jnp.bfloat16),
            jax.ShapeDtypeStruct((HD, tokens), jnp.bfloat16),
            jax.ShapeDtypeStruct((rows * GQ * steps, 2 * HD), jnp.bfloat16),
            jax.ShapeDtypeStruct((HD + KEEP_ROWS, width), jnp.float32),
        ],
        in_specs=[HBM] * len(needed),
        out_specs=[VMEM] * 5,
        scratch_shapes=[
            (pltpu.SMEM if array.dtype == jnp.int32 else pltpu.VMEM)(array.shape, array.dtype)
            for array in needed
        ]
        + [
            pltpu.VMEM((tokens * 2, HD), jnp.float32),
            pltpu.VMEM((tokens, HD), jnp.bfloat16),
            pltpu.SemaphoreType.DMA((len(needed),)),
        ],
        compiler_params=roomy,
        name="attend_leaving",
    )(*in_hbm(needed))

    k, count = 1, senders // 2
    send, late_deltas = lax.optimization_barrier((send, late_deltas))
    passed = exchange(send, k)
    *sent, mine = place(behind + own, late_deltas)
    got = got_ahead[1:] + [hand(message, k) for message, (k, _, _) in zip(sent, behind)]
    keep = pl.pallas_call(
        second_kernel,
        out_shape=staying(senders),
        in_specs=[VMEM] * 4,
        out_specs=VMEM,
        compiler_params=roomy,
        name="attend_staying",
    )(*common)
    while count > 1:
        send, keep = pl.pallas_call(
            join_kernel,
            out_shape=[leaving(count), staying(count)],
            in_specs=[VMEM] * 2,
            out_specs=[VMEM] * 2,
            compiler_params=small,
            name="join",
        )(keep, passed)
        k, count = 2 * k, count // 2
        passed = exchange(send, k)
    settled = ahead[:1] + own
    pages = pl.pallas_call(
        functools.partial(settle_kernel, settled),
        out_shape=whole,
        in_specs=[ANY] * len(settled),
        out_specs=HBM,
        scratch_shapes=[pltpu.SemaphoreType.DMA((len(settled),))],
        compiler_params=small,
        name="settle",
    )(got_ahead[0], mine)
    attended, pages = pl.pallas_call(
        functools.partial(finish_kernel, ahead[1:] + behind),
        out_shape=[jax.ShapeDtypeStruct((width, HD), jnp.bfloat16), whole],
        in_specs=[VMEM] * 2 + [HBM] + [ANY] * len(got),
        out_specs=[HBM, HBM],
        scratch_shapes=[
            pltpu.VMEM((width, HD), jnp.bfloat16),
            pltpu.SemaphoreType.DMA((len(got) + 1,)),
        ],
        input_output_aliases={2: 1},
        compiler_params=small,
        name="finish",
    )(keep, passed, pages, *got)
    pages = pages.reshape(blocks, tokens // blocks, 2, HD)
    attended = (
        attended.reshape(rows_dev, GQ, steps, HD).transpose(0, 2, 1, 3).reshape(rows_dev, steps, GQ * HD)
    )
    return pages, attended


def solution(mesh):
    placed = (
        P("groups"),
        P(("groups", "seq")),
        P("groups"),
        P(("groups", "seq"), None, "tp"),
        P(("groups", "seq"), None, "tp"),
        P("groups", "tp"),
        P("groups", None, "tp"),
        P(("groups", "seq"), None, None, "tp"),
    )
    return jax.shard_map(
        per_device,
        mesh=mesh,
        in_specs=placed,
        out_specs=(P(("groups", "seq"), None, None, "tp"), P(("groups", "seq"), None, "tp")),
        check_vma=False,
    )
```

```python
import functools

import jax
import jax.numpy as jnp
from jax import lax
from jax.experimental import pallas as pl
from jax.experimental.pallas import tpu as pltpu
from jax.sharding import PartitionSpec as P

HD = 128
GQ = 8
STEPS = 2
STAT_ROWS = 16
KEEP_ROWS = 8
FAR = -1e30
RATE = HD ** (-0.5) * 1.4426950408889634

VMEM = pl.BlockSpec(memory_space=pltpu.VMEM)
HBM = pl.BlockSpec(memory_space=pltpu.HBM)
ANY = pl.BlockSpec(memory_space=pl.ANY)
SMEM = pl.BlockSpec(memory_space=pltpu.SMEM)


def inner(device, count):
    return (device ^ (device // (count // 2))) & 1


def partner(device, k, count):
    far = count // 2
    if k == far:
        return device ^ (1 + inner(device, count) * (far - 1))
    if k == 1:
        return device ^ (far - inner(device, count) * (far - 1))
    return device ^ k


def source(device, k, count):
    far = count // 2
    if k == far:
        return device ^ (far - inner(device, count) * (far - 1))
    if k == 1:
        return device ^ (1 + inner(device, count) * (far - 1))
    return device ^ k


def exchange(message, k):
    count = lax.axis_size("seq")
    return lax.ppermute(message, "seq", [(i, i ^ k) for i in range(count)])


def hand(message, k):
    count = lax.axis_size("seq")
    return lax.ppermute(message, "seq", [(i, partner(i, k, count)) for i in range(count)])


def messages(count, capacity):
    half = capacity // 2
    ahead = [(count - 1, 0, capacity)]
    behind = [(k, 0, capacity) for k in reversed(range(count // 2, count - 1))]
    behind += [(k, first, half) for k in reversed(range(1, count // 2)) for first in (0, half)]
    return ahead, behind, [(0, 0, capacity)]


def place_kernel(plan, owner_any, deltas_any, anchors_any, scales_any, *refs):
    receivers = lax.axis_size("seq")
    me = lax.axis_index("seq")
    outs = refs[:-7]
    owner_ref, source_ref, count_ref, deltas_ref, anchors_ref, scales_ref, sems = refs[-7:]
    blocks = owner_ref.shape[0]
    rows = deltas_ref.shape[0] // blocks
    capacity = blocks // receivers
    loads = [
        pltpu.make_async_copy(source, target, sems.at[index])
        for index, (source, target) in enumerate(
            [
                (owner_any, owner_ref),
                (scales_any, scales_ref),
                (anchors_any, anchors_ref),
                (deltas_any, deltas_ref),
            ]
        )
    ]
    for load in loads:
        load.start()
    bits = capacity.bit_length()
    narrow = receivers * bits < 32
    if not narrow:
        for owner in range(receivers):
            count_ref[owner] = owner * capacity
    loads[0].wait()

    def find(block, counts):
        owner = owner_ref[block]
        if narrow:
            shift = owner * bits
            slot = owner * capacity + ((counts >> shift) & ((1 << bits) - 1))
            counts = counts + (jnp.int32(1) << shift)
        else:
            slot = count_ref[owner]
            count_ref[owner] = slot + 1
        source_ref[slot] = block
        return counts

    lax.fori_loop(0, blocks, find, jnp.int32(0), unroll=16)
    for load in loads[1:]:
        load.wait()
    odd = lax.broadcasted_iota(jnp.int32, (8, HD), 0) % 2 == 1
    scale = jnp.where(odd, scales_ref[1:2, :], scales_ref[0:1, :])[None]
    for (k, start, count), out_ref in zip(plan, outs):
        first = partner(me, k, receivers) * capacity + start

        def one_slot(slot, carry, first=first, out_ref=out_ref):
            block = source_ref[first + slot]
            anchor = jnp.where(
                odd, anchors_ref[pl.ds(2 * block + 1, 1), :], anchors_ref[pl.ds(2 * block, 1), :]
            )[None]
            here = pl.ds(pl.multiple_of(block * rows, rows), rows)
            delta = deltas_ref[here, :].astype(jnp.float32)
            decoded = anchor + scale * delta.reshape(rows // 8, 8, HD)
            out_ref[pl.ds(pl.multiple_of(slot * rows, rows), rows), :] = decoded.reshape(rows, HD).astype(
                jnp.bfloat16
            )
            return carry

        lax.fori_loop(0, count, one_slot, 0, unroll=min(8, count))


def pieces(values):
    high = values.astype(jnp.bfloat16)
    rest = values - high.astype(jnp.float32)
    middle = rest.astype(jnp.bfloat16)
    low = (rest - middle.astype(jnp.float32)).astype(jnp.bfloat16)
    return [high, middle, low]


def packed(partial):
    summed, top, total = partial
    stats = pieces(top) + pieces(total)
    rest = jnp.zeros((STAT_ROWS - len(stats), top.shape[1]), jnp.bfloat16)
    return jnp.concatenate([summed.astype(jnp.bfloat16)] + stats + [rest], axis=0)


def unpacked(block):
    stats = block[HD:, :].astype(jnp.float32)
    top = stats[0:1] + stats[1:2] + stats[2:3]
    total = stats[3:4] + stats[4:5] + stats[5:6]
    return block[0:HD, :].astype(jnp.float32), top, total


def held(partial):
    summed, top, total = partial
    rest = jnp.zeros((KEEP_ROWS - 2, top.shape[1]), jnp.float32)
    return jnp.concatenate([summed, top, total, rest], axis=0)


def taken(block):
    return block[0:HD, :], block[HD : HD + 1, :], block[HD + 1 : HD + 2, :]


def joined(one, other):
    top = jnp.maximum(one[1], other[1])
    scale_one = jnp.exp2((one[1] - top) * RATE)
    scale_other = jnp.exp2((other[1] - top) * RATE)
    return (
        one[0] * scale_one + other[0] * scale_other,
        top,
        one[2] * scale_one + other[2] * scale_other,
    )


def attend(parity, width, keys_ref, turned_ref, asked_ref, store):
    me = lax.axis_index("seq")
    asked = asked_ref.shape[0]

    def partial_of(here):
        scores = lax.dot_general(
            keys_ref[...], here, (((1,), (1,)), ((), ())), preferred_element_type=jnp.float32
        )
        top = jnp.max(scores, axis=0, keepdims=True)
        weights = jnp.exp2((scores - top) * RATE)
        total = jnp.sum(weights, axis=0, keepdims=True)
        summed = jnp.dot(turned_ref[...], weights.astype(jnp.bfloat16), preferred_element_type=jnp.float32)
        return summed, top, total

    if width % HD == 0:
        for index in range(asked // width // 2):
            there = (me ^ (2 * index + parity)) * width
            store(index, partial_of(asked_ref[pl.ds(pl.multiple_of(there, width), width), :]))
        return
    tile = min(2 * HD, asked)
    parts = tile // width

    def one_tile(tile_index, carry):
        here = asked_ref[pl.ds(pl.multiple_of(tile_index * tile, tile), tile), :]
        summed, top, total = partial_of(here)
        for part in range(parts):
            lanes = slice(part * width, (part + 1) * width)
            apart = (tile_index * parts + part) ^ me

            @pl.when(apart % 2 == parity)
            def _(lanes=lanes, apart=apart):
                store(apart // 2, (summed[:, lanes], top[:, lanes], total[:, lanes]))

        return carry

    lax.fori_loop(0, asked // tile, one_tile, 0)


def first_kernel(*refs):
    me = lax.axis_index("seq")
    sources, send_ref, keys_ref, turned_ref, asked_ref, own_ref, *targets = refs[:7], *refs[7:-3]
    wide_ref, values_ref, sems = refs[-3:]
    loads = [
        pltpu.make_async_copy(source, target, sems.at[index])
        for index, (source, target) in enumerate(zip(sources, targets))
    ]
    for load in loads:
        load.start()
    deltas_ref, anchors_ref, scales_ref, lengths_ref, request_ref, queries_ref, new_ref = targets
    blocks = anchors_ref.shape[0] // 2
    rows = deltas_ref.shape[0] // blocks
    tokens = rows // 2
    requests = lengths_ref.shape[0]
    asked = queries_ref.shape[0]
    per_row = asked // request_ref.shape[0]
    width = send_ref.shape[2]
    for load in loads[2:]:
        load.wait()

    lane = lax.broadcasted_iota(jnp.int32, (1, HD), 1)
    first = jnp.zeros((1, HD), jnp.int32)
    last = jnp.zeros((1, HD), jnp.int32)
    end = 0 - me * (blocks * tokens)
    for request in range(requests):
        start = end
        end = end + lengths_ref[request]
        first = jnp.where(lane == request, start, first)
        last = jnp.where(lane == request, end, last)
    place = lax.broadcasted_iota(jnp.int32, (blocks * tokens, HD), 0)
    keys_ref[:, HD:] = jnp.where((place >= first) & (place < last), 1.0, 0.0).astype(jnp.bfloat16)

    asked_ref[:, 0:HD] = queries_ref[...]
    wide_lane = lax.broadcasted_iota(jnp.int32, (per_row, HD), 1)

    def one_row(row, carry):
        asked_ref[pl.ds(pl.multiple_of(row * per_row, per_row), per_row), HD:] = jnp.where(
            (wide_lane == request_ref[row]) | (wide_lane >= requests), 0.0, FAR
        ).astype(jnp.bfloat16)
        return carry

    lax.fori_loop(0, request_ref.shape[0], one_row, 0, unroll=16)

    fresh = new_ref.shape[0] // 4
    new = new_ref[...].astype(jnp.float32).reshape(fresh, 4, HD)
    mine = queries_ref[pl.ds(pl.multiple_of(me * width, width), width), :]
    of_row = lax.broadcasted_iota(jnp.int32, (fresh, width), 1) // (GQ * STEPS)
    same = of_row == lax.broadcasted_iota(jnp.int32, (fresh, width), 0)
    step = lax.broadcasted_iota(jnp.int32, (1, width), 1) % STEPS
    own_scores = []
    for which in range(STEPS):
        scored = lax.dot_general(
            new[:, 2 * which, :].astype(jnp.bfloat16),
            mine,
            (((1,), (1,)), ((), ())),
            preferred_element_type=jnp.float32,
        )
        picked = jnp.sum(jnp.where(same, scored, 0.0), axis=0, keepdims=True)
        own_scores.append(jnp.where(step >= which, picked, FAR))
    own_top = jnp.maximum(own_scores[0], own_scores[1])
    own_total = jnp.zeros((1, width), jnp.float32)
    own_summed = jnp.zeros((HD, width), jnp.float32)
    for which in range(STEPS):
        weight = jnp.exp2((own_scores[which] - own_top) * RATE)
        own_total = own_total + weight
        spread = jnp.where(same, weight, 0.0).astype(jnp.bfloat16)
        own_summed = own_summed + lax.dot_general(
            new[:, 2 * which + 1, :].astype(jnp.bfloat16),
            spread,
            (((0,), (0,)), ((), ())),
            preferred_element_type=jnp.float32,
        )
    own_ref[...] = held((own_summed, own_top, own_total))

    for load in loads[:2]:
        load.wait()
    wide_ref[...] = deltas_ref[...].astype(jnp.float32)
    scale_key = scales_ref[0:1, :]
    scale_value = scales_ref[1:2, :]

    def one_block(block, carry):
        here = pl.ds(pl.multiple_of(block * tokens, tokens), tokens)
        key = wide_ref[pl.ds(block * rows, tokens, stride=2), :]
        value = wide_ref[pl.ds(block * rows + 1, tokens, stride=2), :]
        keys_ref[here, 0:HD] = (anchors_ref[pl.ds(2 * block, 1), :] + scale_key * key).astype(jnp.bfloat16)
        values_ref[here, :] = (anchors_ref[pl.ds(2 * block + 1, 1), :] + scale_value * value).astype(
            jnp.bfloat16
        )
        return carry

    lax.fori_loop(0, blocks, one_block, 0, unroll=16)
    turned_ref[...] = values_ref[...].T

    def store(index, partial):
        send_ref[index] = packed(partial)

    attend(1, width, keys_ref, turned_ref, asked_ref, store)


def second_kernel(keys_ref, turned_ref, asked_ref, own_ref, keep_ref):
    def store(index, partial):
        keep_ref[index] = held(partial)

    attend(0, keep_ref.shape[2], keys_ref, turned_ref, asked_ref, store)
    keep_ref[0] = held(joined(taken(keep_ref[0]), taken(own_ref[...])))


def join_kernel(keep_ref, got_ref, send_ref, next_ref):
    for index in range(keep_ref.shape[0]):
        partial = joined(taken(keep_ref[index]), unpacked(got_ref[index]))
        if index % 2 == 1:
            send_ref[index // 2] = packed(partial)
        else:
            next_ref[index // 2] = held(partial)


def settle(plan, handed, pages, sems):
    receivers = lax.axis_size("seq")
    me = lax.axis_index("seq")
    rows = pages.shape[0] // receivers
    copies = []
    for index, (k, start, slots) in enumerate(plan):
        size = handed[index].shape[0]
        sender = source(me, k, receivers) if k else me
        first = pl.multiple_of(sender * rows + start * (size // slots), size)
        copies.append(pltpu.make_async_copy(handed[index], pages.at[pl.ds(first, size), :], sems.at[index]))
        copies[-1].start()
    return copies


def settle_kernel(plan, *refs):
    *handed, pages, sems = refs
    for copy in settle(plan, handed, pages, sems):
        copy.wait()


def finish_kernel(plan, keep_ref, got_ref, _, *refs):
    *handed, out_any, pages, out_ref, sems = refs
    copies = settle(plan, handed, pages, sems)
    summed, _, total = joined(taken(keep_ref[0]), unpacked(got_ref[0]))
    out_ref[...] = (summed / total).T.astype(jnp.bfloat16)
    copies.append(pltpu.make_async_copy(out_ref, out_any, sems.at[len(copies)]))
    copies[-1].start()
    for copy in copies:
        copy.wait()


def in_hbm(arrays):
    return [pltpu.with_memory_space_constraint(array, pltpu.HBM) for array in arrays]


def per_device(lengths, owner_map, row_request, deltas, anchors, scales, queries, new_kv):
    blocks = anchors.shape[0]
    tokens = deltas.shape[0]
    senders = lax.axis_size("seq")
    me = lax.axis_index("seq")
    rows, steps, _ = queries.shape
    rows_dev = new_kv.shape[0]
    width = rows_dev * GQ * steps
    small = pltpu.CompilerParams(vmem_limit_bytes=8 * 1024 * 1024)

    flat_deltas = deltas.reshape(tokens * 2, HD)
    flat_anchors = anchors.reshape(blocks * 2, HD)
    flat_queries = queries.reshape(rows, steps, GQ, HD).transpose(0, 2, 1, 3).reshape(-1, HD)
    flat_new = new_kv.reshape(rows_dev * 4, HD)

    whole = jax.ShapeDtypeStruct((tokens * 2, HD), jnp.bfloat16)
    ahead, behind, own = messages(senders, blocks // senders)
    block_rows = tokens * 2 // blocks

    def place(plan, deltas):
        return pl.pallas_call(
            functools.partial(place_kernel, plan),
            out_shape=[jax.ShapeDtypeStruct((slots * block_rows, HD), jnp.bfloat16) for _, _, slots in plan],
            in_specs=[HBM] * 4,
            out_specs=[VMEM] * len(plan),
            scratch_shapes=[
                pltpu.SMEM((blocks,), jnp.int32),
                pltpu.SMEM((blocks,), jnp.int32),
                pltpu.SMEM((senders,), jnp.int32),
                pltpu.VMEM((tokens * 2, HD), jnp.bfloat16),
                pltpu.VMEM((blocks * 2, HD), jnp.float32),
                pltpu.VMEM((2, HD), jnp.float32),
                pltpu.SemaphoreType.DMA((4,)),
            ],
            compiler_params=small,
            name="place",
        )(*in_hbm([owner_map, deltas, flat_anchors, scales]))

    sent = place(ahead, flat_deltas)
    sent, late_deltas = lax.optimization_barrier((sent, flat_deltas))
    got_ahead = [hand(message, k) for message, (k, _, _) in zip(sent, ahead)]

    def leaving(count):
        return jax.ShapeDtypeStruct((count // 2, HD + STAT_ROWS, width), jnp.bfloat16)

    def staying(count):
        return jax.ShapeDtypeStruct((count // 2, HD + KEEP_ROWS, width), jnp.float32)

    needed = (late_deltas, flat_anchors, scales, lengths, row_request, flat_queries, flat_new)
    roomy = pltpu.CompilerParams(vmem_limit_bytes=32 * 1024 * 1024)
    send, *common = pl.pallas_call(
        first_kernel,
        out_shape=[
            leaving(senders),
            jax.ShapeDtypeStruct((tokens, 2 * HD), jnp.bfloat16),
            jax.ShapeDtypeStruct((HD, tokens), jnp.bfloat16),
            jax.ShapeDtypeStruct((rows * GQ * steps, 2 * HD), jnp.bfloat16),
            jax.ShapeDtypeStruct((HD + KEEP_ROWS, width), jnp.float32),
        ],
        in_specs=[HBM] * len(needed),
        out_specs=[VMEM] * 5,
        scratch_shapes=[
            (pltpu.SMEM if array.dtype == jnp.int32 else pltpu.VMEM)(array.shape, array.dtype)
            for array in needed
        ]
        + [
            pltpu.VMEM((tokens * 2, HD), jnp.float32),
            pltpu.VMEM((tokens, HD), jnp.bfloat16),
            pltpu.SemaphoreType.DMA((len(needed),)),
        ],
        compiler_params=roomy,
        name="attend_leaving",
    )(*in_hbm(needed))

    k, count = 1, senders // 2
    send, late_deltas = lax.optimization_barrier((send, late_deltas))
    passed = exchange(send, k)
    *sent, mine = place(behind + own, late_deltas)
    got = got_ahead[1:] + [hand(message, k) for message, (k, _, _) in zip(sent, behind)]
    keep = pl.pallas_call(
        second_kernel,
        out_shape=staying(senders),
        in_specs=[VMEM] * 4,
        out_specs=VMEM,
        compiler_params=roomy,
        name="attend_staying",
    )(*common)
    while count > 1:
        send, keep = pl.pallas_call(
            join_kernel,
            out_shape=[leaving(count), staying(count)],
            in_specs=[VMEM] * 2,
            out_specs=[VMEM] * 2,
            compiler_params=small,
            name="join",
        )(keep, passed)
        k, count = 2 * k, count // 2
        passed = exchange(send, k)
    settled = ahead[:1] + own
    pages = pl.pallas_call(
        functools.partial(settle_kernel, settled),
        out_shape=whole,
        in_specs=[ANY] * len(settled),
        out_specs=HBM,
        scratch_shapes=[pltpu.SemaphoreType.DMA((len(settled),))],
        compiler_params=small,
        name="settle",
    )(got_ahead[0], mine)
    attended, pages = pl.pallas_call(
        functools.partial(finish_kernel, ahead[1:] + behind),
        out_shape=[jax.ShapeDtypeStruct((width, HD), jnp.bfloat16), whole],
        in_specs=[VMEM] * 2 + [HBM] + [ANY] * len(got),
        out_specs=[HBM, HBM],
        scratch_shapes=[
            pltpu.VMEM((width, HD), jnp.bfloat16),
            pltpu.SemaphoreType.DMA((len(got) + 1,)),
        ],
        input_output_aliases={2: 1},
        compiler_params=small,
        name="finish",
    )(keep, passed, pages, *got)
    pages = pages.reshape(blocks, tokens // blocks, 2, HD)
    attended = (
        attended.reshape(rows_dev, GQ, steps, HD).transpose(0, 2, 1, 3).reshape(rows_dev, steps, GQ * HD)
    )
    return pages, attended


def solution(mesh):
    placed = (
        P("groups"),
        P(("groups", "seq")),
        P("groups"),
        P(("groups", "seq"), None, "tp"),
        P(("groups", "seq"), None, "tp"),
        P("groups", "tp"),
        P("groups", None, "tp"),
        P(("groups", "seq"), None, None, "tp"),
    )
    return jax.shard_map(
        per_device,
        mesh=mesh,
        in_specs=placed,
        out_specs=(P(("groups", "seq"), None, None, "tp"), P(("groups", "seq"), None, "tp")),
        check_vma=False,
    )
```

```python
import functools

import jax
import jax.numpy as jnp
from jax import lax
from jax.experimental import pallas as pl
from jax.experimental.pallas import tpu as pltpu
from jax.sharding import PartitionSpec as P

HD = 128
GQ = 8
STEPS = 2
STAT_ROWS = 8
KEEP_ROWS = 8
FAR = -1e30
RATE = HD ** (-0.5) * 1.4426950408889634

VMEM = pl.BlockSpec(memory_space=pltpu.VMEM)
HBM = pl.BlockSpec(memory_space=pltpu.HBM)
ANY = pl.BlockSpec(memory_space=pl.ANY)
SMEM = pl.BlockSpec(memory_space=pltpu.SMEM)


def inner(device, count):
    return (device ^ (device // (count // 2))) & 1


def partner(device, k, count):
    far = count // 2
    if k == far:
        return device ^ (1 + inner(device, count) * (far - 1))
    if k == 1:
        return device ^ (far - inner(device, count) * (far - 1))
    return device ^ k


def source(device, k, count):
    far = count // 2
    if k == far:
        return device ^ (far - inner(device, count) * (far - 1))
    if k == 1:
        return device ^ (1 + inner(device, count) * (far - 1))
    return device ^ k


def exchange(message, k):
    count = lax.axis_size("seq")
    return lax.ppermute(message, "seq", [(i, i ^ k) for i in range(count)])


def hand(message, k):
    count = lax.axis_size("seq")
    return lax.ppermute(message, "seq", [(i, partner(i, k, count)) for i in range(count)])


def messages(count, capacity):
    half = capacity // 2
    ahead = [(k, 0, capacity) for k in range(count // 2, count)]
    behind = [(k, first, half) for k in reversed(range(1, count // 2)) for first in (0, half)]
    return ahead, behind, [(0, 0, capacity)]


def place_kernel(plan, owner_any, deltas_any, anchors_any, scales_any, *refs):
    receivers = lax.axis_size("seq")
    me = lax.axis_index("seq")
    outs = refs[:-7]
    owner_ref, source_ref, count_ref, deltas_ref, anchors_ref, scales_ref, sems = refs[-7:]
    blocks = owner_ref.shape[0]
    rows = deltas_ref.shape[0] // blocks
    capacity = blocks // receivers
    loads = [
        pltpu.make_async_copy(source, target, sems.at[index])
        for index, (source, target) in enumerate(
            [
                (owner_any, owner_ref),
                (scales_any, scales_ref),
                (anchors_any, anchors_ref),
                (deltas_any, deltas_ref),
            ]
        )
    ]
    for load in loads:
        load.start()
    bits = capacity.bit_length()
    narrow = receivers * bits < 32
    if not narrow:
        for owner in range(receivers):
            count_ref[owner] = owner * capacity
    loads[0].wait()

    def find(block, counts):
        owner = owner_ref[block]
        if narrow:
            shift = owner * bits
            slot = owner * capacity + ((counts >> shift) & ((1 << bits) - 1))
            counts = counts + (jnp.int32(1) << shift)
        else:
            slot = count_ref[owner]
            count_ref[owner] = slot + 1
        source_ref[slot] = block
        return counts

    lax.fori_loop(0, blocks, find, jnp.int32(0), unroll=16)
    for load in loads[1:]:
        load.wait()
    odd = lax.broadcasted_iota(jnp.int32, (8, HD), 0) % 2 == 1
    scale = jnp.where(odd, scales_ref[1:2, :], scales_ref[0:1, :])[None]
    for (k, start, count), out_ref in zip(plan, outs):
        first = partner(me, k, receivers) * capacity + start

        def one_slot(slot, carry, first=first, out_ref=out_ref):
            block = source_ref[first + slot]
            anchor = jnp.where(
                odd, anchors_ref[pl.ds(2 * block + 1, 1), :], anchors_ref[pl.ds(2 * block, 1), :]
            )[None]
            here = pl.ds(pl.multiple_of(block * rows, rows), rows)
            delta = deltas_ref[here, :].astype(jnp.float32)
            decoded = anchor + scale * delta.reshape(rows // 8, 8, HD)
            out_ref[pl.ds(pl.multiple_of(slot * rows, rows), rows), :] = decoded.reshape(rows, HD).astype(
                jnp.bfloat16
            )
            return carry

        lax.fori_loop(0, count, one_slot, 0, unroll=min(8, count))


def pieces(values):
    high = values.astype(jnp.bfloat16)
    rest = values - high.astype(jnp.float32)
    middle = rest.astype(jnp.bfloat16)
    low = (rest - middle.astype(jnp.float32)).astype(jnp.bfloat16)
    return [high, middle, low]


def packed(partial):
    summed, top, total = partial
    stats = pieces(top) + pieces(total)
    rest = jnp.zeros((STAT_ROWS - len(stats), top.shape[1]), jnp.bfloat16)
    return jnp.concatenate([summed.astype(jnp.bfloat16)] + stats + [rest], axis=0)


def unpacked(block):
    stats = block[HD:, :].astype(jnp.float32)
    top = stats[0:1] + stats[1:2] + stats[2:3]
    total = stats[3:4] + stats[4:5] + stats[5:6]
    return block[0:HD, :].astype(jnp.float32), top, total


def held(partial):
    summed, top, total = partial
    rest = jnp.zeros((KEEP_ROWS - 2, top.shape[1]), jnp.float32)
    return jnp.concatenate([summed, top, total, rest], axis=0)


def taken(block):
    return block[0:HD, :], block[HD : HD + 1, :], block[HD + 1 : HD + 2, :]


def joined(one, other):
    top = jnp.maximum(one[1], other[1])
    scale_one = jnp.exp2((one[1] - top) * RATE)
    scale_other = jnp.exp2((other[1] - top) * RATE)
    return (
        one[0] * scale_one + other[0] * scale_other,
        top,
        one[2] * scale_one + other[2] * scale_other,
    )


def attend(parity, width, keys_ref, turned_ref, asked_ref, store):
    me = lax.axis_index("seq")
    asked = asked_ref.shape[0]

    def partial_of(here):
        scores = lax.dot_general(
            keys_ref[...], here, (((1,), (1,)), ((), ())), preferred_element_type=jnp.float32
        )
        top = jnp.max(scores, axis=0, keepdims=True)
        weights = jnp.exp2((scores - top) * RATE)
        total = jnp.sum(weights, axis=0, keepdims=True)
        summed = jnp.dot(turned_ref[...], weights.astype(jnp.bfloat16), preferred_element_type=jnp.float32)
        return summed, top, total

    if width % HD == 0:
        for index in range(asked // width // 2):
            there = (me ^ (2 * index + parity)) * width
            store(index, partial_of(asked_ref[pl.ds(pl.multiple_of(there, width), width), :]))
        return
    tile = min(2 * HD, asked)
    parts = tile // width

    def one_tile(tile_index, carry):
        here = asked_ref[pl.ds(pl.multiple_of(tile_index * tile, tile), tile), :]
        summed, top, total = partial_of(here)
        for part in range(parts):
            lanes = slice(part * width, (part + 1) * width)
            apart = (tile_index * parts + part) ^ me

            @pl.when(apart % 2 == parity)
            def _(lanes=lanes, apart=apart):
                store(apart // 2, (summed[:, lanes], top[:, lanes], total[:, lanes]))

        return carry

    lax.fori_loop(0, asked // tile, one_tile, 0)


def first_kernel(*refs):
    me = lax.axis_index("seq")
    sources, send_ref, keys_ref, turned_ref, asked_ref, own_ref, *targets = refs[:7], *refs[7:-3]
    wide_ref, values_ref, sems = refs[-3:]
    loads = [
        pltpu.make_async_copy(source, target, sems.at[index])
        for index, (source, target) in enumerate(zip(sources, targets))
    ]
    for load in loads:
        load.start()
    deltas_ref, anchors_ref, scales_ref, lengths_ref, request_ref, queries_ref, new_ref = targets
    blocks = anchors_ref.shape[0] // 2
    rows = deltas_ref.shape[0] // blocks
    tokens = rows // 2
    requests = lengths_ref.shape[0]
    asked = queries_ref.shape[0]
    per_row = asked // request_ref.shape[0]
    width = send_ref.shape[2]
    for load in loads[2:]:
        load.wait()

    lane = lax.broadcasted_iota(jnp.int32, (1, HD), 1)
    first = jnp.zeros((1, HD), jnp.int32)
    last = jnp.zeros((1, HD), jnp.int32)
    end = 0 - me * (blocks * tokens)
    for request in range(requests):
        start = end
        end = end + lengths_ref[request]
        first = jnp.where(lane == request, start, first)
        last = jnp.where(lane == request, end, last)
    place = lax.broadcasted_iota(jnp.int32, (blocks * tokens, HD), 0)
    keys_ref[:, HD:] = jnp.where((place >= first) & (place < last), 1.0, 0.0).astype(jnp.bfloat16)

    asked_ref[:, 0:HD] = queries_ref[...]
    wide_lane = lax.broadcasted_iota(jnp.int32, (per_row, HD), 1)

    def one_row(row, carry):
        asked_ref[pl.ds(pl.multiple_of(row * per_row, per_row), per_row), HD:] = jnp.where(
            (wide_lane == request_ref[row]) | (wide_lane >= requests), 0.0, FAR
        ).astype(jnp.bfloat16)
        return carry

    lax.fori_loop(0, request_ref.shape[0], one_row, 0, unroll=16)

    fresh = new_ref.shape[0] // 4
    new = new_ref[...].astype(jnp.float32).reshape(fresh, 4, HD)
    mine = queries_ref[pl.ds(pl.multiple_of(me * width, width), width), :]
    of_row = lax.broadcasted_iota(jnp.int32, (fresh, width), 1) // (GQ * STEPS)
    same = of_row == lax.broadcasted_iota(jnp.int32, (fresh, width), 0)
    step = lax.broadcasted_iota(jnp.int32, (1, width), 1) % STEPS
    own_scores = []
    for which in range(STEPS):
        scored = lax.dot_general(
            new[:, 2 * which, :].astype(jnp.bfloat16),
            mine,
            (((1,), (1,)), ((), ())),
            preferred_element_type=jnp.float32,
        )
        picked = jnp.sum(jnp.where(same, scored, 0.0), axis=0, keepdims=True)
        own_scores.append(jnp.where(step >= which, picked, FAR))
    own_top = jnp.maximum(own_scores[0], own_scores[1])
    own_total = jnp.zeros((1, width), jnp.float32)
    own_summed = jnp.zeros((HD, width), jnp.float32)
    for which in range(STEPS):
        weight = jnp.exp2((own_scores[which] - own_top) * RATE)
        own_total = own_total + weight
        spread = jnp.where(same, weight, 0.0).astype(jnp.bfloat16)
        own_summed = own_summed + lax.dot_general(
            new[:, 2 * which + 1, :].astype(jnp.bfloat16),
            spread,
            (((0,), (0,)), ((), ())),
            preferred_element_type=jnp.float32,
        )
    own_ref[...] = held((own_summed, own_top, own_total))

    for load in loads[:2]:
        load.wait()
    wide_ref[...] = deltas_ref[...].astype(jnp.float32)
    scale_key = scales_ref[0:1, :]
    scale_value = scales_ref[1:2, :]

    def one_block(block, carry):
        here = pl.ds(pl.multiple_of(block * tokens, tokens), tokens)
        key = wide_ref[pl.ds(block * rows, tokens, stride=2), :]
        value = wide_ref[pl.ds(block * rows + 1, tokens, stride=2), :]
        keys_ref[here, 0:HD] = (anchors_ref[pl.ds(2 * block, 1), :] + scale_key * key).astype(jnp.bfloat16)
        values_ref[here, :] = (anchors_ref[pl.ds(2 * block + 1, 1), :] + scale_value * value).astype(
            jnp.bfloat16
        )
        return carry

    lax.fori_loop(0, blocks, one_block, 0, unroll=16)
    turned_ref[...] = values_ref[...].T

    def store(index, partial):
        send_ref[index] = packed(partial)

    attend(1, width, keys_ref, turned_ref, asked_ref, store)


def second_kernel(keys_ref, turned_ref, asked_ref, own_ref, keep_ref):
    def store(index, partial):
        keep_ref[index] = held(partial)

    attend(0, keep_ref.shape[2], keys_ref, turned_ref, asked_ref, store)
    keep_ref[0] = held(joined(taken(keep_ref[0]), taken(own_ref[...])))


def join_kernel(keep_ref, got_ref, send_ref, next_ref):
    for index in range(keep_ref.shape[0]):
        partial = joined(taken(keep_ref[index]), unpacked(got_ref[index]))
        if index % 2 == 1:
            send_ref[index // 2] = packed(partial)
        else:
            next_ref[index // 2] = held(partial)


def settle(plan, handed, pages, sems):
    receivers = lax.axis_size("seq")
    me = lax.axis_index("seq")
    rows = pages.shape[0] // receivers
    copies = []
    for index, (k, start, slots) in enumerate(plan):
        size = handed[index].shape[0]
        sender = source(me, k, receivers) if k else me
        first = pl.multiple_of(sender * rows + start * (size // slots), size)
        copies.append(pltpu.make_async_copy(handed[index], pages.at[pl.ds(first, size), :], sems.at[index]))
        copies[-1].start()
    return copies


def settle_kernel(plan, *refs):
    *handed, pages, sems = refs
    for copy in settle(plan, handed, pages, sems):
        copy.wait()


def finish_kernel(plan, keep_ref, got_ref, _, *refs):
    *handed, out_any, pages, out_ref, sems = refs
    copies = settle(plan, handed, pages, sems)
    summed, _, total = joined(taken(keep_ref[0]), unpacked(got_ref[0]))
    out_ref[...] = (summed / total).T.astype(jnp.bfloat16)
    copies.append(pltpu.make_async_copy(out_ref, out_any, sems.at[len(copies)]))
    copies[-1].start()
    for copy in copies:
        copy.wait()


def in_hbm(arrays):
    return [pltpu.with_memory_space_constraint(array, pltpu.HBM) for array in arrays]


def per_device(lengths, owner_map, row_request, deltas, anchors, scales, queries, new_kv):
    blocks = anchors.shape[0]
    tokens = deltas.shape[0]
    senders = lax.axis_size("seq")
    me = lax.axis_index("seq")
    rows, steps, _ = queries.shape
    rows_dev = new_kv.shape[0]
    width = rows_dev * GQ * steps
    small = pltpu.CompilerParams(vmem_limit_bytes=8 * 1024 * 1024)

    flat_deltas = deltas.reshape(tokens * 2, HD)
    flat_anchors = anchors.reshape(blocks * 2, HD)
    flat_queries = queries.reshape(rows, steps, GQ, HD).transpose(0, 2, 1, 3).reshape(-1, HD)
    flat_new = new_kv.reshape(rows_dev * 4, HD)

    whole = jax.ShapeDtypeStruct((tokens * 2, HD), jnp.bfloat16)
    ahead, behind, own = messages(senders, blocks // senders)
    block_rows = tokens * 2 // blocks

    def place(plan, deltas):
        return pl.pallas_call(
            functools.partial(place_kernel, plan),
            out_shape=[jax.ShapeDtypeStruct((slots * block_rows, HD), jnp.bfloat16) for _, _, slots in plan],
            in_specs=[HBM] * 4,
            out_specs=[VMEM] * len(plan),
            scratch_shapes=[
                pltpu.SMEM((blocks,), jnp.int32),
                pltpu.SMEM((blocks,), jnp.int32),
                pltpu.SMEM((senders,), jnp.int32),
                pltpu.VMEM((tokens * 2, HD), jnp.bfloat16),
                pltpu.VMEM((blocks * 2, HD), jnp.float32),
                pltpu.VMEM((2, HD), jnp.float32),
                pltpu.SemaphoreType.DMA((4,)),
            ],
            compiler_params=small,
            name="place",
        )(*in_hbm([owner_map, deltas, flat_anchors, scales]))

    sent = place(ahead, flat_deltas)
    sent, late_deltas = lax.optimization_barrier((sent, flat_deltas))
    got_ahead = [hand(message, k) for message, (k, _, _) in zip(sent, ahead)]

    def leaving(count):
        return jax.ShapeDtypeStruct((count // 2, HD + STAT_ROWS, width), jnp.bfloat16)

    def staying(count):
        return jax.ShapeDtypeStruct((count // 2, HD + KEEP_ROWS, width), jnp.float32)

    needed = (late_deltas, flat_anchors, scales, lengths, row_request, flat_queries, flat_new)
    roomy = pltpu.CompilerParams(vmem_limit_bytes=32 * 1024 * 1024)
    send, *common = pl.pallas_call(
        first_kernel,
        out_shape=[
            leaving(senders),
            jax.ShapeDtypeStruct((tokens, 2 * HD), jnp.bfloat16),
            jax.ShapeDtypeStruct((HD, tokens), jnp.bfloat16),
            jax.ShapeDtypeStruct((rows * GQ * steps, 2 * HD), jnp.bfloat16),
            jax.ShapeDtypeStruct((HD + KEEP_ROWS, width), jnp.float32),
        ],
        in_specs=[HBM] * len(needed),
        out_specs=[VMEM] * 5,
        scratch_shapes=[
            (pltpu.SMEM if array.dtype == jnp.int32 else pltpu.VMEM)(array.shape, array.dtype)
            for array in needed
        ]
        + [
            pltpu.VMEM((tokens * 2, HD), jnp.float32),
            pltpu.VMEM((tokens, HD), jnp.bfloat16),
            pltpu.SemaphoreType.DMA((len(needed),)),
        ],
        compiler_params=roomy,
        name="attend_leaving",
    )(*in_hbm(needed))

    k, count = 1, senders // 2
    send, late_deltas = lax.optimization_barrier((send, late_deltas))
    passed = exchange(send, k)
    *sent, mine = place(behind + own, late_deltas)
    got = got_ahead[1:] + [hand(message, k) for message, (k, _, _) in zip(sent, behind)]
    keep = pl.pallas_call(
        second_kernel,
        out_shape=staying(senders),
        in_specs=[VMEM] * 4,
        out_specs=VMEM,
        compiler_params=roomy,
        name="attend_staying",
    )(*common)
    while count > 1:
        send, keep = pl.pallas_call(
            join_kernel,
            out_shape=[leaving(count), staying(count)],
            in_specs=[VMEM] * 2,
            out_specs=[VMEM] * 2,
            compiler_params=small,
            name="join",
        )(keep, passed)
        k, count = 2 * k, count // 2
        passed = exchange(send, k)
    settled = ahead[:1] + own
    pages = pl.pallas_call(
        functools.partial(settle_kernel, settled),
        out_shape=whole,
        in_specs=[ANY] * len(settled),
        out_specs=HBM,
        scratch_shapes=[pltpu.SemaphoreType.DMA((len(settled),))],
        compiler_params=small,
        name="settle",
    )(got_ahead[0], mine)
    attended, pages = pl.pallas_call(
        functools.partial(finish_kernel, ahead[1:] + behind),
        out_shape=[jax.ShapeDtypeStruct((width, HD), jnp.bfloat16), whole],
        in_specs=[VMEM] * 2 + [HBM] + [ANY] * len(got),
        out_specs=[HBM, HBM],
        scratch_shapes=[
            pltpu.VMEM((width, HD), jnp.bfloat16),
            pltpu.SemaphoreType.DMA((len(got) + 1,)),
        ],
        input_output_aliases={2: 1},
        compiler_params=small,
        name="finish",
    )(keep, passed, pages, *got)
    pages = pages.reshape(blocks, tokens // blocks, 2, HD)
    attended = (
        attended.reshape(rows_dev, GQ, steps, HD).transpose(0, 2, 1, 3).reshape(rows_dev, steps, GQ * HD)
    )
    return pages, attended


def solution(mesh):
    placed = (
        P("groups"),
        P(("groups", "seq")),
        P("groups"),
        P(("groups", "seq"), None, "tp"),
        P(("groups", "seq"), None, "tp"),
        P("groups", "tp"),
        P("groups", None, "tp"),
        P(("groups", "seq"), None, None, "tp"),
    )
    return jax.shard_map(
        per_device,
        mesh=mesh,
        in_specs=placed,
        out_specs=(P(("groups", "seq"), None, None, "tp"), P(("groups", "seq"), None, "tp")),
        check_vma=False,
    )
```

```python
import functools

import jax
import jax.numpy as jnp
from jax import lax
from jax.experimental import pallas as pl
from jax.experimental.pallas import tpu as pltpu
from jax.sharding import PartitionSpec as P

HD = 128
GQ = 8
STEPS = 2
STAT_ROWS = 8
KEEP_ROWS = 8
FAR = -1e30
RATE = HD ** (-0.5) * 1.4426950408889634

VMEM = pl.BlockSpec(memory_space=pltpu.VMEM)
HBM = pl.BlockSpec(memory_space=pltpu.HBM)
ANY = pl.BlockSpec(memory_space=pl.ANY)
SMEM = pl.BlockSpec(memory_space=pltpu.SMEM)


def inner(device, count):
    return (device ^ (device // (count // 2))) & 1


def partner(device, k, count):
    far = count // 2
    if k == far:
        return device ^ (1 + inner(device, count) * (far - 1))
    if k == 1:
        return device ^ (far - inner(device, count) * (far - 1))
    return device ^ k


def source(device, k, count):
    far = count // 2
    if k == far:
        return device ^ (far - inner(device, count) * (far - 1))
    if k == 1:
        return device ^ (1 + inner(device, count) * (far - 1))
    return device ^ k


def exchange(message, k):
    count = lax.axis_size("seq")
    return lax.ppermute(message, "seq", [(i, i ^ k) for i in range(count)])


def hand(message, k, kinds=(0, 1)):
    count = lax.axis_size("seq")
    senders = [i for i in range(count) if inner(i, count) in kinds]
    return lax.ppermute(message, "seq", [(i, partner(i, k, count)) for i in senders])


def messages(count, capacity):
    far = count // 2
    ahead = [(k, 0, capacity) for k in [far, 1] + [k for k in reversed(range(2, count)) if k != far]]
    behind = [(1, first, capacity // 2) for first in (0, capacity // 2)]
    return ahead, behind, [(0, 0, capacity)]


def place_kernel(plan, owner_any, deltas_any, anchors_any, scales_any, *refs):
    receivers = lax.axis_size("seq")
    me = lax.axis_index("seq")
    outs = refs[:-7]
    owner_ref, source_ref, count_ref, deltas_ref, anchors_ref, scales_ref, sems = refs[-7:]
    blocks = owner_ref.shape[0]
    rows = deltas_ref.shape[0] // blocks
    capacity = blocks // receivers
    loads = [
        pltpu.make_async_copy(source, target, sems.at[index])
        for index, (source, target) in enumerate(
            [
                (owner_any, owner_ref),
                (scales_any, scales_ref),
                (anchors_any, anchors_ref),
                (deltas_any, deltas_ref),
            ]
        )
    ]
    for load in loads:
        load.start()
    bits = capacity.bit_length()
    narrow = receivers * bits < 32
    if not narrow:
        for owner in range(receivers):
            count_ref[owner] = owner * capacity
    loads[0].wait()

    def find(block, counts):
        owner = owner_ref[block]
        if narrow:
            shift = owner * bits
            slot = owner * capacity + ((counts >> shift) & ((1 << bits) - 1))
            counts = counts + (jnp.int32(1) << shift)
        else:
            slot = count_ref[owner]
            count_ref[owner] = slot + 1
        source_ref[slot] = block
        return counts

    lax.fori_loop(0, blocks, find, jnp.int32(0), unroll=16)
    for load in loads[1:]:
        load.wait()
    odd = lax.broadcasted_iota(jnp.int32, (8, HD), 0) % 2 == 1
    scale = jnp.where(odd, scales_ref[1:2, :], scales_ref[0:1, :])[None]
    for (k, start, count), out_ref in zip(plan, outs):
        first = partner(me, k, receivers) * capacity + start

        def one_slot(slot, carry, first=first, out_ref=out_ref):
            block = source_ref[first + slot]
            anchor = jnp.where(
                odd, anchors_ref[pl.ds(2 * block + 1, 1), :], anchors_ref[pl.ds(2 * block, 1), :]
            )[None]
            here = pl.ds(pl.multiple_of(block * rows, rows), rows)
            delta = deltas_ref[here, :].astype(jnp.float32)
            decoded = anchor + scale * delta.reshape(rows // 8, 8, HD)
            out_ref[pl.ds(pl.multiple_of(slot * rows, rows), rows), :] = decoded.reshape(rows, HD).astype(
                jnp.bfloat16
            )
            return carry

        lax.fori_loop(0, count, one_slot, 0, unroll=min(8, count))


def pieces(values):
    high = values.astype(jnp.bfloat16)
    rest = values - high.astype(jnp.float32)
    middle = rest.astype(jnp.bfloat16)
    low = (rest - middle.astype(jnp.float32)).astype(jnp.bfloat16)
    return [high, middle, low]


def packed(partial):
    summed, top, total = partial
    stats = pieces(top) + pieces(total)
    rest = jnp.zeros((STAT_ROWS - len(stats), top.shape[1]), jnp.bfloat16)
    return jnp.concatenate([summed.astype(jnp.bfloat16)] + stats + [rest], axis=0)


def unpacked(block):
    stats = block[HD:, :].astype(jnp.float32)
    top = stats[0:1] + stats[1:2] + stats[2:3]
    total = stats[3:4] + stats[4:5] + stats[5:6]
    return block[0:HD, :].astype(jnp.float32), top, total


def held(partial):
    summed, top, total = partial
    rest = jnp.zeros((KEEP_ROWS - 2, top.shape[1]), jnp.float32)
    return jnp.concatenate([summed, top, total, rest], axis=0)


def taken(block):
    return block[0:HD, :], block[HD : HD + 1, :], block[HD + 1 : HD + 2, :]


def joined(one, other):
    top = jnp.maximum(one[1], other[1])
    scale_one = jnp.exp2((one[1] - top) * RATE)
    scale_other = jnp.exp2((other[1] - top) * RATE)
    return (
        one[0] * scale_one + other[0] * scale_other,
        top,
        one[2] * scale_one + other[2] * scale_other,
    )


def attend(parity, width, keys_ref, turned_ref, asked_ref, store):
    me = lax.axis_index("seq")
    asked = asked_ref.shape[0]

    def partial_of(here):
        scores = lax.dot_general(
            keys_ref[...], here, (((1,), (1,)), ((), ())), preferred_element_type=jnp.float32
        )
        top = jnp.max(scores, axis=0, keepdims=True)
        weights = jnp.exp2((scores - top) * RATE)
        total = jnp.sum(weights, axis=0, keepdims=True)
        summed = jnp.dot(turned_ref[...], weights.astype(jnp.bfloat16), preferred_element_type=jnp.float32)
        return summed, top, total

    if width % HD == 0:
        for index in range(asked // width // 2):
            there = (me ^ (2 * index + parity)) * width
            store(index, partial_of(asked_ref[pl.ds(pl.multiple_of(there, width), width), :]))
        return
    tile = min(2 * HD, asked)
    parts = tile // width

    def one_tile(tile_index, carry):
        here = asked_ref[pl.ds(pl.multiple_of(tile_index * tile, tile), tile), :]
        summed, top, total = partial_of(here)
        for part in range(parts):
            lanes = slice(part * width, (part + 1) * width)
            apart = (tile_index * parts + part) ^ me

            @pl.when(apart % 2 == parity)
            def _(lanes=lanes, apart=apart):
                store(apart // 2, (summed[:, lanes], top[:, lanes], total[:, lanes]))

        return carry

    lax.fori_loop(0, asked // tile, one_tile, 0)


def first_kernel(*refs):
    me = lax.axis_index("seq")
    sources, send_ref, keys_ref, turned_ref, asked_ref, own_ref, *targets = refs[:7], *refs[7:-3]
    wide_ref, values_ref, sems = refs[-3:]
    loads = [
        pltpu.make_async_copy(source, target, sems.at[index])
        for index, (source, target) in enumerate(zip(sources, targets))
    ]
    for load in loads:
        load.start()
    deltas_ref, anchors_ref, scales_ref, lengths_ref, request_ref, queries_ref, new_ref = targets
    blocks = anchors_ref.shape[0] // 2
    rows = deltas_ref.shape[0] // blocks
    tokens = rows // 2
    requests = lengths_ref.shape[0]
    asked = queries_ref.shape[0]
    per_row = asked // request_ref.shape[0]
    width = send_ref.shape[2]
    for load in loads[2:]:
        load.wait()

    lane = lax.broadcasted_iota(jnp.int32, (1, HD), 1)
    first = jnp.zeros((1, HD), jnp.int32)
    last = jnp.zeros((1, HD), jnp.int32)
    end = 0 - me * (blocks * tokens)
    for request in range(requests):
        start = end
        end = end + lengths_ref[request]
        first = jnp.where(lane == request, start, first)
        last = jnp.where(lane == request, end, last)
    place = lax.broadcasted_iota(jnp.int32, (blocks * tokens, HD), 0)
    keys_ref[:, HD:] = jnp.where((place >= first) & (place < last), 1.0, 0.0).astype(jnp.bfloat16)

    asked_ref[:, 0:HD] = queries_ref[...]
    wide_lane = lax.broadcasted_iota(jnp.int32, (per_row, HD), 1)

    def one_row(row, carry):
        asked_ref[pl.ds(pl.multiple_of(row * per_row, per_row), per_row), HD:] = jnp.where(
            (wide_lane == request_ref[row]) | (wide_lane >= requests), 0.0, FAR
        ).astype(jnp.bfloat16)
        return carry

    lax.fori_loop(0, request_ref.shape[0], one_row, 0, unroll=16)

    fresh = new_ref.shape[0] // 4
    new = new_ref[...].astype(jnp.float32).reshape(fresh, 4, HD)
    mine = queries_ref[pl.ds(pl.multiple_of(me * width, width), width), :]
    of_row = lax.broadcasted_iota(jnp.int32, (fresh, width), 1) // (GQ * STEPS)
    same = of_row == lax.broadcasted_iota(jnp.int32, (fresh, width), 0)
    step = lax.broadcasted_iota(jnp.int32, (1, width), 1) % STEPS
    own_scores = []
    for which in range(STEPS):
        scored = lax.dot_general(
            new[:, 2 * which, :].astype(jnp.bfloat16),
            mine,
            (((1,), (1,)), ((), ())),
            preferred_element_type=jnp.float32,
        )
        picked = jnp.sum(jnp.where(same, scored, 0.0), axis=0, keepdims=True)
        own_scores.append(jnp.where(step >= which, picked, FAR))
    own_top = jnp.maximum(own_scores[0], own_scores[1])
    own_total = jnp.zeros((1, width), jnp.float32)
    own_summed = jnp.zeros((HD, width), jnp.float32)
    for which in range(STEPS):
        weight = jnp.exp2((own_scores[which] - own_top) * RATE)
        own_total = own_total + weight
        spread = jnp.where(same, weight, 0.0).astype(jnp.bfloat16)
        own_summed = own_summed + lax.dot_general(
            new[:, 2 * which + 1, :].astype(jnp.bfloat16),
            spread,
            (((0,), (0,)), ((), ())),
            preferred_element_type=jnp.float32,
        )
    own_ref[...] = held((own_summed, own_top, own_total))

    for load in loads[:2]:
        load.wait()
    wide_ref[...] = deltas_ref[...].astype(jnp.float32)
    scale_key = scales_ref[0:1, :]
    scale_value = scales_ref[1:2, :]

    def one_block(block, carry):
        here = pl.ds(pl.multiple_of(block * tokens, tokens), tokens)
        key = wide_ref[pl.ds(block * rows, tokens, stride=2), :]
        value = wide_ref[pl.ds(block * rows + 1, tokens, stride=2), :]
        keys_ref[here, 0:HD] = (anchors_ref[pl.ds(2 * block, 1), :] + scale_key * key).astype(jnp.bfloat16)
        values_ref[here, :] = (anchors_ref[pl.ds(2 * block + 1, 1), :] + scale_value * value).astype(
            jnp.bfloat16
        )
        return carry

    lax.fori_loop(0, blocks, one_block, 0, unroll=16)
    turned_ref[...] = values_ref[...].T

    def store(index, partial):
        send_ref[index] = packed(partial)

    attend(1, width, keys_ref, turned_ref, asked_ref, store)


def second_kernel(keys_ref, turned_ref, asked_ref, own_ref, keep_ref):
    def store(index, partial):
        keep_ref[index] = held(partial)

    attend(0, keep_ref.shape[2], keys_ref, turned_ref, asked_ref, store)
    keep_ref[0] = held(joined(taken(keep_ref[0]), taken(own_ref[...])))


def join_kernel(keep_ref, got_ref, send_ref, next_ref):
    for index in range(keep_ref.shape[0]):
        partial = joined(taken(keep_ref[index]), unpacked(got_ref[index]))
        if index % 2 == 1:
            send_ref[index // 2] = packed(partial)
        else:
            next_ref[index // 2] = held(partial)


def settle(plan, handed, pages, sems):
    receivers = lax.axis_size("seq")
    me = lax.axis_index("seq")
    rows = pages.shape[0] // receivers
    copies = []
    for index, (k, start, slots) in enumerate(plan):
        size = handed[index].shape[0]
        sender = source(me, k, receivers) if k else me
        first = pl.multiple_of(sender * rows + start * (size // slots), size)
        copies.append(pltpu.make_async_copy(handed[index], pages.at[pl.ds(first, size), :], sems.at[index]))
    return copies


def started(copies, some, kind):
    here = inner(lax.axis_index("seq"), lax.axis_size("seq")) == kind

    def every(act):
        for index, copy in enumerate(copies):
            if index in some:
                pl.when(here)(functools.partial(act, copy))
            else:
                act(copy)

    every(lambda copy: copy.start())
    return functools.partial(every, lambda copy: copy.wait())


def settle_kernel(plan, *refs):
    *handed, pages, sems = refs
    started(settle(plan, handed, pages, sems), [index for index, (k, _, _) in enumerate(plan) if k == 1], 0)()


def finish_kernel(plan, keep_ref, got_ref, _, *refs):
    *handed, out_any, pages, out_ref, sems = refs
    wait = started(
        settle(plan, handed, pages, sems), [index for index, (k, _, _) in enumerate(plan) if k == 1], 1
    )
    summed, _, total = joined(taken(keep_ref[0]), unpacked(got_ref[0]))
    out_ref[...] = (summed / total).T.astype(jnp.bfloat16)
    store = pltpu.make_async_copy(out_ref, out_any, sems.at[len(handed)])
    store.start()
    wait()
    store.wait()


def in_hbm(arrays):
    return [pltpu.with_memory_space_constraint(array, pltpu.HBM) for array in arrays]


def per_device(lengths, owner_map, row_request, deltas, anchors, scales, queries, new_kv):
    blocks = anchors.shape[0]
    tokens = deltas.shape[0]
    senders = lax.axis_size("seq")
    me = lax.axis_index("seq")
    rows, steps, _ = queries.shape
    rows_dev = new_kv.shape[0]
    width = rows_dev * GQ * steps
    small = pltpu.CompilerParams(vmem_limit_bytes=8 * 1024 * 1024)

    flat_deltas = deltas.reshape(tokens * 2, HD)
    flat_anchors = anchors.reshape(blocks * 2, HD)
    flat_queries = queries.reshape(rows, steps, GQ, HD).transpose(0, 2, 1, 3).reshape(-1, HD)
    flat_new = new_kv.reshape(rows_dev * 4, HD)

    whole = jax.ShapeDtypeStruct((tokens * 2, HD), jnp.bfloat16)
    ahead, behind, own = messages(senders, blocks // senders)
    block_rows = tokens * 2 // blocks

    def place(plan, deltas):
        return pl.pallas_call(
            functools.partial(place_kernel, plan),
            out_shape=[jax.ShapeDtypeStruct((slots * block_rows, HD), jnp.bfloat16) for _, _, slots in plan],
            in_specs=[HBM] * 4,
            out_specs=[VMEM] * len(plan),
            scratch_shapes=[
                pltpu.SMEM((blocks,), jnp.int32),
                pltpu.SMEM((blocks,), jnp.int32),
                pltpu.SMEM((senders,), jnp.int32),
                pltpu.VMEM((tokens * 2, HD), jnp.bfloat16),
                pltpu.VMEM((blocks * 2, HD), jnp.float32),
                pltpu.VMEM((2, HD), jnp.float32),
                pltpu.SemaphoreType.DMA((4,)),
            ],
            compiler_params=small,
            name="place",
        )(*in_hbm([owner_map, deltas, flat_anchors, scales]))

    sent = place(ahead, flat_deltas)
    sent, late_deltas = lax.optimization_barrier((sent, flat_deltas))
    got_ahead = [
        hand(message, k, (1,) if k == 1 else (0, 1)) for message, (k, _, _) in zip(sent, ahead)
    ]

    def leaving(count):
        return jax.ShapeDtypeStruct((count // 2, HD + STAT_ROWS, width), jnp.bfloat16)

    def staying(count):
        return jax.ShapeDtypeStruct((count // 2, HD + KEEP_ROWS, width), jnp.float32)

    needed = (late_deltas, flat_anchors, scales, lengths, row_request, flat_queries, flat_new)
    roomy = pltpu.CompilerParams(vmem_limit_bytes=32 * 1024 * 1024)
    send, *common = pl.pallas_call(
        first_kernel,
        out_shape=[
            leaving(senders),
            jax.ShapeDtypeStruct((tokens, 2 * HD), jnp.bfloat16),
            jax.ShapeDtypeStruct((HD, tokens), jnp.bfloat16),
            jax.ShapeDtypeStruct((rows * GQ * steps, 2 * HD), jnp.bfloat16),
            jax.ShapeDtypeStruct((HD + KEEP_ROWS, width), jnp.float32),
        ],
        in_specs=[HBM] * len(needed),
        out_specs=[VMEM] * 5,
        scratch_shapes=[
            (pltpu.SMEM if array.dtype == jnp.int32 else pltpu.VMEM)(array.shape, array.dtype)
            for array in needed
        ]
        + [
            pltpu.VMEM((tokens * 2, HD), jnp.float32),
            pltpu.VMEM((tokens, HD), jnp.bfloat16),
            pltpu.SemaphoreType.DMA((len(needed),)),
        ],
        compiler_params=roomy,
        name="attend_leaving",
    )(*in_hbm(needed))

    k, count = 1, senders // 2
    send, late_deltas = lax.optimization_barrier((send, late_deltas))
    passed = exchange(send, k)
    *sent, mine = place(behind + own, late_deltas)
    settled = ahead[:2] + own
    pages = pl.pallas_call(
        functools.partial(settle_kernel, settled),
        out_shape=whole,
        in_specs=[ANY] * len(settled),
        out_specs=HBM,
        scratch_shapes=[pltpu.SemaphoreType.DMA((len(settled),))],
        compiler_params=small,
        name="settle",
    )(*got_ahead[:2], mine)
    sent, pages = lax.optimization_barrier((sent, pages))
    got = got_ahead[2:] + [hand(message, k, (0,)) for message, (k, _, _) in zip(sent, behind)]
    keep = pl.pallas_call(
        second_kernel,
        out_shape=staying(senders),
        in_specs=[VMEM] * 4,
        out_specs=VMEM,
        compiler_params=roomy,
        name="attend_staying",
    )(*common)
    while count > 1:
        send, keep = pl.pallas_call(
            join_kernel,
            out_shape=[leaving(count), staying(count)],
            in_specs=[VMEM] * 2,
            out_specs=[VMEM] * 2,
            compiler_params=small,
            name="join",
        )(keep, passed)
        k, count = 2 * k, count // 2
        passed = exchange(send, k)
    attended, pages = pl.pallas_call(
        functools.partial(finish_kernel, ahead[2:] + behind),
        out_shape=[jax.ShapeDtypeStruct((width, HD), jnp.bfloat16), whole],
        in_specs=[VMEM] * 2 + [HBM] + [ANY] * len(got),
        out_specs=[HBM, HBM],
        scratch_shapes=[
            pltpu.VMEM((width, HD), jnp.bfloat16),
            pltpu.SemaphoreType.DMA((len(got) + 1,)),
        ],
        input_output_aliases={2: 1},
        compiler_params=small,
        name="finish",
    )(keep, passed, pages, *got)
    pages = pages.reshape(blocks, tokens // blocks, 2, HD)
    attended = (
        attended.reshape(rows_dev, GQ, steps, HD).transpose(0, 2, 1, 3).reshape(rows_dev, steps, GQ * HD)
    )
    return pages, attended


def solution(mesh):
    placed = (
        P("groups"),
        P(("groups", "seq")),
        P("groups"),
        P(("groups", "seq"), None, "tp"),
        P(("groups", "seq"), None, "tp"),
        P("groups", "tp"),
        P("groups", None, "tp"),
        P(("groups", "seq"), None, None, "tp"),
    )
    return jax.shard_map(
        per_device,
        mesh=mesh,
        in_specs=placed,
        out_specs=(P(("groups", "seq"), None, None, "tp"), P(("groups", "seq"), None, "tp")),
        check_vma=False,
    )
```

```python
import functools

import jax
import jax.numpy as jnp
from jax import lax
from jax.experimental import pallas as pl
from jax.experimental.pallas import tpu as pltpu
from jax.sharding import PartitionSpec as P

HD = 128
GQ = 8
STEPS = 2
STAT_ROWS = 8
KEEP_ROWS = 8
FAR = -1e30
RATE = HD ** (-0.5) * 1.4426950408889634

VMEM = pl.BlockSpec(memory_space=pltpu.VMEM)
HBM = pl.BlockSpec(memory_space=pltpu.HBM)
ANY = pl.BlockSpec(memory_space=pl.ANY)
SMEM = pl.BlockSpec(memory_space=pltpu.SMEM)


def inner(device, count):
    return (device ^ (device // (count // 2))) & 1


def partner(device, k, count):
    far = count // 2
    if k == far:
        return device ^ (1 + inner(device, count) * (far - 1))
    if k == 1:
        return device ^ (far - inner(device, count) * (far - 1))
    return device ^ k


def source(device, k, count):
    far = count // 2
    if k == far:
        return device ^ (far - inner(device, count) * (far - 1))
    if k == 1:
        return device ^ (1 + inner(device, count) * (far - 1))
    return device ^ k


def exchange(message, k):
    count = lax.axis_size("seq")
    return lax.ppermute(message, "seq", [(i, i ^ k) for i in range(count)])


def hand(message, k):
    count = lax.axis_size("seq")
    return lax.ppermute(message, "seq", [(i, partner(i, k, count)) for i in range(count)])


def messages(count, capacity):
    far = count // 2
    ahead = [(k, 0, capacity) for k in (far, 1)]
    rest = [k for k in reversed(range(2, count)) if k != far]
    behind = [(k, first, capacity // 2) for k in rest for first in (0, capacity // 2)]
    return ahead, behind, [(0, 0, capacity)]


def place_kernel(plan, owner_any, deltas_any, anchors_any, scales_any, *refs):
    receivers = lax.axis_size("seq")
    me = lax.axis_index("seq")
    outs = refs[:-7]
    owner_ref, source_ref, count_ref, deltas_ref, anchors_ref, scales_ref, sems = refs[-7:]
    blocks = owner_ref.shape[0]
    rows = deltas_ref.shape[0] // blocks
    capacity = blocks // receivers
    loads = [
        pltpu.make_async_copy(source, target, sems.at[index])
        for index, (source, target) in enumerate(
            [
                (owner_any, owner_ref),
                (scales_any, scales_ref),
                (anchors_any, anchors_ref),
                (deltas_any, deltas_ref),
            ]
        )
    ]
    for load in loads:
        load.start()
    bits = capacity.bit_length()
    narrow = receivers * bits < 32
    if not narrow:
        for owner in range(receivers):
            count_ref[owner] = owner * capacity
    loads[0].wait()

    def find(block, counts):
        owner = owner_ref[block]
        if narrow:
            shift = owner * bits
            slot = owner * capacity + ((counts >> shift) & ((1 << bits) - 1))
            counts = counts + (jnp.int32(1) << shift)
        else:
            slot = count_ref[owner]
            count_ref[owner] = slot + 1
        source_ref[slot] = block
        return counts

    lax.fori_loop(0, blocks, find, jnp.int32(0), unroll=16)
    for load in loads[1:]:
        load.wait()
    odd = lax.broadcasted_iota(jnp.int32, (8, HD), 0) % 2 == 1
    scale = jnp.where(odd, scales_ref[1:2, :], scales_ref[0:1, :])[None]
    for (k, start, count), out_ref in zip(plan, outs):
        first = partner(me, k, receivers) * capacity + start

        def one_slot(slot, carry, first=first, out_ref=out_ref):
            block = source_ref[first + slot]
            anchor = jnp.where(
                odd, anchors_ref[pl.ds(2 * block + 1, 1), :], anchors_ref[pl.ds(2 * block, 1), :]
            )[None]
            here = pl.ds(pl.multiple_of(block * rows, rows), rows)
            delta = deltas_ref[here, :].astype(jnp.float32)
            decoded = anchor + scale * delta.reshape(rows // 8, 8, HD)
            out_ref[pl.ds(pl.multiple_of(slot * rows, rows), rows), :] = decoded.reshape(rows, HD).astype(
                jnp.bfloat16
            )
            return carry

        lax.fori_loop(0, count, one_slot, 0, unroll=min(8, count))


def pieces(values):
    high = values.astype(jnp.bfloat16)
    rest = values - high.astype(jnp.float32)
    middle = rest.astype(jnp.bfloat16)
    low = (rest - middle.astype(jnp.float32)).astype(jnp.bfloat16)
    return [high, middle, low]


def packed(partial):
    summed, top, total = partial
    stats = pieces(top) + pieces(total)
    rest = jnp.zeros((STAT_ROWS - len(stats), top.shape[1]), jnp.bfloat16)
    return jnp.concatenate([summed.astype(jnp.bfloat16)] + stats + [rest], axis=0)


def unpacked(block):
    stats = block[HD:, :].astype(jnp.float32)
    top = stats[0:1] + stats[1:2] + stats[2:3]
    total = stats[3:4] + stats[4:5] + stats[5:6]
    return block[0:HD, :].astype(jnp.float32), top, total


def held(partial):
    summed, top, total = partial
    rest = jnp.zeros((KEEP_ROWS - 2, top.shape[1]), jnp.float32)
    return jnp.concatenate([summed, top, total, rest], axis=0)


def taken(block):
    return block[0:HD, :], block[HD : HD + 1, :], block[HD + 1 : HD + 2, :]


def joined(one, other):
    top = jnp.maximum(one[1], other[1])
    scale_one = jnp.exp2((one[1] - top) * RATE)
    scale_other = jnp.exp2((other[1] - top) * RATE)
    return (
        one[0] * scale_one + other[0] * scale_other,
        top,
        one[2] * scale_one + other[2] * scale_other,
    )


def attend(parity, width, keys_ref, turned_ref, asked_ref, store):
    me = lax.axis_index("seq")
    asked = asked_ref.shape[0]

    def partial_of(here):
        scores = lax.dot_general(
            keys_ref[...], here, (((1,), (1,)), ((), ())), preferred_element_type=jnp.float32
        )
        top = jnp.max(scores, axis=0, keepdims=True)
        weights = jnp.exp2((scores - top) * RATE)
        total = jnp.sum(weights, axis=0, keepdims=True)
        summed = jnp.dot(turned_ref[...], weights.astype(jnp.bfloat16), preferred_element_type=jnp.float32)
        return summed, top, total

    if width % HD == 0:
        for index in range(asked // width // 2):
            there = (me ^ (2 * index + parity)) * width
            store(index, partial_of(asked_ref[pl.ds(pl.multiple_of(there, width), width), :]))
        return
    tile = min(2 * HD, asked)
    parts = tile // width

    def one_tile(tile_index, carry):
        here = asked_ref[pl.ds(pl.multiple_of(tile_index * tile, tile), tile), :]
        summed, top, total = partial_of(here)
        for part in range(parts):
            lanes = slice(part * width, (part + 1) * width)
            apart = (tile_index * parts + part) ^ me

            @pl.when(apart % 2 == parity)
            def _(lanes=lanes, apart=apart):
                store(apart // 2, (summed[:, lanes], top[:, lanes], total[:, lanes]))

        return carry

    lax.fori_loop(0, asked // tile, one_tile, 0)


def first_kernel(*refs):
    me = lax.axis_index("seq")
    sources, send_ref, keys_ref, turned_ref, asked_ref, own_ref, *targets = refs[:7], *refs[7:-3]
    wide_ref, values_ref, sems = refs[-3:]
    loads = [
        pltpu.make_async_copy(source, target, sems.at[index])
        for index, (source, target) in enumerate(zip(sources, targets))
    ]
    for load in loads:
        load.start()
    deltas_ref, anchors_ref, scales_ref, lengths_ref, request_ref, queries_ref, new_ref = targets
    blocks = anchors_ref.shape[0] // 2
    rows = deltas_ref.shape[0] // blocks
    tokens = rows // 2
    requests = lengths_ref.shape[0]
    asked = queries_ref.shape[0]
    per_row = asked // request_ref.shape[0]
    width = send_ref.shape[2]
    for load in loads[2:]:
        load.wait()

    lane = lax.broadcasted_iota(jnp.int32, (1, HD), 1)
    first = jnp.zeros((1, HD), jnp.int32)
    last = jnp.zeros((1, HD), jnp.int32)
    end = 0 - me * (blocks * tokens)
    for request in range(requests):
        start = end
        end = end + lengths_ref[request]
        first = jnp.where(lane == request, start, first)
        last = jnp.where(lane == request, end, last)
    place = lax.broadcasted_iota(jnp.int32, (blocks * tokens, HD), 0)
    keys_ref[:, HD:] = jnp.where((place >= first) & (place < last), 1.0, 0.0).astype(jnp.bfloat16)

    asked_ref[:, 0:HD] = queries_ref[...]
    wide_lane = lax.broadcasted_iota(jnp.int32, (per_row, HD), 1)

    def one_row(row, carry):
        asked_ref[pl.ds(pl.multiple_of(row * per_row, per_row), per_row), HD:] = jnp.where(
            (wide_lane == request_ref[row]) | (wide_lane >= requests), 0.0, FAR
        ).astype(jnp.bfloat16)
        return carry

    lax.fori_loop(0, request_ref.shape[0], one_row, 0, unroll=16)

    fresh = new_ref.shape[0] // 4
    new = new_ref[...].astype(jnp.float32).reshape(fresh, 4, HD)
    mine = queries_ref[pl.ds(pl.multiple_of(me * width, width), width), :]
    of_row = lax.broadcasted_iota(jnp.int32, (fresh, width), 1) // (GQ * STEPS)
    same = of_row == lax.broadcasted_iota(jnp.int32, (fresh, width), 0)
    step = lax.broadcasted_iota(jnp.int32, (1, width), 1) % STEPS
    own_scores = []
    for which in range(STEPS):
        scored = lax.dot_general(
            new[:, 2 * which, :].astype(jnp.bfloat16),
            mine,
            (((1,), (1,)), ((), ())),
            preferred_element_type=jnp.float32,
        )
        picked = jnp.sum(jnp.where(same, scored, 0.0), axis=0, keepdims=True)
        own_scores.append(jnp.where(step >= which, picked, FAR))
    own_top = jnp.maximum(own_scores[0], own_scores[1])
    own_total = jnp.zeros((1, width), jnp.float32)
    own_summed = jnp.zeros((HD, width), jnp.float32)
    for which in range(STEPS):
        weight = jnp.exp2((own_scores[which] - own_top) * RATE)
        own_total = own_total + weight
        spread = jnp.where(same, weight, 0.0).astype(jnp.bfloat16)
        own_summed = own_summed + lax.dot_general(
            new[:, 2 * which + 1, :].astype(jnp.bfloat16),
            spread,
            (((0,), (0,)), ((), ())),
            preferred_element_type=jnp.float32,
        )
    own_ref[...] = held((own_summed, own_top, own_total))

    for load in loads[:2]:
        load.wait()
    wide_ref[...] = deltas_ref[...].astype(jnp.float32)
    scale_key = scales_ref[0:1, :]
    scale_value = scales_ref[1:2, :]

    def one_block(block, carry):
        here = pl.ds(pl.multiple_of(block * tokens, tokens), tokens)
        key = wide_ref[pl.ds(block * rows, tokens, stride=2), :]
        value = wide_ref[pl.ds(block * rows + 1, tokens, stride=2), :]
        keys_ref[here, 0:HD] = (anchors_ref[pl.ds(2 * block, 1), :] + scale_key * key).astype(jnp.bfloat16)
        values_ref[here, :] = (anchors_ref[pl.ds(2 * block + 1, 1), :] + scale_value * value).astype(
            jnp.bfloat16
        )
        return carry

    lax.fori_loop(0, blocks, one_block, 0, unroll=16)
    turned_ref[...] = values_ref[...].T

    def store(index, partial):
        send_ref[index] = packed(partial)

    attend(1, width, keys_ref, turned_ref, asked_ref, store)


def second_kernel(keys_ref, turned_ref, asked_ref, own_ref, keep_ref):
    def store(index, partial):
        keep_ref[index] = held(partial)

    attend(0, keep_ref.shape[2], keys_ref, turned_ref, asked_ref, store)
    keep_ref[0] = held(joined(taken(keep_ref[0]), taken(own_ref[...])))


def join_kernel(keep_ref, got_ref, send_ref, next_ref):
    for index in range(keep_ref.shape[0]):
        partial = joined(taken(keep_ref[index]), unpacked(got_ref[index]))
        if index % 2 == 1:
            send_ref[index // 2] = packed(partial)
        else:
            next_ref[index // 2] = held(partial)


def settle(plan, handed, pages, sems):
    receivers = lax.axis_size("seq")
    me = lax.axis_index("seq")
    rows = pages.shape[0] // receivers
    copies = []
    for index, (k, start, slots) in enumerate(plan):
        size = handed[index].shape[0]
        sender = source(me, k, receivers) if k else me
        first = pl.multiple_of(sender * rows + start * (size // slots), size)
        copies.append(pltpu.make_async_copy(handed[index], pages.at[pl.ds(first, size), :], sems.at[index]))
        copies[-1].start()
    return copies


def settle_kernel(plan, *refs):
    *handed, pages, sems = refs
    for copy in settle(plan, handed, pages, sems):
        copy.wait()


def finish_kernel(plan, keep_ref, got_ref, _, *refs):
    *handed, out_any, pages, out_ref, sems = refs
    copies = settle(plan, handed, pages, sems)
    summed, _, total = joined(taken(keep_ref[0]), unpacked(got_ref[0]))
    out_ref[...] = (summed / total).T.astype(jnp.bfloat16)
    copies.append(pltpu.make_async_copy(out_ref, out_any, sems.at[len(copies)]))
    copies[-1].start()
    for copy in copies:
        copy.wait()


def in_hbm(arrays):
    return [pltpu.with_memory_space_constraint(array, pltpu.HBM) for array in arrays]


def per_device(lengths, owner_map, row_request, deltas, anchors, scales, queries, new_kv):
    blocks = anchors.shape[0]
    tokens = deltas.shape[0]
    senders = lax.axis_size("seq")
    me = lax.axis_index("seq")
    rows, steps, _ = queries.shape
    rows_dev = new_kv.shape[0]
    width = rows_dev * GQ * steps
    small = pltpu.CompilerParams(vmem_limit_bytes=8 * 1024 * 1024)

    flat_deltas = deltas.reshape(tokens * 2, HD)
    flat_anchors = anchors.reshape(blocks * 2, HD)
    flat_queries = queries.reshape(rows, steps, GQ, HD).transpose(0, 2, 1, 3).reshape(-1, HD)
    flat_new = new_kv.reshape(rows_dev * 4, HD)

    whole = jax.ShapeDtypeStruct((tokens * 2, HD), jnp.bfloat16)
    ahead, behind, own = messages(senders, blocks // senders)
    block_rows = tokens * 2 // blocks

    def place(plan, deltas):
        return pl.pallas_call(
            functools.partial(place_kernel, plan),
            out_shape=[jax.ShapeDtypeStruct((slots * block_rows, HD), jnp.bfloat16) for _, _, slots in plan],
            in_specs=[HBM] * 4,
            out_specs=[VMEM] * len(plan),
            scratch_shapes=[
                pltpu.SMEM((blocks,), jnp.int32),
                pltpu.SMEM((blocks,), jnp.int32),
                pltpu.SMEM((senders,), jnp.int32),
                pltpu.VMEM((tokens * 2, HD), jnp.bfloat16),
                pltpu.VMEM((blocks * 2, HD), jnp.float32),
                pltpu.VMEM((2, HD), jnp.float32),
                pltpu.SemaphoreType.DMA((4,)),
            ],
            compiler_params=small,
            name="place",
        )(*in_hbm([owner_map, deltas, flat_anchors, scales]))

    sent = place(ahead, flat_deltas)
    sent, late_deltas = lax.optimization_barrier((sent, flat_deltas))
    got_ahead = [hand(message, k) for message, (k, _, _) in zip(sent, ahead)]

    def leaving(count):
        return jax.ShapeDtypeStruct((count // 2, HD + STAT_ROWS, width), jnp.bfloat16)

    def staying(count):
        return jax.ShapeDtypeStruct((count // 2, HD + KEEP_ROWS, width), jnp.float32)

    needed = (late_deltas, flat_anchors, scales, lengths, row_request, flat_queries, flat_new)
    roomy = pltpu.CompilerParams(vmem_limit_bytes=32 * 1024 * 1024)
    send, *common = pl.pallas_call(
        first_kernel,
        out_shape=[
            leaving(senders),
            jax.ShapeDtypeStruct((tokens, 2 * HD), jnp.bfloat16),
            jax.ShapeDtypeStruct((HD, tokens), jnp.bfloat16),
            jax.ShapeDtypeStruct((rows * GQ * steps, 2 * HD), jnp.bfloat16),
            jax.ShapeDtypeStruct((HD + KEEP_ROWS, width), jnp.float32),
        ],
        in_specs=[HBM] * len(needed),
        out_specs=[VMEM] * 5,
        scratch_shapes=[
            (pltpu.SMEM if array.dtype == jnp.int32 else pltpu.VMEM)(array.shape, array.dtype)
            for array in needed
        ]
        + [
            pltpu.VMEM((tokens * 2, HD), jnp.float32),
            pltpu.VMEM((tokens, HD), jnp.bfloat16),
            pltpu.SemaphoreType.DMA((len(needed),)),
        ],
        compiler_params=roomy,
        name="attend_leaving",
    )(*in_hbm(needed))

    k, count = 1, senders // 2
    send, late_deltas = lax.optimization_barrier((send, late_deltas))
    passed = exchange(send, k)
    *sent, mine = place(behind + own, late_deltas)
    got = [hand(message, k) for message, (k, _, _) in zip(sent, behind)]
    keep = pl.pallas_call(
        second_kernel,
        out_shape=staying(senders),
        in_specs=[VMEM] * 4,
        out_specs=VMEM,
        compiler_params=roomy,
        name="attend_staying",
    )(*common)
    while count > 1:
        send, keep = pl.pallas_call(
            join_kernel,
            out_shape=[leaving(count), staying(count)],
            in_specs=[VMEM] * 2,
            out_specs=[VMEM] * 2,
            compiler_params=small,
            name="join",
        )(keep, passed)
        k, count = 2 * k, count // 2
        passed = exchange(send, k)
    settled = ahead + own
    pages = pl.pallas_call(
        functools.partial(settle_kernel, settled),
        out_shape=whole,
        in_specs=[ANY] * len(settled),
        out_specs=HBM,
        scratch_shapes=[pltpu.SemaphoreType.DMA((len(settled),))],
        compiler_params=small,
        name="settle",
    )(*got_ahead, mine)
    attended, pages = pl.pallas_call(
        functools.partial(finish_kernel, behind),
        out_shape=[jax.ShapeDtypeStruct((width, HD), jnp.bfloat16), whole],
        in_specs=[VMEM] * 2 + [HBM] + [ANY] * len(got),
        out_specs=[HBM, HBM],
        scratch_shapes=[
            pltpu.VMEM((width, HD), jnp.bfloat16),
            pltpu.SemaphoreType.DMA((len(got) + 1,)),
        ],
        input_output_aliases={2: 1},
        compiler_params=small,
        name="finish",
    )(keep, passed, pages, *got)
    pages = pages.reshape(blocks, tokens // blocks, 2, HD)
    attended = (
        attended.reshape(rows_dev, GQ, steps, HD).transpose(0, 2, 1, 3).reshape(rows_dev, steps, GQ * HD)
    )
    return pages, attended


def solution(mesh):
    placed = (
        P("groups"),
        P(("groups", "seq")),
        P("groups"),
        P(("groups", "seq"), None, "tp"),
        P(("groups", "seq"), None, "tp"),
        P("groups", "tp"),
        P("groups", None, "tp"),
        P(("groups", "seq"), None, None, "tp"),
    )
    return jax.shard_map(
        per_device,
        mesh=mesh,
        in_specs=placed,
        out_specs=(P(("groups", "seq"), None, None, "tp"), P(("groups", "seq"), None, "tp")),
        check_vma=False,
    )
```

```python
import functools

import jax
import jax.numpy as jnp
from jax import lax
from jax.experimental import pallas as pl
from jax.experimental.pallas import tpu as pltpu
from jax.sharding import PartitionSpec as P

HD = 128
GQ = 8
STEPS = 2
STAT_ROWS = 8
KEEP_ROWS = 8
FAR = -1e30
RATE = HD ** (-0.5) * 1.4426950408889634

VMEM = pl.BlockSpec(memory_space=pltpu.VMEM)
HBM = pl.BlockSpec(memory_space=pltpu.HBM)
ANY = pl.BlockSpec(memory_space=pl.ANY)
SMEM = pl.BlockSpec(memory_space=pltpu.SMEM)


def inner(device, count):
    return (device ^ (device // (count // 2))) & 1


def partner(device, k, count):
    far = count // 2
    if k == far:
        return device ^ (1 + inner(device, count) * (far - 1))
    if k == 1:
        return device ^ (far - inner(device, count) * (far - 1))
    return device ^ k


def source(device, k, count):
    far = count // 2
    if k == far:
        return device ^ (far - inner(device, count) * (far - 1))
    if k == 1:
        return device ^ (1 + inner(device, count) * (far - 1))
    return device ^ k


def exchange(message, k):
    count = lax.axis_size("seq")
    return lax.ppermute(message, "seq", [(i, i ^ k) for i in range(count)])


def hand(message, k):
    count = lax.axis_size("seq")
    return lax.ppermute(message, "seq", [(i, partner(i, k, count)) for i in range(count)])


def messages(count, capacity):
    half = capacity // 2
    ahead = [(k, 0, capacity) for k in range(count // 2, count)]
    behind = [(k, first, half) for k in reversed(range(1, count // 2)) for first in (0, half)]
    return ahead, behind, [(0, 0, capacity)]


def place_kernel(plan, owner_any, deltas_any, anchors_any, scales_any, *refs):
    receivers = lax.axis_size("seq")
    me = lax.axis_index("seq")
    outs = refs[:-7]
    owner_ref, source_ref, count_ref, deltas_ref, anchors_ref, scales_ref, sems = refs[-7:]
    blocks = owner_ref.shape[0]
    rows = deltas_ref.shape[0] // blocks
    capacity = blocks // receivers
    loads = [
        pltpu.make_async_copy(source, target, sems.at[index])
        for index, (source, target) in enumerate(
            [
                (owner_any, owner_ref),
                (scales_any, scales_ref),
                (anchors_any, anchors_ref),
                (deltas_any, deltas_ref),
            ]
        )
    ]
    for load in loads:
        load.start()
    bits = capacity.bit_length()
    narrow = receivers * bits < 32
    if not narrow:
        for owner in range(receivers):
            count_ref[owner] = owner * capacity
    loads[0].wait()

    def find(block, counts):
        owner = owner_ref[block]
        if narrow:
            shift = owner * bits
            slot = owner * capacity + ((counts >> shift) & ((1 << bits) - 1))
            counts = counts + (jnp.int32(1) << shift)
        else:
            slot = count_ref[owner]
            count_ref[owner] = slot + 1
        source_ref[slot] = block
        return counts

    lax.fori_loop(0, blocks, find, jnp.int32(0), unroll=16)
    for load in loads[1:]:
        load.wait()
    odd = lax.broadcasted_iota(jnp.int32, (8, HD), 0) % 2 == 1
    scale = jnp.where(odd, scales_ref[1:2, :], scales_ref[0:1, :])[None]
    for (k, start, count), out_ref in zip(plan, outs):
        first = partner(me, k, receivers) * capacity + start

        def one_slot(slot, carry, first=first, out_ref=out_ref):
            block = source_ref[first + slot]
            anchor = jnp.where(
                odd, anchors_ref[pl.ds(2 * block + 1, 1), :], anchors_ref[pl.ds(2 * block, 1), :]
            )[None]
            here = pl.ds(pl.multiple_of(block * rows, rows), rows)
            delta = deltas_ref[here, :].astype(jnp.float32)
            decoded = anchor + scale * delta.reshape(rows // 8, 8, HD)
            out_ref[pl.ds(pl.multiple_of(slot * rows, rows), rows), :] = decoded.reshape(rows, HD).astype(
                jnp.bfloat16
            )
            return carry

        lax.fori_loop(0, count, one_slot, 0, unroll=min(8, count))


def pieces(values):
    high = values.astype(jnp.bfloat16)
    rest = values - high.astype(jnp.float32)
    middle = rest.astype(jnp.bfloat16)
    low = (rest - middle.astype(jnp.float32)).astype(jnp.bfloat16)
    return [high, middle, low]


def packed(partial):
    summed, top, total = partial
    stats = pieces(top) + pieces(total)
    rest = jnp.zeros((STAT_ROWS - len(stats), top.shape[1]), jnp.bfloat16)
    return jnp.concatenate([summed.astype(jnp.bfloat16)] + stats + [rest], axis=0)


def unpacked(block):
    stats = block[HD:, :].astype(jnp.float32)
    top = stats[0:1] + stats[1:2] + stats[2:3]
    total = stats[3:4] + stats[4:5] + stats[5:6]
    return block[0:HD, :].astype(jnp.float32), top, total


def held(partial):
    summed, top, total = partial
    rest = jnp.zeros((KEEP_ROWS - 2, top.shape[1]), jnp.float32)
    return jnp.concatenate([summed, top, total, rest], axis=0)


def taken(block):
    return block[0:HD, :], block[HD : HD + 1, :], block[HD + 1 : HD + 2, :]


def joined(one, other):
    top = jnp.maximum(one[1], other[1])
    scale_one = jnp.exp2((one[1] - top) * RATE)
    scale_other = jnp.exp2((other[1] - top) * RATE)
    return (
        one[0] * scale_one + other[0] * scale_other,
        top,
        one[2] * scale_one + other[2] * scale_other,
    )


def attend(parity, width, keys_ref, turned_ref, asked_ref, store):
    me = lax.axis_index("seq")
    asked = asked_ref.shape[0]

    def partial_of(here):
        scores = lax.dot_general(
            keys_ref[...], here, (((1,), (1,)), ((), ())), preferred_element_type=jnp.float32
        )
        top = jnp.max(scores, axis=0, keepdims=True)
        weights = jnp.exp2((scores - top) * RATE)
        total = jnp.sum(weights, axis=0, keepdims=True)
        summed = jnp.dot(turned_ref[...], weights.astype(jnp.bfloat16), preferred_element_type=jnp.float32)
        return summed, top, total

    if width % HD == 0:
        for index in range(asked // width // 2):
            there = (me ^ (2 * index + parity)) * width
            store(index, partial_of(asked_ref[pl.ds(pl.multiple_of(there, width), width), :]))
        return
    tile = min(2 * HD, asked)
    parts = tile // width

    def one_tile(tile_index, carry):
        here = asked_ref[pl.ds(pl.multiple_of(tile_index * tile, tile), tile), :]
        summed, top, total = partial_of(here)
        for part in range(parts):
            lanes = slice(part * width, (part + 1) * width)
            apart = (tile_index * parts + part) ^ me

            @pl.when(apart % 2 == parity)
            def _(lanes=lanes, apart=apart):
                store(apart // 2, (summed[:, lanes], top[:, lanes], total[:, lanes]))

        return carry

    lax.fori_loop(0, asked // tile, one_tile, 0)


def first_kernel(*refs):
    me = lax.axis_index("seq")
    *targets, wide_ref, values_ref, sems = refs[-10:]
    sources, *send, keys_ref, turned_ref, asked_ref, own_ref = refs[:7], *refs[7:-10]
    loads = [
        pltpu.make_async_copy(source, target, sems.at[index])
        for index, (source, target) in enumerate(zip(sources, targets))
    ]
    for load in loads:
        load.start()
    deltas_ref, anchors_ref, scales_ref, lengths_ref, request_ref, queries_ref, new_ref = targets
    blocks = anchors_ref.shape[0] // 2
    rows = deltas_ref.shape[0] // blocks
    tokens = rows // 2
    requests = lengths_ref.shape[0]
    asked = queries_ref.shape[0]
    per_row = asked // request_ref.shape[0]
    width = own_ref.shape[1]
    for load in loads[2:]:
        load.wait()

    lane = lax.broadcasted_iota(jnp.int32, (1, HD), 1)
    first = jnp.zeros((1, HD), jnp.int32)
    last = jnp.zeros((1, HD), jnp.int32)
    end = 0 - me * (blocks * tokens)
    for request in range(requests):
        start = end
        end = end + lengths_ref[request]
        first = jnp.where(lane == request, start, first)
        last = jnp.where(lane == request, end, last)
    place = lax.broadcasted_iota(jnp.int32, (blocks * tokens, HD), 0)
    keys_ref[:, HD:] = jnp.where((place >= first) & (place < last), 1.0, 0.0).astype(jnp.bfloat16)

    asked_ref[:, 0:HD] = queries_ref[...]
    wide_lane = lax.broadcasted_iota(jnp.int32, (per_row, HD), 1)

    def one_row(row, carry):
        asked_ref[pl.ds(pl.multiple_of(row * per_row, per_row), per_row), HD:] = jnp.where(
            (wide_lane == request_ref[row]) | (wide_lane >= requests), 0.0, FAR
        ).astype(jnp.bfloat16)
        return carry

    lax.fori_loop(0, request_ref.shape[0], one_row, 0, unroll=16)

    fresh = new_ref.shape[0] // 4
    new = new_ref[...].astype(jnp.float32).reshape(fresh, 4, HD)
    mine = queries_ref[pl.ds(pl.multiple_of(me * width, width), width), :]
    of_row = lax.broadcasted_iota(jnp.int32, (fresh, width), 1) // (GQ * STEPS)
    same = of_row == lax.broadcasted_iota(jnp.int32, (fresh, width), 0)
    step = lax.broadcasted_iota(jnp.int32, (1, width), 1) % STEPS
    own_scores = []
    for which in range(STEPS):
        scored = lax.dot_general(
            new[:, 2 * which, :].astype(jnp.bfloat16),
            mine,
            (((1,), (1,)), ((), ())),
            preferred_element_type=jnp.float32,
        )
        picked = jnp.sum(jnp.where(same, scored, 0.0), axis=0, keepdims=True)
        own_scores.append(jnp.where(step >= which, picked, FAR))
    own_top = jnp.maximum(own_scores[0], own_scores[1])
    own_total = jnp.zeros((1, width), jnp.float32)
    own_summed = jnp.zeros((HD, width), jnp.float32)
    for which in range(STEPS):
        weight = jnp.exp2((own_scores[which] - own_top) * RATE)
        own_total = own_total + weight
        spread = jnp.where(same, weight, 0.0).astype(jnp.bfloat16)
        own_summed = own_summed + lax.dot_general(
            new[:, 2 * which + 1, :].astype(jnp.bfloat16),
            spread,
            (((0,), (0,)), ((), ())),
            preferred_element_type=jnp.float32,
        )
    own_ref[...] = held((own_summed, own_top, own_total))

    for load in loads[:2]:
        load.wait()
    wide_ref[...] = deltas_ref[...].astype(jnp.float32)
    scale_key = scales_ref[0:1, :]
    scale_value = scales_ref[1:2, :]

    def one_block(block, carry):
        here = pl.ds(pl.multiple_of(block * tokens, tokens), tokens)
        key = wide_ref[pl.ds(block * rows, tokens, stride=2), :]
        value = wide_ref[pl.ds(block * rows + 1, tokens, stride=2), :]
        keys_ref[here, 0:HD] = (anchors_ref[pl.ds(2 * block, 1), :] + scale_key * key).astype(jnp.bfloat16)
        values_ref[here, :] = (anchors_ref[pl.ds(2 * block + 1, 1), :] + scale_value * value).astype(
            jnp.bfloat16
        )
        return carry

    lax.fori_loop(0, blocks, one_block, 0, unroll=16)
    turned_ref[...] = values_ref[...].T

    def store(index, partial):
        many = send[0].shape[0]
        if isinstance(index, int):
            send[index // many][index % many] = packed(partial)
            return
        for piece, send_ref in enumerate(send):

            @pl.when(index // many == piece)
            def _(piece=piece, send_ref=send_ref):
                send_ref[index - piece * many] = packed(partial)

    attend(1, width, keys_ref, turned_ref, asked_ref, store)


def second_kernel(keys_ref, turned_ref, asked_ref, own_ref, keep_ref):
    def store(index, partial):
        keep_ref[index] = held(partial)

    attend(0, keep_ref.shape[2], keys_ref, turned_ref, asked_ref, store)
    keep_ref[0] = held(joined(taken(keep_ref[0]), taken(own_ref[...])))


def join_kernel(came, keep_ref, *refs):
    got, send, next_ref = refs[:came], refs[came:-1], refs[-1]
    for index in range(keep_ref.shape[0]):
        many = got[0].shape[0]
        partial = joined(taken(keep_ref[index]), unpacked(got[index // many][index % many]))
        if index % 2 == 1:
            many = send[0].shape[0]
            send[index // 2 // many][index // 2 % many] = packed(partial)
        else:
            next_ref[index // 2] = held(partial)


def settle(plan, handed, pages, sems):
    receivers = lax.axis_size("seq")
    me = lax.axis_index("seq")
    rows = pages.shape[0] // receivers
    copies = []
    for index, (k, start, slots) in enumerate(plan):
        size = handed[index].shape[0]
        sender = source(me, k, receivers) if k else me
        first = pl.multiple_of(sender * rows + start * (size // slots), size)
        copies.append(pltpu.make_async_copy(handed[index], pages.at[pl.ds(first, size), :], sems.at[index]))
        copies[-1].start()
    return copies


def settle_kernel(plan, *refs):
    *handed, pages, sems = refs
    for copy in settle(plan, handed, pages, sems):
        copy.wait()


def finish_kernel(plan, keep_ref, got_ref, _, *refs):
    *handed, out_any, pages, out_ref, sems = refs
    copies = settle(plan, handed, pages, sems)
    summed, _, total = joined(taken(keep_ref[0]), unpacked(got_ref[0]))
    out_ref[...] = (summed / total).T.astype(jnp.bfloat16)
    copies.append(pltpu.make_async_copy(out_ref, out_any, sems.at[len(copies)]))
    copies[-1].start()
    for copy in copies:
        copy.wait()


def in_hbm(arrays):
    return [pltpu.with_memory_space_constraint(array, pltpu.HBM) for array in arrays]


def per_device(lengths, owner_map, row_request, deltas, anchors, scales, queries, new_kv):
    blocks = anchors.shape[0]
    tokens = deltas.shape[0]
    senders = lax.axis_size("seq")
    me = lax.axis_index("seq")
    rows, steps, _ = queries.shape
    rows_dev = new_kv.shape[0]
    width = rows_dev * GQ * steps
    small = pltpu.CompilerParams(vmem_limit_bytes=8 * 1024 * 1024)

    flat_deltas = deltas.reshape(tokens * 2, HD)
    flat_anchors = anchors.reshape(blocks * 2, HD)
    flat_queries = queries.reshape(rows, steps, GQ, HD).transpose(0, 2, 1, 3).reshape(-1, HD)
    flat_new = new_kv.reshape(rows_dev * 4, HD)

    whole = jax.ShapeDtypeStruct((tokens * 2, HD), jnp.bfloat16)
    ahead, behind, own = messages(senders, blocks // senders)
    block_rows = tokens * 2 // blocks

    def place(plan, deltas):
        return pl.pallas_call(
            functools.partial(place_kernel, plan),
            out_shape=[jax.ShapeDtypeStruct((slots * block_rows, HD), jnp.bfloat16) for _, _, slots in plan],
            in_specs=[HBM] * 4,
            out_specs=[VMEM] * len(plan),
            scratch_shapes=[
                pltpu.SMEM((blocks,), jnp.int32),
                pltpu.SMEM((blocks,), jnp.int32),
                pltpu.SMEM((senders,), jnp.int32),
                pltpu.VMEM((tokens * 2, HD), jnp.bfloat16),
                pltpu.VMEM((blocks * 2, HD), jnp.float32),
                pltpu.VMEM((2, HD), jnp.float32),
                pltpu.SemaphoreType.DMA((4,)),
            ],
            compiler_params=small,
            name="place",
        )(*in_hbm([owner_map, deltas, flat_anchors, scales]))

    sent = place(ahead, flat_deltas)
    sent, late_deltas = lax.optimization_barrier((sent, flat_deltas))
    got_ahead = [hand(message, k) for message, (k, _, _) in zip(sent, ahead)]

    def leaving(count):
        many = max(1, count // 4)
        return [jax.ShapeDtypeStruct((many, HD + STAT_ROWS, width), jnp.bfloat16)] * (count // 2 // many)

    def staying(count):
        return jax.ShapeDtypeStruct((count // 2, HD + KEEP_ROWS, width), jnp.float32)

    needed = (late_deltas, flat_anchors, scales, lengths, row_request, flat_queries, flat_new)
    roomy = pltpu.CompilerParams(vmem_limit_bytes=32 * 1024 * 1024)
    outs = pl.pallas_call(
        first_kernel,
        out_shape=[
            *leaving(senders),
            jax.ShapeDtypeStruct((tokens, 2 * HD), jnp.bfloat16),
            jax.ShapeDtypeStruct((HD, tokens), jnp.bfloat16),
            jax.ShapeDtypeStruct((rows * GQ * steps, 2 * HD), jnp.bfloat16),
            jax.ShapeDtypeStruct((HD + KEEP_ROWS, width), jnp.float32),
        ],
        in_specs=[HBM] * len(needed),
        out_specs=[VMEM] * (len(leaving(senders)) + 4),
        scratch_shapes=[
            (pltpu.SMEM if array.dtype == jnp.int32 else pltpu.VMEM)(array.shape, array.dtype)
            for array in needed
        ]
        + [
            pltpu.VMEM((tokens * 2, HD), jnp.float32),
            pltpu.VMEM((tokens, HD), jnp.bfloat16),
            pltpu.SemaphoreType.DMA((len(needed),)),
        ],
        compiler_params=roomy,
        name="attend_leaving",
    )(*in_hbm(needed))
    send, common = outs[:-4], outs[-4:]

    k, count = 1, senders // 2
    send, late_deltas = lax.optimization_barrier((send, late_deltas))
    passed = [exchange(message, k) for message in send]
    *sent, mine = place(behind + own, late_deltas)
    keep = pl.pallas_call(
        second_kernel,
        out_shape=staying(senders),
        in_specs=[VMEM] * 4,
        out_specs=VMEM,
        compiler_params=roomy,
        name="attend_staying",
    )(*common)
    while count > 1:
        *send, keep = pl.pallas_call(
            functools.partial(join_kernel, len(passed)),
            out_shape=leaving(count) + [staying(count)],
            in_specs=[VMEM] * (len(passed) + 1),
            out_specs=[VMEM] * (len(leaving(count)) + 1),
            compiler_params=small,
            name="join",
        )(keep, *passed)
        if k == 1:
            sent, send = lax.optimization_barrier((sent, send))
            got = [hand(message, k) for message, (k, _, _) in zip(sent, behind)]
        k, count = 2 * k, count // 2
        passed = [exchange(message, k) for message in send]
    settled = ahead + own
    pages = pl.pallas_call(
        functools.partial(settle_kernel, settled),
        out_shape=whole,
        in_specs=[ANY] * len(settled),
        out_specs=HBM,
        scratch_shapes=[pltpu.SemaphoreType.DMA((len(settled),))],
        compiler_params=small,
        name="settle",
    )(*got_ahead, mine)
    attended, pages = pl.pallas_call(
        functools.partial(finish_kernel, behind),
        out_shape=[jax.ShapeDtypeStruct((width, HD), jnp.bfloat16), whole],
        in_specs=[VMEM] * 2 + [HBM] + [ANY] * len(got),
        out_specs=[HBM, HBM],
        scratch_shapes=[
            pltpu.VMEM((width, HD), jnp.bfloat16),
            pltpu.SemaphoreType.DMA((len(got) + 1,)),
        ],
        input_output_aliases={2: 1},
        compiler_params=small,
        name="finish",
    )(keep, *passed, pages, *got)
    pages = pages.reshape(blocks, tokens // blocks, 2, HD)
    attended = (
        attended.reshape(rows_dev, GQ, steps, HD).transpose(0, 2, 1, 3).reshape(rows_dev, steps, GQ * HD)
    )
    return pages, attended


def solution(mesh):
    placed = (
        P("groups"),
        P(("groups", "seq")),
        P("groups"),
        P(("groups", "seq"), None, "tp"),
        P(("groups", "seq"), None, "tp"),
        P("groups", "tp"),
        P("groups", None, "tp"),
        P(("groups", "seq"), None, None, "tp"),
    )
    return jax.shard_map(
        per_device,
        mesh=mesh,
        in_specs=placed,
        out_specs=(P(("groups", "seq"), None, None, "tp"), P(("groups", "seq"), None, "tp")),
        check_vma=False,
    )
```

```python
import functools

import jax
import jax.numpy as jnp
from jax import lax
from jax.experimental import pallas as pl
from jax.experimental.pallas import tpu as pltpu
from jax.sharding import PartitionSpec as P

HD = 128
GQ = 8
STEPS = 2
STAT_ROWS = 8
KEEP_ROWS = 8
FAR = -1e30
RATE = HD ** (-0.5) * 1.4426950408889634

VMEM = pl.BlockSpec(memory_space=pltpu.VMEM)
HBM = pl.BlockSpec(memory_space=pltpu.HBM)
ANY = pl.BlockSpec(memory_space=pl.ANY)
SMEM = pl.BlockSpec(memory_space=pltpu.SMEM)


def inner(device, count):
    return (device ^ (device // (count // 2))) & 1


def partner(device, k, count):
    far = count // 2
    if k == far:
        return device ^ (1 + inner(device, count) * (far - 1))
    if k == 1:
        return device ^ (far - inner(device, count) * (far - 1))
    return device ^ k


def source(device, k, count):
    far = count // 2
    if k == far:
        return device ^ (far - inner(device, count) * (far - 1))
    if k == 1:
        return device ^ (1 + inner(device, count) * (far - 1))
    return device ^ k


def exchange(message, k):
    count = lax.axis_size("seq")
    return lax.ppermute(message, "seq", [(i, i ^ k) for i in range(count)])


def hand(message, k):
    count = lax.axis_size("seq")
    return lax.ppermute(message, "seq", [(i, partner(i, k, count)) for i in range(count)])


def messages(count, capacity):
    half = capacity // 2
    ahead = [(k, 0, capacity) for k in range(count // 2, count)]
    behind = [(k, first, half) for k in reversed(range(1, count // 2)) for first in (0, half)]
    return ahead, behind, [(0, 0, capacity)]


def place_kernel(plan, owner_any, deltas_any, anchors_any, scales_any, *refs):
    receivers = lax.axis_size("seq")
    me = lax.axis_index("seq")
    outs = refs[:-7]
    owner_ref, source_ref, count_ref, deltas_ref, anchors_ref, scales_ref, sems = refs[-7:]
    blocks = owner_ref.shape[0]
    rows = deltas_ref.shape[0] // blocks
    capacity = blocks // receivers
    quarter = deltas_ref.shape[0] // 4
    parts = [pl.ds(index * quarter, quarter) for index in range(4)]
    loads = [
        pltpu.make_async_copy(source, target, sems.at[index])
        for index, (source, target) in enumerate(
            [(owner_any, owner_ref), (scales_any, scales_ref), (anchors_any, anchors_ref)]
            + [(deltas_any.at[part], deltas_ref.at[part]) for part in parts]
        )
    ]
    for load in loads:
        load.start()
    bits = capacity.bit_length()
    narrow = receivers * bits < 32
    if not narrow:
        for owner in range(receivers):
            count_ref[owner] = owner * capacity
    loads[0].wait()

    def find(block, counts):
        owner = owner_ref[block]
        if narrow:
            shift = owner * bits
            slot = owner * capacity + ((counts >> shift) & ((1 << bits) - 1))
            counts = counts + (jnp.int32(1) << shift)
        else:
            slot = count_ref[owner]
            count_ref[owner] = slot + 1
        source_ref[slot] = block
        return counts

    lax.fori_loop(0, blocks, find, jnp.int32(0), unroll=16)
    for load in loads[1:]:
        load.wait()
    odd = lax.broadcasted_iota(jnp.int32, (8, HD), 0) % 2 == 1
    scale = jnp.where(odd, scales_ref[1:2, :], scales_ref[0:1, :])[None]
    for (k, start, count), out_ref in zip(plan, outs):
        first = partner(me, k, receivers) * capacity + start

        def one_slot(slot, carry, first=first, out_ref=out_ref):
            block = source_ref[first + slot]
            anchor = jnp.where(
                odd, anchors_ref[pl.ds(2 * block + 1, 1), :], anchors_ref[pl.ds(2 * block, 1), :]
            )[None]
            here = pl.ds(pl.multiple_of(block * rows, rows), rows)
            delta = deltas_ref[here, :].astype(jnp.float32)
            decoded = anchor + scale * delta.reshape(rows // 8, 8, HD)
            out_ref[pl.ds(pl.multiple_of(slot * rows, rows), rows), :] = decoded.reshape(rows, HD).astype(
                jnp.bfloat16
            )
            return carry

        lax.fori_loop(0, count, one_slot, 0, unroll=min(16, count))


def pieces(values):
    high = values.astype(jnp.bfloat16)
    rest = values - high.astype(jnp.float32)
    middle = rest.astype(jnp.bfloat16)
    low = (rest - middle.astype(jnp.float32)).astype(jnp.bfloat16)
    return [high, middle, low]


def packed(partial):
    summed, top, total = partial
    stats = pieces(top) + pieces(total)
    rest = jnp.zeros((STAT_ROWS - len(stats), top.shape[1]), jnp.bfloat16)
    return jnp.concatenate([summed.astype(jnp.bfloat16)] + stats + [rest], axis=0)


def unpacked(block):
    stats = block[HD:, :].astype(jnp.float32)
    top = stats[0:1] + stats[1:2] + stats[2:3]
    total = stats[3:4] + stats[4:5] + stats[5:6]
    return block[0:HD, :].astype(jnp.float32), top, total


def held(partial):
    summed, top, total = partial
    rest = jnp.zeros((KEEP_ROWS - 2, top.shape[1]), jnp.float32)
    return jnp.concatenate([summed, top, total, rest], axis=0)


def taken(block):
    return block[0:HD, :], block[HD : HD + 1, :], block[HD + 1 : HD + 2, :]


def joined(one, other):
    top = jnp.maximum(one[1], other[1])
    scale_one = jnp.exp2((one[1] - top) * RATE)
    scale_other = jnp.exp2((other[1] - top) * RATE)
    return (
        one[0] * scale_one + other[0] * scale_other,
        top,
        one[2] * scale_one + other[2] * scale_other,
    )


def attend(parity, width, keys_ref, turned_ref, asked_ref, store):
    me = lax.axis_index("seq")
    asked = asked_ref.shape[0]

    def partial_of(here):
        scores = lax.dot_general(
            keys_ref[...], here, (((1,), (1,)), ((), ())), preferred_element_type=jnp.float32
        )
        top = jnp.max(scores, axis=0, keepdims=True)
        weights = jnp.exp2((scores - top) * RATE)
        total = jnp.sum(weights, axis=0, keepdims=True)
        summed = jnp.dot(turned_ref[...], weights.astype(jnp.bfloat16), preferred_element_type=jnp.float32)
        return summed, top, total

    if width % HD == 0:
        for index in range(asked // width // 2):
            there = (me ^ (2 * index + parity)) * width
            store(index, partial_of(asked_ref[pl.ds(pl.multiple_of(there, width), width), :]))
        return
    tile = min(2 * HD, asked)
    parts = tile // width

    def one_tile(tile_index, carry):
        here = asked_ref[pl.ds(pl.multiple_of(tile_index * tile, tile), tile), :]
        summed, top, total = partial_of(here)
        for part in range(parts):
            lanes = slice(part * width, (part + 1) * width)
            apart = (tile_index * parts + part) ^ me

            @pl.when(apart % 2 == parity)
            def _(lanes=lanes, apart=apart):
                store(apart // 2, (summed[:, lanes], top[:, lanes], total[:, lanes]))

        return carry

    lax.fori_loop(0, asked // tile, one_tile, 0)


def first_kernel(*refs):
    me = lax.axis_index("seq")
    sources, send_ref, keys_ref, turned_ref, asked_ref, own_ref, *targets = refs[:7], *refs[7:-3]
    wide_ref, values_ref, sems = refs[-3:]
    loads = [
        pltpu.make_async_copy(source, target, sems.at[index])
        for index, (source, target) in enumerate(zip(sources, targets))
    ]
    for load in loads:
        load.start()
    deltas_ref, anchors_ref, scales_ref, lengths_ref, request_ref, queries_ref, new_ref = targets
    blocks = anchors_ref.shape[0] // 2
    rows = deltas_ref.shape[0] // blocks
    tokens = rows // 2
    requests = lengths_ref.shape[0]
    asked = queries_ref.shape[0]
    per_row = asked // request_ref.shape[0]
    width = send_ref.shape[2]
    for load in loads[2:]:
        load.wait()

    lane = lax.broadcasted_iota(jnp.int32, (1, HD), 1)
    first = jnp.zeros((1, HD), jnp.int32)
    last = jnp.zeros((1, HD), jnp.int32)
    end = 0 - me * (blocks * tokens)
    for request in range(requests):
        start = end
        end = end + lengths_ref[request]
        first = jnp.where(lane == request, start, first)
        last = jnp.where(lane == request, end, last)
    place = lax.broadcasted_iota(jnp.int32, (blocks * tokens, HD), 0)
    keys_ref[:, HD:] = jnp.where((place >= first) & (place < last), 1.0, 0.0).astype(jnp.bfloat16)

    asked_ref[:, 0:HD] = queries_ref[...]
    wide_lane = lax.broadcasted_iota(jnp.int32, (per_row, HD), 1)

    def one_row(row, carry):
        asked_ref[pl.ds(pl.multiple_of(row * per_row, per_row), per_row), HD:] = jnp.where(
            (wide_lane == request_ref[row]) | (wide_lane >= requests), 0.0, FAR
        ).astype(jnp.bfloat16)
        return carry

    lax.fori_loop(0, request_ref.shape[0], one_row, 0, unroll=16)

    fresh = new_ref.shape[0] // 4
    new = new_ref[...].astype(jnp.float32).reshape(fresh, 4, HD)
    mine = queries_ref[pl.ds(pl.multiple_of(me * width, width), width), :]
    of_row = lax.broadcasted_iota(jnp.int32, (fresh, width), 1) // (GQ * STEPS)
    same = of_row == lax.broadcasted_iota(jnp.int32, (fresh, width), 0)
    step = lax.broadcasted_iota(jnp.int32, (1, width), 1) % STEPS
    own_scores = []
    for which in range(STEPS):
        scored = lax.dot_general(
            new[:, 2 * which, :].astype(jnp.bfloat16),
            mine,
            (((1,), (1,)), ((), ())),
            preferred_element_type=jnp.float32,
        )
        picked = jnp.sum(jnp.where(same, scored, 0.0), axis=0, keepdims=True)
        own_scores.append(jnp.where(step >= which, picked, FAR))
    own_top = jnp.maximum(own_scores[0], own_scores[1])
    own_total = jnp.zeros((1, width), jnp.float32)
    own_summed = jnp.zeros((HD, width), jnp.float32)
    for which in range(STEPS):
        weight = jnp.exp2((own_scores[which] - own_top) * RATE)
        own_total = own_total + weight
        spread = jnp.where(same, weight, 0.0).astype(jnp.bfloat16)
        own_summed = own_summed + lax.dot_general(
            new[:, 2 * which + 1, :].astype(jnp.bfloat16),
            spread,
            (((0,), (0,)), ((), ())),
            preferred_element_type=jnp.float32,
        )
    own_ref[...] = held((own_summed, own_top, own_total))

    for load in loads[:2]:
        load.wait()
    wide_ref[...] = deltas_ref[...].astype(jnp.float32)
    scale_key = scales_ref[0:1, :]
    scale_value = scales_ref[1:2, :]

    def one_block(block, carry):
        here = pl.ds(pl.multiple_of(block * tokens, tokens), tokens)
        key = wide_ref[pl.ds(block * rows, tokens, stride=2), :]
        value = wide_ref[pl.ds(block * rows + 1, tokens, stride=2), :]
        keys_ref[here, 0:HD] = (anchors_ref[pl.ds(2 * block, 1), :] + scale_key * key).astype(jnp.bfloat16)
        values_ref[here, :] = (anchors_ref[pl.ds(2 * block + 1, 1), :] + scale_value * value).astype(
            jnp.bfloat16
        )
        return carry

    lax.fori_loop(0, blocks, one_block, 0, unroll=16)
    turned_ref[...] = values_ref[...].T

    def store(index, partial):
        send_ref[index] = packed(partial)

    attend(1, width, keys_ref, turned_ref, asked_ref, store)


def second_kernel(keys_ref, turned_ref, asked_ref, own_ref, keep_ref):
    def store(index, partial):
        keep_ref[index] = held(partial)

    attend(0, keep_ref.shape[2], keys_ref, turned_ref, asked_ref, store)
    keep_ref[0] = held(joined(taken(keep_ref[0]), taken(own_ref[...])))


def join_kernel(keep_ref, got_ref, send_ref, next_ref):
    for index in range(keep_ref.shape[0]):
        partial = joined(taken(keep_ref[index]), unpacked(got_ref[index]))
        if index % 2 == 1:
            send_ref[index // 2] = packed(partial)
        else:
            next_ref[index // 2] = held(partial)


def settle(plan, handed, pages, sems):
    receivers = lax.axis_size("seq")
    me = lax.axis_index("seq")
    rows = pages.shape[0] // receivers
    copies = []
    for index, (k, start, slots) in enumerate(plan):
        size = handed[index].shape[0]
        sender = source(me, k, receivers) if k else me
        first = pl.multiple_of(sender * rows + start * (size // slots), size)
        copies.append(pltpu.make_async_copy(handed[index], pages.at[pl.ds(first, size), :], sems.at[index]))
        copies[-1].start()
    return copies


def settle_kernel(plan, *refs):
    *handed, pages, sems = refs
    for copy in settle(plan, handed, pages, sems):
        copy.wait()


def finish_kernel(plan, keep_ref, got_ref, _, *refs):
    *handed, out_any, pages, out_ref, sems = refs
    copies = settle(plan, handed, pages, sems)
    summed, _, total = joined(taken(keep_ref[0]), unpacked(got_ref[0]))
    out_ref[...] = (summed / total).T.astype(jnp.bfloat16)
    copies.append(pltpu.make_async_copy(out_ref, out_any, sems.at[len(copies)]))
    copies[-1].start()
    for copy in copies:
        copy.wait()


def in_hbm(arrays):
    return [pltpu.with_memory_space_constraint(array, pltpu.HBM) for array in arrays]


def per_device(lengths, owner_map, row_request, deltas, anchors, scales, queries, new_kv):
    blocks = anchors.shape[0]
    tokens = deltas.shape[0]
    senders = lax.axis_size("seq")
    me = lax.axis_index("seq")
    rows, steps, _ = queries.shape
    rows_dev = new_kv.shape[0]
    width = rows_dev * GQ * steps
    small = pltpu.CompilerParams(vmem_limit_bytes=8 * 1024 * 1024)

    flat_deltas = deltas.reshape(tokens * 2, HD)
    flat_anchors = anchors.reshape(blocks * 2, HD)
    flat_queries = queries.reshape(rows, steps, GQ, HD).transpose(0, 2, 1, 3).reshape(-1, HD)
    flat_new = new_kv.reshape(rows_dev * 4, HD)

    whole = jax.ShapeDtypeStruct((tokens * 2, HD), jnp.bfloat16)
    ahead, behind, own = messages(senders, blocks // senders)
    block_rows = tokens * 2 // blocks

    def place(plan, deltas):
        return pl.pallas_call(
            functools.partial(place_kernel, plan),
            out_shape=[jax.ShapeDtypeStruct((slots * block_rows, HD), jnp.bfloat16) for _, _, slots in plan],
            in_specs=[HBM] * 4,
            out_specs=[VMEM] * len(plan),
            scratch_shapes=[
                pltpu.SMEM((blocks,), jnp.int32),
                pltpu.SMEM((blocks,), jnp.int32),
                pltpu.SMEM((senders,), jnp.int32),
                pltpu.VMEM((tokens * 2, HD), jnp.bfloat16),
                pltpu.VMEM((blocks * 2, HD), jnp.float32),
                pltpu.VMEM((2, HD), jnp.float32),
                pltpu.SemaphoreType.DMA((7,)),
            ],
            compiler_params=small,
            name="place",
        )(*in_hbm([owner_map, deltas, flat_anchors, scales]))

    sent = place(ahead, flat_deltas)
    sent, late_deltas = lax.optimization_barrier((sent, flat_deltas))
    got_ahead = [hand(message, k) for message, (k, _, _) in zip(sent, ahead)]

    def leaving(count):
        return jax.ShapeDtypeStruct((count // 2, HD + STAT_ROWS, width), jnp.bfloat16)

    def staying(count):
        return jax.ShapeDtypeStruct((count // 2, HD + KEEP_ROWS, width), jnp.float32)

    needed = (late_deltas, flat_anchors, scales, lengths, row_request, flat_queries, flat_new)
    roomy = pltpu.CompilerParams(vmem_limit_bytes=32 * 1024 * 1024)
    send, *common = pl.pallas_call(
        first_kernel,
        out_shape=[
            leaving(senders),
            jax.ShapeDtypeStruct((tokens, 2 * HD), jnp.bfloat16),
            jax.ShapeDtypeStruct((HD, tokens), jnp.bfloat16),
            jax.ShapeDtypeStruct((rows * GQ * steps, 2 * HD), jnp.bfloat16),
            jax.ShapeDtypeStruct((HD + KEEP_ROWS, width), jnp.float32),
        ],
        in_specs=[HBM] * len(needed),
        out_specs=[VMEM] * 5,
        scratch_shapes=[
            (pltpu.SMEM if array.dtype == jnp.int32 else pltpu.VMEM)(array.shape, array.dtype)
            for array in needed
        ]
        + [
            pltpu.VMEM((tokens * 2, HD), jnp.float32),
            pltpu.VMEM((tokens, HD), jnp.bfloat16),
            pltpu.SemaphoreType.DMA((len(needed),)),
        ],
        compiler_params=roomy,
        name="attend_leaving",
    )(*in_hbm(needed))

    k, count = 1, senders // 2
    send, late_deltas = lax.optimization_barrier((send, late_deltas))
    passed = exchange(send, k)
    *sent, mine = place(behind + own, late_deltas)
    got = got_ahead[1:] + [hand(message, k) for message, (k, _, _) in zip(sent, behind)]
    keep = pl.pallas_call(
        second_kernel,
        out_shape=staying(senders),
        in_specs=[VMEM] * 4,
        out_specs=VMEM,
        compiler_params=roomy,
        name="attend_staying",
    )(*common)
    while count > 1:
        send, keep = pl.pallas_call(
            join_kernel,
            out_shape=[leaving(count), staying(count)],
            in_specs=[VMEM] * 2,
            out_specs=[VMEM] * 2,
            compiler_params=small,
            name="join",
        )(keep, passed)
        k, count = 2 * k, count // 2
        passed = exchange(send, k)
    settled = ahead[:1] + own
    pages = pl.pallas_call(
        functools.partial(settle_kernel, settled),
        out_shape=whole,
        in_specs=[ANY] * len(settled),
        out_specs=HBM,
        scratch_shapes=[pltpu.SemaphoreType.DMA((len(settled),))],
        compiler_params=small,
        name="settle",
    )(got_ahead[0], mine)
    attended, pages = pl.pallas_call(
        functools.partial(finish_kernel, ahead[1:] + behind),
        out_shape=[jax.ShapeDtypeStruct((width, HD), jnp.bfloat16), whole],
        in_specs=[VMEM] * 2 + [HBM] + [ANY] * len(got),
        out_specs=[HBM, HBM],
        scratch_shapes=[
            pltpu.VMEM((width, HD), jnp.bfloat16),
            pltpu.SemaphoreType.DMA((len(got) + 1,)),
        ],
        input_output_aliases={2: 1},
        compiler_params=small,
        name="finish",
    )(keep, passed, pages, *got)
    pages = pages.reshape(blocks, tokens // blocks, 2, HD)
    attended = (
        attended.reshape(rows_dev, GQ, steps, HD).transpose(0, 2, 1, 3).reshape(rows_dev, steps, GQ * HD)
    )
    return pages, attended


def solution(mesh):
    placed = (
        P("groups"),
        P(("groups", "seq")),
        P("groups"),
        P(("groups", "seq"), None, "tp"),
        P(("groups", "seq"), None, "tp"),
        P("groups", "tp"),
        P("groups", None, "tp"),
        P(("groups", "seq"), None, None, "tp"),
    )
    return jax.shard_map(
        per_device,
        mesh=mesh,
        in_specs=placed,
        out_specs=(P(("groups", "seq"), None, None, "tp"), P(("groups", "seq"), None, "tp")),
        check_vma=False,
    )
```

```python
import functools

import jax
import jax.numpy as jnp
from jax import lax
from jax.experimental import pallas as pl
from jax.experimental.pallas import tpu as pltpu
from jax.sharding import PartitionSpec as P

HD = 128
GQ = 8
STEPS = 2
STAT_ROWS = 8
KEEP_ROWS = 8
FAR = -1e30
RATE = HD ** (-0.5) * 1.4426950408889634

VMEM = pl.BlockSpec(memory_space=pltpu.VMEM)
HBM = pl.BlockSpec(memory_space=pltpu.HBM)
ANY = pl.BlockSpec(memory_space=pl.ANY)
SMEM = pl.BlockSpec(memory_space=pltpu.SMEM)


def inner(device, count):
    return (device ^ (device // (count // 2))) & 1


def partner(device, k, count):
    far = count // 2
    if k == far:
        return device ^ (1 + inner(device, count) * (far - 1))
    if k == 1:
        return device ^ (far - inner(device, count) * (far - 1))
    return device ^ k


def source(device, k, count):
    far = count // 2
    if k == far:
        return device ^ (far - inner(device, count) * (far - 1))
    if k == 1:
        return device ^ (1 + inner(device, count) * (far - 1))
    return device ^ k


def exchange(message, k):
    count = lax.axis_size("seq")
    return lax.ppermute(message, "seq", [(i, i ^ k) for i in range(count)])


def hand(message, k):
    count = lax.axis_size("seq")
    return lax.ppermute(message, "seq", [(i, partner(i, k, count)) for i in range(count)])


def messages(count, capacity):
    ahead = [(k, 0, capacity) for k in range(count // 2, count)]
    first = capacity // 2
    second = (capacity - first) // 2
    ends = [0, first, first + second, capacity]
    near = [
        [(k, start, end - start) for k in reversed(range(1, count // 2)) if end > start]
        for start, end in zip(ends, ends[1:])
    ]
    return ahead, *near, [(0, 0, capacity)]


def place_kernel(plan, owner_any, deltas_any, anchors_any, scales_any, *refs):
    receivers = lax.axis_size("seq")
    me = lax.axis_index("seq")
    outs = refs[:-7]
    owner_ref, source_ref, count_ref, deltas_ref, anchors_ref, scales_ref, sems = refs[-7:]
    blocks = owner_ref.shape[0]
    rows = deltas_ref.shape[0] // blocks
    capacity = blocks // receivers
    loads = [
        pltpu.make_async_copy(source, target, sems.at[index])
        for index, (source, target) in enumerate(
            [
                (owner_any, owner_ref),
                (scales_any, scales_ref),
                (anchors_any, anchors_ref),
                (deltas_any, deltas_ref),
            ]
        )
    ]
    for load in loads:
        load.start()
    bits = capacity.bit_length()
    narrow = receivers * bits < 32
    if not narrow:
        for owner in range(receivers):
            count_ref[owner] = owner * capacity
    loads[0].wait()

    def find(block, counts):
        owner = owner_ref[block]
        if narrow:
            shift = owner * bits
            slot = owner * capacity + ((counts >> shift) & ((1 << bits) - 1))
            counts = counts + (jnp.int32(1) << shift)
        else:
            slot = count_ref[owner]
            count_ref[owner] = slot + 1
        source_ref[slot] = block
        return counts

    lax.fori_loop(0, blocks, find, jnp.int32(0), unroll=16)
    for load in loads[1:]:
        load.wait()
    odd = lax.broadcasted_iota(jnp.int32, (8, HD), 0) % 2 == 1
    scale = jnp.where(odd, scales_ref[1:2, :], scales_ref[0:1, :])[None]
    for (k, start, count), out_ref in zip(plan, outs):
        first = partner(me, k, receivers) * capacity + start

        def one_slot(slot, carry, first=first, out_ref=out_ref):
            block = source_ref[first + slot]
            anchor = jnp.where(
                odd, anchors_ref[pl.ds(2 * block + 1, 1), :], anchors_ref[pl.ds(2 * block, 1), :]
            )[None]
            here = pl.ds(pl.multiple_of(block * rows, rows), rows)
            delta = deltas_ref[here, :].astype(jnp.float32)
            decoded = anchor + scale * delta.reshape(rows // 8, 8, HD)
            out_ref[pl.ds(pl.multiple_of(slot * rows, rows), rows), :] = decoded.reshape(rows, HD).astype(
                jnp.bfloat16
            )
            return carry

        lax.fori_loop(0, count, one_slot, 0, unroll=min(8, count))


def pieces(values):
    high = values.astype(jnp.bfloat16)
    rest = values - high.astype(jnp.float32)
    middle = rest.astype(jnp.bfloat16)
    low = (rest - middle.astype(jnp.float32)).astype(jnp.bfloat16)
    return [high, middle, low]


def packed(partial):
    summed, top, total = partial
    stats = pieces(top) + pieces(total)
    rest = jnp.zeros((STAT_ROWS - len(stats), top.shape[1]), jnp.bfloat16)
    return jnp.concatenate([summed.astype(jnp.bfloat16)] + stats + [rest], axis=0)


def unpacked(block):
    stats = block[HD:, :].astype(jnp.float32)
    top = stats[0:1] + stats[1:2] + stats[2:3]
    total = stats[3:4] + stats[4:5] + stats[5:6]
    return block[0:HD, :].astype(jnp.float32), top, total


def held(partial):
    summed, top, total = partial
    rest = jnp.zeros((KEEP_ROWS - 2, top.shape[1]), jnp.float32)
    return jnp.concatenate([summed, top, total, rest], axis=0)


def taken(block):
    return block[0:HD, :], block[HD : HD + 1, :], block[HD + 1 : HD + 2, :]


def joined(one, other):
    top = jnp.maximum(one[1], other[1])
    scale_one = jnp.exp2((one[1] - top) * RATE)
    scale_other = jnp.exp2((other[1] - top) * RATE)
    return (
        one[0] * scale_one + other[0] * scale_other,
        top,
        one[2] * scale_one + other[2] * scale_other,
    )


def attend(parity, width, keys_ref, turned_ref, asked_ref, store):
    me = lax.axis_index("seq")
    asked = asked_ref.shape[0]

    def partial_of(here):
        scores = lax.dot_general(
            keys_ref[...], here, (((1,), (1,)), ((), ())), preferred_element_type=jnp.float32
        )
        top = jnp.max(scores, axis=0, keepdims=True)
        weights = jnp.exp2((scores - top) * RATE)
        total = jnp.sum(weights, axis=0, keepdims=True)
        summed = jnp.dot(turned_ref[...], weights.astype(jnp.bfloat16), preferred_element_type=jnp.float32)
        return summed, top, total

    if width % HD == 0:
        for index in range(asked // width // 2):
            there = (me ^ (2 * index + parity)) * width
            store(index, partial_of(asked_ref[pl.ds(pl.multiple_of(there, width), width), :]))
        return
    tile = min(2 * HD, asked)
    parts = tile // width

    def one_tile(tile_index, carry):
        here = asked_ref[pl.ds(pl.multiple_of(tile_index * tile, tile), tile), :]
        summed, top, total = partial_of(here)
        for part in range(parts):
            lanes = slice(part * width, (part + 1) * width)
            apart = (tile_index * parts + part) ^ me

            @pl.when(apart % 2 == parity)
            def _(lanes=lanes, apart=apart):
                store(apart // 2, (summed[:, lanes], top[:, lanes], total[:, lanes]))

        return carry

    lax.fori_loop(0, asked // tile, one_tile, 0)


def first_kernel(*refs):
    me = lax.axis_index("seq")
    sources, send_ref, keys_ref, turned_ref, asked_ref, own_ref, *targets = refs[:7], *refs[7:-3]
    wide_ref, values_ref, sems = refs[-3:]
    loads = [
        pltpu.make_async_copy(source, target, sems.at[index])
        for index, (source, target) in enumerate(zip(sources, targets))
    ]
    for load in loads:
        load.start()
    deltas_ref, anchors_ref, scales_ref, lengths_ref, request_ref, queries_ref, new_ref = targets
    blocks = anchors_ref.shape[0] // 2
    rows = deltas_ref.shape[0] // blocks
    tokens = rows // 2
    requests = lengths_ref.shape[0]
    asked = queries_ref.shape[0]
    per_row = asked // request_ref.shape[0]
    width = send_ref.shape[2]
    for load in loads[2:]:
        load.wait()

    lane = lax.broadcasted_iota(jnp.int32, (1, HD), 1)
    first = jnp.zeros((1, HD), jnp.int32)
    last = jnp.zeros((1, HD), jnp.int32)
    end = 0 - me * (blocks * tokens)
    for request in range(requests):
        start = end
        end = end + lengths_ref[request]
        first = jnp.where(lane == request, start, first)
        last = jnp.where(lane == request, end, last)
    place = lax.broadcasted_iota(jnp.int32, (blocks * tokens, HD), 0)
    keys_ref[:, HD:] = jnp.where((place >= first) & (place < last), 1.0, 0.0).astype(jnp.bfloat16)

    asked_ref[:, 0:HD] = queries_ref[...]
    wide_lane = lax.broadcasted_iota(jnp.int32, (per_row, HD), 1)

    def one_row(row, carry):
        asked_ref[pl.ds(pl.multiple_of(row * per_row, per_row), per_row), HD:] = jnp.where(
            (wide_lane == request_ref[row]) | (wide_lane >= requests), 0.0, FAR
        ).astype(jnp.bfloat16)
        return carry

    lax.fori_loop(0, request_ref.shape[0], one_row, 0, unroll=16)

    fresh = new_ref.shape[0] // 4
    new = new_ref[...].astype(jnp.float32).reshape(fresh, 4, HD)
    mine = queries_ref[pl.ds(pl.multiple_of(me * width, width), width), :]
    of_row = lax.broadcasted_iota(jnp.int32, (fresh, width), 1) // (GQ * STEPS)
    same = of_row == lax.broadcasted_iota(jnp.int32, (fresh, width), 0)
    step = lax.broadcasted_iota(jnp.int32, (1, width), 1) % STEPS
    own_scores = []
    for which in range(STEPS):
        scored = lax.dot_general(
            new[:, 2 * which, :].astype(jnp.bfloat16),
            mine,
            (((1,), (1,)), ((), ())),
            preferred_element_type=jnp.float32,
        )
        picked = jnp.sum(jnp.where(same, scored, 0.0), axis=0, keepdims=True)
        own_scores.append(jnp.where(step >= which, picked, FAR))
    own_top = jnp.maximum(own_scores[0], own_scores[1])
    own_total = jnp.zeros((1, width), jnp.float32)
    own_summed = jnp.zeros((HD, width), jnp.float32)
    for which in range(STEPS):
        weight = jnp.exp2((own_scores[which] - own_top) * RATE)
        own_total = own_total + weight
        spread = jnp.where(same, weight, 0.0).astype(jnp.bfloat16)
        own_summed = own_summed + lax.dot_general(
            new[:, 2 * which + 1, :].astype(jnp.bfloat16),
            spread,
            (((0,), (0,)), ((), ())),
            preferred_element_type=jnp.float32,
        )
    own_ref[...] = held((own_summed, own_top, own_total))

    for load in loads[:2]:
        load.wait()
    wide_ref[...] = deltas_ref[...].astype(jnp.float32)
    scale_key = scales_ref[0:1, :]
    scale_value = scales_ref[1:2, :]

    def one_block(block, carry):
        here = pl.ds(pl.multiple_of(block * tokens, tokens), tokens)
        key = wide_ref[pl.ds(block * rows, tokens, stride=2), :]
        value = wide_ref[pl.ds(block * rows + 1, tokens, stride=2), :]
        keys_ref[here, 0:HD] = (anchors_ref[pl.ds(2 * block, 1), :] + scale_key * key).astype(jnp.bfloat16)
        values_ref[here, :] = (anchors_ref[pl.ds(2 * block + 1, 1), :] + scale_value * value).astype(
            jnp.bfloat16
        )
        return carry

    lax.fori_loop(0, blocks, one_block, 0, unroll=16)
    turned_ref[...] = values_ref[...].T

    def store(index, partial):
        send_ref[index] = packed(partial)

    attend(1, width, keys_ref, turned_ref, asked_ref, store)


def second_kernel(keys_ref, turned_ref, asked_ref, own_ref, keep_ref):
    def store(index, partial):
        keep_ref[index] = held(partial)

    attend(0, keep_ref.shape[2], keys_ref, turned_ref, asked_ref, store)
    keep_ref[0] = held(joined(taken(keep_ref[0]), taken(own_ref[...])))


def join_kernel(keep_ref, got_ref, send_ref, next_ref):
    for index in range(keep_ref.shape[0]):
        partial = joined(taken(keep_ref[index]), unpacked(got_ref[index]))
        if index % 2 == 1:
            send_ref[index // 2] = packed(partial)
        else:
            next_ref[index // 2] = held(partial)


def settle(plan, handed, pages, sems):
    receivers = lax.axis_size("seq")
    me = lax.axis_index("seq")
    rows = pages.shape[0] // receivers
    copies = []
    for index, (k, start, slots) in enumerate(plan):
        size = handed[index].shape[0]
        sender = source(me, k, receivers) if k else me
        first = pl.multiple_of(sender * rows + start * (size // slots), size)
        copies.append(pltpu.make_async_copy(handed[index], pages.at[pl.ds(first, size), :], sems.at[index]))
        copies[-1].start()
    return copies


def settle_kernel(plan, *refs):
    *handed, pages, sems = refs
    for copy in settle(plan, handed, pages, sems):
        copy.wait()


def finish_kernel(plan, keep_ref, got_ref, _, *refs):
    *handed, out_any, pages, out_ref, sems = refs
    copies = settle(plan, handed, pages, sems)
    summed, _, total = joined(taken(keep_ref[0]), unpacked(got_ref[0]))
    out_ref[...] = (summed / total).T.astype(jnp.bfloat16)
    copies.append(pltpu.make_async_copy(out_ref, out_any, sems.at[len(copies)]))
    copies[-1].start()
    for copy in copies:
        copy.wait()


def in_hbm(arrays):
    return [pltpu.with_memory_space_constraint(array, pltpu.HBM) for array in arrays]


def per_device(lengths, owner_map, row_request, deltas, anchors, scales, queries, new_kv):
    blocks = anchors.shape[0]
    tokens = deltas.shape[0]
    senders = lax.axis_size("seq")
    me = lax.axis_index("seq")
    rows, steps, _ = queries.shape
    rows_dev = new_kv.shape[0]
    width = rows_dev * GQ * steps
    small = pltpu.CompilerParams(vmem_limit_bytes=8 * 1024 * 1024)

    flat_deltas = deltas.reshape(tokens * 2, HD)
    flat_anchors = anchors.reshape(blocks * 2, HD)
    flat_queries = queries.reshape(rows, steps, GQ, HD).transpose(0, 2, 1, 3).reshape(-1, HD)
    flat_new = new_kv.reshape(rows_dev * 4, HD)

    whole = jax.ShapeDtypeStruct((tokens * 2, HD), jnp.bfloat16)
    ahead, first, second, third, own = messages(senders, blocks // senders)
    block_rows = tokens * 2 // blocks

    def place(plan, deltas):
        return pl.pallas_call(
            functools.partial(place_kernel, plan),
            out_shape=[jax.ShapeDtypeStruct((slots * block_rows, HD), jnp.bfloat16) for _, _, slots in plan],
            in_specs=[HBM] * 4,
            out_specs=[VMEM] * len(plan),
            scratch_shapes=[
                pltpu.SMEM((blocks,), jnp.int32),
                pltpu.SMEM((blocks,), jnp.int32),
                pltpu.SMEM((senders,), jnp.int32),
                pltpu.VMEM((tokens * 2, HD), jnp.bfloat16),
                pltpu.VMEM((blocks * 2, HD), jnp.float32),
                pltpu.VMEM((2, HD), jnp.float32),
                pltpu.SemaphoreType.DMA((4,)),
            ],
            compiler_params=small,
            name="place",
        )(*in_hbm([owner_map, deltas, flat_anchors, scales]))

    sent = place(ahead, flat_deltas)
    sent, late_deltas = lax.optimization_barrier((sent, flat_deltas))
    got_ahead = [hand(message, k) for message, (k, _, _) in zip(sent, ahead)]

    def leaving(count):
        return jax.ShapeDtypeStruct((count // 2, HD + STAT_ROWS, width), jnp.bfloat16)

    def staying(count):
        return jax.ShapeDtypeStruct((count // 2, HD + KEEP_ROWS, width), jnp.float32)

    needed = (late_deltas, flat_anchors, scales, lengths, row_request, flat_queries, flat_new)
    roomy = pltpu.CompilerParams(vmem_limit_bytes=32 * 1024 * 1024)
    send, *common = pl.pallas_call(
        first_kernel,
        out_shape=[
            leaving(senders),
            jax.ShapeDtypeStruct((tokens, 2 * HD), jnp.bfloat16),
            jax.ShapeDtypeStruct((HD, tokens), jnp.bfloat16),
            jax.ShapeDtypeStruct((rows * GQ * steps, 2 * HD), jnp.bfloat16),
            jax.ShapeDtypeStruct((HD + KEEP_ROWS, width), jnp.float32),
        ],
        in_specs=[HBM] * len(needed),
        out_specs=[VMEM] * 5,
        scratch_shapes=[
            (pltpu.SMEM if array.dtype == jnp.int32 else pltpu.VMEM)(array.shape, array.dtype)
            for array in needed
        ]
        + [
            pltpu.VMEM((tokens * 2, HD), jnp.float32),
            pltpu.VMEM((tokens, HD), jnp.bfloat16),
            pltpu.SemaphoreType.DMA((len(needed),)),
        ],
        compiler_params=roomy,
        name="attend_leaving",
    )(*in_hbm(needed))

    k, count = 1, senders // 2
    send, late_deltas = lax.optimization_barrier((send, late_deltas))
    passed = exchange(send, k)
    behind = first + second + third
    *sent, mine = place(behind + own, late_deltas)
    later = sent[len(first) : len(first) + len(second)]
    last = sent[len(first) + len(second) :]
    got = [hand(message, partner) for message, (partner, _, _) in zip(sent, first)]
    keep = pl.pallas_call(
        second_kernel,
        out_shape=staying(senders),
        in_specs=[VMEM] * 4,
        out_specs=VMEM,
        compiler_params=roomy,
        name="attend_staying",
    )(*common)
    while count > 1:
        send, keep = pl.pallas_call(
            join_kernel,
            out_shape=[leaving(count), staying(count)],
            in_specs=[VMEM] * 2,
            out_specs=[VMEM] * 2,
            compiler_params=small,
            name="join",
        )(keep, passed)
        if k == 1:
            later, send = lax.optimization_barrier((later, send))
            got += [hand(message, partner) for message, (partner, _, _) in zip(later, second)]
        k, count = 2 * k, count // 2
        passed = exchange(send, k)
    settled = ahead + first + own
    pages = pl.pallas_call(
        functools.partial(settle_kernel, settled),
        out_shape=whole,
        in_specs=[ANY] * len(settled),
        out_specs=HBM,
        scratch_shapes=[pltpu.SemaphoreType.DMA((len(settled),))],
        compiler_params=small,
        name="settle",
    )(*got_ahead, *got[: len(first)], mine)
    last, passed, pages = lax.optimization_barrier((last, passed, pages))
    got += [hand(message, partner) for message, (partner, _, _) in zip(last, third)]
    attended, pages = pl.pallas_call(
        functools.partial(finish_kernel, second + third),
        out_shape=[jax.ShapeDtypeStruct((width, HD), jnp.bfloat16), whole],
        in_specs=[VMEM] * 2 + [HBM] + [ANY] * len(second + third),
        out_specs=[HBM, HBM],
        scratch_shapes=[
            pltpu.VMEM((width, HD), jnp.bfloat16),
            pltpu.SemaphoreType.DMA((len(second + third) + 1,)),
        ],
        input_output_aliases={2: 1},
        compiler_params=small,
        name="finish",
    )(keep, passed, pages, *got[len(first) :])
    pages = pages.reshape(blocks, tokens // blocks, 2, HD)
    attended = (
        attended.reshape(rows_dev, GQ, steps, HD).transpose(0, 2, 1, 3).reshape(rows_dev, steps, GQ * HD)
    )
    return pages, attended


def solution(mesh):
    placed = (
        P("groups"),
        P(("groups", "seq")),
        P("groups"),
        P(("groups", "seq"), None, "tp"),
        P(("groups", "seq"), None, "tp"),
        P("groups", "tp"),
        P("groups", None, "tp"),
        P(("groups", "seq"), None, None, "tp"),
    )
    return jax.shard_map(
        per_device,
        mesh=mesh,
        in_specs=placed,
        out_specs=(P(("groups", "seq"), None, None, "tp"), P(("groups", "seq"), None, "tp")),
        check_vma=False,
    )
```

```python
import functools

import jax
import jax.numpy as jnp
from jax import lax
from jax.experimental import pallas as pl
from jax.experimental.pallas import tpu as pltpu
from jax.sharding import PartitionSpec as P

HD = 128
GQ = 8
STEPS = 2
STAT_ROWS = 8
KEEP_ROWS = 8
FAR = -1e30
RATE = HD ** (-0.5) * 1.4426950408889634

VMEM = pl.BlockSpec(memory_space=pltpu.VMEM)
HBM = pl.BlockSpec(memory_space=pltpu.HBM)
ANY = pl.BlockSpec(memory_space=pl.ANY)
SMEM = pl.BlockSpec(memory_space=pltpu.SMEM)


def inner(device, count):
    return (device ^ (device // (count // 2))) & 1


def partner(device, k, count):
    far = count // 2
    if k == far:
        return device ^ (1 + inner(device, count) * (far - 1))
    if k == 1:
        return device ^ (far - inner(device, count) * (far - 1))
    return device ^ k


def source(device, k, count):
    far = count // 2
    if k == far:
        return device ^ (far - inner(device, count) * (far - 1))
    if k == 1:
        return device ^ (1 + inner(device, count) * (far - 1))
    return device ^ k


def exchange(message, k):
    count = lax.axis_size("seq")
    return lax.ppermute(message, "seq", [(i, i ^ k) for i in range(count)])


def hand(message, k):
    count = lax.axis_size("seq")
    return lax.ppermute(message, "seq", [(i, partner(i, k, count)) for i in range(count)])


def messages(count, capacity):
    half = capacity // 2
    ahead = [(k, 0, capacity) for k in range(count // 2, count)]
    behind = [(k, first, half) for k in reversed(range(1, count // 2)) for first in (0, half)]
    return ahead, behind, [(0, 0, capacity)]


def place_kernel(plan, owner_any, deltas_any, anchors_any, scales_any, *refs):
    receivers = lax.axis_size("seq")
    me = lax.axis_index("seq")
    outs = refs[:-7]
    owner_ref, source_ref, count_ref, deltas_ref, anchors_ref, scales_ref, sems = refs[-7:]
    blocks = owner_ref.shape[0]
    rows = deltas_ref.shape[0] // blocks
    capacity = blocks // receivers
    quarter = deltas_ref.shape[0] // 4
    parts = [pl.ds(index * quarter, quarter) for index in range(4)]
    loads = [
        pltpu.make_async_copy(source, target, sems.at[index])
        for index, (source, target) in enumerate(
            [(owner_any, owner_ref), (scales_any, scales_ref), (anchors_any, anchors_ref)]
            + [(deltas_any.at[part], deltas_ref.at[part]) for part in parts]
        )
    ]
    for load in loads:
        load.start()
    bits = capacity.bit_length()
    narrow = receivers * bits < 32
    if not narrow:
        for owner in range(receivers):
            count_ref[owner] = owner * capacity
    loads[0].wait()

    def find(block, counts):
        owner = owner_ref[block]
        if narrow:
            shift = owner * bits
            slot = owner * capacity + ((counts >> shift) & ((1 << bits) - 1))
            counts = counts + (jnp.int32(1) << shift)
        else:
            slot = count_ref[owner]
            count_ref[owner] = slot + 1
        source_ref[slot] = block
        return counts

    lax.fori_loop(0, blocks, find, jnp.int32(0), unroll=16)
    for load in loads[1:]:
        load.wait()
    odd = lax.broadcasted_iota(jnp.int32, (8, HD), 0) % 2 == 1
    scale = jnp.where(odd, scales_ref[1:2, :], scales_ref[0:1, :])[None]
    for (k, start, count), out_ref in zip(plan, outs):
        first = partner(me, k, receivers) * capacity + start

        def one_slot(slot, carry, first=first, out_ref=out_ref):
            block = source_ref[first + slot]
            anchor = jnp.where(
                odd, anchors_ref[pl.ds(2 * block + 1, 1), :], anchors_ref[pl.ds(2 * block, 1), :]
            )[None]
            here = pl.ds(pl.multiple_of(block * rows, rows), rows)
            delta = deltas_ref[here, :].astype(jnp.float32)
            decoded = anchor + scale * delta.reshape(rows // 8, 8, HD)
            out_ref[pl.ds(pl.multiple_of(slot * rows, rows), rows), :] = decoded.reshape(rows, HD).astype(
                jnp.bfloat16
            )
            return carry

        lax.fori_loop(0, count, one_slot, 0, unroll=min(16, count))


def pieces(values):
    high = values.astype(jnp.bfloat16)
    rest = values - high.astype(jnp.float32)
    middle = rest.astype(jnp.bfloat16)
    low = (rest - middle.astype(jnp.float32)).astype(jnp.bfloat16)
    return [high, middle, low]


def packed(partial):
    summed, top, total = partial
    stats = pieces(top) + pieces(total)
    rest = jnp.zeros((STAT_ROWS - len(stats), top.shape[1]), jnp.bfloat16)
    return jnp.concatenate([summed.astype(jnp.bfloat16)] + stats + [rest], axis=0)


def unpacked(block):
    stats = block[HD:, :].astype(jnp.float32)
    top = stats[0:1] + stats[1:2] + stats[2:3]
    total = stats[3:4] + stats[4:5] + stats[5:6]
    return block[0:HD, :].astype(jnp.float32), top, total


def held(partial):
    summed, top, total = partial
    rest = jnp.zeros((KEEP_ROWS - 2, top.shape[1]), jnp.float32)
    return jnp.concatenate([summed, top, total, rest], axis=0)


def taken(block):
    return block[0:HD, :], block[HD : HD + 1, :], block[HD + 1 : HD + 2, :]


def joined(one, other):
    top = jnp.maximum(one[1], other[1])
    scale_one = jnp.exp2((one[1] - top) * RATE)
    scale_other = jnp.exp2((other[1] - top) * RATE)
    return (
        one[0] * scale_one + other[0] * scale_other,
        top,
        one[2] * scale_one + other[2] * scale_other,
    )


def difference(index):
    total = 0
    while index:
        total, index = total ^ index, index >> 1
    return total


def attend(parity, width, keys_ref, turned_ref, asked_ref, store):
    me = lax.axis_index("seq")
    asked = asked_ref.shape[0]

    def partial_of(here):
        scores = lax.dot_general(
            keys_ref[...], here, (((1,), (1,)), ((), ())), preferred_element_type=jnp.float32
        )
        top = jnp.max(scores, axis=0, keepdims=True)
        weights = jnp.exp2((scores - top) * RATE)
        total = jnp.sum(weights, axis=0, keepdims=True)
        summed = jnp.dot(turned_ref[...], weights.astype(jnp.bfloat16), preferred_element_type=jnp.float32)
        return summed, top, total

    if width % HD == 0:
        for index in range(asked // width // 2):
            there = (me ^ difference(2 * index + parity)) * width
            store(index, partial_of(asked_ref[pl.ds(pl.multiple_of(there, width), width), :]))
        return
    tile = min(2 * HD, asked)
    parts = tile // width

    def one_tile(tile_index, carry):
        here = asked_ref[pl.ds(pl.multiple_of(tile_index * tile, tile), tile), :]
        summed, top, total = partial_of(here)
        for part in range(parts):
            lanes = slice(part * width, (part + 1) * width)
            apart = (tile_index * parts + part) ^ me
            place = apart ^ (apart >> 1)

            @pl.when(place % 2 == parity)
            def _(lanes=lanes, place=place):
                store(place // 2, (summed[:, lanes], top[:, lanes], total[:, lanes]))

        return carry

    lax.fori_loop(0, asked // tile, one_tile, 0)


def first_kernel(*refs):
    me = lax.axis_index("seq")
    sources, send_ref, keys_ref, turned_ref, asked_ref, own_ref, *targets = refs[:7], *refs[7:-3]
    wide_ref, values_ref, sems = refs[-3:]
    loads = [
        pltpu.make_async_copy(source, target, sems.at[index])
        for index, (source, target) in enumerate(zip(sources, targets))
    ]
    for load in loads:
        load.start()
    deltas_ref, anchors_ref, scales_ref, lengths_ref, request_ref, queries_ref, new_ref = targets
    blocks = anchors_ref.shape[0] // 2
    rows = deltas_ref.shape[0] // blocks
    tokens = rows // 2
    requests = lengths_ref.shape[0]
    asked = queries_ref.shape[0]
    per_row = asked // request_ref.shape[0]
    width = send_ref.shape[2]
    for load in loads[2:]:
        load.wait()

    lane = lax.broadcasted_iota(jnp.int32, (1, HD), 1)
    first = jnp.zeros((1, HD), jnp.int32)
    last = jnp.zeros((1, HD), jnp.int32)
    end = 0 - me * (blocks * tokens)
    for request in range(requests):
        start = end
        end = end + lengths_ref[request]
        first = jnp.where(lane == request, start, first)
        last = jnp.where(lane == request, end, last)
    place = lax.broadcasted_iota(jnp.int32, (blocks * tokens, HD), 0)
    keys_ref[:, HD:] = jnp.where((place >= first) & (place < last), 1.0, 0.0).astype(jnp.bfloat16)

    asked_ref[:, 0:HD] = queries_ref[...]
    wide_lane = lax.broadcasted_iota(jnp.int32, (per_row, HD), 1)

    def one_row(row, carry):
        asked_ref[pl.ds(pl.multiple_of(row * per_row, per_row), per_row), HD:] = jnp.where(
            (wide_lane == request_ref[row]) | (wide_lane >= requests), 0.0, FAR
        ).astype(jnp.bfloat16)
        return carry

    lax.fori_loop(0, request_ref.shape[0], one_row, 0, unroll=16)

    fresh = new_ref.shape[0] // 4
    new = new_ref[...].astype(jnp.float32).reshape(fresh, 4, HD)
    mine = queries_ref[pl.ds(pl.multiple_of(me * width, width), width), :]
    of_row = lax.broadcasted_iota(jnp.int32, (fresh, width), 1) // (GQ * STEPS)
    same = of_row == lax.broadcasted_iota(jnp.int32, (fresh, width), 0)
    step = lax.broadcasted_iota(jnp.int32, (1, width), 1) % STEPS
    own_scores = []
    for which in range(STEPS):
        scored = lax.dot_general(
            new[:, 2 * which, :].astype(jnp.bfloat16),
            mine,
            (((1,), (1,)), ((), ())),
            preferred_element_type=jnp.float32,
        )
        picked = jnp.sum(jnp.where(same, scored, 0.0), axis=0, keepdims=True)
        own_scores.append(jnp.where(step >= which, picked, FAR))
    own_top = jnp.maximum(own_scores[0], own_scores[1])
    own_total = jnp.zeros((1, width), jnp.float32)
    own_summed = jnp.zeros((HD, width), jnp.float32)
    for which in range(STEPS):
        weight = jnp.exp2((own_scores[which] - own_top) * RATE)
        own_total = own_total + weight
        spread = jnp.where(same, weight, 0.0).astype(jnp.bfloat16)
        own_summed = own_summed + lax.dot_general(
            new[:, 2 * which + 1, :].astype(jnp.bfloat16),
            spread,
            (((0,), (0,)), ((), ())),
            preferred_element_type=jnp.float32,
        )
    own_ref[...] = held((own_summed, own_top, own_total))

    for load in loads[:2]:
        load.wait()
    wide_ref[...] = deltas_ref[...].astype(jnp.float32)
    scale_key = scales_ref[0:1, :]
    scale_value = scales_ref[1:2, :]

    def one_block(block, carry):
        here = pl.ds(pl.multiple_of(block * tokens, tokens), tokens)
        key = wide_ref[pl.ds(block * rows, tokens, stride=2), :]
        value = wide_ref[pl.ds(block * rows + 1, tokens, stride=2), :]
        keys_ref[here, 0:HD] = (anchors_ref[pl.ds(2 * block, 1), :] + scale_key * key).astype(jnp.bfloat16)
        values_ref[here, :] = (anchors_ref[pl.ds(2 * block + 1, 1), :] + scale_value * value).astype(
            jnp.bfloat16
        )
        return carry

    lax.fori_loop(0, blocks, one_block, 0, unroll=16)
    turned_ref[...] = values_ref[...].T

    def store(index, partial):
        send_ref[index] = packed(partial)

    attend(1, width, keys_ref, turned_ref, asked_ref, store)


def second_kernel(keys_ref, turned_ref, asked_ref, own_ref, keep_ref):
    def store(index, partial):
        keep_ref[index] = held(partial)

    attend(0, keep_ref.shape[2], keys_ref, turned_ref, asked_ref, store)
    keep_ref[0] = held(joined(taken(keep_ref[0]), taken(own_ref[...])))


def join_kernel(keep_ref, got_ref, send_ref, next_ref):
    for index in range(keep_ref.shape[0]):
        partial = joined(taken(keep_ref[index]), unpacked(got_ref[index]))
        if index % 2 == 1:
            send_ref[index // 2] = packed(partial)
        else:
            next_ref[index // 2] = held(partial)


def settle(plan, handed, pages, sems):
    receivers = lax.axis_size("seq")
    me = lax.axis_index("seq")
    rows = pages.shape[0] // receivers
    copies = []
    for index, (k, start, slots) in enumerate(plan):
        size = handed[index].shape[0]
        sender = source(me, k, receivers) if k else me
        first = pl.multiple_of(sender * rows + start * (size // slots), size)
        copies.append(pltpu.make_async_copy(handed[index], pages.at[pl.ds(first, size), :], sems.at[index]))
        copies[-1].start()
    return copies


def settle_kernel(plan, *refs):
    *handed, pages, sems = refs
    for copy in settle(plan, handed, pages, sems):
        copy.wait()


def finish_kernel(plan, keep_ref, got_ref, _, *refs):
    *handed, out_any, pages, out_ref, sems = refs
    copies = settle(plan, handed, pages, sems)
    summed, _, total = joined(taken(keep_ref[0]), unpacked(got_ref[0]))
    out_ref[...] = (summed / total).T.astype(jnp.bfloat16)
    copies.append(pltpu.make_async_copy(out_ref, out_any, sems.at[len(copies)]))
    copies[-1].start()
    for copy in copies:
        copy.wait()


def in_hbm(arrays):
    return [pltpu.with_memory_space_constraint(array, pltpu.HBM) for array in arrays]


def per_device(lengths, owner_map, row_request, deltas, anchors, scales, queries, new_kv):
    blocks = anchors.shape[0]
    tokens = deltas.shape[0]
    senders = lax.axis_size("seq")
    me = lax.axis_index("seq")
    rows, steps, _ = queries.shape
    rows_dev = new_kv.shape[0]
    width = rows_dev * GQ * steps
    small = pltpu.CompilerParams(vmem_limit_bytes=8 * 1024 * 1024)

    flat_deltas = deltas.reshape(tokens * 2, HD)
    flat_anchors = anchors.reshape(blocks * 2, HD)
    flat_queries = queries.reshape(rows, steps, GQ, HD).transpose(0, 2, 1, 3).reshape(-1, HD)
    flat_new = new_kv.reshape(rows_dev * 4, HD)

    whole = jax.ShapeDtypeStruct((tokens * 2, HD), jnp.bfloat16)
    ahead, behind, own = messages(senders, blocks // senders)
    block_rows = tokens * 2 // blocks

    def place(plan, deltas):
        return pl.pallas_call(
            functools.partial(place_kernel, plan),
            out_shape=[jax.ShapeDtypeStruct((slots * block_rows, HD), jnp.bfloat16) for _, _, slots in plan],
            in_specs=[HBM] * 4,
            out_specs=[VMEM] * len(plan),
            scratch_shapes=[
                pltpu.SMEM((blocks,), jnp.int32),
                pltpu.SMEM((blocks,), jnp.int32),
                pltpu.SMEM((senders,), jnp.int32),
                pltpu.VMEM((tokens * 2, HD), jnp.bfloat16),
                pltpu.VMEM((blocks * 2, HD), jnp.float32),
                pltpu.VMEM((2, HD), jnp.float32),
                pltpu.SemaphoreType.DMA((7,)),
            ],
            compiler_params=small,
            name="place",
        )(*in_hbm([owner_map, deltas, flat_anchors, scales]))

    sent = place(ahead, flat_deltas)
    sent, late_deltas = lax.optimization_barrier((sent, flat_deltas))
    got_ahead = [hand(message, k) for message, (k, _, _) in zip(sent, ahead)]

    def leaving(count):
        return jax.ShapeDtypeStruct((count // 2, HD + STAT_ROWS, width), jnp.bfloat16)

    def staying(count):
        return jax.ShapeDtypeStruct((count // 2, HD + KEEP_ROWS, width), jnp.float32)

    needed = (late_deltas, flat_anchors, scales, lengths, row_request, flat_queries, flat_new)
    roomy = pltpu.CompilerParams(vmem_limit_bytes=32 * 1024 * 1024)
    send, *common = pl.pallas_call(
        first_kernel,
        out_shape=[
            leaving(senders),
            jax.ShapeDtypeStruct((tokens, 2 * HD), jnp.bfloat16),
            jax.ShapeDtypeStruct((HD, tokens), jnp.bfloat16),
            jax.ShapeDtypeStruct((rows * GQ * steps, 2 * HD), jnp.bfloat16),
            jax.ShapeDtypeStruct((HD + KEEP_ROWS, width), jnp.float32),
        ],
        in_specs=[HBM] * len(needed),
        out_specs=[VMEM] * 5,
        scratch_shapes=[
            (pltpu.SMEM if array.dtype == jnp.int32 else pltpu.VMEM)(array.shape, array.dtype)
            for array in needed
        ]
        + [
            pltpu.VMEM((tokens * 2, HD), jnp.float32),
            pltpu.VMEM((tokens, HD), jnp.bfloat16),
            pltpu.SemaphoreType.DMA((len(needed),)),
        ],
        compiler_params=roomy,
        name="attend_leaving",
    )(*in_hbm(needed))

    k, count = 1, senders // 2
    send, late_deltas = lax.optimization_barrier((send, late_deltas))
    passed = exchange(send, k)
    *sent, mine = place(behind + own, late_deltas)
    got = got_ahead[1:] + [hand(message, k) for message, (k, _, _) in zip(sent, behind)]
    keep = pl.pallas_call(
        second_kernel,
        out_shape=staying(senders),
        in_specs=[VMEM] * 4,
        out_specs=VMEM,
        compiler_params=roomy,
        name="attend_staying",
    )(*common)
    while count > 1:
        send, keep = pl.pallas_call(
            join_kernel,
            out_shape=[leaving(count), staying(count)],
            in_specs=[VMEM] * 2,
            out_specs=[VMEM] * 2,
            compiler_params=small,
            name="join",
        )(keep, passed)
        k, count = 2 * k + 1, count // 2
        passed = exchange(send, k)
    settled = ahead[:1] + own
    pages = pl.pallas_call(
        functools.partial(settle_kernel, settled),
        out_shape=whole,
        in_specs=[ANY] * len(settled),
        out_specs=HBM,
        scratch_shapes=[pltpu.SemaphoreType.DMA((len(settled),))],
        compiler_params=small,
        name="settle",
    )(got_ahead[0], mine)
    attended, pages = pl.pallas_call(
        functools.partial(finish_kernel, ahead[1:] + behind),
        out_shape=[jax.ShapeDtypeStruct((width, HD), jnp.bfloat16), whole],
        in_specs=[VMEM] * 2 + [HBM] + [ANY] * len(got),
        out_specs=[HBM, HBM],
        scratch_shapes=[
            pltpu.VMEM((width, HD), jnp.bfloat16),
            pltpu.SemaphoreType.DMA((len(got) + 1,)),
        ],
        input_output_aliases={2: 1},
        compiler_params=small,
        name="finish",
    )(keep, passed, pages, *got)
    pages = pages.reshape(blocks, tokens // blocks, 2, HD)
    attended = (
        attended.reshape(rows_dev, GQ, steps, HD).transpose(0, 2, 1, 3).reshape(rows_dev, steps, GQ * HD)
    )
    return pages, attended


def solution(mesh):
    placed = (
        P("groups"),
        P(("groups", "seq")),
        P("groups"),
        P(("groups", "seq"), None, "tp"),
        P(("groups", "seq"), None, "tp"),
        P("groups", "tp"),
        P("groups", None, "tp"),
        P(("groups", "seq"), None, None, "tp"),
    )
    return jax.shard_map(
        per_device,
        mesh=mesh,
        in_specs=placed,
        out_specs=(P(("groups", "seq"), None, None, "tp"), P(("groups", "seq"), None, "tp")),
        check_vma=False,
    )
```

```python
import functools

import jax
import jax.numpy as jnp
from jax import lax
from jax.experimental import pallas as pl
from jax.experimental.pallas import tpu as pltpu
from jax.sharding import PartitionSpec as P

HD = 128
GQ = 8
STEPS = 2
STAT_ROWS = 8
KEEP_ROWS = 8
FAR = -1e30
RATE = HD ** (-0.5) * 1.4426950408889634

VMEM = pl.BlockSpec(memory_space=pltpu.VMEM)
HBM = pl.BlockSpec(memory_space=pltpu.HBM)
ANY = pl.BlockSpec(memory_space=pl.ANY)
SMEM = pl.BlockSpec(memory_space=pltpu.SMEM)


def partner(device, k, count):
    far = count // 2
    upper = device // far
    if k == far:
        return device ^ (far + upper)
    if k == far + 1:
        return device ^ (far + 1 - upper)
    return device ^ k


def source(device, k, count):
    far = count // 2
    upper = device // far
    if k == far:
        return device ^ (far + 1 - upper)
    if k == far + 1:
        return device ^ (far + upper)
    return device ^ k


def exchange(message, k):
    count = lax.axis_size("seq")
    return lax.ppermute(message, "seq", [(i, i ^ k) for i in range(count)])


def hand(message, k):
    count = lax.axis_size("seq")
    return lax.ppermute(message, "seq", [(i, partner(i, k, count)) for i in range(count)])


def messages(count, capacity):
    half = capacity // 2
    ahead = [(k, 0, capacity) for k in reversed(range(count // 2, count))]
    behind = [(k, first, half) for k in reversed(range(1, count // 2)) for first in (0, half)]
    return ahead, behind, [(0, 0, capacity)]


def place_kernel(plan, owner_any, deltas_any, anchors_any, scales_any, *refs):
    receivers = lax.axis_size("seq")
    me = lax.axis_index("seq")
    outs = refs[:-7]
    owner_ref, source_ref, count_ref, deltas_ref, anchors_ref, scales_ref, sems = refs[-7:]
    blocks = owner_ref.shape[0]
    rows = deltas_ref.shape[0] // blocks
    capacity = blocks // receivers
    quarter = deltas_ref.shape[0] // 4
    parts = [pl.ds(index * quarter, quarter) for index in range(4)]
    loads = [
        pltpu.make_async_copy(source, target, sems.at[index])
        for index, (source, target) in enumerate(
            [(owner_any, owner_ref), (scales_any, scales_ref), (anchors_any, anchors_ref)]
            + [(deltas_any.at[part], deltas_ref.at[part]) for part in parts]
        )
    ]
    for load in loads:
        load.start()
    bits = capacity.bit_length()
    narrow = receivers * bits < 32
    if not narrow:
        for owner in range(receivers):
            count_ref[owner] = owner * capacity
    loads[0].wait()

    def find(block, counts):
        owner = owner_ref[block]
        if narrow:
            shift = owner * bits
            slot = owner * capacity + ((counts >> shift) & ((1 << bits) - 1))
            counts = counts + (jnp.int32(1) << shift)
        else:
            slot = count_ref[owner]
            count_ref[owner] = slot + 1
        source_ref[slot] = block
        return counts

    lax.fori_loop(0, blocks, find, jnp.int32(0), unroll=16)
    for load in loads[1:]:
        load.wait()
    odd = lax.broadcasted_iota(jnp.int32, (8, HD), 0) % 2 == 1
    scale = jnp.where(odd, scales_ref[1:2, :], scales_ref[0:1, :])[None]
    for (k, start, count), out_ref in zip(plan, outs):
        first = partner(me, k, receivers) * capacity + start

        def one_slot(slot, carry, first=first, out_ref=out_ref):
            block = source_ref[first + slot]
            anchor = jnp.where(
                odd, anchors_ref[pl.ds(2 * block + 1, 1), :], anchors_ref[pl.ds(2 * block, 1), :]
            )[None]
            here = pl.ds(pl.multiple_of(block * rows, rows), rows)
            delta = deltas_ref[here, :].astype(jnp.float32)
            decoded = anchor + scale * delta.reshape(rows // 8, 8, HD)
            out_ref[pl.ds(pl.multiple_of(slot * rows, rows), rows), :] = decoded.reshape(rows, HD).astype(
                jnp.bfloat16
            )
            return carry

        lax.fori_loop(0, count, one_slot, 0, unroll=min(16, count))


def pieces(values):
    high = values.astype(jnp.bfloat16)
    rest = values - high.astype(jnp.float32)
    middle = rest.astype(jnp.bfloat16)
    low = (rest - middle.astype(jnp.float32)).astype(jnp.bfloat16)
    return [high, middle, low]


def packed(partial):
    summed, top, total = partial
    stats = pieces(top) + pieces(total)
    rest = jnp.zeros((STAT_ROWS - len(stats), top.shape[1]), jnp.bfloat16)
    return jnp.concatenate([summed.astype(jnp.bfloat16)] + stats + [rest], axis=0)


def unpacked(block):
    stats = block[HD:, :].astype(jnp.float32)
    top = stats[0:1] + stats[1:2] + stats[2:3]
    total = stats[3:4] + stats[4:5] + stats[5:6]
    return block[0:HD, :].astype(jnp.float32), top, total


def held(partial):
    summed, top, total = partial
    rest = jnp.zeros((KEEP_ROWS - 2, top.shape[1]), jnp.float32)
    return jnp.concatenate([summed, top, total, rest], axis=0)


def taken(block):
    return block[0:HD, :], block[HD : HD + 1, :], block[HD + 1 : HD + 2, :]


def joined(one, other):
    top = jnp.maximum(one[1], other[1])
    scale_one = jnp.exp2((one[1] - top) * RATE)
    scale_other = jnp.exp2((other[1] - top) * RATE)
    return (
        one[0] * scale_one + other[0] * scale_other,
        top,
        one[2] * scale_one + other[2] * scale_other,
    )


def difference(index):
    total = 0
    while index:
        total, index = total ^ index, index >> 1
    return total


def attend(parity, width, keys_ref, turned_ref, asked_ref, store):
    me = lax.axis_index("seq")
    asked = asked_ref.shape[0]

    def partial_of(here):
        scores = lax.dot_general(
            keys_ref[...], here, (((1,), (1,)), ((), ())), preferred_element_type=jnp.float32
        )
        top = jnp.max(scores, axis=0, keepdims=True)
        weights = jnp.exp2((scores - top) * RATE)
        total = jnp.sum(weights, axis=0, keepdims=True)
        summed = jnp.dot(turned_ref[...], weights.astype(jnp.bfloat16), preferred_element_type=jnp.float32)
        return summed, top, total

    if width % HD == 0:
        for index in range(asked // width // 2):
            there = (me ^ difference(2 * index + parity)) * width
            store(index, partial_of(asked_ref[pl.ds(pl.multiple_of(there, width), width), :]))
        return
    tile = min(2 * HD, asked)
    parts = tile // width

    def one_tile(tile_index, carry):
        here = asked_ref[pl.ds(pl.multiple_of(tile_index * tile, tile), tile), :]
        summed, top, total = partial_of(here)
        for part in range(parts):
            lanes = slice(part * width, (part + 1) * width)
            apart = (tile_index * parts + part) ^ me
            place = apart ^ (apart >> 1)

            @pl.when(place % 2 == parity)
            def _(lanes=lanes, place=place):
                store(place // 2, (summed[:, lanes], top[:, lanes], total[:, lanes]))

        return carry

    lax.fori_loop(0, asked // tile, one_tile, 0)


def first_kernel(*refs):
    me = lax.axis_index("seq")
    sources, send_ref, keys_ref, turned_ref, asked_ref, own_ref, *targets = refs[:7], *refs[7:-3]
    wide_ref, values_ref, sems = refs[-3:]
    loads = [
        pltpu.make_async_copy(source, target, sems.at[index])
        for index, (source, target) in enumerate(zip(sources, targets))
    ]
    for load in loads:
        load.start()
    deltas_ref, anchors_ref, scales_ref, lengths_ref, request_ref, queries_ref, new_ref = targets
    blocks = anchors_ref.shape[0] // 2
    rows = deltas_ref.shape[0] // blocks
    tokens = rows // 2
    requests = lengths_ref.shape[0]
    asked = queries_ref.shape[0]
    per_row = asked // request_ref.shape[0]
    width = send_ref.shape[2]
    for load in loads[2:]:
        load.wait()

    lane = lax.broadcasted_iota(jnp.int32, (1, HD), 1)
    first = jnp.zeros((1, HD), jnp.int32)
    last = jnp.zeros((1, HD), jnp.int32)
    end = 0 - me * (blocks * tokens)
    for request in range(requests):
        start = end
        end = end + lengths_ref[request]
        first = jnp.where(lane == request, start, first)
        last = jnp.where(lane == request, end, last)
    place = lax.broadcasted_iota(jnp.int32, (blocks * tokens, HD), 0)
    keys_ref[:, HD:] = jnp.where((place >= first) & (place < last), 1.0, 0.0).astype(jnp.bfloat16)

    asked_ref[:, 0:HD] = queries_ref[...]
    wide_lane = lax.broadcasted_iota(jnp.int32, (per_row, HD), 1)

    def one_row(row, carry):
        asked_ref[pl.ds(pl.multiple_of(row * per_row, per_row), per_row), HD:] = jnp.where(
            (wide_lane == request_ref[row]) | (wide_lane >= requests), 0.0, FAR
        ).astype(jnp.bfloat16)
        return carry

    lax.fori_loop(0, request_ref.shape[0], one_row, 0, unroll=16)

    fresh = new_ref.shape[0] // 4
    new = new_ref[...].astype(jnp.float32).reshape(fresh, 4, HD)
    mine = queries_ref[pl.ds(pl.multiple_of(me * width, width), width), :]
    of_row = lax.broadcasted_iota(jnp.int32, (fresh, width), 1) // (GQ * STEPS)
    same = of_row == lax.broadcasted_iota(jnp.int32, (fresh, width), 0)
    step = lax.broadcasted_iota(jnp.int32, (1, width), 1) % STEPS
    own_scores = []
    for which in range(STEPS):
        scored = lax.dot_general(
            new[:, 2 * which, :].astype(jnp.bfloat16),
            mine,
            (((1,), (1,)), ((), ())),
            preferred_element_type=jnp.float32,
        )
        picked = jnp.sum(jnp.where(same, scored, 0.0), axis=0, keepdims=True)
        own_scores.append(jnp.where(step >= which, picked, FAR))
    own_top = jnp.maximum(own_scores[0], own_scores[1])
    own_total = jnp.zeros((1, width), jnp.float32)
    own_summed = jnp.zeros((HD, width), jnp.float32)
    for which in range(STEPS):
        weight = jnp.exp2((own_scores[which] - own_top) * RATE)
        own_total = own_total + weight
        spread = jnp.where(same, weight, 0.0).astype(jnp.bfloat16)
        own_summed = own_summed + lax.dot_general(
            new[:, 2 * which + 1, :].astype(jnp.bfloat16),
            spread,
            (((0,), (0,)), ((), ())),
            preferred_element_type=jnp.float32,
        )
    own_ref[...] = held((own_summed, own_top, own_total))

    for load in loads[:2]:
        load.wait()
    wide_ref[...] = deltas_ref[...].astype(jnp.float32)
    scale_key = scales_ref[0:1, :]
    scale_value = scales_ref[1:2, :]

    def one_block(block, carry):
        here = pl.ds(pl.multiple_of(block * tokens, tokens), tokens)
        key = wide_ref[pl.ds(block * rows, tokens, stride=2), :]
        value = wide_ref[pl.ds(block * rows + 1, tokens, stride=2), :]
        keys_ref[here, 0:HD] = (anchors_ref[pl.ds(2 * block, 1), :] + scale_key * key).astype(jnp.bfloat16)
        values_ref[here, :] = (anchors_ref[pl.ds(2 * block + 1, 1), :] + scale_value * value).astype(
            jnp.bfloat16
        )
        return carry

    lax.fori_loop(0, blocks, one_block, 0, unroll=16)
    turned_ref[...] = values_ref[...].T

    def store(index, partial):
        send_ref[index] = packed(partial)

    attend(1, width, keys_ref, turned_ref, asked_ref, store)


def second_kernel(keys_ref, turned_ref, asked_ref, own_ref, keep_ref):
    def store(index, partial):
        keep_ref[index] = held(partial)

    attend(0, keep_ref.shape[2], keys_ref, turned_ref, asked_ref, store)
    keep_ref[0] = held(joined(taken(keep_ref[0]), taken(own_ref[...])))


def join_kernel(keep_ref, got_ref, send_ref, next_ref):
    for index in range(keep_ref.shape[0]):
        partial = joined(taken(keep_ref[index]), unpacked(got_ref[index]))
        if index % 2 == 1:
            send_ref[index // 2] = packed(partial)
        else:
            next_ref[index // 2] = held(partial)


def settle(plan, handed, pages, sems):
    receivers = lax.axis_size("seq")
    me = lax.axis_index("seq")
    rows = pages.shape[0] // receivers
    copies = []
    for index, (k, start, slots) in enumerate(plan):
        size = handed[index].shape[0]
        sender = source(me, k, receivers) if k else me
        first = pl.multiple_of(sender * rows + start * (size // slots), size)
        copies.append(pltpu.make_async_copy(handed[index], pages.at[pl.ds(first, size), :], sems.at[index]))
        copies[-1].start()
    return copies


def settle_kernel(plan, *refs):
    *handed, pages, sems = refs
    for copy in settle(plan, handed, pages, sems):
        copy.wait()


def finish_kernel(plan, keep_ref, got_ref, _, *refs):
    *handed, out_any, pages, out_ref, sems = refs
    copies = settle(plan, handed, pages, sems)
    summed, _, total = joined(taken(keep_ref[0]), unpacked(got_ref[0]))
    out_ref[...] = (summed / total).T.astype(jnp.bfloat16)
    copies.append(pltpu.make_async_copy(out_ref, out_any, sems.at[len(copies)]))
    copies[-1].start()
    for copy in copies:
        copy.wait()


def in_hbm(arrays):
    return [pltpu.with_memory_space_constraint(array, pltpu.HBM) for array in arrays]


def per_device(lengths, owner_map, row_request, deltas, anchors, scales, queries, new_kv):
    blocks = anchors.shape[0]
    tokens = deltas.shape[0]
    senders = lax.axis_size("seq")
    me = lax.axis_index("seq")
    rows, steps, _ = queries.shape
    rows_dev = new_kv.shape[0]
    width = rows_dev * GQ * steps
    small = pltpu.CompilerParams(vmem_limit_bytes=8 * 1024 * 1024)

    flat_deltas = deltas.reshape(tokens * 2, HD)
    flat_anchors = anchors.reshape(blocks * 2, HD)
    flat_queries = queries.reshape(rows, steps, GQ, HD).transpose(0, 2, 1, 3).reshape(-1, HD)
    flat_new = new_kv.reshape(rows_dev * 4, HD)

    whole = jax.ShapeDtypeStruct((tokens * 2, HD), jnp.bfloat16)
    ahead, behind, own = messages(senders, blocks // senders)
    block_rows = tokens * 2 // blocks

    def place(plan, deltas):
        return pl.pallas_call(
            functools.partial(place_kernel, plan),
            out_shape=[jax.ShapeDtypeStruct((slots * block_rows, HD), jnp.bfloat16) for _, _, slots in plan],
            in_specs=[HBM] * 4,
            out_specs=[VMEM] * len(plan),
            scratch_shapes=[
                pltpu.SMEM((blocks,), jnp.int32),
                pltpu.SMEM((blocks,), jnp.int32),
                pltpu.SMEM((senders,), jnp.int32),
                pltpu.VMEM((tokens * 2, HD), jnp.bfloat16),
                pltpu.VMEM((blocks * 2, HD), jnp.float32),
                pltpu.VMEM((2, HD), jnp.float32),
                pltpu.SemaphoreType.DMA((7,)),
            ],
            compiler_params=small,
            name="place",
        )(*in_hbm([owner_map, deltas, flat_anchors, scales]))

    sent = place(ahead, flat_deltas)
    sent, late_deltas = lax.optimization_barrier((sent, flat_deltas))
    got_ahead = [hand(message, k) for message, (k, _, _) in zip(sent, ahead)]

    def leaving(count):
        return jax.ShapeDtypeStruct((count // 2, HD + STAT_ROWS, width), jnp.bfloat16)

    def staying(count):
        return jax.ShapeDtypeStruct((count // 2, HD + KEEP_ROWS, width), jnp.float32)

    needed = (late_deltas, flat_anchors, scales, lengths, row_request, flat_queries, flat_new)
    roomy = pltpu.CompilerParams(vmem_limit_bytes=32 * 1024 * 1024)
    send, *common = pl.pallas_call(
        first_kernel,
        out_shape=[
            leaving(senders),
            jax.ShapeDtypeStruct((tokens, 2 * HD), jnp.bfloat16),
            jax.ShapeDtypeStruct((HD, tokens), jnp.bfloat16),
            jax.ShapeDtypeStruct((rows * GQ * steps, 2 * HD), jnp.bfloat16),
            jax.ShapeDtypeStruct((HD + KEEP_ROWS, width), jnp.float32),
        ],
        in_specs=[HBM] * len(needed),
        out_specs=[VMEM] * 5,
        scratch_shapes=[
            (pltpu.SMEM if array.dtype == jnp.int32 else pltpu.VMEM)(array.shape, array.dtype)
            for array in needed
        ]
        + [
            pltpu.VMEM((tokens * 2, HD), jnp.float32),
            pltpu.VMEM((tokens, HD), jnp.bfloat16),
            pltpu.SemaphoreType.DMA((len(needed),)),
        ],
        compiler_params=roomy,
        name="attend_leaving",
    )(*in_hbm(needed))

    k, count = 1, senders // 2
    send, late_deltas = lax.optimization_barrier((send, late_deltas))
    passed = exchange(send, k)
    *sent, mine = place(behind + own, late_deltas)
    got = got_ahead[1:] + [hand(message, k) for message, (k, _, _) in zip(sent, behind)]
    keep = pl.pallas_call(
        second_kernel,
        out_shape=staying(senders),
        in_specs=[VMEM] * 4,
        out_specs=VMEM,
        compiler_params=roomy,
        name="attend_staying",
    )(*common)
    while count > 1:
        send, keep = pl.pallas_call(
            join_kernel,
            out_shape=[leaving(count), staying(count)],
            in_specs=[VMEM] * 2,
            out_specs=[VMEM] * 2,
            compiler_params=small,
            name="join",
        )(keep, passed)
        k, count = 2 * k + 1, count // 2
        passed = exchange(send, k)
    settled = ahead[:1] + own
    pages = pl.pallas_call(
        functools.partial(settle_kernel, settled),
        out_shape=whole,
        in_specs=[ANY] * len(settled),
        out_specs=HBM,
        scratch_shapes=[pltpu.SemaphoreType.DMA((len(settled),))],
        compiler_params=small,
        name="settle",
    )(got_ahead[0], mine)
    attended, pages = pl.pallas_call(
        functools.partial(finish_kernel, ahead[1:] + behind),
        out_shape=[jax.ShapeDtypeStruct((width, HD), jnp.bfloat16), whole],
        in_specs=[VMEM] * 2 + [HBM] + [ANY] * len(got),
        out_specs=[HBM, HBM],
        scratch_shapes=[
            pltpu.VMEM((width, HD), jnp.bfloat16),
            pltpu.SemaphoreType.DMA((len(got) + 1,)),
        ],
        input_output_aliases={2: 1},
        compiler_params=small,
        name="finish",
    )(keep, passed, pages, *got)
    pages = pages.reshape(blocks, tokens // blocks, 2, HD)
    attended = (
        attended.reshape(rows_dev, GQ, steps, HD).transpose(0, 2, 1, 3).reshape(rows_dev, steps, GQ * HD)
    )
    return pages, attended


def solution(mesh):
    placed = (
        P("groups"),
        P(("groups", "seq")),
        P("groups"),
        P(("groups", "seq"), None, "tp"),
        P(("groups", "seq"), None, "tp"),
        P("groups", "tp"),
        P("groups", None, "tp"),
        P(("groups", "seq"), None, None, "tp"),
    )
    return jax.shard_map(
        per_device,
        mesh=mesh,
        in_specs=placed,
        out_specs=(P(("groups", "seq"), None, None, "tp"), P(("groups", "seq"), None, "tp")),
        check_vma=False,
    )
```

```python
import functools

import jax
import jax.numpy as jnp
from jax import lax
from jax.experimental import pallas as pl
from jax.experimental.pallas import tpu as pltpu
from jax.sharding import PartitionSpec as P

HD = 128
GQ = 8
STEPS = 2
STAT_ROWS = 8
KEEP_ROWS = 8
FAR = -1e30
RATE = HD ** (-0.5) * 1.4426950408889634

VMEM = pl.BlockSpec(memory_space=pltpu.VMEM)
HBM = pl.BlockSpec(memory_space=pltpu.HBM)
ANY = pl.BlockSpec(memory_space=pl.ANY)
SMEM = pl.BlockSpec(memory_space=pltpu.SMEM)


def inner(device, count):
    return (device ^ (device // (count // 2))) & 1


def partner(device, k, count):
    far = count // 2
    if k == far:
        return device ^ (1 + inner(device, count) * (far - 1))
    if k == 1:
        return device ^ (far - inner(device, count) * (far - 1))
    return device ^ k


def source(device, k, count):
    far = count // 2
    if k == far:
        return device ^ (far - inner(device, count) * (far - 1))
    if k == 1:
        return device ^ (1 + inner(device, count) * (far - 1))
    return device ^ k


def exchange(message, k):
    count = lax.axis_size("seq")
    return lax.ppermute(message, "seq", [(i, i ^ k) for i in range(count)])


def hand(message, k):
    count = lax.axis_size("seq")
    return lax.ppermute(message, "seq", [(i, partner(i, k, count)) for i in range(count)])


def messages(count, capacity):
    half = capacity // 2
    ahead = [(k, 0, capacity) for k in reversed(range(count // 2, count))]
    behind = [(k, first, half) for k in reversed(range(1, count // 2)) for first in (0, half)]
    return ahead, behind, [(0, 0, capacity)]


def place_kernel(plan, owner_any, deltas_any, anchors_any, scales_any, *refs):
    receivers = lax.axis_size("seq")
    me = lax.axis_index("seq")
    outs = refs[:-7]
    owner_ref, source_ref, count_ref, deltas_ref, anchors_ref, scales_ref, sems = refs[-7:]
    blocks = owner_ref.shape[0]
    rows = deltas_ref.shape[0] // blocks
    capacity = blocks // receivers
    quarter = deltas_ref.shape[0] // 4
    parts = [pl.ds(index * quarter, quarter) for index in range(4)]
    loads = [
        pltpu.make_async_copy(source, target, sems.at[index])
        for index, (source, target) in enumerate(
            [(owner_any, owner_ref), (scales_any, scales_ref), (anchors_any, anchors_ref)]
            + [(deltas_any.at[part], deltas_ref.at[part]) for part in parts]
        )
    ]
    for load in loads:
        load.start()
    bits = capacity.bit_length()
    narrow = receivers * bits < 32
    if not narrow:
        for owner in range(receivers):
            count_ref[owner] = owner * capacity
    loads[0].wait()

    def find(block, counts):
        owner = owner_ref[block]
        if narrow:
            shift = owner * bits
            slot = owner * capacity + ((counts >> shift) & ((1 << bits) - 1))
            counts = counts + (jnp.int32(1) << shift)
        else:
            slot = count_ref[owner]
            count_ref[owner] = slot + 1
        source_ref[slot] = block
        return counts

    lax.fori_loop(0, blocks, find, jnp.int32(0), unroll=16)
    for load in loads[1:]:
        load.wait()
    odd = lax.broadcasted_iota(jnp.int32, (8, HD), 0) % 2 == 1
    scale = jnp.where(odd, scales_ref[1:2, :], scales_ref[0:1, :])[None]
    for (k, start, count), out_ref in zip(plan, outs):
        first = partner(me, k, receivers) * capacity + start

        def one_slot(slot, carry, first=first, out_ref=out_ref):
            block = source_ref[first + slot]
            anchor = jnp.where(
                odd, anchors_ref[pl.ds(2 * block + 1, 1), :], anchors_ref[pl.ds(2 * block, 1), :]
            )[None]
            here = pl.ds(pl.multiple_of(block * rows, rows), rows)
            delta = deltas_ref[here, :].astype(jnp.float32)
            decoded = anchor + scale * delta.reshape(rows // 8, 8, HD)
            out_ref[pl.ds(pl.multiple_of(slot * rows, rows), rows), :] = decoded.reshape(rows, HD).astype(
                jnp.bfloat16
            )
            return carry

        lax.fori_loop(0, count, one_slot, 0, unroll=min(16, count))


def pieces(values):
    high = values.astype(jnp.bfloat16)
    rest = values - high.astype(jnp.float32)
    middle = rest.astype(jnp.bfloat16)
    low = (rest - middle.astype(jnp.float32)).astype(jnp.bfloat16)
    return [high, middle, low]


def packed(partial):
    summed, top, total = partial
    stats = pieces(top) + pieces(total)
    rest = jnp.zeros((STAT_ROWS - len(stats), top.shape[1]), jnp.bfloat16)
    return jnp.concatenate([summed.astype(jnp.bfloat16)] + stats + [rest], axis=0)


def unpacked(block):
    stats = block[HD:, :].astype(jnp.float32)
    top = stats[0:1] + stats[1:2] + stats[2:3]
    total = stats[3:4] + stats[4:5] + stats[5:6]
    return block[0:HD, :].astype(jnp.float32), top, total


def held(partial):
    summed, top, total = partial
    rest = jnp.zeros((KEEP_ROWS - 2, top.shape[1]), jnp.float32)
    return jnp.concatenate([summed, top, total, rest], axis=0)


def taken(block):
    return block[0:HD, :], block[HD : HD + 1, :], block[HD + 1 : HD + 2, :]


def joined(one, other):
    top = jnp.maximum(one[1], other[1])
    scale_one = jnp.exp2((one[1] - top) * RATE)
    scale_other = jnp.exp2((other[1] - top) * RATE)
    return (
        one[0] * scale_one + other[0] * scale_other,
        top,
        one[2] * scale_one + other[2] * scale_other,
    )


def difference(index):
    total = 0
    while index:
        total, index = total ^ index, index >> 1
    return total


def attend(parity, width, keys_ref, turned_ref, asked_ref, store):
    me = lax.axis_index("seq")
    asked = asked_ref.shape[0]

    def partial_of(here):
        scores = lax.dot_general(
            keys_ref[...], here, (((1,), (1,)), ((), ())), preferred_element_type=jnp.float32
        )
        top = jnp.max(scores, axis=0, keepdims=True)
        weights = jnp.exp2((scores - top) * RATE)
        total = jnp.sum(weights, axis=0, keepdims=True)
        summed = jnp.dot(turned_ref[...], weights.astype(jnp.bfloat16), preferred_element_type=jnp.float32)
        return summed, top, total

    if width % HD == 0:
        for index in range(asked // width // 2):
            there = (me ^ difference(2 * index + parity)) * width
            store(index, partial_of(asked_ref[pl.ds(pl.multiple_of(there, width), width), :]))
        return
    tile = min(2 * HD, asked)
    parts = tile // width

    def one_tile(tile_index, carry):
        here = asked_ref[pl.ds(pl.multiple_of(tile_index * tile, tile), tile), :]
        summed, top, total = partial_of(here)
        for part in range(parts):
            lanes = slice(part * width, (part + 1) * width)
            apart = (tile_index * parts + part) ^ me
            place = apart ^ (apart >> 1)

            @pl.when(place % 2 == parity)
            def _(lanes=lanes, place=place):
                store(place // 2, (summed[:, lanes], top[:, lanes], total[:, lanes]))

        return carry

    lax.fori_loop(0, asked // tile, one_tile, 0)


def first_kernel(*refs):
    me = lax.axis_index("seq")
    sources, send_ref, keys_ref, turned_ref, asked_ref, own_ref, *targets = refs[:7], *refs[7:-3]
    wide_ref, values_ref, sems = refs[-3:]
    loads = [
        pltpu.make_async_copy(source, target, sems.at[index])
        for index, (source, target) in enumerate(zip(sources, targets))
    ]
    for load in loads:
        load.start()
    deltas_ref, anchors_ref, scales_ref, lengths_ref, request_ref, queries_ref, new_ref = targets
    blocks = anchors_ref.shape[0] // 2
    rows = deltas_ref.shape[0] // blocks
    tokens = rows // 2
    requests = lengths_ref.shape[0]
    asked = queries_ref.shape[0]
    per_row = asked // request_ref.shape[0]
    width = send_ref.shape[2]
    for load in loads[2:]:
        load.wait()

    lane = lax.broadcasted_iota(jnp.int32, (1, HD), 1)
    first = jnp.zeros((1, HD), jnp.int32)
    last = jnp.zeros((1, HD), jnp.int32)
    end = 0 - me * (blocks * tokens)
    for request in range(requests):
        start = end
        end = end + lengths_ref[request]
        first = jnp.where(lane == request, start, first)
        last = jnp.where(lane == request, end, last)
    place = lax.broadcasted_iota(jnp.int32, (blocks * tokens, HD), 0)
    keys_ref[:, HD:] = jnp.where((place >= first) & (place < last), 1.0, 0.0).astype(jnp.bfloat16)

    asked_ref[:, 0:HD] = queries_ref[...]
    wide_lane = lax.broadcasted_iota(jnp.int32, (per_row, HD), 1)

    def one_row(row, carry):
        asked_ref[pl.ds(pl.multiple_of(row * per_row, per_row), per_row), HD:] = jnp.where(
            (wide_lane == request_ref[row]) | (wide_lane >= requests), 0.0, FAR
        ).astype(jnp.bfloat16)
        return carry

    lax.fori_loop(0, request_ref.shape[0], one_row, 0, unroll=16)

    fresh = new_ref.shape[0] // 4
    new = new_ref[...].astype(jnp.float32).reshape(fresh, 4, HD)
    mine = queries_ref[pl.ds(pl.multiple_of(me * width, width), width), :]
    of_row = lax.broadcasted_iota(jnp.int32, (fresh, width), 1) // (GQ * STEPS)
    same = of_row == lax.broadcasted_iota(jnp.int32, (fresh, width), 0)
    step = lax.broadcasted_iota(jnp.int32, (1, width), 1) % STEPS
    own_scores = []
    for which in range(STEPS):
        scored = lax.dot_general(
            new[:, 2 * which, :].astype(jnp.bfloat16),
            mine,
            (((1,), (1,)), ((), ())),
            preferred_element_type=jnp.float32,
        )
        picked = jnp.sum(jnp.where(same, scored, 0.0), axis=0, keepdims=True)
        own_scores.append(jnp.where(step >= which, picked, FAR))
    own_top = jnp.maximum(own_scores[0], own_scores[1])
    own_total = jnp.zeros((1, width), jnp.float32)
    own_summed = jnp.zeros((HD, width), jnp.float32)
    for which in range(STEPS):
        weight = jnp.exp2((own_scores[which] - own_top) * RATE)
        own_total = own_total + weight
        spread = jnp.where(same, weight, 0.0).astype(jnp.bfloat16)
        own_summed = own_summed + lax.dot_general(
            new[:, 2 * which + 1, :].astype(jnp.bfloat16),
            spread,
            (((0,), (0,)), ((), ())),
            preferred_element_type=jnp.float32,
        )
    own_ref[...] = held((own_summed, own_top, own_total))

    for load in loads[:2]:
        load.wait()
    wide_ref[...] = deltas_ref[...].astype(jnp.float32)
    scale_key = scales_ref[0:1, :]
    scale_value = scales_ref[1:2, :]

    def one_block(block, carry):
        here = pl.ds(pl.multiple_of(block * tokens, tokens), tokens)
        key = wide_ref[pl.ds(block * rows, tokens, stride=2), :]
        value = wide_ref[pl.ds(block * rows + 1, tokens, stride=2), :]
        keys_ref[here, 0:HD] = (anchors_ref[pl.ds(2 * block, 1), :] + scale_key * key).astype(jnp.bfloat16)
        values_ref[here, :] = (anchors_ref[pl.ds(2 * block + 1, 1), :] + scale_value * value).astype(
            jnp.bfloat16
        )
        return carry

    lax.fori_loop(0, blocks, one_block, 0, unroll=16)
    turned_ref[...] = values_ref[...].T

    def store(index, partial):
        send_ref[index] = packed(partial)

    attend(1, width, keys_ref, turned_ref, asked_ref, store)


def second_kernel(keys_ref, turned_ref, asked_ref, own_ref, keep_ref):
    def store(index, partial):
        keep_ref[index] = held(partial)

    attend(0, keep_ref.shape[2], keys_ref, turned_ref, asked_ref, store)
    keep_ref[0] = held(joined(taken(keep_ref[0]), taken(own_ref[...])))


def join_kernel(keep_ref, got_ref, send_ref, next_ref):
    for index in range(keep_ref.shape[0]):
        partial = joined(taken(keep_ref[index]), unpacked(got_ref[index]))
        if index % 2 == 1:
            send_ref[index // 2] = packed(partial)
        else:
            next_ref[index // 2] = held(partial)


def settle(plan, handed, pages, sems):
    receivers = lax.axis_size("seq")
    me = lax.axis_index("seq")
    rows = pages.shape[0] // receivers
    copies = []
    for index, (k, start, slots) in enumerate(plan):
        size = handed[index].shape[0]
        sender = source(me, k, receivers) if k else me
        first = pl.multiple_of(sender * rows + start * (size // slots), size)
        copies.append(pltpu.make_async_copy(handed[index], pages.at[pl.ds(first, size), :], sems.at[index]))
        copies[-1].start()
    return copies


def settle_kernel(plan, *refs):
    *handed, pages, sems = refs
    for copy in settle(plan, handed, pages, sems):
        copy.wait()


def finish_kernel(plan, keep_ref, got_ref, _, *refs):
    *handed, out_any, pages, out_ref, sems = refs
    copies = settle(plan, handed, pages, sems)
    summed, _, total = joined(taken(keep_ref[0]), unpacked(got_ref[0]))
    out_ref[...] = (summed / total).T.astype(jnp.bfloat16)
    copies.append(pltpu.make_async_copy(out_ref, out_any, sems.at[len(copies)]))
    copies[-1].start()
    for copy in copies:
        copy.wait()


def in_hbm(arrays):
    return [pltpu.with_memory_space_constraint(array, pltpu.HBM) for array in arrays]


def per_device(lengths, owner_map, row_request, deltas, anchors, scales, queries, new_kv):
    blocks = anchors.shape[0]
    tokens = deltas.shape[0]
    senders = lax.axis_size("seq")
    me = lax.axis_index("seq")
    rows, steps, _ = queries.shape
    rows_dev = new_kv.shape[0]
    width = rows_dev * GQ * steps
    small = pltpu.CompilerParams(vmem_limit_bytes=8 * 1024 * 1024)

    flat_deltas = deltas.reshape(tokens * 2, HD)
    flat_anchors = anchors.reshape(blocks * 2, HD)
    flat_queries = queries.reshape(rows, steps, GQ, HD).transpose(0, 2, 1, 3).reshape(-1, HD)
    flat_new = new_kv.reshape(rows_dev * 4, HD)

    whole = jax.ShapeDtypeStruct((tokens * 2, HD), jnp.bfloat16)
    ahead, behind, own = messages(senders, blocks // senders)
    block_rows = tokens * 2 // blocks

    def place(plan, deltas):
        return pl.pallas_call(
            functools.partial(place_kernel, plan),
            out_shape=[jax.ShapeDtypeStruct((slots * block_rows, HD), jnp.bfloat16) for _, _, slots in plan],
            in_specs=[HBM] * 4,
            out_specs=[VMEM] * len(plan),
            scratch_shapes=[
                pltpu.SMEM((blocks,), jnp.int32),
                pltpu.SMEM((blocks,), jnp.int32),
                pltpu.SMEM((senders,), jnp.int32),
                pltpu.VMEM((tokens * 2, HD), jnp.bfloat16),
                pltpu.VMEM((blocks * 2, HD), jnp.float32),
                pltpu.VMEM((2, HD), jnp.float32),
                pltpu.SemaphoreType.DMA((7,)),
            ],
            compiler_params=small,
            name="place",
        )(*in_hbm([owner_map, deltas, flat_anchors, scales]))

    sent = place(ahead, flat_deltas)
    sent, late_deltas = lax.optimization_barrier((sent, flat_deltas))
    got_ahead = [hand(message, k) for message, (k, _, _) in zip(sent, ahead)]

    def leaving(count):
        return jax.ShapeDtypeStruct((count // 2, HD + STAT_ROWS, width), jnp.bfloat16)

    def staying(count):
        return jax.ShapeDtypeStruct((count // 2, HD + KEEP_ROWS, width), jnp.float32)

    needed = (late_deltas, flat_anchors, scales, lengths, row_request, flat_queries, flat_new)
    roomy = pltpu.CompilerParams(vmem_limit_bytes=32 * 1024 * 1024)
    send, *common = pl.pallas_call(
        first_kernel,
        out_shape=[
            leaving(senders),
            jax.ShapeDtypeStruct((tokens, 2 * HD), jnp.bfloat16),
            jax.ShapeDtypeStruct((HD, tokens), jnp.bfloat16),
            jax.ShapeDtypeStruct((rows * GQ * steps, 2 * HD), jnp.bfloat16),
            jax.ShapeDtypeStruct((HD + KEEP_ROWS, width), jnp.float32),
        ],
        in_specs=[HBM] * len(needed),
        out_specs=[VMEM] * 5,
        scratch_shapes=[
            (pltpu.SMEM if array.dtype == jnp.int32 else pltpu.VMEM)(array.shape, array.dtype)
            for array in needed
        ]
        + [
            pltpu.VMEM((tokens * 2, HD), jnp.float32),
            pltpu.VMEM((tokens, HD), jnp.bfloat16),
            pltpu.SemaphoreType.DMA((len(needed),)),
        ],
        compiler_params=roomy,
        name="attend_leaving",
    )(*in_hbm(needed))

    k, count = 1, senders // 2
    send, late_deltas = lax.optimization_barrier((send, late_deltas))
    passed = exchange(send, k)
    *sent, mine = place(behind + own, late_deltas)
    got = got_ahead[1:] + [hand(message, k) for message, (k, _, _) in zip(sent, behind)]
    keep = pl.pallas_call(
        second_kernel,
        out_shape=staying(senders),
        in_specs=[VMEM] * 4,
        out_specs=VMEM,
        compiler_params=roomy,
        name="attend_staying",
    )(*common)
    while count > 1:
        send, keep = pl.pallas_call(
            join_kernel,
            out_shape=[leaving(count), staying(count)],
            in_specs=[VMEM] * 2,
            out_specs=[VMEM] * 2,
            compiler_params=small,
            name="join",
        )(keep, passed)
        k, count = 2 * k + 1, count // 2
        passed = exchange(send, k)
    settled = ahead[:1] + own
    pages = pl.pallas_call(
        functools.partial(settle_kernel, settled),
        out_shape=whole,
        in_specs=[ANY] * len(settled),
        out_specs=HBM,
        scratch_shapes=[pltpu.SemaphoreType.DMA((len(settled),))],
        compiler_params=small,
        name="settle",
    )(got_ahead[0], mine)
    attended, pages = pl.pallas_call(
        functools.partial(finish_kernel, ahead[1:] + behind),
        out_shape=[jax.ShapeDtypeStruct((width, HD), jnp.bfloat16), whole],
        in_specs=[VMEM] * 2 + [HBM] + [ANY] * len(got),
        out_specs=[HBM, HBM],
        scratch_shapes=[
            pltpu.VMEM((width, HD), jnp.bfloat16),
            pltpu.SemaphoreType.DMA((len(got) + 1,)),
        ],
        input_output_aliases={2: 1},
        compiler_params=small,
        name="finish",
    )(keep, passed, pages, *got)
    pages = pages.reshape(blocks, tokens // blocks, 2, HD)
    attended = (
        attended.reshape(rows_dev, GQ, steps, HD).transpose(0, 2, 1, 3).reshape(rows_dev, steps, GQ * HD)
    )
    return pages, attended


def solution(mesh):
    placed = (
        P("groups"),
        P(("groups", "seq")),
        P("groups"),
        P(("groups", "seq"), None, "tp"),
        P(("groups", "seq"), None, "tp"),
        P("groups", "tp"),
        P("groups", None, "tp"),
        P(("groups", "seq"), None, None, "tp"),
    )
    return jax.shard_map(
        per_device,
        mesh=mesh,
        in_specs=placed,
        out_specs=(P(("groups", "seq"), None, None, "tp"), P(("groups", "seq"), None, "tp")),
        check_vma=False,
    )
```

```python
import functools

import jax
import jax.numpy as jnp
from jax import lax
from jax.experimental import pallas as pl
from jax.experimental.pallas import tpu as pltpu
from jax.sharding import PartitionSpec as P

HD = 128
GQ = 8
STEPS = 2
STAT_ROWS = 8
KEEP_ROWS = 8
FAR = -1e30
RATE = HD ** (-0.5) * 1.4426950408889634

VMEM = pl.BlockSpec(memory_space=pltpu.VMEM)
HBM = pl.BlockSpec(memory_space=pltpu.HBM)
ANY = pl.BlockSpec(memory_space=pl.ANY)
SMEM = pl.BlockSpec(memory_space=pltpu.SMEM)


def partner(device, k, count):
    far = count // 2
    odd = device & 1
    if k == far + 1:
        return device ^ (1 + odd * far)
    if k == 1:
        return device ^ (1 + (1 - odd) * far)
    return device ^ k


def source(device, k, count):
    far = count // 2
    odd = device & 1
    if k == far + 1:
        return device ^ (1 + (1 - odd) * far)
    if k == 1:
        return device ^ (1 + odd * far)
    return device ^ k


def exchange(message, k):
    count = lax.axis_size("seq")
    return lax.ppermute(message, "seq", [(i, i ^ k) for i in range(count)])


def hand(message, k):
    count = lax.axis_size("seq")
    return lax.ppermute(message, "seq", [(i, partner(i, k, count)) for i in range(count)])


def messages(count, capacity):
    half = capacity // 2
    ahead = [(k, 0, capacity) for k in reversed(range(count // 2, count))]
    behind = [(k, first, half) for k in reversed(range(1, count // 2)) for first in (0, half)]
    return ahead, behind, [(0, 0, capacity)]


def place_kernel(plan, owner_any, deltas_any, anchors_any, scales_any, *refs):
    receivers = lax.axis_size("seq")
    me = lax.axis_index("seq")
    outs = refs[:-7]
    owner_ref, source_ref, count_ref, deltas_ref, anchors_ref, scales_ref, sems = refs[-7:]
    blocks = owner_ref.shape[0]
    rows = deltas_ref.shape[0] // blocks
    capacity = blocks // receivers
    quarter = deltas_ref.shape[0] // 4
    parts = [pl.ds(index * quarter, quarter) for index in range(4)]
    loads = [
        pltpu.make_async_copy(source, target, sems.at[index])
        for index, (source, target) in enumerate(
            [(owner_any, owner_ref), (scales_any, scales_ref), (anchors_any, anchors_ref)]
            + [(deltas_any.at[part], deltas_ref.at[part]) for part in parts]
        )
    ]
    for load in loads:
        load.start()
    bits = capacity.bit_length()
    narrow = receivers * bits < 32
    if not narrow:
        for owner in range(receivers):
            count_ref[owner] = owner * capacity
    loads[0].wait()

    def find(block, counts):
        owner = owner_ref[block]
        if narrow:
            shift = owner * bits
            slot = owner * capacity + ((counts >> shift) & ((1 << bits) - 1))
            counts = counts + (jnp.int32(1) << shift)
        else:
            slot = count_ref[owner]
            count_ref[owner] = slot + 1
        source_ref[slot] = block
        return counts

    lax.fori_loop(0, blocks, find, jnp.int32(0), unroll=16)
    for load in loads[1:]:
        load.wait()
    odd = lax.broadcasted_iota(jnp.int32, (8, HD), 0) % 2 == 1
    scale = jnp.where(odd, scales_ref[1:2, :], scales_ref[0:1, :])[None]
    for (k, start, count), out_ref in zip(plan, outs):
        first = partner(me, k, receivers) * capacity + start

        def one_slot(slot, carry, first=first, out_ref=out_ref):
            block = source_ref[first + slot]
            anchor = jnp.where(
                odd, anchors_ref[pl.ds(2 * block + 1, 1), :], anchors_ref[pl.ds(2 * block, 1), :]
            )[None]
            here = pl.ds(pl.multiple_of(block * rows, rows), rows)
            delta = deltas_ref[here, :].astype(jnp.float32)
            decoded = anchor + scale * delta.reshape(rows // 8, 8, HD)
            out_ref[pl.ds(pl.multiple_of(slot * rows, rows), rows), :] = decoded.reshape(rows, HD).astype(
                jnp.bfloat16
            )
            return carry

        lax.fori_loop(0, count, one_slot, 0, unroll=min(16, count))


def pieces(values):
    high = values.astype(jnp.bfloat16)
    rest = values - high.astype(jnp.float32)
    middle = rest.astype(jnp.bfloat16)
    low = (rest - middle.astype(jnp.float32)).astype(jnp.bfloat16)
    return [high, middle, low]


def packed(partial):
    summed, top, total = partial
    stats = pieces(top) + pieces(total)
    rest = jnp.zeros((STAT_ROWS - len(stats), top.shape[1]), jnp.bfloat16)
    return jnp.concatenate([summed.astype(jnp.bfloat16)] + stats + [rest], axis=0)


def unpacked(block):
    stats = block[HD:, :].astype(jnp.float32)
    top = stats[0:1] + stats[1:2] + stats[2:3]
    total = stats[3:4] + stats[4:5] + stats[5:6]
    return block[0:HD, :].astype(jnp.float32), top, total


def held(partial):
    summed, top, total = partial
    rest = jnp.zeros((KEEP_ROWS - 2, top.shape[1]), jnp.float32)
    return jnp.concatenate([summed, top, total, rest], axis=0)


def taken(block):
    return block[0:HD, :], block[HD : HD + 1, :], block[HD + 1 : HD + 2, :]


def joined(one, other):
    top = jnp.maximum(one[1], other[1])
    scale_one = jnp.exp2((one[1] - top) * RATE)
    scale_other = jnp.exp2((other[1] - top) * RATE)
    return (
        one[0] * scale_one + other[0] * scale_other,
        top,
        one[2] * scale_one + other[2] * scale_other,
    )


def difference(index):
    total = 0
    while index:
        total, index = total ^ index, index >> 1
    return total


def attend(parity, width, keys_ref, turned_ref, asked_ref, store):
    me = lax.axis_index("seq")
    asked = asked_ref.shape[0]

    def partial_of(here):
        scores = lax.dot_general(
            keys_ref[...], here, (((1,), (1,)), ((), ())), preferred_element_type=jnp.float32
        )
        top = jnp.max(scores, axis=0, keepdims=True)
        weights = jnp.exp2((scores - top) * RATE)
        total = jnp.sum(weights, axis=0, keepdims=True)
        summed = jnp.dot(turned_ref[...], weights.astype(jnp.bfloat16), preferred_element_type=jnp.float32)
        return summed, top, total

    if width % HD == 0:
        for index in range(asked // width // 2):
            there = (me ^ difference(2 * index + parity)) * width
            store(index, partial_of(asked_ref[pl.ds(pl.multiple_of(there, width), width), :]))
        return
    tile = min(2 * HD, asked)
    parts = tile // width

    def one_tile(tile_index, carry):
        here = asked_ref[pl.ds(pl.multiple_of(tile_index * tile, tile), tile), :]
        summed, top, total = partial_of(here)
        for part in range(parts):
            lanes = slice(part * width, (part + 1) * width)
            apart = (tile_index * parts + part) ^ me
            place = apart ^ (apart >> 1)

            @pl.when(place % 2 == parity)
            def _(lanes=lanes, place=place):
                store(place // 2, (summed[:, lanes], top[:, lanes], total[:, lanes]))

        return carry

    lax.fori_loop(0, asked // tile, one_tile, 0)


def first_kernel(*refs):
    me = lax.axis_index("seq")
    sources, send_ref, keys_ref, turned_ref, asked_ref, own_ref, *targets = refs[:7], *refs[7:-3]
    wide_ref, values_ref, sems = refs[-3:]
    loads = [
        pltpu.make_async_copy(source, target, sems.at[index])
        for index, (source, target) in enumerate(zip(sources, targets))
    ]
    for load in loads:
        load.start()
    deltas_ref, anchors_ref, scales_ref, lengths_ref, request_ref, queries_ref, new_ref = targets
    blocks = anchors_ref.shape[0] // 2
    rows = deltas_ref.shape[0] // blocks
    tokens = rows // 2
    requests = lengths_ref.shape[0]
    asked = queries_ref.shape[0]
    per_row = asked // request_ref.shape[0]
    width = send_ref.shape[2]
    for load in loads[2:]:
        load.wait()

    lane = lax.broadcasted_iota(jnp.int32, (1, HD), 1)
    first = jnp.zeros((1, HD), jnp.int32)
    last = jnp.zeros((1, HD), jnp.int32)
    end = 0 - me * (blocks * tokens)
    for request in range(requests):
        start = end
        end = end + lengths_ref[request]
        first = jnp.where(lane == request, start, first)
        last = jnp.where(lane == request, end, last)
    place = lax.broadcasted_iota(jnp.int32, (blocks * tokens, HD), 0)
    keys_ref[:, HD:] = jnp.where((place >= first) & (place < last), 1.0, 0.0).astype(jnp.bfloat16)

    asked_ref[:, 0:HD] = queries_ref[...]
    wide_lane = lax.broadcasted_iota(jnp.int32, (per_row, HD), 1)

    def one_row(row, carry):
        asked_ref[pl.ds(pl.multiple_of(row * per_row, per_row), per_row), HD:] = jnp.where(
            (wide_lane == request_ref[row]) | (wide_lane >= requests), 0.0, FAR
        ).astype(jnp.bfloat16)
        return carry

    lax.fori_loop(0, request_ref.shape[0], one_row, 0, unroll=16)

    fresh = new_ref.shape[0] // 4
    new = new_ref[...].astype(jnp.float32).reshape(fresh, 4, HD)
    mine = queries_ref[pl.ds(pl.multiple_of(me * width, width), width), :]
    of_row = lax.broadcasted_iota(jnp.int32, (fresh, width), 1) // (GQ * STEPS)
    same = of_row == lax.broadcasted_iota(jnp.int32, (fresh, width), 0)
    step = lax.broadcasted_iota(jnp.int32, (1, width), 1) % STEPS
    own_scores = []
    for which in range(STEPS):
        scored = lax.dot_general(
            new[:, 2 * which, :].astype(jnp.bfloat16),
            mine,
            (((1,), (1,)), ((), ())),
            preferred_element_type=jnp.float32,
        )
        picked = jnp.sum(jnp.where(same, scored, 0.0), axis=0, keepdims=True)
        own_scores.append(jnp.where(step >= which, picked, FAR))
    own_top = jnp.maximum(own_scores[0], own_scores[1])
    own_total = jnp.zeros((1, width), jnp.float32)
    own_summed = jnp.zeros((HD, width), jnp.float32)
    for which in range(STEPS):
        weight = jnp.exp2((own_scores[which] - own_top) * RATE)
        own_total = own_total + weight
        spread = jnp.where(same, weight, 0.0).astype(jnp.bfloat16)
        own_summed = own_summed + lax.dot_general(
            new[:, 2 * which + 1, :].astype(jnp.bfloat16),
            spread,
            (((0,), (0,)), ((), ())),
            preferred_element_type=jnp.float32,
        )
    own_ref[...] = held((own_summed, own_top, own_total))

    for load in loads[:2]:
        load.wait()
    wide_ref[...] = deltas_ref[...].astype(jnp.float32)
    scale_key = scales_ref[0:1, :]
    scale_value = scales_ref[1:2, :]

    def one_block(block, carry):
        here = pl.ds(pl.multiple_of(block * tokens, tokens), tokens)
        key = wide_ref[pl.ds(block * rows, tokens, stride=2), :]
        value = wide_ref[pl.ds(block * rows + 1, tokens, stride=2), :]
        keys_ref[here, 0:HD] = (anchors_ref[pl.ds(2 * block, 1), :] + scale_key * key).astype(jnp.bfloat16)
        values_ref[here, :] = (anchors_ref[pl.ds(2 * block + 1, 1), :] + scale_value * value).astype(
            jnp.bfloat16
        )
        return carry

    lax.fori_loop(0, blocks, one_block, 0, unroll=16)
    turned_ref[...] = values_ref[...].T

    def store(index, partial):
        send_ref[index] = packed(partial)

    attend(1, width, keys_ref, turned_ref, asked_ref, store)


def second_kernel(keys_ref, turned_ref, asked_ref, own_ref, keep_ref):
    def store(index, partial):
        keep_ref[index] = held(partial)

    attend(0, keep_ref.shape[2], keys_ref, turned_ref, asked_ref, store)
    keep_ref[0] = held(joined(taken(keep_ref[0]), taken(own_ref[...])))


def join_kernel(keep_ref, got_ref, send_ref, next_ref):
    for index in range(keep_ref.shape[0]):
        partial = joined(taken(keep_ref[index]), unpacked(got_ref[index]))
        if index % 2 == 1:
            send_ref[index // 2] = packed(partial)
        else:
            next_ref[index // 2] = held(partial)


def settle(plan, handed, pages, sems):
    receivers = lax.axis_size("seq")
    me = lax.axis_index("seq")
    rows = pages.shape[0] // receivers
    copies = []
    for index, (k, start, slots) in enumerate(plan):
        size = handed[index].shape[0]
        sender = source(me, k, receivers) if k else me
        first = pl.multiple_of(sender * rows + start * (size // slots), size)
        copies.append(pltpu.make_async_copy(handed[index], pages.at[pl.ds(first, size), :], sems.at[index]))
        copies[-1].start()
    return copies


def settle_kernel(plan, *refs):
    *handed, pages, sems = refs
    for copy in settle(plan, handed, pages, sems):
        copy.wait()


def finish_kernel(plan, keep_ref, got_ref, _, *refs):
    *handed, out_any, pages, out_ref, sems = refs
    copies = settle(plan, handed, pages, sems)
    summed, _, total = joined(taken(keep_ref[0]), unpacked(got_ref[0]))
    out_ref[...] = (summed / total).T.astype(jnp.bfloat16)
    copies.append(pltpu.make_async_copy(out_ref, out_any, sems.at[len(copies)]))
    copies[-1].start()
    for copy in copies:
        copy.wait()


def in_hbm(arrays):
    return [pltpu.with_memory_space_constraint(array, pltpu.HBM) for array in arrays]


def per_device(lengths, owner_map, row_request, deltas, anchors, scales, queries, new_kv):
    blocks = anchors.shape[0]
    tokens = deltas.shape[0]
    senders = lax.axis_size("seq")
    me = lax.axis_index("seq")
    rows, steps, _ = queries.shape
    rows_dev = new_kv.shape[0]
    width = rows_dev * GQ * steps
    small = pltpu.CompilerParams(vmem_limit_bytes=8 * 1024 * 1024)

    flat_deltas = deltas.reshape(tokens * 2, HD)
    flat_anchors = anchors.reshape(blocks * 2, HD)
    flat_queries = queries.reshape(rows, steps, GQ, HD).transpose(0, 2, 1, 3).reshape(-1, HD)
    flat_new = new_kv.reshape(rows_dev * 4, HD)

    whole = jax.ShapeDtypeStruct((tokens * 2, HD), jnp.bfloat16)
    ahead, behind, own = messages(senders, blocks // senders)
    block_rows = tokens * 2 // blocks

    def place(plan, deltas):
        return pl.pallas_call(
            functools.partial(place_kernel, plan),
            out_shape=[jax.ShapeDtypeStruct((slots * block_rows, HD), jnp.bfloat16) for _, _, slots in plan],
            in_specs=[HBM] * 4,
            out_specs=[VMEM] * len(plan),
            scratch_shapes=[
                pltpu.SMEM((blocks,), jnp.int32),
                pltpu.SMEM((blocks,), jnp.int32),
                pltpu.SMEM((senders,), jnp.int32),
                pltpu.VMEM((tokens * 2, HD), jnp.bfloat16),
                pltpu.VMEM((blocks * 2, HD), jnp.float32),
                pltpu.VMEM((2, HD), jnp.float32),
                pltpu.SemaphoreType.DMA((7,)),
            ],
            compiler_params=small,
            name="place",
        )(*in_hbm([owner_map, deltas, flat_anchors, scales]))

    sent = place(ahead, flat_deltas)
    sent, late_deltas = lax.optimization_barrier((sent, flat_deltas))
    got_ahead = [hand(message, k) for message, (k, _, _) in zip(sent, ahead)]

    def leaving(count):
        return jax.ShapeDtypeStruct((count // 2, HD + STAT_ROWS, width), jnp.bfloat16)

    def staying(count):
        return jax.ShapeDtypeStruct((count // 2, HD + KEEP_ROWS, width), jnp.float32)

    needed = (late_deltas, flat_anchors, scales, lengths, row_request, flat_queries, flat_new)
    roomy = pltpu.CompilerParams(vmem_limit_bytes=32 * 1024 * 1024)
    send, *common = pl.pallas_call(
        first_kernel,
        out_shape=[
            leaving(senders),
            jax.ShapeDtypeStruct((tokens, 2 * HD), jnp.bfloat16),
            jax.ShapeDtypeStruct((HD, tokens), jnp.bfloat16),
            jax.ShapeDtypeStruct((rows * GQ * steps, 2 * HD), jnp.bfloat16),
            jax.ShapeDtypeStruct((HD + KEEP_ROWS, width), jnp.float32),
        ],
        in_specs=[HBM] * len(needed),
        out_specs=[VMEM] * 5,
        scratch_shapes=[
            (pltpu.SMEM if array.dtype == jnp.int32 else pltpu.VMEM)(array.shape, array.dtype)
            for array in needed
        ]
        + [
            pltpu.VMEM((tokens * 2, HD), jnp.float32),
            pltpu.VMEM((tokens, HD), jnp.bfloat16),
            pltpu.SemaphoreType.DMA((len(needed),)),
        ],
        compiler_params=roomy,
        name="attend_leaving",
    )(*in_hbm(needed))

    k, count = 1, senders // 2
    send, late_deltas = lax.optimization_barrier((send, late_deltas))
    passed = exchange(send, k)
    *sent, mine = place(behind + own, late_deltas)
    got = got_ahead[1:] + [hand(message, k) for message, (k, _, _) in zip(sent, behind)]
    keep = pl.pallas_call(
        second_kernel,
        out_shape=staying(senders),
        in_specs=[VMEM] * 4,
        out_specs=VMEM,
        compiler_params=roomy,
        name="attend_staying",
    )(*common)
    while count > 1:
        send, keep = pl.pallas_call(
            join_kernel,
            out_shape=[leaving(count), staying(count)],
            in_specs=[VMEM] * 2,
            out_specs=[VMEM] * 2,
            compiler_params=small,
            name="join",
        )(keep, passed)
        k, count = 2 * k + 1, count // 2
        passed = exchange(send, k)
    settled = ahead[:1] + own
    pages = pl.pallas_call(
        functools.partial(settle_kernel, settled),
        out_shape=whole,
        in_specs=[ANY] * len(settled),
        out_specs=HBM,
        scratch_shapes=[pltpu.SemaphoreType.DMA((len(settled),))],
        compiler_params=small,
        name="settle",
    )(got_ahead[0], mine)
    attended, pages = pl.pallas_call(
        functools.partial(finish_kernel, ahead[1:] + behind),
        out_shape=[jax.ShapeDtypeStruct((width, HD), jnp.bfloat16), whole],
        in_specs=[VMEM] * 2 + [HBM] + [ANY] * len(got),
        out_specs=[HBM, HBM],
        scratch_shapes=[
            pltpu.VMEM((width, HD), jnp.bfloat16),
            pltpu.SemaphoreType.DMA((len(got) + 1,)),
        ],
        input_output_aliases={2: 1},
        compiler_params=small,
        name="finish",
    )(keep, passed, pages, *got)
    pages = pages.reshape(blocks, tokens // blocks, 2, HD)
    attended = (
        attended.reshape(rows_dev, GQ, steps, HD).transpose(0, 2, 1, 3).reshape(rows_dev, steps, GQ * HD)
    )
    return pages, attended


def solution(mesh):
    placed = (
        P("groups"),
        P(("groups", "seq")),
        P("groups"),
        P(("groups", "seq"), None, "tp"),
        P(("groups", "seq"), None, "tp"),
        P("groups", "tp"),
        P("groups", None, "tp"),
        P(("groups", "seq"), None, None, "tp"),
    )
    return jax.shard_map(
        per_device,
        mesh=mesh,
        in_specs=placed,
        out_specs=(P(("groups", "seq"), None, None, "tp"), P(("groups", "seq"), None, "tp")),
        check_vma=False,
    )
```

```python
import functools

import jax
import jax.numpy as jnp
from jax import lax
from jax.experimental import pallas as pl
from jax.experimental.pallas import tpu as pltpu
from jax.sharding import PartitionSpec as P

HD = 128
GQ = 8
STEPS = 2
STAT_ROWS = 16
KEEP_ROWS = 8
FAR = -1e30
RATE = HD ** (-0.5) * 1.4426950408889634

VMEM = pl.BlockSpec(memory_space=pltpu.VMEM)
HBM = pl.BlockSpec(memory_space=pltpu.HBM)
ANY = pl.BlockSpec(memory_space=pl.ANY)
SMEM = pl.BlockSpec(memory_space=pltpu.SMEM)


def inner(device, count):
    return (device ^ (device // (count // 2))) & 1


def partner(device, k, count):
    far = count // 2
    if k == far:
        return device ^ (1 + inner(device, count) * (far - 1))
    if k == 1:
        return device ^ (far - inner(device, count) * (far - 1))
    return device ^ k


def source(device, k, count):
    far = count // 2
    if k == far:
        return device ^ (far - inner(device, count) * (far - 1))
    if k == 1:
        return device ^ (1 + inner(device, count) * (far - 1))
    return device ^ k


def exchange(message, k):
    count = lax.axis_size("seq")
    return lax.ppermute(message, "seq", [(i, i ^ k) for i in range(count)])


def hand(message, k):
    count = lax.axis_size("seq")
    return lax.ppermute(message, "seq", [(i, partner(i, k, count)) for i in range(count)])


def messages(count, capacity):
    half = capacity // 2
    ahead = [(k, 0, capacity) for k in range(count // 2, count)]
    behind = [(k, first, half) for k in reversed(range(1, count // 2)) for first in (0, half)]
    return ahead, behind, [(0, 0, capacity)]


def place_kernel(plan, owner_any, deltas_any, anchors_any, scales_any, *refs):
    receivers = lax.axis_size("seq")
    me = lax.axis_index("seq")
    outs = refs[:-7]
    owner_ref, source_ref, count_ref, deltas_ref, anchors_ref, scales_ref, sems = refs[-7:]
    blocks = owner_ref.shape[0]
    rows = deltas_ref.shape[0] // blocks
    capacity = blocks // receivers
    quarter = deltas_ref.shape[0] // 4
    parts = [pl.ds(index * quarter, quarter) for index in range(4)]
    loads = [
        pltpu.make_async_copy(source, target, sems.at[index])
        for index, (source, target) in enumerate(
            [(owner_any, owner_ref), (scales_any, scales_ref), (anchors_any, anchors_ref)]
            + [(deltas_any.at[part], deltas_ref.at[part]) for part in parts]
        )
    ]
    for load in loads:
        load.start()
    bits = capacity.bit_length()
    narrow = receivers * bits < 32
    if not narrow:
        for owner in range(receivers):
            count_ref[owner] = owner * capacity
    loads[0].wait()

    def find(block, counts):
        owner = owner_ref[block]
        if narrow:
            shift = owner * bits
            slot = owner * capacity + ((counts >> shift) & ((1 << bits) - 1))
            counts = counts + (jnp.int32(1) << shift)
        else:
            slot = count_ref[owner]
            count_ref[owner] = slot + 1
        source_ref[slot] = block
        return counts

    lax.fori_loop(0, blocks, find, jnp.int32(0), unroll=16)
    for load in loads[1:]:
        load.wait()
    odd = lax.broadcasted_iota(jnp.int32, (8, HD), 0) % 2 == 1
    scale = jnp.where(odd, scales_ref[1:2, :], scales_ref[0:1, :])[None]
    for (k, start, count), out_ref in zip(plan, outs):
        first = partner(me, k, receivers) * capacity + start

        def one_slot(slot, carry, first=first, out_ref=out_ref):
            block = source_ref[first + slot]
            anchor = jnp.where(
                odd, anchors_ref[pl.ds(2 * block + 1, 1), :], anchors_ref[pl.ds(2 * block, 1), :]
            )[None]
            here = pl.ds(pl.multiple_of(block * rows, rows), rows)
            delta = deltas_ref[here, :].astype(jnp.float32)
            decoded = anchor + scale * delta.reshape(rows // 8, 8, HD)
            out_ref[pl.ds(pl.multiple_of(slot * rows, rows), rows), :] = decoded.reshape(rows, HD).astype(
                jnp.bfloat16
            )
            return carry

        lax.fori_loop(0, count, one_slot, 0, unroll=min(16, count))


def pieces(values):
    high = values.astype(jnp.bfloat16)
    rest = values - high.astype(jnp.float32)
    middle = rest.astype(jnp.bfloat16)
    low = (rest - middle.astype(jnp.float32)).astype(jnp.bfloat16)
    return [high, middle, low]


def packed(partial):
    summed, top, total = partial
    stats = pieces(top) + pieces(total)
    rest = jnp.zeros((STAT_ROWS - len(stats), top.shape[1]), jnp.bfloat16)
    return jnp.concatenate([summed.astype(jnp.bfloat16)] + stats + [rest], axis=0)


def unpacked(block):
    stats = block[HD:, :].astype(jnp.float32)
    top = stats[0:1] + stats[1:2] + stats[2:3]
    total = stats[3:4] + stats[4:5] + stats[5:6]
    return block[0:HD, :].astype(jnp.float32), top, total


def held(partial):
    summed, top, total = partial
    rest = jnp.zeros((KEEP_ROWS - 2, top.shape[1]), jnp.float32)
    return jnp.concatenate([summed, top, total, rest], axis=0)


def taken(block):
    return block[0:HD, :], block[HD : HD + 1, :], block[HD + 1 : HD + 2, :]


def joined(one, other):
    top = jnp.maximum(one[1], other[1])
    scale_one = jnp.exp2((one[1] - top) * RATE)
    scale_other = jnp.exp2((other[1] - top) * RATE)
    return (
        one[0] * scale_one + other[0] * scale_other,
        top,
        one[2] * scale_one + other[2] * scale_other,
    )


def difference(index):
    total = 0
    while index:
        total, index = total ^ index, index >> 1
    return total


def attend(parity, width, keys_ref, turned_ref, asked_ref, store):
    me = lax.axis_index("seq")
    asked = asked_ref.shape[0]

    def partial_of(here):
        scores = lax.dot_general(
            keys_ref[...], here, (((1,), (1,)), ((), ())), preferred_element_type=jnp.float32
        )
        top = jnp.max(scores, axis=0, keepdims=True)
        weights = jnp.exp2((scores - top) * RATE)
        total = jnp.sum(weights, axis=0, keepdims=True)
        summed = jnp.dot(turned_ref[...], weights.astype(jnp.bfloat16), preferred_element_type=jnp.float32)
        return summed, top, total

    if width % HD == 0:
        for index in range(asked // width // 2):
            there = (me ^ difference(2 * index + parity)) * width
            store(index, partial_of(asked_ref[pl.ds(pl.multiple_of(there, width), width), :]))
        return
    tile = min(2 * HD, asked)
    parts = tile // width

    def one_tile(tile_index, carry):
        here = asked_ref[pl.ds(pl.multiple_of(tile_index * tile, tile), tile), :]
        summed, top, total = partial_of(here)
        for part in range(parts):
            lanes = slice(part * width, (part + 1) * width)
            apart = (tile_index * parts + part) ^ me
            place = apart ^ (apart >> 1)

            @pl.when(place % 2 == parity)
            def _(lanes=lanes, place=place):
                store(place // 2, (summed[:, lanes], top[:, lanes], total[:, lanes]))

        return carry

    lax.fori_loop(0, asked // tile, one_tile, 0)


def first_kernel(*refs):
    me = lax.axis_index("seq")
    sources, send_ref, keys_ref, turned_ref, asked_ref, own_ref, *targets = refs[:7], *refs[7:-3]
    wide_ref, values_ref, sems = refs[-3:]
    loads = [
        pltpu.make_async_copy(source, target, sems.at[index])
        for index, (source, target) in enumerate(zip(sources, targets))
    ]
    for load in loads:
        load.start()
    deltas_ref, anchors_ref, scales_ref, lengths_ref, request_ref, queries_ref, new_ref = targets
    blocks = anchors_ref.shape[0] // 2
    rows = deltas_ref.shape[0] // blocks
    tokens = rows // 2
    requests = lengths_ref.shape[0]
    asked = queries_ref.shape[0]
    per_row = asked // request_ref.shape[0]
    width = send_ref.shape[2]
    for load in loads[2:]:
        load.wait()

    lane = lax.broadcasted_iota(jnp.int32, (1, HD), 1)
    first = jnp.zeros((1, HD), jnp.int32)
    last = jnp.zeros((1, HD), jnp.int32)
    end = 0 - me * (blocks * tokens)
    for request in range(requests):
        start = end
        end = end + lengths_ref[request]
        first = jnp.where(lane == request, start, first)
        last = jnp.where(lane == request, end, last)
    place = lax.broadcasted_iota(jnp.int32, (blocks * tokens, HD), 0)
    keys_ref[:, HD:] = jnp.where((place >= first) & (place < last), 1.0, 0.0).astype(jnp.bfloat16)

    asked_ref[:, 0:HD] = queries_ref[...]
    wide_lane = lax.broadcasted_iota(jnp.int32, (per_row, HD), 1)

    def one_row(row, carry):
        asked_ref[pl.ds(pl.multiple_of(row * per_row, per_row), per_row), HD:] = jnp.where(
            (wide_lane == request_ref[row]) | (wide_lane >= requests), 0.0, FAR
        ).astype(jnp.bfloat16)
        return carry

    lax.fori_loop(0, request_ref.shape[0], one_row, 0, unroll=16)

    fresh = new_ref.shape[0] // 4
    new = new_ref[...].astype(jnp.float32).reshape(fresh, 4, HD)
    mine = queries_ref[pl.ds(pl.multiple_of(me * width, width), width), :]
    of_row = lax.broadcasted_iota(jnp.int32, (fresh, width), 1) // (GQ * STEPS)
    same = of_row == lax.broadcasted_iota(jnp.int32, (fresh, width), 0)
    step = lax.broadcasted_iota(jnp.int32, (1, width), 1) % STEPS
    own_scores = []
    for which in range(STEPS):
        scored = lax.dot_general(
            new[:, 2 * which, :].astype(jnp.bfloat16),
            mine,
            (((1,), (1,)), ((), ())),
            preferred_element_type=jnp.float32,
        )
        picked = jnp.sum(jnp.where(same, scored, 0.0), axis=0, keepdims=True)
        own_scores.append(jnp.where(step >= which, picked, FAR))
    own_top = jnp.maximum(own_scores[0], own_scores[1])
    own_total = jnp.zeros((1, width), jnp.float32)
    own_summed = jnp.zeros((HD, width), jnp.float32)
    for which in range(STEPS):
        weight = jnp.exp2((own_scores[which] - own_top) * RATE)
        own_total = own_total + weight
        spread = jnp.where(same, weight, 0.0).astype(jnp.bfloat16)
        own_summed = own_summed + lax.dot_general(
            new[:, 2 * which + 1, :].astype(jnp.bfloat16),
            spread,
            (((0,), (0,)), ((), ())),
            preferred_element_type=jnp.float32,
        )
    own_ref[...] = held((own_summed, own_top, own_total))

    for load in loads[:2]:
        load.wait()
    wide_ref[0 : blocks * rows, :] = deltas_ref[...].astype(jnp.float32)
    scale_key = scales_ref[0:1, :]
    scale_value = scales_ref[1:2, :]

    def one_block(block, carry):
        here = pl.ds(pl.multiple_of(block * tokens, tokens), tokens)
        key = wide_ref[pl.ds(block * rows, tokens, stride=2), :]
        value = wide_ref[pl.ds(block * rows + 1, tokens, stride=2), :]
        keys_ref[here, 0:HD] = (anchors_ref[pl.ds(2 * block, 1), :] + scale_key * key).astype(jnp.bfloat16)
        values_ref[here, :] = (anchors_ref[pl.ds(2 * block + 1, 1), :] + scale_value * value).astype(
            jnp.bfloat16
        )
        return carry

    lax.fori_loop(0, blocks, one_block, 0, unroll=16)
    turned_ref[...] = values_ref[...].T

    def store(index, partial):
        send_ref[index] = packed(partial)

    attend(1, width, keys_ref, turned_ref, asked_ref, store)


def second_kernel(keys_ref, turned_ref, asked_ref, own_ref, keep_ref):
    def store(index, partial):
        keep_ref[index] = held(partial)

    attend(0, keep_ref.shape[2], keys_ref, turned_ref, asked_ref, store)
    keep_ref[0] = held(joined(taken(keep_ref[0]), taken(own_ref[...])))


def join_kernel(keep_ref, got_ref, send_ref, next_ref):
    for index in range(keep_ref.shape[0]):
        partial = joined(taken(keep_ref[index]), unpacked(got_ref[index]))
        if index % 2 == 1:
            send_ref[index // 2] = packed(partial)
        else:
            next_ref[index // 2] = held(partial)


def settle(plan, handed, pages, sems):
    receivers = lax.axis_size("seq")
    me = lax.axis_index("seq")
    rows = pages.shape[0] // receivers
    copies = []
    for index, (k, start, slots) in enumerate(plan):
        size = handed[index].shape[0]
        sender = source(me, k, receivers) if k else me
        first = pl.multiple_of(sender * rows + start * (size // slots), size)
        copies.append(pltpu.make_async_copy(handed[index], pages.at[pl.ds(first, size), :], sems.at[index]))
        copies[-1].start()
    return copies


def settle_kernel(plan, *refs):
    *handed, pages, sems = refs
    for copy in settle(plan, handed, pages, sems):
        copy.wait()


def finish_kernel(plan, keep_ref, got_ref, _, *refs):
    *handed, out_any, pages, out_ref, sems = refs
    copies = settle(plan, handed, pages, sems)
    summed, _, total = joined(taken(keep_ref[0]), unpacked(got_ref[0]))
    out_ref[...] = (summed / total).T.astype(jnp.bfloat16)
    copies.append(pltpu.make_async_copy(out_ref, out_any, sems.at[len(copies)]))
    copies[-1].start()
    for copy in copies:
        copy.wait()


def in_hbm(arrays):
    return [pltpu.with_memory_space_constraint(array, pltpu.HBM) for array in arrays]


def per_device(lengths, owner_map, row_request, deltas, anchors, scales, queries, new_kv):
    blocks = anchors.shape[0]
    tokens = deltas.shape[0]
    senders = lax.axis_size("seq")
    me = lax.axis_index("seq")
    rows, steps, _ = queries.shape
    rows_dev = new_kv.shape[0]
    width = rows_dev * GQ * steps
    small = pltpu.CompilerParams(vmem_limit_bytes=8 * 1024 * 1024)

    flat_deltas = deltas.reshape(tokens * 2, HD)
    flat_anchors = anchors.reshape(blocks * 2, HD)
    flat_queries = queries.reshape(rows, steps, GQ, HD).transpose(0, 2, 1, 3).reshape(-1, HD)
    flat_new = new_kv.reshape(rows_dev * 4, HD)

    whole = jax.ShapeDtypeStruct((tokens * 2, HD), jnp.bfloat16)
    ahead, behind, own = messages(senders, blocks // senders)
    block_rows = tokens * 2 // blocks

    def place(plan, deltas):
        return pl.pallas_call(
            functools.partial(place_kernel, plan),
            out_shape=[jax.ShapeDtypeStruct((slots * block_rows, HD), jnp.bfloat16) for _, _, slots in plan],
            in_specs=[HBM] * 4,
            out_specs=[VMEM] * len(plan),
            scratch_shapes=[
                pltpu.SMEM((blocks,), jnp.int32),
                pltpu.SMEM((blocks,), jnp.int32),
                pltpu.SMEM((senders,), jnp.int32),
                pltpu.VMEM((tokens * 2, HD), jnp.bfloat16),
                pltpu.VMEM((blocks * 2, HD), jnp.float32),
                pltpu.VMEM((2, HD), jnp.float32),
                pltpu.SemaphoreType.DMA((7,)),
            ],
            compiler_params=small,
            name="place",
        )(*in_hbm([owner_map, deltas, flat_anchors, scales]))

    sent = place(ahead, flat_deltas)
    sent, late_deltas = lax.optimization_barrier((sent, flat_deltas))
    got_ahead = [hand(message, k) for message, (k, _, _) in zip(sent, ahead)]

    def leaving(count):
        return jax.ShapeDtypeStruct((count // 2, HD + STAT_ROWS, width), jnp.bfloat16)

    def staying(count):
        return jax.ShapeDtypeStruct((count // 2, HD + KEEP_ROWS, width), jnp.float32)

    needed = (late_deltas, flat_anchors, scales, lengths, row_request, flat_queries, flat_new)
    roomy = pltpu.CompilerParams(vmem_limit_bytes=32 * 1024 * 1024)
    send, *common = pl.pallas_call(
        first_kernel,
        out_shape=[
            leaving(senders),
            jax.ShapeDtypeStruct((tokens, 2 * HD), jnp.bfloat16),
            jax.ShapeDtypeStruct((HD, tokens), jnp.bfloat16),
            jax.ShapeDtypeStruct((rows * GQ * steps, 2 * HD), jnp.bfloat16),
            jax.ShapeDtypeStruct((HD + KEEP_ROWS, width), jnp.float32),
        ],
        in_specs=[HBM] * len(needed),
        out_specs=[VMEM] * 5,
        scratch_shapes=[
            (pltpu.SMEM if array.dtype == jnp.int32 else pltpu.VMEM)(array.shape, array.dtype)
            for array in needed
        ]
        + [
            pltpu.VMEM((tokens * 2 + 16, HD), jnp.float32),
            pltpu.VMEM((tokens, HD), jnp.bfloat16),
            pltpu.SemaphoreType.DMA((len(needed),)),
        ],
        compiler_params=roomy,
        name="attend_leaving",
    )(*in_hbm(needed))

    k, count = 1, senders // 2
    send, late_deltas = lax.optimization_barrier((send, late_deltas))
    passed = exchange(send, k)
    *sent, mine = place(behind + own, late_deltas)
    got = got_ahead[1:] + [hand(message, k) for message, (k, _, _) in zip(sent, behind)]
    keep = pl.pallas_call(
        second_kernel,
        out_shape=staying(senders),
        in_specs=[VMEM] * 4,
        out_specs=VMEM,
        compiler_params=roomy,
        name="attend_staying",
    )(*common)
    while count > 1:
        send, keep = pl.pallas_call(
            join_kernel,
            out_shape=[leaving(count), staying(count)],
            in_specs=[VMEM] * 2,
            out_specs=[VMEM] * 2,
            compiler_params=small,
            name="join",
        )(keep, passed)
        k, count = 2 * k + 1, count // 2
        passed = exchange(send, k)
    settled = ahead[:1] + own
    pages = pl.pallas_call(
        functools.partial(settle_kernel, settled),
        out_shape=whole,
        in_specs=[ANY] * len(settled),
        out_specs=HBM,
        scratch_shapes=[pltpu.SemaphoreType.DMA((len(settled),))],
        compiler_params=small,
        name="settle",
    )(got_ahead[0], mine)
    attended, pages = pl.pallas_call(
        functools.partial(finish_kernel, ahead[1:] + behind),
        out_shape=[jax.ShapeDtypeStruct((width, HD), jnp.bfloat16), whole],
        in_specs=[VMEM] * 2 + [HBM] + [ANY] * len(got),
        out_specs=[HBM, HBM],
        scratch_shapes=[
            pltpu.VMEM((width, HD), jnp.bfloat16),
            pltpu.SemaphoreType.DMA((len(got) + 1,)),
        ],
        input_output_aliases={2: 1},
        compiler_params=small,
        name="finish",
    )(keep, passed, pages, *got)
    pages = pages.reshape(blocks, tokens // blocks, 2, HD)
    attended = (
        attended.reshape(rows_dev, GQ, steps, HD).transpose(0, 2, 1, 3).reshape(rows_dev, steps, GQ * HD)
    )
    return pages, attended


def solution(mesh):
    placed = (
        P("groups"),
        P(("groups", "seq")),
        P("groups"),
        P(("groups", "seq"), None, "tp"),
        P(("groups", "seq"), None, "tp"),
        P("groups", "tp"),
        P("groups", None, "tp"),
        P(("groups", "seq"), None, None, "tp"),
    )
    return jax.shard_map(
        per_device,
        mesh=mesh,
        in_specs=placed,
        out_specs=(P(("groups", "seq"), None, None, "tp"), P(("groups", "seq"), None, "tp")),
        check_vma=False,
    )
```

```python
import functools

import jax
import jax.numpy as jnp
from jax import lax
from jax.experimental import pallas as pl
from jax.experimental.pallas import tpu as pltpu
from jax.sharding import PartitionSpec as P

HD = 128
GQ = 8
STEPS = 2
STAT_ROWS = 6
KEEP_ROWS = 8
FAR = -1e30
RATE = HD ** (-0.5) * 1.4426950408889634

VMEM = pl.BlockSpec(memory_space=pltpu.VMEM)
HBM = pl.BlockSpec(memory_space=pltpu.HBM)
ANY = pl.BlockSpec(memory_space=pl.ANY)
SMEM = pl.BlockSpec(memory_space=pltpu.SMEM)


def inner(device, count):
    return (device ^ (device // (count // 2))) & 1


def partner(device, k, count):
    far = count // 2
    if k == far:
        return device ^ (1 + inner(device, count) * (far - 1))
    if k == 1:
        return device ^ (far - inner(device, count) * (far - 1))
    return device ^ k


def source(device, k, count):
    far = count // 2
    if k == far:
        return device ^ (far - inner(device, count) * (far - 1))
    if k == 1:
        return device ^ (1 + inner(device, count) * (far - 1))
    return device ^ k


def exchange(message, k):
    count = lax.axis_size("seq")
    return lax.ppermute(message, "seq", [(i, i ^ k) for i in range(count)])


def hand(message, k):
    count = lax.axis_size("seq")
    return lax.ppermute(message, "seq", [(i, partner(i, k, count)) for i in range(count)])


def messages(count, capacity):
    half = capacity // 2
    ahead = [(k, 0, capacity) for k in range(count // 2, count)]
    behind = [(k, first, half) for k in reversed(range(1, count // 2)) for first in (0, half)]
    return ahead, behind, [(0, 0, capacity)]


def place_kernel(plan, owner_any, deltas_any, anchors_any, scales_any, *refs):
    receivers = lax.axis_size("seq")
    me = lax.axis_index("seq")
    outs = refs[:-7]
    owner_ref, source_ref, count_ref, deltas_ref, anchors_ref, scales_ref, sems = refs[-7:]
    blocks = owner_ref.shape[0]
    rows = deltas_ref.shape[0] // blocks
    capacity = blocks // receivers
    quarter = deltas_ref.shape[0] // 4
    parts = [pl.ds(index * quarter, quarter) for index in range(4)]
    loads = [
        pltpu.make_async_copy(source, target, sems.at[index])
        for index, (source, target) in enumerate(
            [(owner_any, owner_ref), (scales_any, scales_ref), (anchors_any, anchors_ref)]
            + [(deltas_any.at[part], deltas_ref.at[part]) for part in parts]
        )
    ]
    for load in loads:
        load.start()
    bits = capacity.bit_length()
    narrow = receivers * bits < 32
    if not narrow:
        for owner in range(receivers):
            count_ref[owner] = owner * capacity
    loads[0].wait()

    def find(block, counts):
        owner = owner_ref[block]
        if narrow:
            shift = owner * bits
            slot = owner * capacity + ((counts >> shift) & ((1 << bits) - 1))
            counts = counts + (jnp.int32(1) << shift)
        else:
            slot = count_ref[owner]
            count_ref[owner] = slot + 1
        source_ref[slot] = block
        return counts

    lax.fori_loop(0, blocks, find, jnp.int32(0), unroll=16)
    for load in loads[1:]:
        load.wait()
    odd = lax.broadcasted_iota(jnp.int32, (8, HD), 0) % 2 == 1
    scale = jnp.where(odd, scales_ref[1:2, :], scales_ref[0:1, :])[None]
    for (k, start, count), out_ref in zip(plan, outs):
        first = partner(me, k, receivers) * capacity + start

        def one_slot(slot, carry, first=first, out_ref=out_ref):
            block = source_ref[first + slot]
            anchor = jnp.where(
                odd, anchors_ref[pl.ds(2 * block + 1, 1), :], anchors_ref[pl.ds(2 * block, 1), :]
            )[None]
            here = pl.ds(pl.multiple_of(block * rows, rows), rows)
            delta = deltas_ref[here, :].astype(jnp.float32)
            decoded = anchor + scale * delta.reshape(rows // 8, 8, HD)
            out_ref[pl.ds(pl.multiple_of(slot * rows, rows), rows), :] = decoded.reshape(rows, HD).astype(
                jnp.bfloat16
            )
            return carry

        lax.fori_loop(0, count, one_slot, 0, unroll=min(16, count))


def pieces(values):
    high = values.astype(jnp.bfloat16)
    rest = values - high.astype(jnp.float32)
    middle = rest.astype(jnp.bfloat16)
    low = (rest - middle.astype(jnp.float32)).astype(jnp.bfloat16)
    return [high, middle, low]


def message_shape(width):
    parts = max(1, width // HD)
    return parts * HD + -(-parts * STAT_ROWS // 16) * 16, width // parts


def packed(partial):
    summed, top, total = partial
    rows, lanes = message_shape(top.shape[1])
    sums = summed.astype(jnp.bfloat16)
    stats = pieces(top) + pieces(total)
    here = [slice(first, first + lanes) for first in range(0, top.shape[1], lanes)]
    filled = [sums[:, part] for part in here] + [row[:, part] for part in here for row in stats]
    rest = rows - len(here) * (HD + STAT_ROWS)
    return jnp.concatenate(filled + [jnp.zeros((rest, lanes), jnp.bfloat16)], axis=0)


def unpacked(block):
    parts = block.shape[0] // HD
    sums = [block[part * HD : (part + 1) * HD, :] for part in range(parts)]
    stats = block[parts * HD :, :].astype(jnp.float32)

    def row(first):
        found = []
        for part in range(parts):
            at = part * STAT_ROWS + first
            found.append(stats[at : at + 1] + stats[at + 1 : at + 2] + stats[at + 2 : at + 3])
        return jnp.concatenate(found, axis=1)

    return jnp.concatenate(sums, axis=1).astype(jnp.float32), row(0), row(3)


def held(partial):
    summed, top, total = partial
    rest = jnp.zeros((KEEP_ROWS - 2, top.shape[1]), jnp.float32)
    return jnp.concatenate([summed, top, total, rest], axis=0)


def taken(block):
    return block[0:HD, :], block[HD : HD + 1, :], block[HD + 1 : HD + 2, :]


def joined(one, other):
    top = jnp.maximum(one[1], other[1])
    scale_one = jnp.exp2((one[1] - top) * RATE)
    scale_other = jnp.exp2((other[1] - top) * RATE)
    return (
        one[0] * scale_one + other[0] * scale_other,
        top,
        one[2] * scale_one + other[2] * scale_other,
    )


def difference(index):
    total = 0
    while index:
        total, index = total ^ index, index >> 1
    return total


def attend(parity, width, keys_ref, turned_ref, asked_ref, store):
    me = lax.axis_index("seq")
    asked = asked_ref.shape[0]

    def partial_of(here):
        scores = lax.dot_general(
            keys_ref[...], here, (((1,), (1,)), ((), ())), preferred_element_type=jnp.float32
        )
        top = jnp.max(scores, axis=0, keepdims=True)
        weights = jnp.exp2((scores - top) * RATE)
        total = jnp.sum(weights, axis=0, keepdims=True)
        summed = jnp.dot(turned_ref[...], weights.astype(jnp.bfloat16), preferred_element_type=jnp.float32)
        return summed, top, total

    if width % HD == 0:
        for index in range(asked // width // 2):
            there = (me ^ difference(2 * index + parity)) * width
            store(index, partial_of(asked_ref[pl.ds(pl.multiple_of(there, width), width), :]))
        return
    tile = min(2 * HD, asked)
    parts = tile // width

    def one_tile(tile_index, carry):
        here = asked_ref[pl.ds(pl.multiple_of(tile_index * tile, tile), tile), :]
        summed, top, total = partial_of(here)
        for part in range(parts):
            lanes = slice(part * width, (part + 1) * width)
            apart = (tile_index * parts + part) ^ me
            place = apart ^ (apart >> 1)

            @pl.when(place % 2 == parity)
            def _(lanes=lanes, place=place):
                store(place // 2, (summed[:, lanes], top[:, lanes], total[:, lanes]))

        return carry

    lax.fori_loop(0, asked // tile, one_tile, 0)


def first_kernel(*refs):
    me = lax.axis_index("seq")
    sources, send_ref, keys_ref, turned_ref, asked_ref, own_ref, *targets = refs[:7], *refs[7:-3]
    wide_ref, values_ref, sems = refs[-3:]
    loads = [
        pltpu.make_async_copy(source, target, sems.at[index])
        for index, (source, target) in enumerate(zip(sources, targets))
    ]
    for load in loads:
        load.start()
    deltas_ref, anchors_ref, scales_ref, lengths_ref, request_ref, queries_ref, new_ref = targets
    blocks = anchors_ref.shape[0] // 2
    rows = deltas_ref.shape[0] // blocks
    tokens = rows // 2
    requests = lengths_ref.shape[0]
    asked = queries_ref.shape[0]
    per_row = asked // request_ref.shape[0]
    width = own_ref.shape[1]
    for load in loads[2:]:
        load.wait()

    lane = lax.broadcasted_iota(jnp.int32, (1, HD), 1)
    first = jnp.zeros((1, HD), jnp.int32)
    last = jnp.zeros((1, HD), jnp.int32)
    end = 0 - me * (blocks * tokens)
    for request in range(requests):
        start = end
        end = end + lengths_ref[request]
        first = jnp.where(lane == request, start, first)
        last = jnp.where(lane == request, end, last)
    place = lax.broadcasted_iota(jnp.int32, (blocks * tokens, HD), 0)
    keys_ref[:, HD:] = jnp.where((place >= first) & (place < last), 1.0, 0.0).astype(jnp.bfloat16)

    asked_ref[:, 0:HD] = queries_ref[...]
    wide_lane = lax.broadcasted_iota(jnp.int32, (per_row, HD), 1)

    def one_row(row, carry):
        asked_ref[pl.ds(pl.multiple_of(row * per_row, per_row), per_row), HD:] = jnp.where(
            (wide_lane == request_ref[row]) | (wide_lane >= requests), 0.0, FAR
        ).astype(jnp.bfloat16)
        return carry

    lax.fori_loop(0, request_ref.shape[0], one_row, 0, unroll=16)

    fresh = new_ref.shape[0] // 4
    new = new_ref[...].astype(jnp.float32).reshape(fresh, 4, HD)
    mine = queries_ref[pl.ds(pl.multiple_of(me * width, width), width), :]
    of_row = lax.broadcasted_iota(jnp.int32, (fresh, width), 1) // (GQ * STEPS)
    same = of_row == lax.broadcasted_iota(jnp.int32, (fresh, width), 0)
    step = lax.broadcasted_iota(jnp.int32, (1, width), 1) % STEPS
    own_scores = []
    for which in range(STEPS):
        scored = lax.dot_general(
            new[:, 2 * which, :].astype(jnp.bfloat16),
            mine,
            (((1,), (1,)), ((), ())),
            preferred_element_type=jnp.float32,
        )
        picked = jnp.sum(jnp.where(same, scored, 0.0), axis=0, keepdims=True)
        own_scores.append(jnp.where(step >= which, picked, FAR))
    own_top = jnp.maximum(own_scores[0], own_scores[1])
    own_total = jnp.zeros((1, width), jnp.float32)
    own_summed = jnp.zeros((HD, width), jnp.float32)
    for which in range(STEPS):
        weight = jnp.exp2((own_scores[which] - own_top) * RATE)
        own_total = own_total + weight
        spread = jnp.where(same, weight, 0.0).astype(jnp.bfloat16)
        own_summed = own_summed + lax.dot_general(
            new[:, 2 * which + 1, :].astype(jnp.bfloat16),
            spread,
            (((0,), (0,)), ((), ())),
            preferred_element_type=jnp.float32,
        )
    own_ref[...] = held((own_summed, own_top, own_total))

    for load in loads[:2]:
        load.wait()
    wide_ref[0 : blocks * rows, :] = deltas_ref[...].astype(jnp.float32)
    scale_key = scales_ref[0:1, :]
    scale_value = scales_ref[1:2, :]

    def one_block(block, carry):
        here = pl.ds(pl.multiple_of(block * tokens, tokens), tokens)
        key = wide_ref[pl.ds(block * rows, tokens, stride=2), :]
        value = wide_ref[pl.ds(block * rows + 1, tokens, stride=2), :]
        keys_ref[here, 0:HD] = (anchors_ref[pl.ds(2 * block, 1), :] + scale_key * key).astype(jnp.bfloat16)
        values_ref[here, :] = (anchors_ref[pl.ds(2 * block + 1, 1), :] + scale_value * value).astype(
            jnp.bfloat16
        )
        return carry

    lax.fori_loop(0, blocks, one_block, 0, unroll=16)
    turned_ref[...] = values_ref[...].T

    def store(index, partial):
        send_ref[index] = packed(partial)

    attend(1, width, keys_ref, turned_ref, asked_ref, store)


def second_kernel(keys_ref, turned_ref, asked_ref, own_ref, keep_ref):
    def store(index, partial):
        keep_ref[index] = held(partial)

    attend(0, keep_ref.shape[2], keys_ref, turned_ref, asked_ref, store)
    keep_ref[0] = held(joined(taken(keep_ref[0]), taken(own_ref[...])))


def join_kernel(keep_ref, got_ref, send_ref, next_ref):
    for index in range(keep_ref.shape[0]):
        partial = joined(taken(keep_ref[index]), unpacked(got_ref[index]))
        if index % 2 == 1:
            send_ref[index // 2] = packed(partial)
        else:
            next_ref[index // 2] = held(partial)


def settle(plan, handed, pages, sems):
    receivers = lax.axis_size("seq")
    me = lax.axis_index("seq")
    rows = pages.shape[0] // receivers
    copies = []
    for index, (k, start, slots) in enumerate(plan):
        size = handed[index].shape[0]
        sender = source(me, k, receivers) if k else me
        first = pl.multiple_of(sender * rows + start * (size // slots), size)
        copies.append(pltpu.make_async_copy(handed[index], pages.at[pl.ds(first, size), :], sems.at[index]))
        copies[-1].start()
    return copies


def settle_kernel(plan, *refs):
    *handed, pages, sems = refs
    for copy in settle(plan, handed, pages, sems):
        copy.wait()


def finish_kernel(plan, keep_ref, got_ref, _, *refs):
    *handed, out_any, pages, out_ref, sems = refs
    copies = settle(plan, handed, pages, sems)
    summed, _, total = joined(taken(keep_ref[0]), unpacked(got_ref[0]))
    out_ref[...] = (summed / total).T.astype(jnp.bfloat16)
    copies.append(pltpu.make_async_copy(out_ref, out_any, sems.at[len(copies)]))
    copies[-1].start()
    for copy in copies:
        copy.wait()


def in_hbm(arrays):
    return [pltpu.with_memory_space_constraint(array, pltpu.HBM) for array in arrays]


def per_device(lengths, owner_map, row_request, deltas, anchors, scales, queries, new_kv):
    blocks = anchors.shape[0]
    tokens = deltas.shape[0]
    senders = lax.axis_size("seq")
    me = lax.axis_index("seq")
    rows, steps, _ = queries.shape
    rows_dev = new_kv.shape[0]
    width = rows_dev * GQ * steps
    small = pltpu.CompilerParams(vmem_limit_bytes=8 * 1024 * 1024)

    flat_deltas = deltas.reshape(tokens * 2, HD)
    flat_anchors = anchors.reshape(blocks * 2, HD)
    flat_queries = queries.reshape(rows, steps, GQ, HD).transpose(0, 2, 1, 3).reshape(-1, HD)
    flat_new = new_kv.reshape(rows_dev * 4, HD)

    whole = jax.ShapeDtypeStruct((tokens * 2, HD), jnp.bfloat16)
    ahead, behind, own = messages(senders, blocks // senders)
    block_rows = tokens * 2 // blocks

    def place(plan, deltas):
        return pl.pallas_call(
            functools.partial(place_kernel, plan),
            out_shape=[jax.ShapeDtypeStruct((slots * block_rows, HD), jnp.bfloat16) for _, _, slots in plan],
            in_specs=[HBM] * 4,
            out_specs=[VMEM] * len(plan),
            scratch_shapes=[
                pltpu.SMEM((blocks,), jnp.int32),
                pltpu.SMEM((blocks,), jnp.int32),
                pltpu.SMEM((senders,), jnp.int32),
                pltpu.VMEM((tokens * 2, HD), jnp.bfloat16),
                pltpu.VMEM((blocks * 2, HD), jnp.float32),
                pltpu.VMEM((2, HD), jnp.float32),
                pltpu.SemaphoreType.DMA((7,)),
            ],
            compiler_params=small,
            name="place",
        )(*in_hbm([owner_map, deltas, flat_anchors, scales]))

    sent = place(ahead, flat_deltas)
    sent, late_deltas = lax.optimization_barrier((sent, flat_deltas))
    got_ahead = [hand(message, k) for message, (k, _, _) in zip(sent, ahead)]

    def leaving(count):
        return jax.ShapeDtypeStruct((count // 2, *message_shape(width)), jnp.bfloat16)

    def staying(count):
        return jax.ShapeDtypeStruct((count // 2, HD + KEEP_ROWS, width), jnp.float32)

    needed = (late_deltas, flat_anchors, scales, lengths, row_request, flat_queries, flat_new)
    roomy = pltpu.CompilerParams(vmem_limit_bytes=32 * 1024 * 1024)
    send, *common = pl.pallas_call(
        first_kernel,
        out_shape=[
            leaving(senders),
            jax.ShapeDtypeStruct((tokens, 2 * HD), jnp.bfloat16),
            jax.ShapeDtypeStruct((HD, tokens), jnp.bfloat16),
            jax.ShapeDtypeStruct((rows * GQ * steps, 2 * HD), jnp.bfloat16),
            jax.ShapeDtypeStruct((HD + KEEP_ROWS, width), jnp.float32),
        ],
        in_specs=[HBM] * len(needed),
        out_specs=[VMEM] * 5,
        scratch_shapes=[
            (pltpu.SMEM if array.dtype == jnp.int32 else pltpu.VMEM)(array.shape, array.dtype)
            for array in needed
        ]
        + [
            pltpu.VMEM((tokens * 2 + 16, HD), jnp.float32),
            pltpu.VMEM((tokens, HD), jnp.bfloat16),
            pltpu.SemaphoreType.DMA((len(needed),)),
        ],
        compiler_params=roomy,
        name="attend_leaving",
    )(*in_hbm(needed))

    k, count = 1, senders // 2
    send, late_deltas = lax.optimization_barrier((send, late_deltas))
    passed = exchange(send, k)
    *sent, mine = place(behind + own, late_deltas)
    got = got_ahead[1:] + [hand(message, k) for message, (k, _, _) in zip(sent, behind)]
    keep = pl.pallas_call(
        second_kernel,
        out_shape=staying(senders),
        in_specs=[VMEM] * 4,
        out_specs=VMEM,
        compiler_params=roomy,
        name="attend_staying",
    )(*common)
    while count > 1:
        send, keep = pl.pallas_call(
            join_kernel,
            out_shape=[leaving(count), staying(count)],
            in_specs=[VMEM] * 2,
            out_specs=[VMEM] * 2,
            compiler_params=small,
            name="join",
        )(keep, passed)
        k, count = 2 * k + 1, count // 2
        passed = exchange(send, k)
    settled = ahead[:1] + own
    pages = pl.pallas_call(
        functools.partial(settle_kernel, settled),
        out_shape=whole,
        in_specs=[ANY] * len(settled),
        out_specs=HBM,
        scratch_shapes=[pltpu.SemaphoreType.DMA((len(settled),))],
        compiler_params=small,
        name="settle",
    )(got_ahead[0], mine)
    attended, pages = pl.pallas_call(
        functools.partial(finish_kernel, ahead[1:] + behind),
        out_shape=[jax.ShapeDtypeStruct((width, HD), jnp.bfloat16), whole],
        in_specs=[VMEM] * 2 + [HBM] + [ANY] * len(got),
        out_specs=[HBM, HBM],
        scratch_shapes=[
            pltpu.VMEM((width, HD), jnp.bfloat16),
            pltpu.SemaphoreType.DMA((len(got) + 1,)),
        ],
        input_output_aliases={2: 1},
        compiler_params=small,
        name="finish",
    )(keep, passed, pages, *got)
    pages = pages.reshape(blocks, tokens // blocks, 2, HD)
    attended = (
        attended.reshape(rows_dev, GQ, steps, HD).transpose(0, 2, 1, 3).reshape(rows_dev, steps, GQ * HD)
    )
    return pages, attended


def solution(mesh):
    placed = (
        P("groups"),
        P(("groups", "seq")),
        P("groups"),
        P(("groups", "seq"), None, "tp"),
        P(("groups", "seq"), None, "tp"),
        P("groups", "tp"),
        P("groups", None, "tp"),
        P(("groups", "seq"), None, None, "tp"),
    )
    return jax.shard_map(
        per_device,
        mesh=mesh,
        in_specs=placed,
        out_specs=(P(("groups", "seq"), None, None, "tp"), P(("groups", "seq"), None, "tp")),
        check_vma=False,
    )
```

```python
import functools

import jax
import jax.numpy as jnp
from jax import lax
from jax.experimental import pallas as pl
from jax.experimental.pallas import tpu as pltpu
from jax.sharding import PartitionSpec as P

HD = 128
GQ = 8
STEPS = 2
STAT_ROWS = 6
KEEP_ROWS = 8
FAR = -1e30
RATE = HD ** (-0.5) * 1.4426950408889634

VMEM = pl.BlockSpec(memory_space=pltpu.VMEM)
HBM = pl.BlockSpec(memory_space=pltpu.HBM)
ANY = pl.BlockSpec(memory_space=pl.ANY)
SMEM = pl.BlockSpec(memory_space=pltpu.SMEM)


def inner(device, count):
    return (device ^ (device // (count // 2))) & 1


def partner(device, k, count):
    far = count // 2
    if k == far:
        return device ^ (1 + inner(device, count) * (far - 1))
    if k == 1:
        return device ^ (far - inner(device, count) * (far - 1))
    return device ^ k


def source(device, k, count):
    far = count // 2
    if k == far:
        return device ^ (far - inner(device, count) * (far - 1))
    if k == 1:
        return device ^ (1 + inner(device, count) * (far - 1))
    return device ^ k


def exchange(message, k):
    count = lax.axis_size("seq")
    last = k == count - 1
    return lax.ppermute(message, "seq", [(i, i ^ k ^ (last and i < count // 2)) for i in range(count)])


def hand(message, k):
    count = lax.axis_size("seq")
    return lax.ppermute(message, "seq", [(i, partner(i, k, count)) for i in range(count)])


def messages(count, capacity):
    half = capacity // 2
    ahead = [(k, 0, capacity) for k in range(count // 2, count)]
    behind = [(k, first, half) for k in reversed(range(1, count // 2)) for first in (0, half)]
    return ahead, behind, [(0, 0, capacity)]


def place_kernel(plan, owner_any, deltas_any, anchors_any, scales_any, *refs):
    receivers = lax.axis_size("seq")
    me = lax.axis_index("seq")
    outs = refs[:-7]
    owner_ref, source_ref, count_ref, deltas_ref, anchors_ref, scales_ref, sems = refs[-7:]
    blocks = owner_ref.shape[0]
    rows = deltas_ref.shape[0] // blocks
    capacity = blocks // receivers
    quarter = deltas_ref.shape[0] // 4
    parts = [pl.ds(index * quarter, quarter) for index in range(4)]
    loads = [
        pltpu.make_async_copy(source, target, sems.at[index])
        for index, (source, target) in enumerate(
            [(owner_any, owner_ref), (scales_any, scales_ref), (anchors_any, anchors_ref)]
            + [(deltas_any.at[part], deltas_ref.at[part]) for part in parts]
        )
    ]
    for load in loads:
        load.start()
    bits = capacity.bit_length()
    narrow = receivers * bits < 32
    if not narrow:
        for owner in range(receivers):
            count_ref[owner] = owner * capacity
    loads[0].wait()

    def find(block, counts):
        owner = owner_ref[block]
        if narrow:
            shift = owner * bits
            slot = owner * capacity + ((counts >> shift) & ((1 << bits) - 1))
            counts = counts + (jnp.int32(1) << shift)
        else:
            slot = count_ref[owner]
            count_ref[owner] = slot + 1
        source_ref[slot] = block
        return counts

    lax.fori_loop(0, blocks, find, jnp.int32(0), unroll=16)
    for load in loads[1:]:
        load.wait()
    odd = lax.broadcasted_iota(jnp.int32, (8, HD), 0) % 2 == 1
    scale = jnp.where(odd, scales_ref[1:2, :], scales_ref[0:1, :])[None]
    for (k, start, count), out_ref in zip(plan, outs):
        first = partner(me, k, receivers) * capacity + start

        def one_slot(slot, carry, first=first, out_ref=out_ref):
            block = source_ref[first + slot]
            anchor = jnp.where(
                odd, anchors_ref[pl.ds(2 * block + 1, 1), :], anchors_ref[pl.ds(2 * block, 1), :]
            )[None]
            here = pl.ds(pl.multiple_of(block * rows, rows), rows)
            delta = deltas_ref[here, :].astype(jnp.float32)
            decoded = anchor + scale * delta.reshape(rows // 8, 8, HD)
            out_ref[pl.ds(pl.multiple_of(slot * rows, rows), rows), :] = decoded.reshape(rows, HD).astype(
                jnp.bfloat16
            )
            return carry

        lax.fori_loop(0, count, one_slot, 0, unroll=min(16, count))


def pieces(values):
    high = values.astype(jnp.bfloat16)
    rest = values - high.astype(jnp.float32)
    middle = rest.astype(jnp.bfloat16)
    low = (rest - middle.astype(jnp.float32)).astype(jnp.bfloat16)
    return [high, middle, low]


def message_shape(width):
    parts = max(1, width // HD)
    return parts * HD + -(-parts * STAT_ROWS // 16) * 16, width // parts


def packed(partial):
    summed, top, total = partial
    rows, lanes = message_shape(top.shape[1])
    sums = summed.astype(jnp.bfloat16)
    stats = pieces(top) + pieces(total)
    here = [slice(first, first + lanes) for first in range(0, top.shape[1], lanes)]
    filled = [sums[:, part] for part in here] + [row[:, part] for part in here for row in stats]
    rest = rows - len(here) * (HD + STAT_ROWS)
    return jnp.concatenate(filled + [jnp.zeros((rest, lanes), jnp.bfloat16)], axis=0)


def unpacked(block):
    parts = block.shape[0] // HD
    sums = [block[part * HD : (part + 1) * HD, :] for part in range(parts)]
    stats = block[parts * HD :, :].astype(jnp.float32)

    def row(first):
        found = []
        for part in range(parts):
            at = part * STAT_ROWS + first
            found.append(stats[at : at + 1] + stats[at + 1 : at + 2] + stats[at + 2 : at + 3])
        return jnp.concatenate(found, axis=1)

    return jnp.concatenate(sums, axis=1).astype(jnp.float32), row(0), row(3)


def held(partial):
    summed, top, total = partial
    rest = jnp.zeros((KEEP_ROWS - 2, top.shape[1]), jnp.float32)
    return jnp.concatenate([summed, top, total, rest], axis=0)


def taken(block):
    return block[0:HD, :], block[HD : HD + 1, :], block[HD + 1 : HD + 2, :]


def joined(one, other):
    top = jnp.maximum(one[1], other[1])
    scale_one = jnp.exp2((one[1] - top) * RATE)
    scale_other = jnp.exp2((other[1] - top) * RATE)
    return (
        one[0] * scale_one + other[0] * scale_other,
        top,
        one[2] * scale_one + other[2] * scale_other,
    )


def difference(index):
    total = 0
    while index:
        total, index = total ^ index, index >> 1
    return total


def attend(parity, width, keys_ref, turned_ref, asked_ref, store):
    me = lax.axis_index("seq")
    far = lax.axis_size("seq") // 2
    lower = 1 - me // far
    asked = asked_ref.shape[0]

    def partial_of(here):
        scores = lax.dot_general(
            keys_ref[...], here, (((1,), (1,)), ((), ())), preferred_element_type=jnp.float32
        )
        top = jnp.max(scores, axis=0, keepdims=True)
        weights = jnp.exp2((scores - top) * RATE)
        total = jnp.sum(weights, axis=0, keepdims=True)
        summed = jnp.dot(turned_ref[...], weights.astype(jnp.bfloat16), preferred_element_type=jnp.float32)
        return summed, top, total

    if width % HD == 0:
        for index in range(asked // width // 2):
            place = 2 * index + parity
            there = (me ^ difference(place) ^ (lower if place >= far else 0)) * width
            store(index, partial_of(asked_ref[pl.ds(pl.multiple_of(there, width), width), :]))
        return
    tile = min(2 * HD, asked)
    parts = tile // width

    def one_tile(tile_index, carry):
        here = asked_ref[pl.ds(pl.multiple_of(tile_index * tile, tile), tile), :]
        summed, top, total = partial_of(here)
        for part in range(parts):
            lanes = slice(part * width, (part + 1) * width)
            apart = (tile_index * parts + part) ^ me
            apart = apart ^ (apart // far * lower)
            place = apart ^ (apart >> 1)

            @pl.when(place % 2 == parity)
            def _(lanes=lanes, place=place):
                store(place // 2, (summed[:, lanes], top[:, lanes], total[:, lanes]))

        return carry

    lax.fori_loop(0, asked // tile, one_tile, 0)


def first_kernel(*refs):
    me = lax.axis_index("seq")
    sources, send_ref, keys_ref, turned_ref, asked_ref, own_ref, *targets = refs[:7], *refs[7:-3]
    wide_ref, values_ref, sems = refs[-3:]
    loads = [
        pltpu.make_async_copy(source, target, sems.at[index])
        for index, (source, target) in enumerate(zip(sources, targets))
    ]
    for load in loads:
        load.start()
    deltas_ref, anchors_ref, scales_ref, lengths_ref, request_ref, queries_ref, new_ref = targets
    blocks = anchors_ref.shape[0] // 2
    rows = deltas_ref.shape[0] // blocks
    tokens = rows // 2
    requests = lengths_ref.shape[0]
    asked = queries_ref.shape[0]
    per_row = asked // request_ref.shape[0]
    width = own_ref.shape[1]
    for load in loads[2:]:
        load.wait()

    lane = lax.broadcasted_iota(jnp.int32, (1, HD), 1)
    first = jnp.zeros((1, HD), jnp.int32)
    last = jnp.zeros((1, HD), jnp.int32)
    end = 0 - me * (blocks * tokens)
    for request in range(requests):
        start = end
        end = end + lengths_ref[request]
        first = jnp.where(lane == request, start, first)
        last = jnp.where(lane == request, end, last)
    place = lax.broadcasted_iota(jnp.int32, (blocks * tokens, HD), 0)
    keys_ref[:, HD:] = jnp.where((place >= first) & (place < last), 1.0, 0.0).astype(jnp.bfloat16)

    asked_ref[:, 0:HD] = queries_ref[...]
    wide_lane = lax.broadcasted_iota(jnp.int32, (per_row, HD), 1)

    def one_row(row, carry):
        asked_ref[pl.ds(pl.multiple_of(row * per_row, per_row), per_row), HD:] = jnp.where(
            (wide_lane == request_ref[row]) | (wide_lane >= requests), 0.0, FAR
        ).astype(jnp.bfloat16)
        return carry

    lax.fori_loop(0, request_ref.shape[0], one_row, 0, unroll=16)

    fresh = new_ref.shape[0] // 4
    new = new_ref[...].astype(jnp.float32).reshape(fresh, 4, HD)
    mine = queries_ref[pl.ds(pl.multiple_of(me * width, width), width), :]
    of_row = lax.broadcasted_iota(jnp.int32, (fresh, width), 1) // (GQ * STEPS)
    same = of_row == lax.broadcasted_iota(jnp.int32, (fresh, width), 0)
    step = lax.broadcasted_iota(jnp.int32, (1, width), 1) % STEPS
    own_scores = []
    for which in range(STEPS):
        scored = lax.dot_general(
            new[:, 2 * which, :].astype(jnp.bfloat16),
            mine,
            (((1,), (1,)), ((), ())),
            preferred_element_type=jnp.float32,
        )
        picked = jnp.sum(jnp.where(same, scored, 0.0), axis=0, keepdims=True)
        own_scores.append(jnp.where(step >= which, picked, FAR))
    own_top = jnp.maximum(own_scores[0], own_scores[1])
    own_total = jnp.zeros((1, width), jnp.float32)
    own_summed = jnp.zeros((HD, width), jnp.float32)
    for which in range(STEPS):
        weight = jnp.exp2((own_scores[which] - own_top) * RATE)
        own_total = own_total + weight
        spread = jnp.where(same, weight, 0.0).astype(jnp.bfloat16)
        own_summed = own_summed + lax.dot_general(
            new[:, 2 * which + 1, :].astype(jnp.bfloat16),
            spread,
            (((0,), (0,)), ((), ())),
            preferred_element_type=jnp.float32,
        )
    own_ref[...] = held((own_summed, own_top, own_total))

    for load in loads[:2]:
        load.wait()
    wide_ref[0 : blocks * rows, :] = deltas_ref[...].astype(jnp.float32)
    scale_key = scales_ref[0:1, :]
    scale_value = scales_ref[1:2, :]

    def one_block(block, carry):
        here = pl.ds(pl.multiple_of(block * tokens, tokens), tokens)
        key = wide_ref[pl.ds(block * rows, tokens, stride=2), :]
        value = wide_ref[pl.ds(block * rows + 1, tokens, stride=2), :]
        keys_ref[here, 0:HD] = (anchors_ref[pl.ds(2 * block, 1), :] + scale_key * key).astype(jnp.bfloat16)
        values_ref[here, :] = (anchors_ref[pl.ds(2 * block + 1, 1), :] + scale_value * value).astype(
            jnp.bfloat16
        )
        return carry

    lax.fori_loop(0, blocks, one_block, 0, unroll=16)
    turned_ref[...] = values_ref[...].T

    def store(index, partial):
        send_ref[index] = packed(partial)

    attend(1, width, keys_ref, turned_ref, asked_ref, store)


def second_kernel(keys_ref, turned_ref, asked_ref, own_ref, keep_ref):
    def store(index, partial):
        keep_ref[index] = held(partial)

    attend(0, keep_ref.shape[2], keys_ref, turned_ref, asked_ref, store)
    keep_ref[0] = held(joined(taken(keep_ref[0]), taken(own_ref[...])))


def join_kernel(keep_ref, got_ref, send_ref, next_ref):
    for index in range(keep_ref.shape[0]):
        partial = joined(taken(keep_ref[index]), unpacked(got_ref[index]))
        if index % 2 == 1:
            send_ref[index // 2] = packed(partial)
        else:
            next_ref[index // 2] = held(partial)


def settle(plan, handed, pages, sems):
    receivers = lax.axis_size("seq")
    me = lax.axis_index("seq")
    rows = pages.shape[0] // receivers
    copies = []
    for index, (k, start, slots) in enumerate(plan):
        size = handed[index].shape[0]
        sender = source(me, k, receivers) if k else me
        first = pl.multiple_of(sender * rows + start * (size // slots), size)
        copies.append(pltpu.make_async_copy(handed[index], pages.at[pl.ds(first, size), :], sems.at[index]))
        copies[-1].start()
    return copies


def settle_kernel(plan, *refs):
    *handed, pages, sems = refs
    for copy in settle(plan, handed, pages, sems):
        copy.wait()


def finish_kernel(plan, keep_ref, got_ref, _, *refs):
    *handed, out_any, pages, out_ref, sems = refs
    copies = settle(plan, handed, pages, sems)
    summed, _, total = joined(taken(keep_ref[0]), unpacked(got_ref[0]))
    out_ref[...] = (summed / total).T.astype(jnp.bfloat16)
    copies.append(pltpu.make_async_copy(out_ref, out_any, sems.at[len(copies)]))
    copies[-1].start()
    for copy in copies:
        copy.wait()


def in_hbm(arrays):
    return [pltpu.with_memory_space_constraint(array, pltpu.HBM) for array in arrays]


def per_device(lengths, owner_map, row_request, deltas, anchors, scales, queries, new_kv):
    blocks = anchors.shape[0]
    tokens = deltas.shape[0]
    senders = lax.axis_size("seq")
    me = lax.axis_index("seq")
    rows, steps, _ = queries.shape
    rows_dev = new_kv.shape[0]
    width = rows_dev * GQ * steps
    small = pltpu.CompilerParams(vmem_limit_bytes=8 * 1024 * 1024)

    flat_deltas = deltas.reshape(tokens * 2, HD)
    flat_anchors = anchors.reshape(blocks * 2, HD)
    flat_queries = queries.reshape(rows, steps, GQ, HD).transpose(0, 2, 1, 3).reshape(-1, HD)
    flat_new = new_kv.reshape(rows_dev * 4, HD)

    whole = jax.ShapeDtypeStruct((tokens * 2, HD), jnp.bfloat16)
    ahead, behind, own = messages(senders, blocks // senders)
    block_rows = tokens * 2 // blocks

    def place(plan, deltas):
        return pl.pallas_call(
            functools.partial(place_kernel, plan),
            out_shape=[jax.ShapeDtypeStruct((slots * block_rows, HD), jnp.bfloat16) for _, _, slots in plan],
            in_specs=[HBM] * 4,
            out_specs=[VMEM] * len(plan),
            scratch_shapes=[
                pltpu.SMEM((blocks,), jnp.int32),
                pltpu.SMEM((blocks,), jnp.int32),
                pltpu.SMEM((senders,), jnp.int32),
                pltpu.VMEM((tokens * 2, HD), jnp.bfloat16),
                pltpu.VMEM((blocks * 2, HD), jnp.float32),
                pltpu.VMEM((2, HD), jnp.float32),
                pltpu.SemaphoreType.DMA((7,)),
            ],
            compiler_params=small,
            name="place",
        )(*in_hbm([owner_map, deltas, flat_anchors, scales]))

    sent = place(ahead, flat_deltas)
    sent, late_deltas = lax.optimization_barrier((sent, flat_deltas))
    got_ahead = [hand(message, k) for message, (k, _, _) in zip(sent, ahead)]

    def leaving(count):
        return jax.ShapeDtypeStruct((count // 2, *message_shape(width)), jnp.bfloat16)

    def staying(count):
        return jax.ShapeDtypeStruct((count // 2, HD + KEEP_ROWS, width), jnp.float32)

    needed = (late_deltas, flat_anchors, scales, lengths, row_request, flat_queries, flat_new)
    roomy = pltpu.CompilerParams(vmem_limit_bytes=32 * 1024 * 1024)
    send, *common = pl.pallas_call(
        first_kernel,
        out_shape=[
            leaving(senders),
            jax.ShapeDtypeStruct((tokens, 2 * HD), jnp.bfloat16),
            jax.ShapeDtypeStruct((HD, tokens), jnp.bfloat16),
            jax.ShapeDtypeStruct((rows * GQ * steps, 2 * HD), jnp.bfloat16),
            jax.ShapeDtypeStruct((HD + KEEP_ROWS, width), jnp.float32),
        ],
        in_specs=[HBM] * len(needed),
        out_specs=[VMEM] * 5,
        scratch_shapes=[
            (pltpu.SMEM if array.dtype == jnp.int32 else pltpu.VMEM)(array.shape, array.dtype)
            for array in needed
        ]
        + [
            pltpu.VMEM((tokens * 2 + 16, HD), jnp.float32),
            pltpu.VMEM((tokens, HD), jnp.bfloat16),
            pltpu.SemaphoreType.DMA((len(needed),)),
        ],
        compiler_params=roomy,
        name="attend_leaving",
    )(*in_hbm(needed))

    k, count = 1, senders // 2
    send, late_deltas = lax.optimization_barrier((send, late_deltas))
    passed = exchange(send, k)
    *sent, mine = place(behind + own, late_deltas)
    got = got_ahead[1:] + [hand(message, k) for message, (k, _, _) in zip(sent, behind)]
    keep = pl.pallas_call(
        second_kernel,
        out_shape=staying(senders),
        in_specs=[VMEM] * 4,
        out_specs=VMEM,
        compiler_params=roomy,
        name="attend_staying",
    )(*common)
    while count > 1:
        send, keep = pl.pallas_call(
            join_kernel,
            out_shape=[leaving(count), staying(count)],
            in_specs=[VMEM] * 2,
            out_specs=[VMEM] * 2,
            compiler_params=small,
            name="join",
        )(keep, passed)
        k, count = 2 * k + 1, count // 2
        passed = exchange(send, k)
    settled = ahead[:1] + own
    pages = pl.pallas_call(
        functools.partial(settle_kernel, settled),
        out_shape=whole,
        in_specs=[ANY] * len(settled),
        out_specs=HBM,
        scratch_shapes=[pltpu.SemaphoreType.DMA((len(settled),))],
        compiler_params=small,
        name="settle",
    )(got_ahead[0], mine)
    attended, pages = pl.pallas_call(
        functools.partial(finish_kernel, ahead[1:] + behind),
        out_shape=[jax.ShapeDtypeStruct((width, HD), jnp.bfloat16), whole],
        in_specs=[VMEM] * 2 + [HBM] + [ANY] * len(got),
        out_specs=[HBM, HBM],
        scratch_shapes=[
            pltpu.VMEM((width, HD), jnp.bfloat16),
            pltpu.SemaphoreType.DMA((len(got) + 1,)),
        ],
        input_output_aliases={2: 1},
        compiler_params=small,
        name="finish",
    )(keep, passed, pages, *got)
    pages = pages.reshape(blocks, tokens // blocks, 2, HD)
    attended = (
        attended.reshape(rows_dev, GQ, steps, HD).transpose(0, 2, 1, 3).reshape(rows_dev, steps, GQ * HD)
    )
    return pages, attended


def solution(mesh):
    placed = (
        P("groups"),
        P(("groups", "seq")),
        P("groups"),
        P(("groups", "seq"), None, "tp"),
        P(("groups", "seq"), None, "tp"),
        P("groups", "tp"),
        P("groups", None, "tp"),
        P(("groups", "seq"), None, None, "tp"),
    )
    return jax.shard_map(
        per_device,
        mesh=mesh,
        in_specs=placed,
        out_specs=(P(("groups", "seq"), None, None, "tp"), P(("groups", "seq"), None, "tp")),
        check_vma=False,
    )
```

```python
import functools

import jax
import jax.numpy as jnp
from jax import lax
from jax.experimental import pallas as pl
from jax.experimental.pallas import tpu as pltpu
from jax.sharding import PartitionSpec as P

HD = 128
GQ = 8
STEPS = 2
STAT_ROWS = 6
KEEP_ROWS = 8
FAR = -1e30
RATE = HD ** (-0.5) * 1.4426950408889634

VMEM = pl.BlockSpec(memory_space=pltpu.VMEM)
HBM = pl.BlockSpec(memory_space=pltpu.HBM)
ANY = pl.BlockSpec(memory_space=pl.ANY)
SMEM = pl.BlockSpec(memory_space=pltpu.SMEM)


def inner(device, count):
    return (device ^ (device // (count // 2))) & 1


def partner(device, k, count):
    far = count // 2
    if k == far:
        return device ^ (1 + inner(device, count) * (far - 1))
    if k == 1:
        return device ^ (far - inner(device, count) * (far - 1))
    return device ^ k


def source(device, k, count):
    far = count // 2
    if k == far:
        return device ^ (far - inner(device, count) * (far - 1))
    if k == 1:
        return device ^ (1 + inner(device, count) * (far - 1))
    return device ^ k


def exchange(message, k):
    count = lax.axis_size("seq")
    return lax.ppermute(message, "seq", [(i, i ^ k) for i in range(count)])


def hand(message, k):
    count = lax.axis_size("seq")
    return lax.ppermute(message, "seq", [(i, partner(i, k, count)) for i in range(count)])


def messages(count, capacity):
    half = capacity // 2
    ahead = [(k, 0, capacity) for k in range(count // 2, count)]
    behind = [(k, first, half) for k in reversed(range(1, count // 2)) for first in (0, half)]
    return ahead, behind, [(0, 0, capacity)]


def place_kernel(plan, owner_any, deltas_any, anchors_any, scales_any, *refs):
    receivers = lax.axis_size("seq")
    me = lax.axis_index("seq")
    outs = refs[:-7]
    owner_ref, source_ref, count_ref, deltas_ref, anchors_ref, scales_ref, sems = refs[-7:]
    blocks = owner_ref.shape[0]
    rows = deltas_ref.shape[0] // blocks
    capacity = blocks // receivers
    quarter = deltas_ref.shape[0] // 4
    parts = [pl.ds(index * quarter, quarter) for index in range(4)]
    loads = [
        pltpu.make_async_copy(source, target, sems.at[index])
        for index, (source, target) in enumerate(
            [(owner_any, owner_ref), (scales_any, scales_ref), (anchors_any, anchors_ref)]
            + [(deltas_any.at[part], deltas_ref.at[part]) for part in parts]
        )
    ]
    for load in loads:
        load.start()
    bits = capacity.bit_length()
    narrow = receivers * bits < 32
    if not narrow:
        for owner in range(receivers):
            count_ref[owner] = owner * capacity
    loads[0].wait()

    def find(block, counts):
        owner = owner_ref[block]
        if narrow:
            shift = owner * bits
            slot = owner * capacity + ((counts >> shift) & ((1 << bits) - 1))
            counts = counts + (jnp.int32(1) << shift)
        else:
            slot = count_ref[owner]
            count_ref[owner] = slot + 1
        source_ref[slot] = block
        return counts

    lax.fori_loop(0, blocks, find, jnp.int32(0), unroll=16)
    for load in loads[1:]:
        load.wait()
    odd = lax.broadcasted_iota(jnp.int32, (8, HD), 0) % 2 == 1
    scale = jnp.where(odd, scales_ref[1:2, :], scales_ref[0:1, :])[None]
    for (k, start, count), out_ref in zip(plan, outs):
        first = partner(me, k, receivers) * capacity + start

        def one_slot(slot, carry, first=first, out_ref=out_ref):
            block = source_ref[first + slot]
            anchor = jnp.where(
                odd, anchors_ref[pl.ds(2 * block + 1, 1), :], anchors_ref[pl.ds(2 * block, 1), :]
            )[None]
            here = pl.ds(pl.multiple_of(block * rows, rows), rows)
            delta = deltas_ref[here, :].astype(jnp.float32)
            decoded = anchor + scale * delta.reshape(rows // 8, 8, HD)
            out_ref[pl.ds(pl.multiple_of(slot * rows, rows), rows), :] = decoded.reshape(rows, HD).astype(
                jnp.bfloat16
            )
            return carry

        lax.fori_loop(0, count, one_slot, 0, unroll=min(16, count))


def pieces(values):
    high = values.astype(jnp.bfloat16)
    rest = values - high.astype(jnp.float32)
    middle = rest.astype(jnp.bfloat16)
    low = (rest - middle.astype(jnp.float32)).astype(jnp.bfloat16)
    return [high, middle, low]


def message_shape(width):
    parts = max(1, width // HD)
    return parts * HD + -(-parts * STAT_ROWS // 16) * 16, width // parts


def packed(partial):
    summed, top, total = partial
    rows, lanes = message_shape(top.shape[1])
    sums = summed.astype(jnp.bfloat16)
    stats = pieces(top) + pieces(total)
    here = [slice(first, first + lanes) for first in range(0, top.shape[1], lanes)]
    filled = [sums[:, part] for part in here] + [row[:, part] for part in here for row in stats]
    rest = rows - len(here) * (HD + STAT_ROWS)
    return jnp.concatenate(filled + [jnp.zeros((rest, lanes), jnp.bfloat16)], axis=0)


def unpacked(block):
    parts = block.shape[0] // HD
    sums = [block[part * HD : (part + 1) * HD, :] for part in range(parts)]
    stats = block[parts * HD :, :].astype(jnp.float32)

    def row(first):
        found = []
        for part in range(parts):
            at = part * STAT_ROWS + first
            found.append(stats[at : at + 1] + stats[at + 1 : at + 2] + stats[at + 2 : at + 3])
        return jnp.concatenate(found, axis=1)

    return jnp.concatenate(sums, axis=1).astype(jnp.float32), row(0), row(3)


def held(partial):
    summed, top, total = partial
    rest = jnp.zeros((KEEP_ROWS - 2, top.shape[1]), jnp.float32)
    return jnp.concatenate([summed, top, total, rest], axis=0)


def taken(block):
    return block[0:HD, :], block[HD : HD + 1, :], block[HD + 1 : HD + 2, :]


def joined(one, other):
    top = jnp.maximum(one[1], other[1])
    scale_one = jnp.exp2((one[1] - top) * RATE)
    scale_other = jnp.exp2((other[1] - top) * RATE)
    return (
        one[0] * scale_one + other[0] * scale_other,
        top,
        one[2] * scale_one + other[2] * scale_other,
    )


def difference(index):
    total = 0
    while index:
        total, index = total ^ index, index >> 1
    return total


def attend(parity, width, keys_ref, turned_ref, asked_ref, store):
    me = lax.axis_index("seq")
    asked = asked_ref.shape[0]

    def partial_of(here):
        scores = lax.dot_general(
            keys_ref[...], here, (((1,), (1,)), ((), ())), preferred_element_type=jnp.float32
        )
        top = jnp.max(scores, axis=0, keepdims=True)
        weights = jnp.exp2((scores - top) * RATE)
        total = jnp.sum(weights, axis=0, keepdims=True)
        summed = jnp.dot(turned_ref[...], weights.astype(jnp.bfloat16), preferred_element_type=jnp.float32)
        return summed, top, total

    if width % HD == 0:
        for index in range(asked // width // 2):
            there = (me ^ difference(2 * index + parity)) * width
            store(index, partial_of(asked_ref[pl.ds(pl.multiple_of(there, width), width), :]))
        return
    tile = min(2 * HD, asked)
    parts = tile // width

    def one_tile(tile_index, carry):
        here = asked_ref[pl.ds(pl.multiple_of(tile_index * tile, tile), tile), :]
        summed, top, total = partial_of(here)
        for part in range(parts):
            lanes = slice(part * width, (part + 1) * width)
            apart = (tile_index * parts + part) ^ me
            place = apart ^ (apart >> 1)

            @pl.when(place % 2 == parity)
            def _(lanes=lanes, place=place):
                store(place // 2, (summed[:, lanes], top[:, lanes], total[:, lanes]))

        return carry

    lax.fori_loop(0, asked // tile, one_tile, 0)


def first_kernel(*refs):
    me = lax.axis_index("seq")
    sources, send_ref, keys_ref, turned_ref, asked_ref, own_ref, *targets = refs[:7], *refs[7:-3]
    wide_ref, values_ref, sems = refs[-3:]
    loads = [
        pltpu.make_async_copy(source, target, sems.at[index])
        for index, (source, target) in enumerate(zip(sources, targets))
    ]
    for load in loads:
        load.start()
    deltas_ref, anchors_ref, scales_ref, lengths_ref, request_ref, queries_ref, new_ref = targets
    blocks = anchors_ref.shape[0] // 2
    rows = deltas_ref.shape[0] // blocks
    tokens = rows // 2
    requests = lengths_ref.shape[0]
    asked = queries_ref.shape[0]
    per_row = asked // request_ref.shape[0]
    width = own_ref.shape[1]
    for load in loads[2:]:
        load.wait()

    lane = lax.broadcasted_iota(jnp.int32, (1, HD), 1)
    first = jnp.zeros((1, HD), jnp.int32)
    last = jnp.zeros((1, HD), jnp.int32)
    end = 0 - me * (blocks * tokens)
    for request in range(requests):
        start = end
        end = end + lengths_ref[request]
        first = jnp.where(lane == request, start, first)
        last = jnp.where(lane == request, end, last)
    place = lax.broadcasted_iota(jnp.int32, (blocks * tokens, HD), 0)
    keys_ref[:, HD:] = jnp.where((place >= first) & (place < last), 1.0, 0.0).astype(jnp.bfloat16)

    asked_ref[:, 0:HD] = queries_ref[...]
    wide_lane = lax.broadcasted_iota(jnp.int32, (per_row, HD), 1)

    def one_row(row, carry):
        asked_ref[pl.ds(pl.multiple_of(row * per_row, per_row), per_row), HD:] = jnp.where(
            (wide_lane == request_ref[row]) | (wide_lane >= requests), 0.0, FAR
        ).astype(jnp.bfloat16)
        return carry

    lax.fori_loop(0, request_ref.shape[0], one_row, 0, unroll=16)

    fresh = new_ref.shape[0] // 4
    new = new_ref[...].astype(jnp.float32).reshape(fresh, 4, HD)
    mine = queries_ref[pl.ds(pl.multiple_of(me * width, width), width), :]
    of_row = lax.broadcasted_iota(jnp.int32, (fresh, width), 1) // (GQ * STEPS)
    same = of_row == lax.broadcasted_iota(jnp.int32, (fresh, width), 0)
    step = lax.broadcasted_iota(jnp.int32, (1, width), 1) % STEPS
    own_scores = []
    for which in range(STEPS):
        scored = lax.dot_general(
            new[:, 2 * which, :].astype(jnp.bfloat16),
            mine,
            (((1,), (1,)), ((), ())),
            preferred_element_type=jnp.float32,
        )
        picked = jnp.sum(jnp.where(same, scored, 0.0), axis=0, keepdims=True)
        own_scores.append(jnp.where(step >= which, picked, FAR))
    own_top = jnp.maximum(own_scores[0], own_scores[1])
    own_total = jnp.zeros((1, width), jnp.float32)
    own_summed = jnp.zeros((HD, width), jnp.float32)
    for which in range(STEPS):
        weight = jnp.exp2((own_scores[which] - own_top) * RATE)
        own_total = own_total + weight
        spread = jnp.where(same, weight, 0.0).astype(jnp.bfloat16)
        own_summed = own_summed + lax.dot_general(
            new[:, 2 * which + 1, :].astype(jnp.bfloat16),
            spread,
            (((0,), (0,)), ((), ())),
            preferred_element_type=jnp.float32,
        )
    own_ref[...] = held((own_summed, own_top, own_total))

    for load in loads[:2]:
        load.wait()
    wide_ref[0 : blocks * rows, :] = deltas_ref[...].astype(jnp.float32)
    scale_key = scales_ref[0:1, :]
    scale_value = scales_ref[1:2, :]

    def one_block(block, carry):
        here = pl.ds(pl.multiple_of(block * tokens, tokens), tokens)
        key = wide_ref[pl.ds(block * rows, tokens, stride=2), :]
        value = wide_ref[pl.ds(block * rows + 1, tokens, stride=2), :]
        keys_ref[here, 0:HD] = (anchors_ref[pl.ds(2 * block, 1), :] + scale_key * key).astype(jnp.bfloat16)
        values_ref[here, :] = (anchors_ref[pl.ds(2 * block + 1, 1), :] + scale_value * value).astype(
            jnp.bfloat16
        )
        return carry

    lax.fori_loop(0, blocks, one_block, 0, unroll=16)
    turned_ref[...] = values_ref[...].T

    def store(index, partial):
        send_ref[index] = packed(partial)

    attend(1, width, keys_ref, turned_ref, asked_ref, store)


def second_kernel(keys_ref, turned_ref, asked_ref, own_ref, keep_ref):
    def store(index, partial):
        keep_ref[index] = held(partial)

    attend(0, keep_ref.shape[2], keys_ref, turned_ref, asked_ref, store)
    keep_ref[0] = held(joined(taken(keep_ref[0]), taken(own_ref[...])))


def join_kernel(keep_ref, got_ref, send_ref, next_ref):
    for index in range(keep_ref.shape[0]):
        partial = joined(taken(keep_ref[index]), unpacked(got_ref[index]))
        if index % 2 == 1:
            send_ref[index // 2] = packed(partial)
        else:
            next_ref[index // 2] = held(partial)


def settle_kernel(plan, *refs):
    pages, sems = refs[-2:]
    receivers = lax.axis_size("seq")
    me = lax.axis_index("seq")
    rows = pages.shape[0] // receivers
    copies = []
    for index, ((k, start, slots), handed) in enumerate(zip(plan, refs)):
        size = handed.shape[0]
        sender = source(me, k, receivers) if k else me
        first = pl.multiple_of(sender * rows + start * (size // slots), size)
        copies.append(pltpu.make_async_copy(handed, pages.at[pl.ds(first, size), :], sems.at[index]))
        copies[-1].start()
    for copy in copies:
        copy.wait()


def finish_kernel(keep_ref, got_ref, out_any, out_ref, sem):
    summed, _, total = joined(taken(keep_ref[0]), unpacked(got_ref[0]))
    out_ref[...] = (summed / total).T.astype(jnp.bfloat16)
    store = pltpu.make_async_copy(out_ref, out_any, sem)
    store.start()
    store.wait()


def in_hbm(arrays):
    return [pltpu.with_memory_space_constraint(array, pltpu.HBM) for array in arrays]


def per_device(lengths, owner_map, row_request, deltas, anchors, scales, queries, new_kv):
    blocks = anchors.shape[0]
    tokens = deltas.shape[0]
    senders = lax.axis_size("seq")
    me = lax.axis_index("seq")
    rows, steps, _ = queries.shape
    rows_dev = new_kv.shape[0]
    width = rows_dev * GQ * steps
    small = pltpu.CompilerParams(vmem_limit_bytes=8 * 1024 * 1024)

    flat_deltas = deltas.reshape(tokens * 2, HD)
    flat_anchors = anchors.reshape(blocks * 2, HD)
    flat_queries = queries.reshape(rows, steps, GQ, HD).transpose(0, 2, 1, 3).reshape(-1, HD)
    flat_new = new_kv.reshape(rows_dev * 4, HD)

    whole = jax.ShapeDtypeStruct((tokens * 2, HD), jnp.bfloat16)
    ahead, behind, own = messages(senders, blocks // senders)
    block_rows = tokens * 2 // blocks

    def place(plan, deltas):
        return pl.pallas_call(
            functools.partial(place_kernel, plan),
            out_shape=[jax.ShapeDtypeStruct((slots * block_rows, HD), jnp.bfloat16) for _, _, slots in plan],
            in_specs=[HBM] * 4,
            out_specs=[VMEM] * len(plan),
            scratch_shapes=[
                pltpu.SMEM((blocks,), jnp.int32),
                pltpu.SMEM((blocks,), jnp.int32),
                pltpu.SMEM((senders,), jnp.int32),
                pltpu.VMEM((tokens * 2, HD), jnp.bfloat16),
                pltpu.VMEM((blocks * 2, HD), jnp.float32),
                pltpu.VMEM((2, HD), jnp.float32),
                pltpu.SemaphoreType.DMA((7,)),
            ],
            compiler_params=small,
            name="place",
        )(*in_hbm([owner_map, deltas, flat_anchors, scales]))

    sent = place(ahead, flat_deltas)
    sent, late_deltas = lax.optimization_barrier((sent, flat_deltas))
    got_ahead = [hand(message, k) for message, (k, _, _) in zip(sent, ahead)]

    def leaving(count):
        return jax.ShapeDtypeStruct((count // 2, *message_shape(width)), jnp.bfloat16)

    def staying(count):
        return jax.ShapeDtypeStruct((count // 2, HD + KEEP_ROWS, width), jnp.float32)

    needed = (late_deltas, flat_anchors, scales, lengths, row_request, flat_queries, flat_new)
    roomy = pltpu.CompilerParams(vmem_limit_bytes=32 * 1024 * 1024)
    send, *common = pl.pallas_call(
        first_kernel,
        out_shape=[
            leaving(senders),
            jax.ShapeDtypeStruct((tokens, 2 * HD), jnp.bfloat16),
            jax.ShapeDtypeStruct((HD, tokens), jnp.bfloat16),
            jax.ShapeDtypeStruct((rows * GQ * steps, 2 * HD), jnp.bfloat16),
            jax.ShapeDtypeStruct((HD + KEEP_ROWS, width), jnp.float32),
        ],
        in_specs=[HBM] * len(needed),
        out_specs=[VMEM] * 5,
        scratch_shapes=[
            (pltpu.SMEM if array.dtype == jnp.int32 else pltpu.VMEM)(array.shape, array.dtype)
            for array in needed
        ]
        + [
            pltpu.VMEM((tokens * 2 + 16, HD), jnp.float32),
            pltpu.VMEM((tokens, HD), jnp.bfloat16),
            pltpu.SemaphoreType.DMA((len(needed),)),
        ],
        compiler_params=roomy,
        name="attend_leaving",
    )(*in_hbm(needed))

    k, count = 1, senders // 2
    send, late_deltas = lax.optimization_barrier((send, late_deltas))
    passed = exchange(send, k)
    *sent, mine = place(behind + own, late_deltas)
    got = got_ahead[1:] + [hand(message, k) for message, (k, _, _) in zip(sent, behind)]
    keep = pl.pallas_call(
        second_kernel,
        out_shape=staying(senders),
        in_specs=[VMEM] * 4,
        out_specs=VMEM,
        compiler_params=roomy,
        name="attend_staying",
    )(*common)
    while count > 1:
        send, keep = pl.pallas_call(
            join_kernel,
            out_shape=[leaving(count), staying(count)],
            in_specs=[VMEM] * 2,
            out_specs=[VMEM] * 2,
            compiler_params=small,
            name="join",
        )(keep, passed)
        k, count = 2 * k + 1, count // 2
        passed = exchange(send, k)
    def settle(plan, handed, pages=None):
        before = [] if pages is None else [pages]
        return pl.pallas_call(
            functools.partial(settle_kernel, plan),
            out_shape=whole,
            in_specs=[ANY] * len(plan) + [HBM] * len(before),
            out_specs=HBM,
            scratch_shapes=[pltpu.SemaphoreType.DMA((len(plan),))],
            input_output_aliases={len(plan): 0} if before else {},
            compiler_params=small,
            name="settle",
        )(*handed, *before)

    pages = settle(ahead[:1] + own, [got_ahead[0], mine])
    pages = settle(ahead[1:] + behind, got, pages)
    keep, pages = lax.optimization_barrier((keep, pages))
    attended = pl.pallas_call(
        finish_kernel,
        out_shape=jax.ShapeDtypeStruct((width, HD), jnp.bfloat16),
        in_specs=[VMEM] * 2,
        out_specs=HBM,
        scratch_shapes=[pltpu.VMEM((width, HD), jnp.bfloat16), pltpu.SemaphoreType.DMA],
        compiler_params=small,
        name="finish",
    )(keep, passed)
    pages = pages.reshape(blocks, tokens // blocks, 2, HD)
    attended = (
        attended.reshape(rows_dev, GQ, steps, HD).transpose(0, 2, 1, 3).reshape(rows_dev, steps, GQ * HD)
    )
    return pages, attended


def solution(mesh):
    placed = (
        P("groups"),
        P(("groups", "seq")),
        P("groups"),
        P(("groups", "seq"), None, "tp"),
        P(("groups", "seq"), None, "tp"),
        P("groups", "tp"),
        P("groups", None, "tp"),
        P(("groups", "seq"), None, None, "tp"),
    )
    return jax.shard_map(
        per_device,
        mesh=mesh,
        in_specs=placed,
        out_specs=(P(("groups", "seq"), None, None, "tp"), P(("groups", "seq"), None, "tp")),
        check_vma=False,
    )
```

```python
import functools

import jax
import jax.numpy as jnp
from jax import lax
from jax.experimental import pallas as pl
from jax.experimental.pallas import tpu as pltpu
from jax.sharding import PartitionSpec as P

HD = 128
GQ = 8
STEPS = 2
STAT_ROWS = 6
KEEP_ROWS = 8
FAR = -1e30
RATE = HD ** (-0.5) * 1.4426950408889634

VMEM = pl.BlockSpec(memory_space=pltpu.VMEM)
HBM = pl.BlockSpec(memory_space=pltpu.HBM)
ANY = pl.BlockSpec(memory_space=pl.ANY)
SMEM = pl.BlockSpec(memory_space=pltpu.SMEM)


def inner(device, count):
    return (device ^ (device // (count // 2))) & 1


def partner(device, k, count):
    far = count // 2
    if k == far:
        return device ^ (1 + inner(device, count) * (far - 1))
    if k == 1:
        return device ^ (far - inner(device, count) * (far - 1))
    return device ^ k


def source(device, k, count):
    far = count // 2
    if k == far:
        return device ^ (far - inner(device, count) * (far - 1))
    if k == 1:
        return device ^ (1 + inner(device, count) * (far - 1))
    return device ^ k


def exchange(message, k):
    count = lax.axis_size("seq")
    return lax.ppermute(message, "seq", [(i, i ^ k) for i in range(count)])


def hand(message, k):
    count = lax.axis_size("seq")
    return lax.ppermute(message, "seq", [(i, partner(i, k, count)) for i in range(count)])


def messages(count, capacity):
    half = capacity // 2
    ahead = [(k, 0, capacity) for k in reversed(range(count // 2, count))]
    behind = [(k, first, half) for k in reversed(range(1, count // 2)) for first in (0, half)]
    return ahead, behind, [(0, 0, capacity)]


def place_kernel(plan, owner_any, deltas_any, anchors_any, scales_any, *refs):
    receivers = lax.axis_size("seq")
    me = lax.axis_index("seq")
    outs = refs[:-7]
    owner_ref, source_ref, count_ref, deltas_ref, anchors_ref, scales_ref, sems = refs[-7:]
    blocks = owner_ref.shape[0]
    rows = deltas_ref.shape[0] // blocks
    capacity = blocks // receivers
    quarter = deltas_ref.shape[0] // 4
    parts = [pl.ds(index * quarter, quarter) for index in range(4)]
    loads = [
        pltpu.make_async_copy(source, target, sems.at[index])
        for index, (source, target) in enumerate(
            [(owner_any, owner_ref), (scales_any, scales_ref), (anchors_any, anchors_ref)]
            + [(deltas_any.at[part], deltas_ref.at[part]) for part in parts]
        )
    ]
    for load in loads:
        load.start()
    bits = capacity.bit_length()
    narrow = receivers * bits < 32
    if not narrow:
        for owner in range(receivers):
            count_ref[owner] = owner * capacity
    loads[0].wait()

    def find(block, counts):
        owner = owner_ref[block]
        if narrow:
            shift = owner * bits
            slot = owner * capacity + ((counts >> shift) & ((1 << bits) - 1))
            counts = counts + (jnp.int32(1) << shift)
        else:
            slot = count_ref[owner]
            count_ref[owner] = slot + 1
        source_ref[slot] = block
        return counts

    lax.fori_loop(0, blocks, find, jnp.int32(0), unroll=16)
    for load in loads[1:]:
        load.wait()
    odd = lax.broadcasted_iota(jnp.int32, (8, HD), 0) % 2 == 1
    scale = jnp.where(odd, scales_ref[1:2, :], scales_ref[0:1, :])[None]
    for (k, start, count), out_ref in zip(plan, outs):
        first = partner(me, k, receivers) * capacity + start

        def one_slot(slot, carry, first=first, out_ref=out_ref):
            block = source_ref[first + slot]
            anchor = jnp.where(
                odd, anchors_ref[pl.ds(2 * block + 1, 1), :], anchors_ref[pl.ds(2 * block, 1), :]
            )[None]
            here = pl.ds(pl.multiple_of(block * rows, rows), rows)
            delta = deltas_ref[here, :].astype(jnp.float32)
            decoded = anchor + scale * delta.reshape(rows // 8, 8, HD)
            out_ref[pl.ds(pl.multiple_of(slot * rows, rows), rows), :] = decoded.reshape(rows, HD).astype(
                jnp.bfloat16
            )
            return carry

        lax.fori_loop(0, count, one_slot, 0, unroll=min(16, count))


def pieces(values):
    high = values.astype(jnp.bfloat16)
    rest = values - high.astype(jnp.float32)
    middle = rest.astype(jnp.bfloat16)
    low = (rest - middle.astype(jnp.float32)).astype(jnp.bfloat16)
    return [high, middle, low]


def message_shape(width):
    parts = max(1, width // HD)
    return parts * HD + -(-parts * STAT_ROWS // 16) * 16, width // parts


def packed(partial):
    summed, top, total = partial
    rows, lanes = message_shape(top.shape[1])
    sums = summed.astype(jnp.bfloat16)
    stats = pieces(top) + pieces(total)
    here = [slice(first, first + lanes) for first in range(0, top.shape[1], lanes)]
    filled = [sums[:, part] for part in here] + [row[:, part] for part in here for row in stats]
    rest = rows - len(here) * (HD + STAT_ROWS)
    return jnp.concatenate(filled + [jnp.zeros((rest, lanes), jnp.bfloat16)], axis=0)


def unpacked(block):
    parts = block.shape[0] // HD
    sums = [block[part * HD : (part + 1) * HD, :] for part in range(parts)]
    stats = block[parts * HD :, :].astype(jnp.float32)

    def row(first):
        found = []
        for part in range(parts):
            at = part * STAT_ROWS + first
            found.append(stats[at : at + 1] + stats[at + 1 : at + 2] + stats[at + 2 : at + 3])
        return jnp.concatenate(found, axis=1)

    return jnp.concatenate(sums, axis=1).astype(jnp.float32), row(0), row(3)


def held(partial):
    summed, top, total = partial
    rest = jnp.zeros((KEEP_ROWS - 2, top.shape[1]), jnp.float32)
    return jnp.concatenate([summed, top, total, rest], axis=0)


def taken(block):
    return block[0:HD, :], block[HD : HD + 1, :], block[HD + 1 : HD + 2, :]


def joined(one, other):
    top = jnp.maximum(one[1], other[1])
    scale_one = jnp.exp2((one[1] - top) * RATE)
    scale_other = jnp.exp2((other[1] - top) * RATE)
    return (
        one[0] * scale_one + other[0] * scale_other,
        top,
        one[2] * scale_one + other[2] * scale_other,
    )


def difference(index):
    total = 0
    while index:
        total, index = total ^ index, index >> 1
    return total


def attend(parity, width, keys_ref, turned_ref, asked_ref, store):
    me = lax.axis_index("seq")
    asked = asked_ref.shape[0]

    def partial_of(here):
        scores = lax.dot_general(
            keys_ref[...], here, (((1,), (1,)), ((), ())), preferred_element_type=jnp.float32
        )
        top = jnp.max(scores, axis=0, keepdims=True)
        weights = jnp.exp2((scores - top) * RATE)
        total = jnp.sum(weights, axis=0, keepdims=True)
        summed = jnp.dot(turned_ref[...], weights.astype(jnp.bfloat16), preferred_element_type=jnp.float32)
        return summed, top, total

    if width % HD == 0:
        for index in range(asked // width // 2):
            there = (me ^ difference(2 * index + parity)) * width
            store(index, partial_of(asked_ref[pl.ds(pl.multiple_of(there, width), width), :]))
        return
    tile = min(2 * HD, asked)
    parts = tile // width

    def one_tile(tile_index, carry):
        here = asked_ref[pl.ds(pl.multiple_of(tile_index * tile, tile), tile), :]
        summed, top, total = partial_of(here)
        for part in range(parts):
            lanes = slice(part * width, (part + 1) * width)
            apart = (tile_index * parts + part) ^ me
            place = apart ^ (apart >> 1)

            @pl.when(place % 2 == parity)
            def _(lanes=lanes, place=place):
                store(place // 2, (summed[:, lanes], top[:, lanes], total[:, lanes]))

        return carry

    lax.fori_loop(0, asked // tile, one_tile, 0)


def first_kernel(*refs):
    me = lax.axis_index("seq")
    sources, send_ref, keys_ref, turned_ref, asked_ref, own_ref, *targets = refs[:7], *refs[7:-3]
    wide_ref, values_ref, sems = refs[-3:]
    loads = [
        pltpu.make_async_copy(source, target, sems.at[index])
        for index, (source, target) in enumerate(zip(sources, targets))
    ]
    for load in loads:
        load.start()
    deltas_ref, anchors_ref, scales_ref, lengths_ref, request_ref, queries_ref, new_ref = targets
    blocks = anchors_ref.shape[0] // 2
    rows = deltas_ref.shape[0] // blocks
    tokens = rows // 2
    requests = lengths_ref.shape[0]
    asked = queries_ref.shape[0]
    per_row = asked // request_ref.shape[0]
    width = own_ref.shape[1]
    for load in loads[2:]:
        load.wait()

    lane = lax.broadcasted_iota(jnp.int32, (1, HD), 1)
    first = jnp.zeros((1, HD), jnp.int32)
    last = jnp.zeros((1, HD), jnp.int32)
    end = 0 - me * (blocks * tokens)
    for request in range(requests):
        start = end
        end = end + lengths_ref[request]
        first = jnp.where(lane == request, start, first)
        last = jnp.where(lane == request, end, last)
    place = lax.broadcasted_iota(jnp.int32, (blocks * tokens, HD), 0)
    keys_ref[:, HD:] = jnp.where((place >= first) & (place < last), 1.0, 0.0).astype(jnp.bfloat16)

    asked_ref[:, 0:HD] = queries_ref[...]
    wide_lane = lax.broadcasted_iota(jnp.int32, (per_row, HD), 1)

    def one_row(row, carry):
        asked_ref[pl.ds(pl.multiple_of(row * per_row, per_row), per_row), HD:] = jnp.where(
            (wide_lane == request_ref[row]) | (wide_lane >= requests), 0.0, FAR
        ).astype(jnp.bfloat16)
        return carry

    lax.fori_loop(0, request_ref.shape[0], one_row, 0, unroll=16)

    fresh = new_ref.shape[0] // 4
    new = new_ref[...].astype(jnp.float32).reshape(fresh, 4, HD)
    mine = queries_ref[pl.ds(pl.multiple_of(me * width, width), width), :]
    of_row = lax.broadcasted_iota(jnp.int32, (fresh, width), 1) // (GQ * STEPS)
    same = of_row == lax.broadcasted_iota(jnp.int32, (fresh, width), 0)
    step = lax.broadcasted_iota(jnp.int32, (1, width), 1) % STEPS
    own_scores = []
    for which in range(STEPS):
        scored = lax.dot_general(
            new[:, 2 * which, :].astype(jnp.bfloat16),
            mine,
            (((1,), (1,)), ((), ())),
            preferred_element_type=jnp.float32,
        )
        picked = jnp.sum(jnp.where(same, scored, 0.0), axis=0, keepdims=True)
        own_scores.append(jnp.where(step >= which, picked, FAR))
    own_top = jnp.maximum(own_scores[0], own_scores[1])
    own_total = jnp.zeros((1, width), jnp.float32)
    own_summed = jnp.zeros((HD, width), jnp.float32)
    for which in range(STEPS):
        weight = jnp.exp2((own_scores[which] - own_top) * RATE)
        own_total = own_total + weight
        spread = jnp.where(same, weight, 0.0).astype(jnp.bfloat16)
        own_summed = own_summed + lax.dot_general(
            new[:, 2 * which + 1, :].astype(jnp.bfloat16),
            spread,
            (((0,), (0,)), ((), ())),
            preferred_element_type=jnp.float32,
        )
    own_ref[...] = held((own_summed, own_top, own_total))

    for load in loads[:2]:
        load.wait()
    wide_ref[0 : blocks * rows, :] = deltas_ref[...].astype(jnp.float32)
    scale_key = scales_ref[0:1, :]
    scale_value = scales_ref[1:2, :]

    def one_block(block, carry):
        here = pl.ds(pl.multiple_of(block * tokens, tokens), tokens)
        key = wide_ref[pl.ds(block * rows, tokens, stride=2), :]
        value = wide_ref[pl.ds(block * rows + 1, tokens, stride=2), :]
        keys_ref[here, 0:HD] = (anchors_ref[pl.ds(2 * block, 1), :] + scale_key * key).astype(jnp.bfloat16)
        values_ref[here, :] = (anchors_ref[pl.ds(2 * block + 1, 1), :] + scale_value * value).astype(
            jnp.bfloat16
        )
        return carry

    lax.fori_loop(0, blocks, one_block, 0, unroll=16)
    turned_ref[...] = values_ref[...].T

    def store(index, partial):
        send_ref[index] = packed(partial)

    attend(1, width, keys_ref, turned_ref, asked_ref, store)


def second_kernel(keys_ref, turned_ref, asked_ref, own_ref, keep_ref):
    def store(index, partial):
        keep_ref[index] = held(partial)

    attend(0, keep_ref.shape[2], keys_ref, turned_ref, asked_ref, store)
    keep_ref[0] = held(joined(taken(keep_ref[0]), taken(own_ref[...])))


def join_kernel(keep_ref, got_ref, send_ref, next_ref):
    for index in range(keep_ref.shape[0]):
        partial = joined(taken(keep_ref[index]), unpacked(got_ref[index]))
        if index % 2 == 1:
            send_ref[index // 2] = packed(partial)
        else:
            next_ref[index // 2] = held(partial)


def settle(plan, handed, pages, sems):
    receivers = lax.axis_size("seq")
    me = lax.axis_index("seq")
    rows = pages.shape[0] // receivers
    copies = []
    for index, (k, start, slots) in enumerate(plan):
        size = handed[index].shape[0]
        sender = source(me, k, receivers) if k else me
        first = pl.multiple_of(sender * rows + start * (size // slots), size)
        copies.append(pltpu.make_async_copy(handed[index], pages.at[pl.ds(first, size), :], sems.at[index]))
        copies[-1].start()
    return copies


def settle_kernel(plan, *refs):
    *handed, pages, sems = refs
    for copy in settle(plan, handed, pages, sems):
        copy.wait()


def finish_kernel(plan, keep_ref, got_ref, _, *refs):
    *handed, out_any, pages, out_ref, sems = refs
    copies = settle(plan, handed, pages, sems)
    summed, _, total = joined(taken(keep_ref[0]), unpacked(got_ref[0]))
    out_ref[...] = (summed / total).T.astype(jnp.bfloat16)
    copies.append(pltpu.make_async_copy(out_ref, out_any, sems.at[len(copies)]))
    copies[-1].start()
    for copy in copies:
        copy.wait()


def in_hbm(arrays):
    return [pltpu.with_memory_space_constraint(array, pltpu.HBM) for array in arrays]


def per_device(lengths, owner_map, row_request, deltas, anchors, scales, queries, new_kv):
    blocks = anchors.shape[0]
    tokens = deltas.shape[0]
    senders = lax.axis_size("seq")
    me = lax.axis_index("seq")
    rows, steps, _ = queries.shape
    rows_dev = new_kv.shape[0]
    width = rows_dev * GQ * steps
    small = pltpu.CompilerParams(vmem_limit_bytes=8 * 1024 * 1024)

    flat_deltas = deltas.reshape(tokens * 2, HD)
    flat_anchors = anchors.reshape(blocks * 2, HD)
    flat_queries = queries.reshape(rows, steps, GQ, HD).transpose(0, 2, 1, 3).reshape(-1, HD)
    flat_new = new_kv.reshape(rows_dev * 4, HD)

    whole = jax.ShapeDtypeStruct((tokens * 2, HD), jnp.bfloat16)
    ahead, behind, own = messages(senders, blocks // senders)
    block_rows = tokens * 2 // blocks

    def place(plan, deltas):
        return pl.pallas_call(
            functools.partial(place_kernel, plan),
            out_shape=[jax.ShapeDtypeStruct((slots * block_rows, HD), jnp.bfloat16) for _, _, slots in plan],
            in_specs=[HBM] * 4,
            out_specs=[VMEM] * len(plan),
            scratch_shapes=[
                pltpu.SMEM((blocks,), jnp.int32),
                pltpu.SMEM((blocks,), jnp.int32),
                pltpu.SMEM((senders,), jnp.int32),
                pltpu.VMEM((tokens * 2, HD), jnp.bfloat16),
                pltpu.VMEM((blocks * 2, HD), jnp.float32),
                pltpu.VMEM((2, HD), jnp.float32),
                pltpu.SemaphoreType.DMA((7,)),
            ],
            compiler_params=small,
            name="place",
        )(*in_hbm([owner_map, deltas, flat_anchors, scales]))

    sent = place(ahead, flat_deltas)
    sent, late_deltas = lax.optimization_barrier((sent, flat_deltas))
    got_ahead = [hand(message, k) for message, (k, _, _) in zip(sent, ahead)]

    def leaving(count):
        return jax.ShapeDtypeStruct((count // 2, *message_shape(width)), jnp.bfloat16)

    def staying(count):
        return jax.ShapeDtypeStruct((count // 2, HD + KEEP_ROWS, width), jnp.float32)

    needed = (late_deltas, flat_anchors, scales, lengths, row_request, flat_queries, flat_new)
    roomy = pltpu.CompilerParams(vmem_limit_bytes=32 * 1024 * 1024)
    send, *common = pl.pallas_call(
        first_kernel,
        out_shape=[
            leaving(senders),
            jax.ShapeDtypeStruct((tokens, 2 * HD), jnp.bfloat16),
            jax.ShapeDtypeStruct((HD, tokens), jnp.bfloat16),
            jax.ShapeDtypeStruct((rows * GQ * steps, 2 * HD), jnp.bfloat16),
            jax.ShapeDtypeStruct((HD + KEEP_ROWS, width), jnp.float32),
        ],
        in_specs=[HBM] * len(needed),
        out_specs=[VMEM] * 5,
        scratch_shapes=[
            (pltpu.SMEM if array.dtype == jnp.int32 else pltpu.VMEM)(array.shape, array.dtype)
            for array in needed
        ]
        + [
            pltpu.VMEM((tokens * 2 + 16, HD), jnp.float32),
            pltpu.VMEM((tokens, HD), jnp.bfloat16),
            pltpu.SemaphoreType.DMA((len(needed),)),
        ],
        compiler_params=roomy,
        name="attend_leaving",
    )(*in_hbm(needed))

    k, count = 1, senders // 2
    send, late_deltas = lax.optimization_barrier((send, late_deltas))
    passed = exchange(send, k)
    *sent, mine = place(behind + own, late_deltas)
    keep = pl.pallas_call(
        second_kernel,
        out_shape=staying(senders),
        in_specs=[VMEM] * 4,
        out_specs=VMEM,
        compiler_params=roomy,
        name="attend_staying",
    )(*common)
    sent, keep = lax.optimization_barrier((sent, keep))
    got = got_ahead[1:] + [hand(message, partner) for message, (partner, _, _) in zip(sent, behind)]
    while count > 1:
        send, keep = pl.pallas_call(
            join_kernel,
            out_shape=[leaving(count), staying(count)],
            in_specs=[VMEM] * 2,
            out_specs=[VMEM] * 2,
            compiler_params=small,
            name="join",
        )(keep, passed)
        k, count = 2 * k + 1, count // 2
        passed = exchange(send, k)
    settled = ahead[:1] + own
    pages = pl.pallas_call(
        functools.partial(settle_kernel, settled),
        out_shape=whole,
        in_specs=[ANY] * len(settled),
        out_specs=HBM,
        scratch_shapes=[pltpu.SemaphoreType.DMA((len(settled),))],
        compiler_params=small,
        name="settle",
    )(got_ahead[0], mine)
    attended, pages = pl.pallas_call(
        functools.partial(finish_kernel, ahead[1:] + behind),
        out_shape=[jax.ShapeDtypeStruct((width, HD), jnp.bfloat16), whole],
        in_specs=[VMEM] * 2 + [HBM] + [ANY] * len(got),
        out_specs=[HBM, HBM],
        scratch_shapes=[
            pltpu.VMEM((width, HD), jnp.bfloat16),
            pltpu.SemaphoreType.DMA((len(got) + 1,)),
        ],
        input_output_aliases={2: 1},
        compiler_params=small,
        name="finish",
    )(keep, passed, pages, *got)
    pages = pages.reshape(blocks, tokens // blocks, 2, HD)
    attended = (
        attended.reshape(rows_dev, GQ, steps, HD).transpose(0, 2, 1, 3).reshape(rows_dev, steps, GQ * HD)
    )
    return pages, attended


def solution(mesh):
    placed = (
        P("groups"),
        P(("groups", "seq")),
        P("groups"),
        P(("groups", "seq"), None, "tp"),
        P(("groups", "seq"), None, "tp"),
        P("groups", "tp"),
        P("groups", None, "tp"),
        P(("groups", "seq"), None, None, "tp"),
    )
    return jax.shard_map(
        per_device,
        mesh=mesh,
        in_specs=placed,
        out_specs=(P(("groups", "seq"), None, None, "tp"), P(("groups", "seq"), None, "tp")),
        check_vma=False,
    )
```

```python
import functools

import jax
import jax.numpy as jnp
from jax import lax
from jax.experimental import pallas as pl
from jax.experimental.pallas import tpu as pltpu
from jax.sharding import PartitionSpec as P

HD = 128
GQ = 8
STEPS = 2
STAT_ROWS = 6
KEEP_ROWS = 8
FAR = -1e30
RATE = HD ** (-0.5) * 1.4426950408889634

VMEM = pl.BlockSpec(memory_space=pltpu.VMEM)
HBM = pl.BlockSpec(memory_space=pltpu.HBM)
ANY = pl.BlockSpec(memory_space=pl.ANY)
SMEM = pl.BlockSpec(memory_space=pltpu.SMEM)


def inner(device, count):
    return (device ^ (device // (count // 2))) & 1


def partner(device, k, count):
    far = count // 2
    if k == far:
        return device ^ (1 + inner(device, count) * (far - 1))
    if k == 1:
        return device ^ (far - inner(device, count) * (far - 1))
    return device ^ k


def source(device, k, count):
    far = count // 2
    if k == far:
        return device ^ (far - inner(device, count) * (far - 1))
    if k == 1:
        return device ^ (1 + inner(device, count) * (far - 1))
    return device ^ k


def exchange(message, k):
    count = lax.axis_size("seq")
    return lax.ppermute(message, "seq", [(i, i ^ k) for i in range(count)])


def hand(message, k):
    count = lax.axis_size("seq")
    return lax.ppermute(message, "seq", [(i, partner(i, k, count)) for i in range(count)])


def messages(count, capacity):
    half = capacity // 2
    ahead = [(k, 0, capacity) for k in range(count // 2, count)]
    behind = [(k, first, half) for k in reversed(range(1, count // 2)) for first in (0, half)]
    return ahead, behind, [(0, 0, capacity)]


def place_kernel(plan, owner_any, deltas_any, anchors_any, scales_any, *refs):
    receivers = lax.axis_size("seq")
    me = lax.axis_index("seq")
    outs = refs[:-7]
    owner_ref, source_ref, count_ref, deltas_ref, anchors_ref, scales_ref, sems = refs[-7:]
    blocks = owner_ref.shape[0]
    rows = deltas_ref.shape[0] // blocks
    capacity = blocks // receivers
    quarter = deltas_ref.shape[0] // 4
    parts = [pl.ds(index * quarter, quarter) for index in range(4)]
    loads = [
        pltpu.make_async_copy(source, target, sems.at[index])
        for index, (source, target) in enumerate(
            [(owner_any, owner_ref), (scales_any, scales_ref), (anchors_any, anchors_ref)]
            + [(deltas_any.at[part], deltas_ref.at[part]) for part in parts]
        )
    ]
    for load in loads:
        load.start()
    bits = capacity.bit_length()
    narrow = receivers * bits < 32
    if not narrow:
        for owner in range(receivers):
            count_ref[owner] = owner * capacity
    loads[0].wait()

    def find(block, counts):
        owner = owner_ref[block]
        if narrow:
            shift = owner * bits
            slot = owner * capacity + ((counts >> shift) & ((1 << bits) - 1))
            counts = counts + (jnp.int32(1) << shift)
        else:
            slot = count_ref[owner]
            count_ref[owner] = slot + 1
        source_ref[slot] = block
        return counts

    lax.fori_loop(0, blocks, find, jnp.int32(0), unroll=16)
    for load in loads[1:]:
        load.wait()
    odd = lax.broadcasted_iota(jnp.int32, (8, HD), 0) % 2 == 1
    scale = jnp.where(odd, scales_ref[1:2, :], scales_ref[0:1, :])[None]
    for (k, start, count), out_ref in zip(plan, outs):
        first = partner(me, k, receivers) * capacity + start

        def one_slot(slot, carry, first=first, out_ref=out_ref):
            block = source_ref[first + slot]
            anchor = jnp.where(
                odd, anchors_ref[pl.ds(2 * block + 1, 1), :], anchors_ref[pl.ds(2 * block, 1), :]
            )[None]
            here = pl.ds(pl.multiple_of(block * rows, rows), rows)
            delta = deltas_ref[here, :].astype(jnp.float32)
            decoded = anchor + scale * delta.reshape(rows // 8, 8, HD)
            out_ref[pl.ds(pl.multiple_of(slot * rows, rows), rows), :] = decoded.reshape(rows, HD).astype(
                jnp.bfloat16
            )
            return carry

        lax.fori_loop(0, count, one_slot, 0, unroll=min(16, count))


def pieces(values):
    high = values.astype(jnp.bfloat16)
    rest = values - high.astype(jnp.float32)
    middle = rest.astype(jnp.bfloat16)
    low = (rest - middle.astype(jnp.float32)).astype(jnp.bfloat16)
    return [high, middle, low]


def message_shape(width):
    parts = max(1, width // HD)
    return parts * HD + -(-parts * STAT_ROWS // 16) * 16, width // parts


def packed(partial):
    summed, top, total = partial
    rows, lanes = message_shape(top.shape[1])
    sums = summed.astype(jnp.bfloat16)
    stats = pieces(top) + pieces(total)
    here = [slice(first, first + lanes) for first in range(0, top.shape[1], lanes)]
    filled = [sums[:, part] for part in here] + [row[:, part] for part in here for row in stats]
    rest = rows - len(here) * (HD + STAT_ROWS)
    return jnp.concatenate(filled + [jnp.zeros((rest, lanes), jnp.bfloat16)], axis=0)


def unpacked(block):
    parts = block.shape[0] // HD
    sums = [block[part * HD : (part + 1) * HD, :] for part in range(parts)]
    stats = block[parts * HD :, :].astype(jnp.float32)

    def row(first):
        found = []
        for part in range(parts):
            at = part * STAT_ROWS + first
            found.append(stats[at : at + 1] + stats[at + 1 : at + 2] + stats[at + 2 : at + 3])
        return jnp.concatenate(found, axis=1)

    return jnp.concatenate(sums, axis=1).astype(jnp.float32), row(0), row(3)


def held(partial):
    summed, top, total = partial
    rest = jnp.zeros((KEEP_ROWS - 2, top.shape[1]), jnp.float32)
    return jnp.concatenate([summed, top, total, rest], axis=0)


def taken(block):
    return block[0:HD, :], block[HD : HD + 1, :], block[HD + 1 : HD + 2, :]


def joined(one, other):
    top = jnp.maximum(one[1], other[1])
    scale_one = jnp.exp2((one[1] - top) * RATE)
    scale_other = jnp.exp2((other[1] - top) * RATE)
    return (
        one[0] * scale_one + other[0] * scale_other,
        top,
        one[2] * scale_one + other[2] * scale_other,
    )


def difference(index):
    total = 0
    while index:
        total, index = total ^ index, index >> 1
    return total


def attend(parity, width, keys_ref, turned_ref, asked_ref, store):
    me = lax.axis_index("seq")
    asked = asked_ref.shape[0]

    def partial_of(here):
        scores = lax.dot_general(
            keys_ref[...], here, (((1,), (1,)), ((), ())), preferred_element_type=jnp.float32
        )
        top = jnp.max(scores, axis=0, keepdims=True)
        weights = jnp.exp2((scores - top) * RATE)
        total = jnp.sum(weights, axis=0, keepdims=True)
        summed = jnp.dot(turned_ref[...], weights.astype(jnp.bfloat16), preferred_element_type=jnp.float32)
        return summed, top, total

    if width % HD == 0:
        for index in range(asked // width // 2):
            there = (me ^ difference(2 * index + parity)) * width
            store(index, partial_of(asked_ref[pl.ds(pl.multiple_of(there, width), width), :]))
        return
    tile = min(2 * HD, asked)
    parts = tile // width

    def one_tile(tile_index, carry):
        here = asked_ref[pl.ds(pl.multiple_of(tile_index * tile, tile), tile), :]
        summed, top, total = partial_of(here)
        for part in range(parts):
            lanes = slice(part * width, (part + 1) * width)
            apart = (tile_index * parts + part) ^ me
            place = apart ^ (apart >> 1)

            @pl.when(place % 2 == parity)
            def _(lanes=lanes, place=place):
                store(place // 2, (summed[:, lanes], top[:, lanes], total[:, lanes]))

        return carry

    lax.fori_loop(0, asked // tile, one_tile, 0)


def first_kernel(*refs):
    me = lax.axis_index("seq")
    sources, send_ref, keys_ref, turned_ref, asked_ref, own_ref, *targets = refs[:7], *refs[7:-3]
    wide_ref, values_ref, sems = refs[-3:]
    loads = [
        pltpu.make_async_copy(source, target, sems.at[index])
        for index, (source, target) in enumerate(zip(sources, targets))
    ]
    for load in loads:
        load.start()
    deltas_ref, anchors_ref, scales_ref, lengths_ref, request_ref, queries_ref, new_ref = targets
    blocks = anchors_ref.shape[0] // 2
    rows = deltas_ref.shape[0] // blocks
    tokens = rows // 2
    requests = lengths_ref.shape[0]
    asked = queries_ref.shape[0]
    per_row = asked // request_ref.shape[0]
    width = own_ref.shape[1]
    for load in loads[2:]:
        load.wait()

    lane = lax.broadcasted_iota(jnp.int32, (1, HD), 1)
    first = jnp.zeros((1, HD), jnp.int32)
    last = jnp.zeros((1, HD), jnp.int32)
    end = 0 - me * (blocks * tokens)
    for request in range(requests):
        start = end
        end = end + lengths_ref[request]
        first = jnp.where(lane == request, start, first)
        last = jnp.where(lane == request, end, last)
    place = lax.broadcasted_iota(jnp.int32, (blocks * tokens, HD), 0)
    keys_ref[:, HD:] = jnp.where((place >= first) & (place < last), 1.0, 0.0).astype(jnp.bfloat16)

    asked_ref[:, 0:HD] = queries_ref[...]
    wide_lane = lax.broadcasted_iota(jnp.int32, (per_row, HD), 1)

    def one_row(row, carry):
        asked_ref[pl.ds(pl.multiple_of(row * per_row, per_row), per_row), HD:] = jnp.where(
            (wide_lane == request_ref[row]) | (wide_lane >= requests), 0.0, FAR
        ).astype(jnp.bfloat16)
        return carry

    lax.fori_loop(0, request_ref.shape[0], one_row, 0, unroll=16)

    fresh = new_ref.shape[0] // 4
    new = new_ref[...].astype(jnp.float32).reshape(fresh, 4, HD)
    mine = queries_ref[pl.ds(pl.multiple_of(me * width, width), width), :]
    of_row = lax.broadcasted_iota(jnp.int32, (fresh, width), 1) // (GQ * STEPS)
    same = of_row == lax.broadcasted_iota(jnp.int32, (fresh, width), 0)
    step = lax.broadcasted_iota(jnp.int32, (1, width), 1) % STEPS
    own_scores = []
    for which in range(STEPS):
        scored = lax.dot_general(
            new[:, 2 * which, :].astype(jnp.bfloat16),
            mine,
            (((1,), (1,)), ((), ())),
            preferred_element_type=jnp.float32,
        )
        picked = jnp.sum(jnp.where(same, scored, 0.0), axis=0, keepdims=True)
        own_scores.append(jnp.where(step >= which, picked, FAR))
    own_top = jnp.maximum(own_scores[0], own_scores[1])
    own_total = jnp.zeros((1, width), jnp.float32)
    own_summed = jnp.zeros((HD, width), jnp.float32)
    for which in range(STEPS):
        weight = jnp.exp2((own_scores[which] - own_top) * RATE)
        own_total = own_total + weight
        spread = jnp.where(same, weight, 0.0).astype(jnp.bfloat16)
        own_summed = own_summed + lax.dot_general(
            new[:, 2 * which + 1, :].astype(jnp.bfloat16),
            spread,
            (((0,), (0,)), ((), ())),
            preferred_element_type=jnp.float32,
        )
    own_ref[...] = held((own_summed, own_top, own_total))

    for load in loads[:2]:
        load.wait()
    wide_ref[0 : blocks * rows, :] = deltas_ref[...].astype(jnp.float32)
    scale_key = scales_ref[0:1, :]
    scale_value = scales_ref[1:2, :]

    def one_block(block, carry):
        here = pl.ds(pl.multiple_of(block * tokens, tokens), tokens)
        key = wide_ref[pl.ds(block * rows, tokens, stride=2), :]
        value = wide_ref[pl.ds(block * rows + 1, tokens, stride=2), :]
        keys_ref[here, 0:HD] = (anchors_ref[pl.ds(2 * block, 1), :] + scale_key * key).astype(jnp.bfloat16)
        values_ref[here, :] = (anchors_ref[pl.ds(2 * block + 1, 1), :] + scale_value * value).astype(
            jnp.bfloat16
        )
        return carry

    lax.fori_loop(0, blocks, one_block, 0, unroll=16)
    turned_ref[...] = values_ref[...].T

    def store(index, partial):
        send_ref[index] = packed(partial)

    attend(1, width, keys_ref, turned_ref, asked_ref, store)


def second_kernel(keys_ref, turned_ref, asked_ref, own_ref, keep_ref):
    def store(index, partial):
        keep_ref[index] = held(partial)

    attend(0, keep_ref.shape[2], keys_ref, turned_ref, asked_ref, store)
    keep_ref[0] = held(joined(taken(keep_ref[0]), taken(own_ref[...])))


def join_kernel(keep_ref, got_ref, send_ref, next_ref):
    for index in range(keep_ref.shape[0]):
        partial = joined(taken(keep_ref[index]), unpacked(got_ref[index]))
        if index % 2 == 1:
            send_ref[index // 2] = packed(partial)
        else:
            next_ref[index // 2] = held(partial)


def settle(plan, handed, pages, sems):
    receivers = lax.axis_size("seq")
    me = lax.axis_index("seq")
    rows = pages.shape[0] // receivers
    copies = []
    for index, (k, start, slots) in enumerate(plan):
        size = handed[index].shape[0]
        sender = source(me, k, receivers) if k else me
        first = pl.multiple_of(sender * rows + start * (size // slots), size)
        copies.append(pltpu.make_async_copy(handed[index], pages.at[pl.ds(first, size), :], sems.at[index]))
        copies[-1].start()
    return copies


def settle_kernel(plan, *refs):
    *handed, pages, sems = refs
    for copy in settle(plan, handed, pages, sems):
        copy.wait()


def finish_kernel(plan, keep_ref, got_ref, _, *refs):
    *handed, out_any, pages, out_ref, sems = refs
    copies = settle(plan, handed, pages, sems)
    summed, _, total = joined(taken(keep_ref[0]), unpacked(got_ref[0]))
    out_ref[...] = (summed / total).T.astype(jnp.bfloat16)
    copies.append(pltpu.make_async_copy(out_ref, out_any, sems.at[len(copies)]))
    copies[-1].start()
    for copy in copies:
        copy.wait()


def in_hbm(arrays):
    return [pltpu.with_memory_space_constraint(array, pltpu.HBM) for array in arrays]


def per_device(lengths, owner_map, row_request, deltas, anchors, scales, queries, new_kv):
    blocks = anchors.shape[0]
    tokens = deltas.shape[0]
    senders = lax.axis_size("seq")
    me = lax.axis_index("seq")
    rows, steps, _ = queries.shape
    rows_dev = new_kv.shape[0]
    width = rows_dev * GQ * steps
    small = pltpu.CompilerParams(vmem_limit_bytes=8 * 1024 * 1024)

    flat_deltas = deltas.reshape(tokens * 2, HD)
    flat_anchors = anchors.reshape(blocks * 2, HD)
    flat_queries = queries.reshape(rows, steps, GQ, HD).transpose(0, 2, 1, 3).reshape(-1, HD)
    flat_new = new_kv.reshape(rows_dev * 4, HD)

    whole = jax.ShapeDtypeStruct((tokens * 2, HD), jnp.bfloat16)
    ahead, behind, own = messages(senders, blocks // senders)
    block_rows = tokens * 2 // blocks

    def place(plan, deltas):
        return pl.pallas_call(
            functools.partial(place_kernel, plan),
            out_shape=[jax.ShapeDtypeStruct((slots * block_rows, HD), jnp.bfloat16) for _, _, slots in plan],
            in_specs=[HBM] * 4,
            out_specs=[VMEM] * len(plan),
            scratch_shapes=[
                pltpu.SMEM((blocks,), jnp.int32),
                pltpu.SMEM((blocks,), jnp.int32),
                pltpu.SMEM((senders,), jnp.int32),
                pltpu.VMEM((tokens * 2, HD), jnp.bfloat16),
                pltpu.VMEM((blocks * 2, HD), jnp.float32),
                pltpu.VMEM((2, HD), jnp.float32),
                pltpu.SemaphoreType.DMA((7,)),
            ],
            compiler_params=small,
            name="place",
        )(*in_hbm([owner_map, deltas, flat_anchors, scales]))

    sent = place(ahead, flat_deltas)
    sent, late_deltas = lax.optimization_barrier((sent, flat_deltas))
    got_ahead = [hand(message, k) for message, (k, _, _) in zip(sent, ahead)]

    def leaving(count):
        return jax.ShapeDtypeStruct((count // 2, *message_shape(width)), jnp.bfloat16)

    def staying(count):
        return jax.ShapeDtypeStruct((count // 2, HD + KEEP_ROWS, width), jnp.float32)

    needed = (late_deltas, flat_anchors, scales, lengths, row_request, flat_queries, flat_new)
    roomy = pltpu.CompilerParams(vmem_limit_bytes=32 * 1024 * 1024)
    send, *common = pl.pallas_call(
        first_kernel,
        out_shape=[
            leaving(senders),
            jax.ShapeDtypeStruct((tokens, 2 * HD), jnp.bfloat16),
            jax.ShapeDtypeStruct((HD, tokens), jnp.bfloat16),
            jax.ShapeDtypeStruct((rows * GQ * steps, 2 * HD), jnp.bfloat16),
            jax.ShapeDtypeStruct((HD + KEEP_ROWS, width), jnp.float32),
        ],
        in_specs=[HBM] * len(needed),
        out_specs=[VMEM] * 5,
        scratch_shapes=[
            (pltpu.SMEM if array.dtype == jnp.int32 else pltpu.VMEM)(array.shape, array.dtype)
            for array in needed
        ]
        + [
            pltpu.VMEM((tokens * 2 + 16, HD), jnp.float32),
            pltpu.VMEM((tokens, HD), jnp.bfloat16),
            pltpu.SemaphoreType.DMA((len(needed),)),
        ],
        compiler_params=roomy,
        name="attend_leaving",
    )(*in_hbm(needed))

    k, count = 1, senders // 2
    send, late_deltas = lax.optimization_barrier((send, late_deltas))
    passed = exchange(send, k)
    *sent, mine = place(behind + own, late_deltas)
    keep = pl.pallas_call(
        second_kernel,
        out_shape=staying(senders),
        in_specs=[VMEM] * 4,
        out_specs=VMEM,
        compiler_params=roomy,
        name="attend_staying",
    )(*common)
    sent, keep = lax.optimization_barrier((sent, keep))
    got = got_ahead[1:] + [hand(message, partner) for message, (partner, _, _) in zip(sent, behind)]
    while count > 1:
        send, keep = pl.pallas_call(
            join_kernel,
            out_shape=[leaving(count), staying(count)],
            in_specs=[VMEM] * 2,
            out_specs=[VMEM] * 2,
            compiler_params=small,
            name="join",
        )(keep, passed)
        k, count = 2 * k + 1, count // 2
        passed = exchange(send, k)
    settled = ahead[:1] + own
    pages = pl.pallas_call(
        functools.partial(settle_kernel, settled),
        out_shape=whole,
        in_specs=[ANY] * len(settled),
        out_specs=HBM,
        scratch_shapes=[pltpu.SemaphoreType.DMA((len(settled),))],
        compiler_params=small,
        name="settle",
    )(got_ahead[0], mine)
    attended, pages = pl.pallas_call(
        functools.partial(finish_kernel, ahead[1:] + behind),
        out_shape=[jax.ShapeDtypeStruct((width, HD), jnp.bfloat16), whole],
        in_specs=[VMEM] * 2 + [HBM] + [ANY] * len(got),
        out_specs=[HBM, HBM],
        scratch_shapes=[
            pltpu.VMEM((width, HD), jnp.bfloat16),
            pltpu.SemaphoreType.DMA((len(got) + 1,)),
        ],
        input_output_aliases={2: 1},
        compiler_params=small,
        name="finish",
    )(keep, passed, pages, *got)
    pages = pages.reshape(blocks, tokens // blocks, 2, HD)
    attended = (
        attended.reshape(rows_dev, GQ, steps, HD).transpose(0, 2, 1, 3).reshape(rows_dev, steps, GQ * HD)
    )
    return pages, attended


def solution(mesh):
    placed = (
        P("groups"),
        P(("groups", "seq")),
        P("groups"),
        P(("groups", "seq"), None, "tp"),
        P(("groups", "seq"), None, "tp"),
        P("groups", "tp"),
        P("groups", None, "tp"),
        P(("groups", "seq"), None, None, "tp"),
    )
    return jax.shard_map(
        per_device,
        mesh=mesh,
        in_specs=placed,
        out_specs=(P(("groups", "seq"), None, None, "tp"), P(("groups", "seq"), None, "tp")),
        check_vma=False,
    )
```

```python
import functools

import jax
import jax.numpy as jnp
from jax import lax
from jax.experimental import pallas as pl
from jax.experimental.pallas import tpu as pltpu
from jax.sharding import PartitionSpec as P

HD = 128
GQ = 8
STEPS = 2
STAT_ROWS = 6
KEEP_ROWS = 8
FAR = -1e30
RATE = HD ** (-0.5) * 1.4426950408889634

VMEM = pl.BlockSpec(memory_space=pltpu.VMEM)
HBM = pl.BlockSpec(memory_space=pltpu.HBM)
ANY = pl.BlockSpec(memory_space=pl.ANY)
SMEM = pl.BlockSpec(memory_space=pltpu.SMEM)


def inner(device, count):
    return (device ^ (device // (count // 2))) & 1


def partner(device, k, count):
    far = count // 2
    if k == far:
        return device ^ (1 + inner(device, count) * (far - 1))
    if k == 1:
        return device ^ (far - inner(device, count) * (far - 1))
    return device ^ k


def source(device, k, count):
    far = count // 2
    if k == far:
        return device ^ (far - inner(device, count) * (far - 1))
    if k == 1:
        return device ^ (1 + inner(device, count) * (far - 1))
    return device ^ k


def exchange(message, k):
    count = lax.axis_size("seq")
    last = k == count - 1
    return lax.ppermute(message, "seq", [(i, i ^ k ^ (last and i < count // 2)) for i in range(count)])


def hand(message, k):
    count = lax.axis_size("seq")
    return lax.ppermute(message, "seq", [(i, partner(i, k, count)) for i in range(count)])


def messages(count, capacity):
    half = capacity // 2
    ahead = [(k, 0, capacity) for k in range(count // 2, count)]
    behind = [(k, first, half) for k in reversed(range(1, count // 2)) for first in (0, half)]
    return ahead, behind, [(0, 0, capacity)]


def place_kernel(plan, owner_any, deltas_any, anchors_any, scales_any, *refs):
    receivers = lax.axis_size("seq")
    me = lax.axis_index("seq")
    outs = refs[:-7]
    owner_ref, source_ref, count_ref, deltas_ref, anchors_ref, scales_ref, sems = refs[-7:]
    blocks = owner_ref.shape[0]
    rows = deltas_ref.shape[0] // blocks
    capacity = blocks // receivers
    quarter = deltas_ref.shape[0] // 4
    parts = [pl.ds(index * quarter, quarter) for index in range(4)]
    loads = [
        pltpu.make_async_copy(source, target, sems.at[index])
        for index, (source, target) in enumerate(
            [(owner_any, owner_ref), (scales_any, scales_ref), (anchors_any, anchors_ref)]
            + [(deltas_any.at[part], deltas_ref.at[part]) for part in parts]
        )
    ]
    for load in loads:
        load.start()
    bits = capacity.bit_length()
    narrow = receivers * bits < 32
    if not narrow:
        for owner in range(receivers):
            count_ref[owner] = owner * capacity
    loads[0].wait()

    def find(block, counts):
        owner = owner_ref[block]
        if narrow:
            shift = owner * bits
            slot = owner * capacity + ((counts >> shift) & ((1 << bits) - 1))
            counts = counts + (jnp.int32(1) << shift)
        else:
            slot = count_ref[owner]
            count_ref[owner] = slot + 1
        source_ref[slot] = block
        return counts

    lax.fori_loop(0, blocks, find, jnp.int32(0), unroll=16)
    for load in loads[1:]:
        load.wait()
    odd = lax.broadcasted_iota(jnp.int32, (8, HD), 0) % 2 == 1
    scale = jnp.where(odd, scales_ref[1:2, :], scales_ref[0:1, :])[None]
    for (k, start, count), out_ref in zip(plan, outs):
        first = partner(me, k, receivers) * capacity + start

        def one_slot(slot, carry, first=first, out_ref=out_ref):
            block = source_ref[first + slot]
            anchor = jnp.where(
                odd, anchors_ref[pl.ds(2 * block + 1, 1), :], anchors_ref[pl.ds(2 * block, 1), :]
            )[None]
            here = pl.ds(pl.multiple_of(block * rows, rows), rows)
            delta = deltas_ref[here, :].astype(jnp.float32)
            decoded = anchor + scale * delta.reshape(rows // 8, 8, HD)
            out_ref[pl.ds(pl.multiple_of(slot * rows, rows), rows), :] = decoded.reshape(rows, HD).astype(
                jnp.bfloat16
            )
            return carry

        lax.fori_loop(0, count, one_slot, 0, unroll=min(16, count))


def pieces(values):
    high = values.astype(jnp.bfloat16)
    rest = values - high.astype(jnp.float32)
    middle = rest.astype(jnp.bfloat16)
    low = (rest - middle.astype(jnp.float32)).astype(jnp.bfloat16)
    return [high, middle, low]


def message_shape(width):
    parts = max(1, width // HD)
    return parts * HD + -(-parts * STAT_ROWS // 16) * 16, width // parts


def packed(partial):
    summed, top, total = partial
    rows, lanes = message_shape(top.shape[1])
    sums = summed.astype(jnp.bfloat16)
    stats = pieces(top) + pieces(total)
    here = [slice(first, first + lanes) for first in range(0, top.shape[1], lanes)]
    filled = [sums[:, part] for part in here] + [row[:, part] for part in here for row in stats]
    rest = rows - len(here) * (HD + STAT_ROWS)
    return jnp.concatenate(filled + [jnp.zeros((rest, lanes), jnp.bfloat16)], axis=0)


def unpacked(block):
    parts = block.shape[0] // HD
    sums = [block[part * HD : (part + 1) * HD, :] for part in range(parts)]
    stats = block[parts * HD :, :].astype(jnp.float32)

    def row(first):
        found = []
        for part in range(parts):
            at = part * STAT_ROWS + first
            found.append(stats[at : at + 1] + stats[at + 1 : at + 2] + stats[at + 2 : at + 3])
        return jnp.concatenate(found, axis=1)

    return jnp.concatenate(sums, axis=1).astype(jnp.float32), row(0), row(3)


def held(partial):
    summed, top, total = partial
    rest = jnp.zeros((KEEP_ROWS - 2, top.shape[1]), jnp.float32)
    return jnp.concatenate([summed, top, total, rest], axis=0)


def taken(block):
    return block[0:HD, :], block[HD : HD + 1, :], block[HD + 1 : HD + 2, :]


def joined(one, other):
    top = jnp.maximum(one[1], other[1])
    scale_one = jnp.exp2((one[1] - top) * RATE)
    scale_other = jnp.exp2((other[1] - top) * RATE)
    return (
        one[0] * scale_one + other[0] * scale_other,
        top,
        one[2] * scale_one + other[2] * scale_other,
    )


def difference(index):
    total = 0
    while index:
        total, index = total ^ index, index >> 1
    return total


def attend(parity, width, keys_ref, turned_ref, asked_ref, store):
    me = lax.axis_index("seq")
    far = lax.axis_size("seq") // 2
    lower = 1 - me // far
    asked = asked_ref.shape[0]

    def partial_of(here):
        scores = lax.dot_general(
            keys_ref[...], here, (((1,), (1,)), ((), ())), preferred_element_type=jnp.float32
        )
        top = jnp.max(scores, axis=0, keepdims=True)
        weights = jnp.exp2((scores - top) * RATE)
        total = jnp.sum(weights, axis=0, keepdims=True)
        summed = jnp.dot(turned_ref[...], weights.astype(jnp.bfloat16), preferred_element_type=jnp.float32)
        return summed, top, total

    if width % HD == 0:
        for index in range(asked // width // 2):
            place = 2 * index + parity
            there = (me ^ difference(place) ^ (lower if place >= far else 0)) * width
            store(index, partial_of(asked_ref[pl.ds(pl.multiple_of(there, width), width), :]))
        return
    tile = min(2 * HD, asked)
    parts = tile // width

    def one_tile(tile_index, carry):
        here = asked_ref[pl.ds(pl.multiple_of(tile_index * tile, tile), tile), :]
        summed, top, total = partial_of(here)
        for part in range(parts):
            lanes = slice(part * width, (part + 1) * width)
            apart = (tile_index * parts + part) ^ me
            apart = apart ^ (apart // far * lower)
            place = apart ^ (apart >> 1)

            @pl.when(place % 2 == parity)
            def _(lanes=lanes, place=place):
                store(place // 2, (summed[:, lanes], top[:, lanes], total[:, lanes]))

        return carry

    lax.fori_loop(0, asked // tile, one_tile, 0)


def first_kernel(*refs):
    me = lax.axis_index("seq")
    sources, send_ref, keys_ref, turned_ref, asked_ref, own_ref, *targets = refs[:7], *refs[7:-3]
    wide_ref, values_ref, sems = refs[-3:]
    loads = [
        pltpu.make_async_copy(source, target, sems.at[index])
        for index, (source, target) in enumerate(zip(sources, targets))
    ]
    for load in loads:
        load.start()
    deltas_ref, anchors_ref, scales_ref, lengths_ref, request_ref, queries_ref, new_ref = targets
    blocks = anchors_ref.shape[0] // 2
    rows = deltas_ref.shape[0] // blocks
    tokens = rows // 2
    requests = lengths_ref.shape[0]
    asked = queries_ref.shape[0]
    per_row = asked // request_ref.shape[0]
    width = own_ref.shape[1]
    for load in loads[2:]:
        load.wait()

    lane = lax.broadcasted_iota(jnp.int32, (1, HD), 1)
    first = jnp.zeros((1, HD), jnp.int32)
    last = jnp.zeros((1, HD), jnp.int32)
    end = 0 - me * (blocks * tokens)
    for request in range(requests):
        start = end
        end = end + lengths_ref[request]
        first = jnp.where(lane == request, start, first)
        last = jnp.where(lane == request, end, last)
    place = lax.broadcasted_iota(jnp.int32, (blocks * tokens, HD), 0)
    keys_ref[:, HD:] = jnp.where((place >= first) & (place < last), 1.0, 0.0).astype(jnp.bfloat16)

    asked_ref[:, 0:HD] = queries_ref[...]
    wide_lane = lax.broadcasted_iota(jnp.int32, (per_row, HD), 1)

    def one_row(row, carry):
        asked_ref[pl.ds(pl.multiple_of(row * per_row, per_row), per_row), HD:] = jnp.where(
            (wide_lane == request_ref[row]) | (wide_lane >= requests), 0.0, FAR
        ).astype(jnp.bfloat16)
        return carry

    lax.fori_loop(0, request_ref.shape[0], one_row, 0, unroll=16)

    fresh = new_ref.shape[0] // 4
    new = new_ref[...].astype(jnp.float32).reshape(fresh, 4, HD)
    mine = queries_ref[pl.ds(pl.multiple_of(me * width, width), width), :]
    of_row = lax.broadcasted_iota(jnp.int32, (fresh, width), 1) // (GQ * STEPS)
    same = of_row == lax.broadcasted_iota(jnp.int32, (fresh, width), 0)
    step = lax.broadcasted_iota(jnp.int32, (1, width), 1) % STEPS
    own_scores = []
    for which in range(STEPS):
        scored = lax.dot_general(
            new[:, 2 * which, :].astype(jnp.bfloat16),
            mine,
            (((1,), (1,)), ((), ())),
            preferred_element_type=jnp.float32,
        )
        picked = jnp.sum(jnp.where(same, scored, 0.0), axis=0, keepdims=True)
        own_scores.append(jnp.where(step >= which, picked, FAR))
    own_top = jnp.maximum(own_scores[0], own_scores[1])
    own_total = jnp.zeros((1, width), jnp.float32)
    own_summed = jnp.zeros((HD, width), jnp.float32)
    for which in range(STEPS):
        weight = jnp.exp2((own_scores[which] - own_top) * RATE)
        own_total = own_total + weight
        spread = jnp.where(same, weight, 0.0).astype(jnp.bfloat16)
        own_summed = own_summed + lax.dot_general(
            new[:, 2 * which + 1, :].astype(jnp.bfloat16),
            spread,
            (((0,), (0,)), ((), ())),
            preferred_element_type=jnp.float32,
        )
    own_ref[...] = held((own_summed, own_top, own_total))

    for load in loads[:2]:
        load.wait()
    wide_ref[0 : blocks * rows, :] = deltas_ref[...].astype(jnp.float32)
    scale_key = scales_ref[0:1, :]
    scale_value = scales_ref[1:2, :]

    def one_block(block, carry):
        here = pl.ds(pl.multiple_of(block * tokens, tokens), tokens)
        key = wide_ref[pl.ds(block * rows, tokens, stride=2), :]
        value = wide_ref[pl.ds(block * rows + 1, tokens, stride=2), :]
        keys_ref[here, 0:HD] = (anchors_ref[pl.ds(2 * block, 1), :] + scale_key * key).astype(jnp.bfloat16)
        values_ref[here, :] = (anchors_ref[pl.ds(2 * block + 1, 1), :] + scale_value * value).astype(
            jnp.bfloat16
        )
        return carry

    lax.fori_loop(0, blocks, one_block, 0, unroll=16)
    turned_ref[...] = values_ref[...].T

    def store(index, partial):
        send_ref[index] = packed(partial)

    attend(1, width, keys_ref, turned_ref, asked_ref, store)


def second_kernel(keys_ref, turned_ref, asked_ref, own_ref, keep_ref):
    def store(index, partial):
        keep_ref[index] = held(partial)

    attend(0, keep_ref.shape[2], keys_ref, turned_ref, asked_ref, store)
    keep_ref[0] = held(joined(taken(keep_ref[0]), taken(own_ref[...])))


def join_kernel(keep_ref, got_ref, send_ref, next_ref):
    for index in range(keep_ref.shape[0]):
        partial = joined(taken(keep_ref[index]), unpacked(got_ref[index]))
        if index % 2 == 1:
            send_ref[index // 2] = packed(partial)
        else:
            next_ref[index // 2] = held(partial)


def settle(plan, handed, pages, sems):
    receivers = lax.axis_size("seq")
    me = lax.axis_index("seq")
    rows = pages.shape[0] // receivers
    copies = []
    for index, (k, start, slots) in enumerate(plan):
        size = handed[index].shape[0]
        sender = source(me, k, receivers) if k else me
        first = pl.multiple_of(sender * rows + start * (size // slots), size)
        copies.append(pltpu.make_async_copy(handed[index], pages.at[pl.ds(first, size), :], sems.at[index]))
        copies[-1].start()
    return copies


def settle_kernel(plan, *refs):
    *handed, pages, sems = refs
    for copy in settle(plan, handed, pages, sems):
        copy.wait()


def finish_kernel(plan, keep_ref, got_ref, _, *refs):
    *handed, out_any, pages, out_ref, sems = refs
    copies = settle(plan, handed, pages, sems)
    summed, _, total = joined(taken(keep_ref[0]), unpacked(got_ref[0]))
    out_ref[...] = (summed / total).T.astype(jnp.bfloat16)
    copies.append(pltpu.make_async_copy(out_ref, out_any, sems.at[len(copies)]))
    copies[-1].start()
    for copy in copies:
        copy.wait()


def in_hbm(arrays):
    return [pltpu.with_memory_space_constraint(array, pltpu.HBM) for array in arrays]


def per_device(lengths, owner_map, row_request, deltas, anchors, scales, queries, new_kv):
    blocks = anchors.shape[0]
    tokens = deltas.shape[0]
    senders = lax.axis_size("seq")
    me = lax.axis_index("seq")
    rows, steps, _ = queries.shape
    rows_dev = new_kv.shape[0]
    width = rows_dev * GQ * steps
    small = pltpu.CompilerParams(vmem_limit_bytes=8 * 1024 * 1024)

    flat_deltas = deltas.reshape(tokens * 2, HD)
    flat_anchors = anchors.reshape(blocks * 2, HD)
    flat_queries = queries.reshape(rows, steps, GQ, HD).transpose(0, 2, 1, 3).reshape(-1, HD)
    flat_new = new_kv.reshape(rows_dev * 4, HD)

    whole = jax.ShapeDtypeStruct((tokens * 2, HD), jnp.bfloat16)
    ahead, behind, own = messages(senders, blocks // senders)
    block_rows = tokens * 2 // blocks

    def place(plan, deltas):
        return pl.pallas_call(
            functools.partial(place_kernel, plan),
            out_shape=[jax.ShapeDtypeStruct((slots * block_rows, HD), jnp.bfloat16) for _, _, slots in plan],
            in_specs=[HBM] * 4,
            out_specs=[VMEM] * len(plan),
            scratch_shapes=[
                pltpu.SMEM((blocks,), jnp.int32),
                pltpu.SMEM((blocks,), jnp.int32),
                pltpu.SMEM((senders,), jnp.int32),
                pltpu.VMEM((tokens * 2, HD), jnp.bfloat16),
                pltpu.VMEM((blocks * 2, HD), jnp.float32),
                pltpu.VMEM((2, HD), jnp.float32),
                pltpu.SemaphoreType.DMA((7,)),
            ],
            compiler_params=small,
            name="place",
        )(*in_hbm([owner_map, deltas, flat_anchors, scales]))

    sent = place(ahead, flat_deltas)
    sent, late_deltas = lax.optimization_barrier((sent, flat_deltas))
    got_ahead = [hand(message, k) for message, (k, _, _) in zip(sent, ahead)]

    def leaving(count):
        return jax.ShapeDtypeStruct((count // 2, *message_shape(width)), jnp.bfloat16)

    def staying(count):
        return jax.ShapeDtypeStruct((count // 2, HD + KEEP_ROWS, width), jnp.float32)

    needed = (late_deltas, flat_anchors, scales, lengths, row_request, flat_queries, flat_new)
    roomy = pltpu.CompilerParams(vmem_limit_bytes=32 * 1024 * 1024)
    send, *common = pl.pallas_call(
        first_kernel,
        out_shape=[
            leaving(senders),
            jax.ShapeDtypeStruct((tokens, 2 * HD), jnp.bfloat16),
            jax.ShapeDtypeStruct((HD, tokens), jnp.bfloat16),
            jax.ShapeDtypeStruct((rows * GQ * steps, 2 * HD), jnp.bfloat16),
            jax.ShapeDtypeStruct((HD + KEEP_ROWS, width), jnp.float32),
        ],
        in_specs=[HBM] * len(needed),
        out_specs=[VMEM] * 5,
        scratch_shapes=[
            (pltpu.SMEM if array.dtype == jnp.int32 else pltpu.VMEM)(array.shape, array.dtype)
            for array in needed
        ]
        + [
            pltpu.VMEM((tokens * 2 + 16, HD), jnp.float32),
            pltpu.VMEM((tokens, HD), jnp.bfloat16),
            pltpu.SemaphoreType.DMA((len(needed),)),
        ],
        compiler_params=roomy,
        name="attend_leaving",
    )(*in_hbm(needed))

    k, count = 1, senders // 2
    send, late_deltas = lax.optimization_barrier((send, late_deltas))
    passed = exchange(send, k)
    *sent, mine = place(behind + own, late_deltas)
    keep = pl.pallas_call(
        second_kernel,
        out_shape=staying(senders),
        in_specs=[VMEM] * 4,
        out_specs=VMEM,
        compiler_params=roomy,
        name="attend_staying",
    )(*common)
    sent, keep = lax.optimization_barrier((sent, keep))
    got = got_ahead[1:] + [hand(message, partner) for message, (partner, _, _) in zip(sent, behind)]
    while count > 1:
        send, keep = pl.pallas_call(
            join_kernel,
            out_shape=[leaving(count), staying(count)],
            in_specs=[VMEM] * 2,
            out_specs=[VMEM] * 2,
            compiler_params=small,
            name="join",
        )(keep, passed)
        k, count = 2 * k + 1, count // 2
        passed = exchange(send, k)
    settled = ahead[:1] + own
    pages = pl.pallas_call(
        functools.partial(settle_kernel, settled),
        out_shape=whole,
        in_specs=[ANY] * len(settled),
        out_specs=HBM,
        scratch_shapes=[pltpu.SemaphoreType.DMA((len(settled),))],
        compiler_params=small,
        name="settle",
    )(got_ahead[0], mine)
    attended, pages = pl.pallas_call(
        functools.partial(finish_kernel, ahead[1:] + behind),
        out_shape=[jax.ShapeDtypeStruct((width, HD), jnp.bfloat16), whole],
        in_specs=[VMEM] * 2 + [HBM] + [ANY] * len(got),
        out_specs=[HBM, HBM],
        scratch_shapes=[
            pltpu.VMEM((width, HD), jnp.bfloat16),
            pltpu.SemaphoreType.DMA((len(got) + 1,)),
        ],
        input_output_aliases={2: 1},
        compiler_params=small,
        name="finish",
    )(keep, passed, pages, *got)
    pages = pages.reshape(blocks, tokens // blocks, 2, HD)
    attended = (
        attended.reshape(rows_dev, GQ, steps, HD).transpose(0, 2, 1, 3).reshape(rows_dev, steps, GQ * HD)
    )
    return pages, attended


def solution(mesh):
    placed = (
        P("groups"),
        P(("groups", "seq")),
        P("groups"),
        P(("groups", "seq"), None, "tp"),
        P(("groups", "seq"), None, "tp"),
        P("groups", "tp"),
        P("groups", None, "tp"),
        P(("groups", "seq"), None, None, "tp"),
    )
    return jax.shard_map(
        per_device,
        mesh=mesh,
        in_specs=placed,
        out_specs=(P(("groups", "seq"), None, None, "tp"), P(("groups", "seq"), None, "tp")),
        check_vma=False,
    )
```

```python
import functools

import jax
import jax.numpy as jnp
from jax import lax
from jax.experimental import pallas as pl
from jax.experimental.pallas import tpu as pltpu
from jax.sharding import PartitionSpec as P

HD = 128
GQ = 8
STEPS = 2
STAT_ROWS = 6
KEEP_ROWS = 8
FAR = -1e30
RATE = HD ** (-0.5) * 1.4426950408889634

VMEM = pl.BlockSpec(memory_space=pltpu.VMEM)
HBM = pl.BlockSpec(memory_space=pltpu.HBM)
ANY = pl.BlockSpec(memory_space=pl.ANY)
SMEM = pl.BlockSpec(memory_space=pltpu.SMEM)


def inner(device, count):
    return (device ^ (device // (count // 2))) & 1


def partner(device, k, count):
    far = count // 2
    if k == far:
        return device ^ (1 + inner(device, count) * (far - 1))
    if k == 1:
        return device ^ (far - inner(device, count) * (far - 1))
    return device ^ k


def source(device, k, count):
    far = count // 2
    if k == far:
        return device ^ (far - inner(device, count) * (far - 1))
    if k == 1:
        return device ^ (1 + inner(device, count) * (far - 1))
    return device ^ k


def exchange(message, k):
    count = lax.axis_size("seq")
    last = k == count - 1
    return lax.ppermute(message, "seq", [(i, i ^ k ^ (last and i < count // 2)) for i in range(count)])


def hand(message, k):
    count = lax.axis_size("seq")
    return lax.ppermute(message, "seq", [(i, partner(i, k, count)) for i in range(count)])


def messages(count, capacity):
    half = capacity // 2
    ahead = [(k, 0, capacity) for k in range(count // 2, count)]
    behind = [(k, first, half) for k in reversed(range(1, count // 2)) for first in (0, half)]
    return ahead, behind, [(0, 0, capacity)]


def place_kernel(plan, owner_any, deltas_any, anchors_any, scales_any, *refs):
    receivers = lax.axis_size("seq")
    me = lax.axis_index("seq")
    outs = refs[:-7]
    owner_ref, source_ref, count_ref, deltas_ref, anchors_ref, scales_ref, sems = refs[-7:]
    blocks = owner_ref.shape[0]
    rows = deltas_ref.shape[0] // blocks
    capacity = blocks // receivers
    quarter = deltas_ref.shape[0] // 4
    parts = [pl.ds(index * quarter, quarter) for index in range(4)]
    loads = [
        pltpu.make_async_copy(source, target, sems.at[index])
        for index, (source, target) in enumerate(
            [(owner_any, owner_ref), (scales_any, scales_ref), (anchors_any, anchors_ref)]
            + [(deltas_any.at[part], deltas_ref.at[part]) for part in parts]
        )
    ]
    for load in loads:
        load.start()
    bits = capacity.bit_length()
    narrow = receivers * bits < 32
    if not narrow:
        for owner in range(receivers):
            count_ref[owner] = owner * capacity
    loads[0].wait()

    def find(block, counts):
        owner = owner_ref[block]
        if narrow:
            shift = owner * bits
            slot = owner * capacity + ((counts >> shift) & ((1 << bits) - 1))
            counts = counts + (jnp.int32(1) << shift)
        else:
            slot = count_ref[owner]
            count_ref[owner] = slot + 1
        source_ref[slot] = block
        return counts

    lax.fori_loop(0, blocks, find, jnp.int32(0), unroll=16)
    for load in loads[1:]:
        load.wait()
    odd = lax.broadcasted_iota(jnp.int32, (8, HD), 0) % 2 == 1
    scale = jnp.where(odd, scales_ref[1:2, :], scales_ref[0:1, :])[None]
    for (k, start, count), out_ref in zip(plan, outs):
        first = partner(me, k, receivers) * capacity + start

        def one_slot(slot, carry, first=first, out_ref=out_ref):
            block = source_ref[first + slot]
            anchor = jnp.where(
                odd, anchors_ref[pl.ds(2 * block + 1, 1), :], anchors_ref[pl.ds(2 * block, 1), :]
            )[None]
            here = pl.ds(pl.multiple_of(block * rows, rows), rows)
            delta = deltas_ref[here, :].astype(jnp.float32)
            decoded = anchor + scale * delta.reshape(rows // 8, 8, HD)
            out_ref[pl.ds(pl.multiple_of(slot * rows, rows), rows), :] = decoded.reshape(rows, HD).astype(
                jnp.bfloat16
            )
            return carry

        lax.fori_loop(0, count, one_slot, 0, unroll=min(16, count))


def pieces(values):
    high = values.astype(jnp.bfloat16)
    rest = values - high.astype(jnp.float32)
    middle = rest.astype(jnp.bfloat16)
    low = (rest - middle.astype(jnp.float32)).astype(jnp.bfloat16)
    return [high, middle, low]


def message_shape(width):
    parts = max(1, width // HD)
    return parts * HD + -(-parts * STAT_ROWS // 16) * 16, width // parts


def packed(partial):
    summed, top, total = partial
    rows, lanes = message_shape(top.shape[1])
    sums = summed.astype(jnp.bfloat16)
    stats = pieces(top) + pieces(total)
    here = [slice(first, first + lanes) for first in range(0, top.shape[1], lanes)]
    filled = [sums[:, part] for part in here] + [row[:, part] for part in here for row in stats]
    rest = rows - len(here) * (HD + STAT_ROWS)
    return jnp.concatenate(filled + [jnp.zeros((rest, lanes), jnp.bfloat16)], axis=0)


def unpacked(block):
    parts = block.shape[0] // HD
    sums = [block[part * HD : (part + 1) * HD, :] for part in range(parts)]
    stats = block[parts * HD :, :].astype(jnp.float32)

    def row(first):
        found = []
        for part in range(parts):
            at = part * STAT_ROWS + first
            found.append(stats[at : at + 1] + stats[at + 1 : at + 2] + stats[at + 2 : at + 3])
        return jnp.concatenate(found, axis=1)

    return jnp.concatenate(sums, axis=1).astype(jnp.float32), row(0), row(3)


def held(partial):
    summed, top, total = partial
    rest = jnp.zeros((KEEP_ROWS - 2, top.shape[1]), jnp.float32)
    return jnp.concatenate([summed, top, total, rest], axis=0)


def taken(block):
    return block[0:HD, :], block[HD : HD + 1, :], block[HD + 1 : HD + 2, :]


def joined(one, other):
    top = jnp.maximum(one[1], other[1])
    scale_one = jnp.exp2((one[1] - top) * RATE)
    scale_other = jnp.exp2((other[1] - top) * RATE)
    return (
        one[0] * scale_one + other[0] * scale_other,
        top,
        one[2] * scale_one + other[2] * scale_other,
    )


def difference(index):
    total = 0
    while index:
        total, index = total ^ index, index >> 1
    return total


def attend(parity, width, keys_ref, turned_ref, asked_ref, store):
    me = lax.axis_index("seq")
    far = lax.axis_size("seq") // 2
    lower = 1 - me // far
    asked = asked_ref.shape[0]

    def partial_of(here):
        scores = lax.dot_general(
            keys_ref[...], here, (((1,), (1,)), ((), ())), preferred_element_type=jnp.float32
        )
        top = jnp.max(scores, axis=0, keepdims=True)
        weights = jnp.exp2((scores - top) * RATE)
        total = jnp.sum(weights, axis=0, keepdims=True)
        summed = jnp.dot(turned_ref[...], weights.astype(jnp.bfloat16), preferred_element_type=jnp.float32)
        return summed, top, total

    if width % HD == 0:
        for index in range(asked // width // 2):
            place = 2 * index + parity
            there = (me ^ difference(place) ^ (lower if place >= far else 0)) * width
            store(index, partial_of(asked_ref[pl.ds(pl.multiple_of(there, width), width), :]))
        return
    tile = min(2 * HD, asked)
    parts = tile // width

    def one_tile(tile_index, carry):
        here = asked_ref[pl.ds(pl.multiple_of(tile_index * tile, tile), tile), :]
        summed, top, total = partial_of(here)
        for part in range(parts):
            lanes = slice(part * width, (part + 1) * width)
            apart = (tile_index * parts + part) ^ me
            apart = apart ^ (apart // far * lower)
            place = apart ^ (apart >> 1)

            @pl.when(place % 2 == parity)
            def _(lanes=lanes, place=place):
                store(place // 2, (summed[:, lanes], top[:, lanes], total[:, lanes]))

        return carry

    lax.fori_loop(0, asked // tile, one_tile, 0)


def first_kernel(*refs):
    me = lax.axis_index("seq")
    sources, send_ref, keys_ref, turned_ref, asked_ref, own_ref, *targets = refs[:7], *refs[7:-3]
    wide_ref, values_ref, sems = refs[-3:]
    loads = [
        pltpu.make_async_copy(source, target, sems.at[index])
        for index, (source, target) in enumerate(zip(sources, targets))
    ]
    for load in loads:
        load.start()
    deltas_ref, anchors_ref, scales_ref, lengths_ref, request_ref, queries_ref, new_ref = targets
    blocks = anchors_ref.shape[0] // 2
    rows = deltas_ref.shape[0] // blocks
    tokens = rows // 2
    requests = lengths_ref.shape[0]
    asked = queries_ref.shape[0]
    per_row = asked // request_ref.shape[0]
    width = own_ref.shape[1]
    for load in loads[2:]:
        load.wait()

    lane = lax.broadcasted_iota(jnp.int32, (1, HD), 1)
    first = jnp.zeros((1, HD), jnp.int32)
    last = jnp.zeros((1, HD), jnp.int32)
    end = 0 - me * (blocks * tokens)
    for request in range(requests):
        start = end
        end = end + lengths_ref[request]
        first = jnp.where(lane == request, start, first)
        last = jnp.where(lane == request, end, last)
    place = lax.broadcasted_iota(jnp.int32, (blocks * tokens, HD), 0)
    keys_ref[:, HD:] = jnp.where((place >= first) & (place < last), 1.0, 0.0).astype(jnp.bfloat16)

    asked_ref[:, 0:HD] = queries_ref[...]
    wide_lane = lax.broadcasted_iota(jnp.int32, (per_row, HD), 1)

    def one_row(row, carry):
        asked_ref[pl.ds(pl.multiple_of(row * per_row, per_row), per_row), HD:] = jnp.where(
            (wide_lane == request_ref[row]) | (wide_lane >= requests), 0.0, FAR
        ).astype(jnp.bfloat16)
        return carry

    lax.fori_loop(0, request_ref.shape[0], one_row, 0, unroll=16)

    fresh = new_ref.shape[0] // 4
    new = new_ref[...].astype(jnp.float32).reshape(fresh, 4, HD)
    mine = queries_ref[pl.ds(pl.multiple_of(me * width, width), width), :]
    of_row = lax.broadcasted_iota(jnp.int32, (fresh, width), 1) // (GQ * STEPS)
    same = of_row == lax.broadcasted_iota(jnp.int32, (fresh, width), 0)
    step = lax.broadcasted_iota(jnp.int32, (1, width), 1) % STEPS
    own_scores = []
    for which in range(STEPS):
        scored = lax.dot_general(
            new[:, 2 * which, :].astype(jnp.bfloat16),
            mine,
            (((1,), (1,)), ((), ())),
            preferred_element_type=jnp.float32,
        )
        picked = jnp.sum(jnp.where(same, scored, 0.0), axis=0, keepdims=True)
        own_scores.append(jnp.where(step >= which, picked, FAR))
    own_top = jnp.maximum(own_scores[0], own_scores[1])
    own_total = jnp.zeros((1, width), jnp.float32)
    own_summed = jnp.zeros((HD, width), jnp.float32)
    for which in range(STEPS):
        weight = jnp.exp2((own_scores[which] - own_top) * RATE)
        own_total = own_total + weight
        spread = jnp.where(same, weight, 0.0).astype(jnp.bfloat16)
        own_summed = own_summed + lax.dot_general(
            new[:, 2 * which + 1, :].astype(jnp.bfloat16),
            spread,
            (((0,), (0,)), ((), ())),
            preferred_element_type=jnp.float32,
        )
    own_ref[...] = held((own_summed, own_top, own_total))

    for load in loads[:2]:
        load.wait()
    wide_ref[0 : blocks * rows, :] = deltas_ref[...].astype(jnp.float32)
    scale_key = scales_ref[0:1, :]
    scale_value = scales_ref[1:2, :]

    def one_block(block, carry):
        here = pl.ds(pl.multiple_of(block * tokens, tokens), tokens)
        key = wide_ref[pl.ds(block * rows, tokens, stride=2), :]
        value = wide_ref[pl.ds(block * rows + 1, tokens, stride=2), :]
        keys_ref[here, 0:HD] = (anchors_ref[pl.ds(2 * block, 1), :] + scale_key * key).astype(jnp.bfloat16)
        values_ref[here, :] = (anchors_ref[pl.ds(2 * block + 1, 1), :] + scale_value * value).astype(
            jnp.bfloat16
        )
        return carry

    lax.fori_loop(0, blocks, one_block, 0, unroll=16)
    turned_ref[...] = values_ref[...].T

    def store(index, partial):
        send_ref[index] = packed(partial)

    attend(1, width, keys_ref, turned_ref, asked_ref, store)


def second_kernel(keys_ref, turned_ref, asked_ref, own_ref, keep_ref):
    def store(index, partial):
        keep_ref[index] = held(partial)

    attend(0, keep_ref.shape[2], keys_ref, turned_ref, asked_ref, store)
    keep_ref[0] = held(joined(taken(keep_ref[0]), taken(own_ref[...])))


def join_kernel(keep_ref, got_ref, send_ref, next_ref):
    for index in range(keep_ref.shape[0]):
        partial = joined(taken(keep_ref[index]), unpacked(got_ref[index]))
        if index % 2 == 1:
            send_ref[index // 2] = packed(partial)
        else:
            next_ref[index // 2] = held(partial)


def settle(plan, handed, pages, sems):
    receivers = lax.axis_size("seq")
    me = lax.axis_index("seq")
    rows = pages.shape[0] // receivers
    copies = []
    for index, (k, start, slots) in enumerate(plan):
        size = handed[index].shape[0]
        sender = source(me, k, receivers) if k else me
        first = pl.multiple_of(sender * rows + start * (size // slots), size)
        copies.append(pltpu.make_async_copy(handed[index], pages.at[pl.ds(first, size), :], sems.at[index]))
        copies[-1].start()
    return copies


def settle_kernel(plan, *refs):
    *handed, pages, sems = refs
    for copy in settle(plan, handed, pages, sems):
        copy.wait()


def finish_kernel(plan, keep_ref, got_ref, _, *refs):
    *handed, out_any, pages, out_ref, sems = refs
    copies = settle(plan, handed, pages, sems)
    summed, _, total = joined(taken(keep_ref[0]), unpacked(got_ref[0]))
    out_ref[...] = (summed / total).T.astype(jnp.bfloat16)
    copies.append(pltpu.make_async_copy(out_ref, out_any, sems.at[len(copies)]))
    copies[-1].start()
    for copy in copies:
        copy.wait()


def in_hbm(arrays):
    return [pltpu.with_memory_space_constraint(array, pltpu.HBM) for array in arrays]


def per_device(lengths, owner_map, row_request, deltas, anchors, scales, queries, new_kv):
    blocks = anchors.shape[0]
    tokens = deltas.shape[0]
    senders = lax.axis_size("seq")
    me = lax.axis_index("seq")
    rows, steps, _ = queries.shape
    rows_dev = new_kv.shape[0]
    width = rows_dev * GQ * steps
    small = pltpu.CompilerParams(vmem_limit_bytes=8 * 1024 * 1024)

    flat_deltas = deltas.reshape(tokens * 2, HD)
    flat_anchors = anchors.reshape(blocks * 2, HD)
    flat_queries = queries.reshape(rows, steps, GQ, HD).transpose(0, 2, 1, 3).reshape(-1, HD)
    flat_new = new_kv.reshape(rows_dev * 4, HD)

    whole = jax.ShapeDtypeStruct((tokens * 2, HD), jnp.bfloat16)
    ahead, behind, own = messages(senders, blocks // senders)
    block_rows = tokens * 2 // blocks

    def place(plan, deltas):
        return pl.pallas_call(
            functools.partial(place_kernel, plan),
            out_shape=[jax.ShapeDtypeStruct((slots * block_rows, HD), jnp.bfloat16) for _, _, slots in plan],
            in_specs=[HBM] * 4,
            out_specs=[VMEM] * len(plan),
            scratch_shapes=[
                pltpu.SMEM((blocks,), jnp.int32),
                pltpu.SMEM((blocks,), jnp.int32),
                pltpu.SMEM((senders,), jnp.int32),
                pltpu.VMEM((tokens * 2, HD), jnp.bfloat16),
                pltpu.VMEM((blocks * 2, HD), jnp.float32),
                pltpu.VMEM((2, HD), jnp.float32),
                pltpu.SemaphoreType.DMA((7,)),
            ],
            compiler_params=small,
            name="place",
        )(*in_hbm([owner_map, deltas, flat_anchors, scales]))

    sent = place(ahead, flat_deltas)
    sent, late_deltas = lax.optimization_barrier((sent, flat_deltas))
    got_ahead = [hand(message, k) for message, (k, _, _) in zip(sent, ahead)]

    def leaving(count):
        return jax.ShapeDtypeStruct((count // 2, *message_shape(width)), jnp.bfloat16)

    def staying(count):
        return jax.ShapeDtypeStruct((count // 2, HD + KEEP_ROWS, width), jnp.float32)

    needed = (late_deltas, flat_anchors, scales, lengths, row_request, flat_queries, flat_new)
    roomy = pltpu.CompilerParams(vmem_limit_bytes=32 * 1024 * 1024)
    send, *common = pl.pallas_call(
        first_kernel,
        out_shape=[
            leaving(senders),
            jax.ShapeDtypeStruct((tokens, 2 * HD), jnp.bfloat16),
            jax.ShapeDtypeStruct((HD, tokens), jnp.bfloat16),
            jax.ShapeDtypeStruct((rows * GQ * steps, 2 * HD), jnp.bfloat16),
            jax.ShapeDtypeStruct((HD + KEEP_ROWS, width), jnp.float32),
        ],
        in_specs=[HBM] * len(needed),
        out_specs=[VMEM] * 5,
        scratch_shapes=[
            (pltpu.SMEM if array.dtype == jnp.int32 else pltpu.VMEM)(array.shape, array.dtype)
            for array in needed
        ]
        + [
            pltpu.VMEM((tokens * 2 + 16, HD), jnp.float32),
            pltpu.VMEM((tokens, HD), jnp.bfloat16),
            pltpu.SemaphoreType.DMA((len(needed),)),
        ],
        compiler_params=roomy,
        name="attend_leaving",
    )(*in_hbm(needed))

    k, count = 1, senders // 2
    send, late_deltas = lax.optimization_barrier((send, late_deltas))
    passed = exchange(send, k)
    *sent, mine = place(behind + own, late_deltas)
    keep = pl.pallas_call(
        second_kernel,
        out_shape=staying(senders),
        in_specs=[VMEM] * 4,
        out_specs=VMEM,
        compiler_params=roomy,
        name="attend_staying",
    )(*common)
    sent, keep = lax.optimization_barrier((sent, keep))
    got = got_ahead[1:] + [hand(message, partner) for message, (partner, _, _) in zip(sent, behind)]
    while count > 1:
        send, keep = pl.pallas_call(
            join_kernel,
            out_shape=[leaving(count), staying(count)],
            in_specs=[VMEM] * 2,
            out_specs=[VMEM] * 2,
            compiler_params=small,
            name="join",
        )(keep, passed)
        k, count = 2 * k + 1, count // 2
        passed = exchange(send, k)
    settled = ahead[:1] + behind + own
    pages = pl.pallas_call(
        functools.partial(settle_kernel, settled),
        out_shape=whole,
        in_specs=[ANY] * len(settled),
        out_specs=HBM,
        scratch_shapes=[pltpu.SemaphoreType.DMA((len(settled),))],
        compiler_params=small,
        name="settle",
    )(got_ahead[0], *got[len(ahead) - 1 :], mine)
    attended, pages = pl.pallas_call(
        functools.partial(finish_kernel, ahead[1:]),
        out_shape=[jax.ShapeDtypeStruct((width, HD), jnp.bfloat16), whole],
        in_specs=[VMEM] * 2 + [HBM] + [ANY] * len(ahead[1:]),
        out_specs=[HBM, HBM],
        scratch_shapes=[
            pltpu.VMEM((width, HD), jnp.bfloat16),
            pltpu.SemaphoreType.DMA((len(ahead),)),
        ],
        input_output_aliases={2: 1},
        compiler_params=small,
        name="finish",
    )(keep, passed, pages, *got_ahead[1:])
    pages = pages.reshape(blocks, tokens // blocks, 2, HD)
    attended = (
        attended.reshape(rows_dev, GQ, steps, HD).transpose(0, 2, 1, 3).reshape(rows_dev, steps, GQ * HD)
    )
    return pages, attended


def solution(mesh):
    placed = (
        P("groups"),
        P(("groups", "seq")),
        P("groups"),
        P(("groups", "seq"), None, "tp"),
        P(("groups", "seq"), None, "tp"),
        P("groups", "tp"),
        P("groups", None, "tp"),
        P(("groups", "seq"), None, None, "tp"),
    )
    return jax.shard_map(
        per_device,
        mesh=mesh,
        in_specs=placed,
        out_specs=(P(("groups", "seq"), None, None, "tp"), P(("groups", "seq"), None, "tp")),
        check_vma=False,
    )
```

```python
import functools

import jax
import jax.numpy as jnp
from jax import lax
from jax.experimental import pallas as pl
from jax.experimental.pallas import tpu as pltpu
from jax.sharding import PartitionSpec as P

HD = 128
GQ = 8
STEPS = 2
STAT_ROWS = 6
KEEP_ROWS = 8
FAR = -1e30
RATE = HD ** (-0.5) * 1.4426950408889634

VMEM = pl.BlockSpec(memory_space=pltpu.VMEM)
HBM = pl.BlockSpec(memory_space=pltpu.HBM)
ANY = pl.BlockSpec(memory_space=pl.ANY)
SMEM = pl.BlockSpec(memory_space=pltpu.SMEM)


def inner(device, count):
    return (device ^ (device // (count // 2))) & 1


def partner(device, k, count):
    far = count // 2
    if k == far:
        return device ^ (1 + inner(device, count) * (far - 1))
    if k == 1:
        return device ^ (far - inner(device, count) * (far - 1))
    return device ^ k


def source(device, k, count):
    far = count // 2
    if k == far:
        return device ^ (far - inner(device, count) * (far - 1))
    if k == 1:
        return device ^ (1 + inner(device, count) * (far - 1))
    return device ^ k


def exchange(message, k):
    count = lax.axis_size("seq")
    return lax.ppermute(message, "seq", [(i, i ^ k) for i in range(count)])


def hand(message, k):
    count = lax.axis_size("seq")
    return lax.ppermute(message, "seq", [(i, partner(i, k, count)) for i in range(count)])


def messages(count, capacity):
    half = capacity // 2
    ahead = [(k, 0, capacity) for k in range(count // 2, count)]
    behind = [(k, first, half) for k in reversed(range(1, count // 2)) for first in (0, half)]
    return ahead, behind, [(0, 0, capacity)]


def place_kernel(plan, owner_any, deltas_any, anchors_any, scales_any, *refs):
    receivers = lax.axis_size("seq")
    me = lax.axis_index("seq")
    outs = refs[:-7]
    owner_ref, source_ref, count_ref, deltas_ref, anchors_ref, scales_ref, sems = refs[-7:]
    blocks = owner_ref.shape[0]
    rows = deltas_ref.shape[0] // blocks
    capacity = blocks // receivers
    quarter = deltas_ref.shape[0] // 4
    parts = [pl.ds(index * quarter, quarter) for index in range(4)]
    loads = [
        pltpu.make_async_copy(source, target, sems.at[index])
        for index, (source, target) in enumerate(
            [(owner_any, owner_ref), (scales_any, scales_ref), (anchors_any, anchors_ref)]
            + [(deltas_any.at[part], deltas_ref.at[part]) for part in parts]
        )
    ]
    for load in loads:
        load.start()
    bits = capacity.bit_length()
    narrow = receivers * bits < 32
    if not narrow:
        for owner in range(receivers):
            count_ref[owner] = owner * capacity
    loads[0].wait()

    def find(block, counts):
        owner = owner_ref[block]
        if narrow:
            shift = owner * bits
            slot = owner * capacity + ((counts >> shift) & ((1 << bits) - 1))
            counts = counts + (jnp.int32(1) << shift)
        else:
            slot = count_ref[owner]
            count_ref[owner] = slot + 1
        source_ref[slot] = block
        return counts

    lax.fori_loop(0, blocks, find, jnp.int32(0), unroll=16)
    for load in loads[1:]:
        load.wait()
    odd = lax.broadcasted_iota(jnp.int32, (8, HD), 0) % 2 == 1
    scale = jnp.where(odd, scales_ref[1:2, :], scales_ref[0:1, :])[None]
    for (k, start, count), out_ref in zip(plan, outs):
        first = partner(me, k, receivers) * capacity + start

        def one_slot(slot, carry, first=first, out_ref=out_ref):
            block = source_ref[first + slot]
            anchor = jnp.where(
                odd, anchors_ref[pl.ds(2 * block + 1, 1), :], anchors_ref[pl.ds(2 * block, 1), :]
            )[None]
            here = pl.ds(pl.multiple_of(block * rows, rows), rows)
            delta = deltas_ref[here, :].astype(jnp.float32)
            decoded = anchor + scale * delta.reshape(rows // 8, 8, HD)
            out_ref[pl.ds(pl.multiple_of(slot * rows, rows), rows), :] = decoded.reshape(rows, HD).astype(
                jnp.bfloat16
            )
            return carry

        lax.fori_loop(0, count, one_slot, 0, unroll=min(16, count))


def pieces(values):
    high = values.astype(jnp.bfloat16)
    rest = values - high.astype(jnp.float32)
    middle = rest.astype(jnp.bfloat16)
    low = (rest - middle.astype(jnp.float32)).astype(jnp.bfloat16)
    return [high, middle, low]


def message_shape(width):
    parts = max(1, width // HD)
    return parts * HD + -(-parts * STAT_ROWS // 16) * 16, width // parts


def packed(partial):
    summed, top, total = partial
    rows, lanes = message_shape(top.shape[1])
    sums = summed.astype(jnp.bfloat16)
    stats = pieces(top) + pieces(total)
    here = [slice(first, first + lanes) for first in range(0, top.shape[1], lanes)]
    filled = [sums[:, part] for part in here] + [row[:, part] for part in here for row in stats]
    rest = rows - len(here) * (HD + STAT_ROWS)
    return jnp.concatenate(filled + [jnp.zeros((rest, lanes), jnp.bfloat16)], axis=0)


def unpacked(block):
    parts = block.shape[0] // HD
    sums = [block[part * HD : (part + 1) * HD, :] for part in range(parts)]
    stats = block[parts * HD :, :].astype(jnp.float32)

    def row(first):
        found = []
        for part in range(parts):
            at = part * STAT_ROWS + first
            found.append(stats[at : at + 1] + stats[at + 1 : at + 2] + stats[at + 2 : at + 3])
        return jnp.concatenate(found, axis=1)

    return jnp.concatenate(sums, axis=1).astype(jnp.float32), row(0), row(3)


def held(partial):
    summed, top, total = partial
    rest = jnp.zeros((KEEP_ROWS - 2, top.shape[1]), jnp.float32)
    return jnp.concatenate([summed, top, total, rest], axis=0)


def taken(block):
    return block[0:HD, :], block[HD : HD + 1, :], block[HD + 1 : HD + 2, :]


def joined(one, other):
    top = jnp.maximum(one[1], other[1])
    scale_one = jnp.exp2((one[1] - top) * RATE)
    scale_other = jnp.exp2((other[1] - top) * RATE)
    return (
        one[0] * scale_one + other[0] * scale_other,
        top,
        one[2] * scale_one + other[2] * scale_other,
    )


def difference(index):
    total = 0
    while index:
        total, index = total ^ index, index >> 1
    return total


def attend(parity, width, keys_ref, turned_ref, asked_ref, store):
    me = lax.axis_index("seq")
    asked = asked_ref.shape[0]

    def partial_of(here):
        scores = lax.dot_general(
            keys_ref[...], here, (((1,), (1,)), ((), ())), preferred_element_type=jnp.float32
        )
        top = jnp.max(scores, axis=0, keepdims=True)
        weights = jnp.exp2((scores - top) * RATE)
        total = jnp.sum(weights, axis=0, keepdims=True)
        summed = jnp.dot(turned_ref[...], weights.astype(jnp.bfloat16), preferred_element_type=jnp.float32)
        return summed, top, total

    if width % HD == 0:
        for index in range(asked // width // 2):
            there = (me ^ difference(2 * index + parity)) * width
            store(index, partial_of(asked_ref[pl.ds(pl.multiple_of(there, width), width), :]))
        return
    tile = min(2 * HD, asked)
    parts = tile // width

    def one_tile(tile_index, carry):
        here = asked_ref[pl.ds(pl.multiple_of(tile_index * tile, tile), tile), :]
        summed, top, total = partial_of(here)
        for part in range(parts):
            lanes = slice(part * width, (part + 1) * width)
            apart = (tile_index * parts + part) ^ me
            place = apart ^ (apart >> 1)

            @pl.when(place % 2 == parity)
            def _(lanes=lanes, place=place):
                store(place // 2, (summed[:, lanes], top[:, lanes], total[:, lanes]))

        return carry

    lax.fori_loop(0, asked // tile, one_tile, 0)


def first_kernel(*refs):
    me = lax.axis_index("seq")
    sources, send_ref, keys_ref, turned_ref, asked_ref, own_ref, *targets = refs[:7], *refs[7:-3]
    wide_ref, values_ref, sems = refs[-3:]
    loads = [
        pltpu.make_async_copy(source, target, sems.at[index])
        for index, (source, target) in enumerate(zip(sources, targets))
    ]
    for load in loads:
        load.start()
    deltas_ref, anchors_ref, scales_ref, lengths_ref, request_ref, queries_ref, new_ref = targets
    blocks = anchors_ref.shape[0] // 2
    rows = deltas_ref.shape[0] // blocks
    tokens = rows // 2
    requests = lengths_ref.shape[0]
    asked = queries_ref.shape[0]
    per_row = asked // request_ref.shape[0]
    width = own_ref.shape[1]
    for load in loads[2:]:
        load.wait()

    lane = lax.broadcasted_iota(jnp.int32, (1, HD), 1)
    first = jnp.zeros((1, HD), jnp.int32)
    last = jnp.zeros((1, HD), jnp.int32)
    end = 0 - me * (blocks * tokens)
    for request in range(requests):
        start = end
        end = end + lengths_ref[request]
        first = jnp.where(lane == request, start, first)
        last = jnp.where(lane == request, end, last)
    place = lax.broadcasted_iota(jnp.int32, (blocks * tokens, HD), 0)
    keys_ref[:, HD:] = jnp.where((place >= first) & (place < last), 1.0, 0.0).astype(jnp.bfloat16)

    asked_ref[:, 0:HD] = queries_ref[...]
    wide_lane = lax.broadcasted_iota(jnp.int32, (per_row, HD), 1)

    def one_row(row, carry):
        asked_ref[pl.ds(pl.multiple_of(row * per_row, per_row), per_row), HD:] = jnp.where(
            (wide_lane == request_ref[row]) | (wide_lane >= requests), 0.0, FAR
        ).astype(jnp.bfloat16)
        return carry

    lax.fori_loop(0, request_ref.shape[0], one_row, 0, unroll=16)

    fresh = new_ref.shape[0] // 4
    new = new_ref[...].astype(jnp.float32).reshape(fresh, 4, HD)
    mine = queries_ref[pl.ds(pl.multiple_of(me * width, width), width), :]
    of_row = lax.broadcasted_iota(jnp.int32, (fresh, width), 1) // (GQ * STEPS)
    same = of_row == lax.broadcasted_iota(jnp.int32, (fresh, width), 0)
    step = lax.broadcasted_iota(jnp.int32, (1, width), 1) % STEPS
    own_scores = []
    for which in range(STEPS):
        scored = lax.dot_general(
            new[:, 2 * which, :].astype(jnp.bfloat16),
            mine,
            (((1,), (1,)), ((), ())),
            preferred_element_type=jnp.float32,
        )
        picked = jnp.sum(jnp.where(same, scored, 0.0), axis=0, keepdims=True)
        own_scores.append(jnp.where(step >= which, picked, FAR))
    own_top = jnp.maximum(own_scores[0], own_scores[1])
    own_total = jnp.zeros((1, width), jnp.float32)
    own_summed = jnp.zeros((HD, width), jnp.float32)
    for which in range(STEPS):
        weight = jnp.exp2((own_scores[which] - own_top) * RATE)
        own_total = own_total + weight
        spread = jnp.where(same, weight, 0.0).astype(jnp.bfloat16)
        own_summed = own_summed + lax.dot_general(
            new[:, 2 * which + 1, :].astype(jnp.bfloat16),
            spread,
            (((0,), (0,)), ((), ())),
            preferred_element_type=jnp.float32,
        )
    own_ref[...] = held((own_summed, own_top, own_total))

    for load in loads[:2]:
        load.wait()
    wide_ref[0 : blocks * rows, :] = deltas_ref[...].astype(jnp.float32)
    scale_key = scales_ref[0:1, :]
    scale_value = scales_ref[1:2, :]

    def one_block(block, carry):
        here = pl.ds(pl.multiple_of(block * tokens, tokens), tokens)
        key = wide_ref[pl.ds(block * rows, tokens, stride=2), :]
        value = wide_ref[pl.ds(block * rows + 1, tokens, stride=2), :]
        keys_ref[here, 0:HD] = (anchors_ref[pl.ds(2 * block, 1), :] + scale_key * key).astype(jnp.bfloat16)
        values_ref[here, :] = (anchors_ref[pl.ds(2 * block + 1, 1), :] + scale_value * value).astype(
            jnp.bfloat16
        )
        return carry

    lax.fori_loop(0, blocks, one_block, 0, unroll=16)
    turned_ref[...] = values_ref[...].T

    def store(index, partial):
        send_ref[index] = packed(partial)

    attend(1, width, keys_ref, turned_ref, asked_ref, store)


def second_kernel(keys_ref, turned_ref, asked_ref, own_ref, keep_ref):
    def store(index, partial):
        keep_ref[index] = held(partial)

    attend(0, keep_ref.shape[2], keys_ref, turned_ref, asked_ref, store)
    keep_ref[0] = held(joined(taken(keep_ref[0]), taken(own_ref[...])))


def join_kernel(keep_ref, got_ref, send_ref, next_ref):
    for index in range(keep_ref.shape[0]):
        partial = joined(taken(keep_ref[index]), unpacked(got_ref[index]))
        if index % 2 == 1:
            send_ref[index // 2] = packed(partial)
        else:
            next_ref[index // 2] = held(partial)


def settle(plan, handed, pages, sems):
    receivers = lax.axis_size("seq")
    me = lax.axis_index("seq")
    rows = pages.shape[0] // receivers
    copies = []
    for index, (k, start, slots) in enumerate(plan):
        size = handed[index].shape[0]
        sender = source(me, k, receivers) if k else me
        first = pl.multiple_of(sender * rows + start * (size // slots), size)
        copies.append(pltpu.make_async_copy(handed[index], pages.at[pl.ds(first, size), :], sems.at[index]))
        copies[-1].start()
    return copies


def settle_kernel(plan, *refs):
    *handed, pages, sems = refs
    for copy in settle(plan, handed, pages, sems):
        copy.wait()


def finish_kernel(plan, keep_ref, got_ref, _, *refs):
    *handed, out_any, pages, out_ref, sems = refs
    copies = settle(plan, handed, pages, sems)
    summed, _, total = joined(taken(keep_ref[0]), unpacked(got_ref[0]))
    out_ref[...] = (summed / total).T.astype(jnp.bfloat16)
    copies.append(pltpu.make_async_copy(out_ref, out_any, sems.at[len(copies)]))
    copies[-1].start()
    for copy in copies:
        copy.wait()


def in_hbm(arrays):
    return [pltpu.with_memory_space_constraint(array, pltpu.HBM) for array in arrays]


def per_device(lengths, owner_map, row_request, deltas, anchors, scales, queries, new_kv):
    blocks = anchors.shape[0]
    tokens = deltas.shape[0]
    senders = lax.axis_size("seq")
    me = lax.axis_index("seq")
    rows, steps, _ = queries.shape
    rows_dev = new_kv.shape[0]
    width = rows_dev * GQ * steps
    small = pltpu.CompilerParams(vmem_limit_bytes=8 * 1024 * 1024)

    flat_deltas = deltas.reshape(tokens * 2, HD)
    flat_anchors = anchors.reshape(blocks * 2, HD)
    flat_queries = queries.reshape(rows, steps, GQ, HD).transpose(0, 2, 1, 3).reshape(-1, HD)
    flat_new = new_kv.reshape(rows_dev * 4, HD)

    whole = jax.ShapeDtypeStruct((tokens * 2, HD), jnp.bfloat16)
    ahead, behind, own = messages(senders, blocks // senders)
    block_rows = tokens * 2 // blocks

    def place(plan, deltas):
        return pl.pallas_call(
            functools.partial(place_kernel, plan),
            out_shape=[jax.ShapeDtypeStruct((slots * block_rows, HD), jnp.bfloat16) for _, _, slots in plan],
            in_specs=[HBM] * 4,
            out_specs=[VMEM] * len(plan),
            scratch_shapes=[
                pltpu.SMEM((blocks,), jnp.int32),
                pltpu.SMEM((blocks,), jnp.int32),
                pltpu.SMEM((senders,), jnp.int32),
                pltpu.VMEM((tokens * 2, HD), jnp.bfloat16),
                pltpu.VMEM((blocks * 2, HD), jnp.float32),
                pltpu.VMEM((2, HD), jnp.float32),
                pltpu.SemaphoreType.DMA((7,)),
            ],
            compiler_params=small,
            name="place",
        )(*in_hbm([owner_map, deltas, flat_anchors, scales]))

    sent = place(ahead, flat_deltas)
    sent, late_deltas = lax.optimization_barrier((sent, flat_deltas))
    got_ahead = [hand(message, k) for message, (k, _, _) in zip(sent, ahead)]

    def leaving(count):
        return jax.ShapeDtypeStruct((count // 2, *message_shape(width)), jnp.bfloat16)

    def staying(count):
        return jax.ShapeDtypeStruct((count // 2, HD + KEEP_ROWS, width), jnp.float32)

    needed = (late_deltas, flat_anchors, scales, lengths, row_request, flat_queries, flat_new)
    roomy = pltpu.CompilerParams(vmem_limit_bytes=32 * 1024 * 1024)
    send, *common = pl.pallas_call(
        first_kernel,
        out_shape=[
            leaving(senders),
            jax.ShapeDtypeStruct((tokens, 2 * HD), jnp.bfloat16),
            jax.ShapeDtypeStruct((HD, tokens), jnp.bfloat16),
            jax.ShapeDtypeStruct((rows * GQ * steps, 2 * HD), jnp.bfloat16),
            jax.ShapeDtypeStruct((HD + KEEP_ROWS, width), jnp.float32),
        ],
        in_specs=[HBM] * len(needed),
        out_specs=[VMEM] * 5,
        scratch_shapes=[
            (pltpu.SMEM if array.dtype == jnp.int32 else pltpu.VMEM)(array.shape, array.dtype)
            for array in needed
        ]
        + [
            pltpu.VMEM((tokens * 2 + 16, HD), jnp.float32),
            pltpu.VMEM((tokens, HD), jnp.bfloat16),
            pltpu.SemaphoreType.DMA((len(needed),)),
        ],
        compiler_params=roomy,
        name="attend_leaving",
    )(*in_hbm(needed))

    k, count = 1, senders // 2
    send, late_deltas = lax.optimization_barrier((send, late_deltas))
    passed = exchange(send, k)
    *sent, mine = place(behind + own, late_deltas)
    keep = pl.pallas_call(
        second_kernel,
        out_shape=staying(senders),
        in_specs=[VMEM] * 4,
        out_specs=VMEM,
        compiler_params=roomy,
        name="attend_staying",
    )(*common)
    sent, keep = lax.optimization_barrier((sent, keep))
    got = got_ahead[1:] + [hand(message, partner) for message, (partner, _, _) in zip(sent, behind)]
    while count > 1:
        send, keep = pl.pallas_call(
            join_kernel,
            out_shape=[leaving(count), staying(count)],
            in_specs=[VMEM] * 2,
            out_specs=[VMEM] * 2,
            compiler_params=small,
            name="join",
        )(keep, passed)
        k, count = 2 * k + 1, count // 2
        passed = exchange(send, k)
    settled = ahead[:1] + behind + own
    pages = pl.pallas_call(
        functools.partial(settle_kernel, settled),
        out_shape=whole,
        in_specs=[ANY] * len(settled),
        out_specs=HBM,
        scratch_shapes=[pltpu.SemaphoreType.DMA((len(settled),))],
        compiler_params=small,
        name="settle",
    )(got_ahead[0], *got[len(ahead) - 1 :], mine)
    attended, pages = pl.pallas_call(
        functools.partial(finish_kernel, ahead[1:]),
        out_shape=[jax.ShapeDtypeStruct((width, HD), jnp.bfloat16), whole],
        in_specs=[VMEM] * 2 + [HBM] + [ANY] * len(ahead[1:]),
        out_specs=[HBM, HBM],
        scratch_shapes=[
            pltpu.VMEM((width, HD), jnp.bfloat16),
            pltpu.SemaphoreType.DMA((len(ahead),)),
        ],
        input_output_aliases={2: 1},
        compiler_params=small,
        name="finish",
    )(keep, passed, pages, *got_ahead[1:])
    pages = pages.reshape(blocks, tokens // blocks, 2, HD)
    attended = (
        attended.reshape(rows_dev, GQ, steps, HD).transpose(0, 2, 1, 3).reshape(rows_dev, steps, GQ * HD)
    )
    return pages, attended


def solution(mesh):
    placed = (
        P("groups"),
        P(("groups", "seq")),
        P("groups"),
        P(("groups", "seq"), None, "tp"),
        P(("groups", "seq"), None, "tp"),
        P("groups", "tp"),
        P("groups", None, "tp"),
        P(("groups", "seq"), None, None, "tp"),
    )
    return jax.shard_map(
        per_device,
        mesh=mesh,
        in_specs=placed,
        out_specs=(P(("groups", "seq"), None, None, "tp"), P(("groups", "seq"), None, "tp")),
        check_vma=False,
    )
```
